32 devices in a mesh: seq: 16 (over z, x, core), dp: 2 (over y).
Axes of the slice: x: 2, y: 2, z: 4, core: 2. Of those that a mesh axis runs over, the one named last changes fastest.
Arguments:
- tokens: bfloat16 [2, 2048, 1024], P('dp', 'seq'), may hold values from -6 to 6
- w_qkv: bfloat16 [1024, 3072], P('seq'), may hold values from -0.1875 to 0.1875
- w_out: bfloat16 [1024, 1024], P('seq'), may hold values from -0.1875 to 0.1875
- w_up: bfloat16 [1024, 4096], P('seq'), may hold values from -0.1875 to 0.1875
- w_down: bfloat16 [4096, 1024], P('seq'), may hold values from -0.09375 to 0.09375
- norm_gains: bfloat16 [4, 1024], P(None, 'seq'), may hold values from 0.099609375 to 1.8984375
- norm_biases: bfloat16 [4, 1024], P(None, 'seq'), may hold values from -1.796875 to 1.796875
- corpus_id: int32 [2, 2048], P('dp', 'seq'), may hold values from 0 to 7
- corpus_weight: float32 [8], replicated, may hold values from 0.25 to 4
- cotangent: bfloat16 [2, 2048, 1024], P('dp', 'seq'), may hold values from -6 to 6
Outputs:
- output: bfloat16 [2, 2048, 1024], P('dp', 'seq')
- grad_tokens: float32 [2, 2048, 1024], P('dp', 'seq')
- grad_qkv: float32 [1024, 3072], P('seq')
- grad_out: float32 [1024, 1024], P('seq')
- grad_up: float32 [1024, 4096], P('seq')
- grad_down: float32 [4096, 1024], P('seq')
- grad_gains: float32 [4, 1024], P(None, 'seq')
- grad_biases: float32 [4, 1024], P(None, 'seq')
The draws below stay inside these ranges and needn't reach their ends.
All inputs are finite; a program needn't handle non-finite values.
Results may differ from the reference program's by a relative error of at most 0.018.
Values may be sent and summed in bfloat16 or wider, within the bound.
A program may use at most 192 MiB of HBM per device.

```python
import math
import jax
import jax.numpy as jnp
from jax import lax

D = 1024
HEADS = 16
HEAD_DIM = 64
FF = 4096
CORPORA = 8
LEN = 2048
SEQS = 2


def set_ends(entries, key, smallest, largest):
    longest = entries.shape.index(max(entries.shape))
    spots = []
    for shift in (0, 1):
        where = [jax.random.randint(jax.random.fold_in(key, axis), (), 0, length) for axis, length in enumerate(entries.shape)]
        where[longest] = (where[longest] + shift) % entries.shape[longest]
        spots.append(tuple(where))
    return entries.at[spots[0]].set(smallest).at[spots[1]].set(largest)


def block_scale(rng, dims, pieces, least, largest):
    def one(dim, parts):
        heights = jax.random.uniform(jax.random.fold_in(jax.random.fold_in(rng, 6), dim), (parts,), jnp.float32, least / len(pieces), largest / len(pieces))
        return jnp.repeat(jnp.exp(heights), dims[dim] // parts).reshape((-1,) + (1,) * (len(dims) - dim - 1))

    level = one(*pieces[0])
    for cut in pieces[1:]:
        level = level * one(*cut)
    return level


def bell_draw(rng, extent, spread, reach, shards=(), kind=jnp.bfloat16):
    factor_of = block_scale(rng, extent, shards, -0.22, 0.18) if shards else 1.0
    drawn = jax.random.normal(rng, extent, jnp.float32) * spread * factor_of
    return jnp.minimum(jnp.maximum(drawn, -reach), reach).astype(kind)


def setup_inputs(seed: int = 0) -> dict:
    keys = jax.random.split(jax.random.key(seed), 11)
    return {
        "tokens": bell_draw(keys[0], (SEQS, LEN, D), 1.0, 6.0, ((0, 2), (1, 16))),
        "w_qkv": bell_draw(keys[1], (D, 3 * D), D ** -0.5, 0.1875, ((0, 16),)),
        "w_out": bell_draw(keys[2], (D, D), D ** -0.5, 0.1875, ((0, 16),)),
        "w_up": bell_draw(keys[3], (D, FF), D ** -0.5, 0.1875, ((0, 16),)),
        "w_down": bell_draw(keys[4], (FF, D), FF ** -0.5, 0.09375, ((0, 16),)),
        "norm_gains": jnp.clip(1.0 + 0.18 * jax.random.normal(keys[5], (4, D), jnp.float32), 0.099609375, 1.8984375).astype(jnp.bfloat16),
        "norm_biases": bell_draw(keys[6], (4, D), 0.3, 1.796875, ((1, 16),)),
        "corpus_id": set_ends(jax.random.randint(keys[7], (SEQS, LEN), 0, CORPORA), jax.random.fold_in(keys[7], 1), 0, CORPORA - 1).astype(jnp.int32),
        "corpus_weight": jnp.clip(jnp.exp(jax.random.uniform(keys[8], (CORPORA,), jnp.float32, math.log(0.25), math.log(4.0))), 0.25, 4.0),
        "cotangent": bell_draw(keys[9], (SEQS, LEN, D), 1.0, 6.0, ((0, 2), (1, 16))),
    }


@jax.custom_vjp
def low(v):
    return lax.optimization_barrier(v.astype(jnp.bfloat16)).astype(jnp.float32)

@jax.custom_vjp
def low_back(v):
    return v

def low_keep(v):
    return (low(v), None)

def low_pass(kept, grad):
    return (grad,)

def back_keep(v):
    return (v, None)

def back_low(kept, grad):
    return (low(grad),)
low.defvjp(low_keep, low_pass)
low_back.defvjp(back_keep, back_low)

def layer_norm(values, gain, bias):
    center = values - lax.optimization_barrier(jnp.mean(values, -1, keepdims=True))
    variance = lax.optimization_barrier(jnp.mean(center * center, -1, keepdims=True))
    return center * lax.rsqrt(variance + 1e-05) * gain + bias

def rotate(values, position, direction):
    half_size = values.shape[-1] // 2
    freq = jnp.exp(jnp.arange(half_size).astype(jnp.float32) * (-2.0 * math.log(10000.0) / values.shape[-1]))
    angle = position[:, None] * freq[None, :]
    cosine = jnp.cos(angle)[:, None, :]
    sine = direction * jnp.sin(angle)[:, None, :]
    first = values[..., :half_size]
    second = values[..., half_size:]
    return jnp.concatenate([first * cosine - second * sine, first * sine + second * cosine], -1)

def attention(query, key, value):
    length = query.shape[0]
    block = math.gcd(length, 512)
    key_pos = jnp.arange(length).astype(jnp.int32)

    def one_block(items):
        q_block, start = items
        scores = low_back(jnp.einsum('qhd,khd->hqk', q_block, key, precision=lax.Precision.HIGHEST)) * HEAD_DIM ** (-0.5)
        allowed = (start + jnp.arange(block).astype(jnp.int32))[:, None] >= key_pos[None, :]
        probs = low(jax.nn.softmax(jnp.where(allowed, scores, -1e+30), axis=-1))
        return jnp.einsum('hqk,khd->qhd', probs, value, precision=lax.Precision.HIGHEST)
    blocks = query.reshape(length // block, block, HEADS, HEAD_DIM)
    starts = (jnp.arange(length // block) * block).astype(jnp.int32)
    return lax.map(jax.checkpoint(one_block), (blocks, starts)).reshape(length, HEADS * HEAD_DIM)

def matmul(left, right):
    return jnp.dot(left, right, precision=lax.Precision.HIGHEST)

def forward_sequence(x, w_qkv, w_out, w_up, w_down, gains, biases):
    length = x.shape[0]
    position = jnp.arange(length).astype(jnp.float32)
    normed_in = low(layer_norm(x, gains[0], biases[0]))
    qkv = low_back(matmul(normed_in, w_qkv))
    query = low(rotate(qkv[:, :D].reshape(length, HEADS, HEAD_DIM), position, 1.0))
    key = low(rotate(qkv[:, D:2 * D].reshape(length, HEADS, HEAD_DIM), position, 1.0))
    value = low(qkv[:, 2 * D:].reshape(length, HEADS, HEAD_DIM))
    attended = low(low_back(attention(query, key, value)))
    proj = low_back(matmul(attended, w_out))
    hidden = x + layer_norm(proj, gains[1], biases[1])
    normed_mid = low(layer_norm(hidden, gains[2], biases[2]))
    up = low_back(matmul(normed_mid, w_up))
    act = low(jax.nn.gelu(up, approximate=True))
    down = low_back(matmul(act, w_down))
    return hidden + layer_norm(down, gains[3], biases[3])

def reference(tokens, w_qkv, w_out, w_up, w_down, norm_gains, norm_biases, corpus_id, corpus_weight, cotangent):

    def whole(x, wq, wo, wu, wd, gains, biases):

        def one(xs):
            return forward_sequence(xs, wq, wo, wu, wd, gains, biases)
        return lax.map(jax.checkpoint(one), x)
    inputs = (tokens.astype(jnp.float32), w_qkv.astype(jnp.float32), w_out.astype(jnp.float32), w_up.astype(jnp.float32), w_down.astype(jnp.float32), norm_gains.astype(jnp.float32), norm_biases.astype(jnp.float32))
    output, pullback = jax.vjp(whole, *inputs)
    row_weight = corpus_weight[corpus_id]
    grads = pullback(cotangent.astype(jnp.float32) * row_weight[..., None])
    return (output.astype(jnp.bfloat16), grads[0], grads[1], grads[2], grads[3], grads[4], grads[5], grads[6])
```

```python
import functools
import math

import jax
import jax.numpy as jnp
import numpy as np
from jax import lax
from jax.experimental import pallas as pl
from jax.experimental.pallas import tpu as pltpu
from jax.sharding import PartitionSpec as P

HEADS = 16
HEAD_DIM = 64
MESH = pl.DeviceIdType.MESH
ANY = pl.BlockSpec(memory_space=pl.ANY)
VMEM = pl.BlockSpec(memory_space=pltpu.VMEM)
DMA = pltpu.SemaphoreType.DMA
TILE = 256


def ring_place():
    me = lax.axis_index("seq")
    chips = lax.axis_size("seq") // 2
    core = me % 2
    column = (me // 2) % 2
    row = me // 4
    place = row + column * (chips - 1 - 2 * row)
    return me, core, place, chips


def ring_device(place, core, chips):
    place = (place + 2 * chips) % chips
    column = place // (chips // 2)
    row = place + column * (chips - 1 - 2 * place)
    return row * 4 + column * 2 + core


def greet(devices):
    barrier = pltpu.get_barrier_semaphore()
    for device in devices:
        pl.semaphore_signal(barrier, inc=1, device_id={"seq": device}, device_id_type=MESH)
    pl.semaphore_wait(barrier, len(devices))


def remote(source, target, send, recv, device):
    return pltpu.make_async_remote_copy(
        src_ref=source,
        dst_ref=target,
        send_sem=send,
        recv_sem=recv,
        device_id={"seq": device},
        device_id_type=MESH,
    )


def gather_kernel(count, *refs):
    ins, outs = refs[:count], refs[count : 2 * count]
    send, recv, side_send, side_recv, local = refs[2 * count :]
    me, core, place, chips = ring_place()
    right = ring_device(place + 1, core, chips)
    left = ring_device(place - 1, core, chips)
    sibling = ring_device(place, 1 - core, chips)
    messages = chips - 1
    greet((left, right, sibling))

    def part(ref, device, half):
        rows = ref.shape[1] // 2
        return ref.at[device, pl.ds(half * rows, rows)]

    def hop(a, way, j):
        half = j % 2 if way == 0 else 1 - j % 2
        step = 1 if way == 0 else -1
        owner = ring_device(place - step * (j // 2), core, chips)
        if j < 2:
            rows = ins[a].shape[0] // 2
            source = ins[a].at[pl.ds(half * rows, rows)]
        else:
            source = part(outs[a], owner, half)
        return remote(
            source,
            part(outs[a], owner, half),
            send.at[a, way, j],
            recv.at[a, way, j],
            right if way == 0 else left,
        )

    def landed(a, way, j):
        half = j % 2 if way == 0 else 1 - j % 2
        step = 1 if way == 0 else -1
        owner = ring_device(place - step * (1 + j // 2), core, chips)
        return part(outs[a], owner, half)

    def across(a, way, j):
        if j < 0:
            return remote(
                ins[a], outs[a].at[me], side_send.at[a, 0, 0], side_recv.at[a, 0, 0], sibling
            )
        ref = landed(a, way, j)
        return remote(
            ref, ref, side_send.at[a, way, j + 1], side_recv.at[a, way, j + 1], sibling
        )

    for a in range(count):
        for j in range(2):
            for way in range(2):
                hop(a, way, j).start()
    for a in range(count):
        across(a, 0, -1).start()
        pltpu.make_async_copy(ins[a], outs[a].at[me], local.at[a]).start()
    for a in range(count):
        for j in range(messages):
            for way in range(2):
                hop(a, way, j).wait_recv()
                if j + 2 < messages:
                    hop(a, way, j + 2).start()
                across(a, way, j).start()
    for a in range(count):
        pltpu.make_async_copy(ins[a], outs[a].at[me], local.at[a]).wait()
        across(a, 0, -1).wait()
        for way in range(2):
            for j in range(messages):
                hop(a, way, j).wait_send()
                across(a, way, j).wait()


def gather(arrays, number):
    size = lax.axis_size("seq")
    count = len(arrays)
    messages = size // 2 - 1
    return pl.pallas_call(
        functools.partial(gather_kernel, count),
        out_shape=[jax.ShapeDtypeStruct((size,) + a.shape, a.dtype) for a in arrays],
        in_specs=[ANY] * count,
        out_specs=[ANY] * count,
        scratch_shapes=[
            DMA((count, 2, messages)),
            DMA((count, 2, messages)),
            DMA((count, 2, messages + 1)),
            DMA((count, 2, messages + 1)),
            DMA((count,)),
        ],
        compiler_params=pltpu.CompilerParams(collective_id=number, has_side_effects=True),
    )(*arrays)


def scatter_kernel(x, out, side, inbox, outbox, send, recv, side_send, side_recv):
    me, core, place, chips = ring_place()
    right = ring_device(place + 1, core, chips)
    left = ring_device(place - 1, core, chips)
    sibling = ring_device(place, 1 - core, chips)
    messages = chips - 1
    rows = x.shape[1] // 2
    greet((left, right, sibling))
    order = [chips // 2]
    for k in range(chips // 2 - 1, 0, -1):
        order += [k, -k]
    order.append(0)

    def chip(k):
        return (place + k + chips) % chips

    def across(k):
        p = chip(k)
        return remote(
            x.at[ring_device(p, 1 - core, chips)],
            side.at[p],
            side_send.at[order.index(k)],
            side_recv.at[order.index(k)],
            sibling,
        )

    def own(k, half):
        p = chip(k)
        span = pl.ds(half * rows, rows)
        mine = x[ring_device(p, core, chips), span].astype(jnp.float32)
        return mine + side[p, span].astype(jnp.float32)

    def hop(way, j):
        return remote(
            outbox.at[way, j],
            inbox.at[way, j],
            send.at[way, j],
            recv.at[way, j],
            right if way == 0 else left,
        )

    for k in order:
        across(k).start()
    waited = set()
    for j in range(messages):
        far = chips // 2 - (j + 1) // 2
        for way in range(2):
            half = j % 2 if way == 0 else 1 - j % 2
            k = far if way == 0 or far == chips // 2 else -far
            if k not in waited:
                across(k).wait_recv()
                waited.add(k)
            total = own(k, half)
            if j >= 2:
                hop(way, j - 2).wait_recv()
                total += inbox[way, j - 2].astype(jnp.float32)
            outbox[way, j] = total.astype(outbox.dtype)
            hop(way, j).start()
    across(0).wait_recv()
    for half in range(2):
        total = own(0, half)
        for way in range(2):
            last = messages - 1 if (half == 0) == (way == 0) else messages - 2
            hop(way, last).wait_recv()
            total += inbox[way, last].astype(jnp.float32)
        out[pl.ds(half * rows, rows)] = total
    for k in order:
        across(k).wait_send()
    for way in range(2):
        for j in range(messages):
            hop(way, j).wait_send()


def scatter(x, number):
    size, rows, columns = x.shape
    chips = size // 2
    messages = chips - 1
    return pl.pallas_call(
        scatter_kernel,
        out_shape=jax.ShapeDtypeStruct((rows, columns), jnp.float32),
        in_specs=[VMEM],
        out_specs=VMEM,
        scratch_shapes=[
            pltpu.VMEM((chips, rows, columns), x.dtype),
            pltpu.VMEM((2, messages, rows // 2, columns), x.dtype),
            pltpu.VMEM((2, messages, rows // 2, columns), x.dtype),
            DMA((2, messages)),
            DMA((2, messages)),
            DMA((chips,)),
            DMA((chips,)),
        ],
        compiler_params=pltpu.CompilerParams(
            collective_id=number, has_side_effects=True, vmem_limit_bytes=48 * 2**20
        ),
    )(x)


def exchange_kernel(count, *refs):
    ins, outs = refs[:count], refs[count : 2 * count]
    send, recv, local = refs[2 * count :]
    me = lax.axis_index("seq")
    size = lax.axis_size("seq")
    greet([(me + i) % size for i in range(1, size)])

    def copy(a, i):
        target = (me + i) % size
        return remote(
            ins[a].at[target], outs[a].at[me], send.at[a, i], recv.at[a, i], target
        )

    def arrival(a, i):
        source = (me + size - i) % size
        return remote(
            ins[a].at[source], outs[a].at[source], send.at[a, i], recv.at[a, i], source
        )

    for a in range(count):
        for i in range(1, size):
            copy(a, i).start()
        pltpu.make_async_copy(ins[a].at[me], outs[a].at[me], local.at[a]).start()
    for a in range(count):
        for i in range(1, size):
            arrival(a, i).wait_recv()
            copy(a, i).wait_send()
        pltpu.make_async_copy(ins[a].at[me], outs[a].at[me], local.at[a]).wait()


def exchange(arrays, number):
    size = lax.axis_size("seq")
    count = len(arrays)
    return pl.pallas_call(
        functools.partial(exchange_kernel, count),
        out_shape=[jax.ShapeDtypeStruct(a.shape, a.dtype) for a in arrays],
        in_specs=[ANY] * count,
        out_specs=[ANY] * count,
        scratch_shapes=[DMA((count, size)), DMA((count, size)), DMA((count,))],
        compiler_params=pltpu.CompilerParams(collective_id=number, has_side_effects=True),
    )(*arrays)


def dot(left, right, contract=((1,), (0,))):
    return lax.dot_general(
        left, right, (contract, ((), ())), preferred_element_type=jnp.float32
    )


NT = ((1,), (1,))
TN = ((0,), (0,))


def attend_kernel(x, w, cos, sin, q_t, k_t, v_t, total, lse, send, k_nat, scores):
    length = x.shape[0]
    half = HEAD_DIM // 2
    tiles = length // TILE
    for t in range(tiles):
        span = pl.ds(t * TILE, TILE)
        qkv = dot(w[...], x[span, :], NT)
        c, s = cos[:, span], sin[:, span]
        for i, (ref, scale) in enumerate(((q_t, HEAD_DIM**-0.5), (k_t, 1.0))):
            first = qkv[i * HEAD_DIM : i * HEAD_DIM + half]
            second = qkv[i * HEAD_DIM + half : (i + 1) * HEAD_DIM]
            turned = jnp.concatenate([first * c - second * s, first * s + second * c], 0)
            ref[:, span] = (turned * scale).astype(jnp.bfloat16)
            if i == 1:
                k_nat[span, :] = turned.T.astype(jnp.bfloat16)
        v_t[:, span] = qkv[2 * HEAD_DIM :].astype(jnp.bfloat16)
    for t in range(tiles):
        span = pl.ds(t * TILE, TILE)
        query = q_t[:, span]
        top = None
        for j in range(t + 1):
            keys = pl.ds(j * TILE, TILE)
            s = dot(k_nat[keys, :], query)
            if j == t:
                key_pos = lax.broadcasted_iota(jnp.int32, s.shape, 0)
                query_pos = lax.broadcasted_iota(jnp.int32, s.shape, 1)
                s = jnp.where(key_pos <= query_pos, s, -1e30)
            scores[keys, :] = s
            here = jnp.max(s, 0, keepdims=True)
            top = here if top is None else jnp.maximum(top, here)
        acc, norm = None, None
        for j in range(t + 1):
            keys = pl.ds(j * TILE, TILE)
            p = jnp.exp(scores[keys, :] - top)
            here = jnp.sum(p, 0, keepdims=True)
            add = dot(v_t[:, keys], p.astype(jnp.bfloat16))
            acc = add if acc is None else acc + add
            norm = here if norm is None else norm + here
        acc = acc / norm
        total[:, span] = acc
        lse[:, span] = top + jnp.log(norm)
        for b in range(TILE // 128):
            send[t * (TILE // 128) + b] = acc[:, b * 128 : (b + 1) * 128].astype(jnp.bfloat16)


def attend(x, w, cos, sin):
    length, width = x.shape
    low = jax.ShapeDtypeStruct((HEAD_DIM, length), jnp.bfloat16)
    return pl.pallas_call(
        attend_kernel,
        out_shape=[
            low,
            low,
            low,
            jax.ShapeDtypeStruct((HEAD_DIM, length), jnp.float32),
            jax.ShapeDtypeStruct((1, length), jnp.float32),
            jax.ShapeDtypeStruct((length // 128, HEAD_DIM, 128), jnp.bfloat16),
        ],
        in_specs=[VMEM] * 4,
        out_specs=[VMEM] * 6,
        scratch_shapes=[
            pltpu.VMEM((length, HEAD_DIM), jnp.bfloat16),
            pltpu.VMEM((length, TILE), jnp.float32),
        ],
        compiler_params=pltpu.CompilerParams(vmem_limit_bytes=48 * 2**20),
    )(x, w, cos, sin)


def attend_back_kernel(
    x, w, cos, sin, q_t, k_t, v_t, total, lse, d_att, d_x, d_w, d_t, q_nat, k_nat, v_nat, do_nat, do_t, dq, delta
):
    length = x.shape[0]
    half = HEAD_DIM // 2
    tiles = length // TILE
    for b in range(length // 128):
        do_t[:, pl.ds(b * 128, 128)] = d_att[b]
    for t in range(tiles):
        span = pl.ds(t * TILE, TILE)
        for ref, nat in ((q_t, q_nat), (k_t, k_nat), (v_t, v_nat), (do_t, do_nat)):
            nat[span, :] = ref[:, span].astype(jnp.float32).T.astype(jnp.bfloat16)
        delta[:, span] = jnp.sum(
            do_t[:, span].astype(jnp.float32) * total[:, span], 0, keepdims=True
        )
    dq[...] = jnp.zeros_like(dq)

    def turned_back(u, span, base):
        c, s = cos[:, span], sin[:, span]
        first, second = u[:half], u[half:]
        d_t[base : base + half, span] = (first * c + second * s).astype(jnp.bfloat16)
        d_t[base + half : base + 2 * half, span] = (second * c - first * s).astype(jnp.bfloat16)

    for j in range(tiles):
        keys = pl.ds(j * TILE, TILE)
        dk, dv = None, None
        for t in range(j, tiles):
            span = pl.ds(t * TILE, TILE)
            s = dot(k_nat[keys, :], q_t[:, span])
            p = jnp.exp(s - lse[:, span])
            if j == t:
                key_pos = lax.broadcasted_iota(jnp.int32, s.shape, 0)
                query_pos = lax.broadcasted_iota(jnp.int32, s.shape, 1)
                p = jnp.where(key_pos <= query_pos, p, 0.0)
            dp = dot(v_nat[keys, :], do_t[:, span])
            ds = (p * (dp - delta[:, span])).astype(jnp.bfloat16)
            dv_add = dot(p.astype(jnp.bfloat16), do_nat[span, :])
            dk_add = dot(ds, q_nat[span, :])
            dv = dv_add if dv is None else dv + dv_add
            dk = dk_add if dk is None else dk + dk_add
            dq[:, span] += dot(k_t[:, keys], ds)
        turned_back(dk.T, keys, HEAD_DIM)
        d_t[2 * HEAD_DIM :, keys] = dv.T.astype(jnp.bfloat16)
    for t in range(tiles):
        span = pl.ds(t * TILE, TILE)
        turned_back(dq[:, span] * HEAD_DIM**-0.5, span, 0)
    for t in range(tiles):
        span = pl.ds(t * TILE, TILE)
        d_x[span, :] = dot(d_t[:, span], w[...], TN).astype(jnp.bfloat16)
    for t in range(x.shape[1] // TILE):
        span = pl.ds(t * TILE, TILE)
        d_w[:, span] = dot(d_t[...], x[:, span]).astype(jnp.bfloat16)


def attend_back(x, w, cos, sin, q_t, k_t, v_t, total, lse, d_att):
    length, width = x.shape
    nat = pltpu.VMEM((length, HEAD_DIM), jnp.bfloat16)
    return pl.pallas_call(
        attend_back_kernel,
        out_shape=[
            jax.ShapeDtypeStruct((length, width), jnp.bfloat16),
            jax.ShapeDtypeStruct((3 * HEAD_DIM, width), jnp.bfloat16),
        ],
        in_specs=[VMEM] * 10,
        out_specs=[VMEM] * 2,
        scratch_shapes=[
            pltpu.VMEM((3 * HEAD_DIM, length), jnp.bfloat16),
            nat,
            nat,
            nat,
            nat,
            pltpu.VMEM((HEAD_DIM, length), jnp.bfloat16),
            pltpu.VMEM((HEAD_DIM, length), jnp.float32),
            pltpu.VMEM((1, length), jnp.float32),
        ],
        compiler_params=pltpu.CompilerParams(vmem_limit_bytes=48 * 2**20),
    )(x, w, cos, sin, q_t, k_t, v_t, total, lse, d_att)


def layer_norm(values, gain, bias):
    center = values - jnp.mean(values, -1, keepdims=True)
    variance = jnp.mean(center * center, -1, keepdims=True)
    return center * lax.rsqrt(variance + 1e-05) * gain + bias


def gelu_tanh(values):
    return jax.nn.gelu(values, approximate=True)


def turn_tables(length):
    half = HEAD_DIM // 2
    freq = np.exp(
        np.arange(half, dtype=np.float32) * np.float32(-2.0 * math.log(10000.0) / HEAD_DIM)
    )
    angle = freq[:, None] * np.arange(length, dtype=np.float32)[None, :]
    return jnp.asarray(np.cos(angle)), jnp.asarray(np.sin(angle))


def split_heads(
    tokens, w_qkv, w_out, w_up, w_down, norm_gains, norm_biases, corpus_id, corpus_weight, cotangent
):
    size = lax.axis_size("seq")
    _, rows, width = tokens.shape
    length = rows * size
    low = jnp.bfloat16
    w_rows = w_qkv.shape[0]
    hidden_units = w_down.shape[0]

    qkv_blocks = w_qkv.reshape(w_rows, 3, HEADS, HEAD_DIM).transpose(2, 0, 1, 3)
    qkv_blocks = qkv_blocks.reshape(HEADS, w_rows, 3 * HEAD_DIM)
    up_blocks = w_up.reshape(w_rows, size, hidden_units).transpose(1, 0, 2)
    norms = jnp.concatenate([norm_gains, norm_biases, norm_gains, norm_biases], 0)
    norms = jnp.concatenate([norms, norms], 1)
    qkv_all, up_all = exchange((qkv_blocks, up_blocks), 1)
    out_all, norms_all = gather((w_out, jnp.concatenate([norms, norms], 0)), 2)
    w_head = qkv_all.reshape(width, 3 * HEAD_DIM).T
    w_up_own = up_all.reshape(width, hidden_units)
    w_out_all = out_all.reshape(width, width)
    norms_all = norms_all[:, :8, :w_rows].transpose(1, 0, 2).reshape(8, width).astype(jnp.float32)
    gains, biases = norms_all[:4], norms_all[4:]

    cos, sin = turn_tables(length)
    x_float = tokens[0].astype(jnp.float32)
    normed_low, input_back = jax.vjp(layer_norm, x_float, gains[0], biases[0])
    normed_low = normed_low.astype(low)
    (normed_all,) = gather((normed_low,), 3)
    normed_all = normed_all.reshape(length, width)
    q_t, k_t, v_t, total, lse, att_blocks = attend(normed_all, w_head, cos, sin)
    (att_t,) = exchange((att_blocks,), 4)
    att_t = att_t.reshape(width, rows)
    proj = dot(att_t, w_out_all, TN)
    normed_proj, proj_back = jax.vjp(layer_norm, proj, gains[1], biases[1])
    hidden = x_float + normed_proj
    mid, mid_back = jax.vjp(layer_norm, hidden, gains[2], biases[2])
    (mid_all,) = gather((mid.astype(low),), 5)
    mid_all = mid_all.reshape(length, width)
    up_proj = dot(mid_all, w_up_own)
    act, gelu_back = jax.vjp(gelu_tanh, up_proj)
    act_low = act.astype(low)
    down_part = dot(act_low, w_down).astype(low)
    down = scatter(down_part.reshape(size, rows, width), 6)
    normed_down, down_back = jax.vjp(layer_norm, down, gains[3], biases[3])
    output = (hidden + normed_down).astype(low)
    matches = (corpus_id[0][:, None] == jnp.arange(corpus_weight.shape[0])).astype(jnp.float32)
    row_weight = jnp.sum(matches * corpus_weight, -1)
    grad_y = cotangent[0].astype(jnp.float32) * row_weight[:, None]
    d_down, gain_three, bias_three = down_back(grad_y)
    (d_down_all,) = gather((d_down.astype(low),), 7)
    d_down_all = d_down_all.reshape(length, width)
    d_act = dot(d_down_all, w_down, NT)
    d_up_low = gelu_back(d_act)[0].astype(low)
    d_mid_part = dot(d_up_low, w_up_own, NT).astype(low)
    d_mid = scatter(d_mid_part.reshape(size, rows, width), 8)
    grad_down = dot(act_low, d_down_all, TN).astype(low)
    grad_up = dot(mid_all, d_up_low, TN).astype(low)
    d_hidden_mid, gain_two, bias_two = mid_back(d_mid)
    d_hidden = grad_y + d_hidden_mid
    d_proj, gain_one, bias_one = proj_back(d_hidden)
    d_proj_low = d_proj.astype(low)
    d_att_t = dot(w_out_all, d_proj_low, NT).astype(low)
    grad_out = dot(att_t, d_proj_low).astype(low)
    d_att_blocks, grad_up_all = exchange(
        (d_att_t.reshape(HEADS, HEAD_DIM, rows), grad_up.reshape(size, w_rows, hidden_units)), 9
    )
    d_normed_part, grad_head = attend_back(
        normed_all, w_head, cos, sin, q_t, k_t, v_t, total, lse, d_att_blocks
    )
    d_normed = scatter(d_normed_part.reshape(size, rows, width), 10)
    grad_out = scatter(grad_out.reshape(size, w_rows, width), 11)
    d_input, gain_zero, bias_zero = input_back(d_normed)
    grad_tokens = d_hidden + d_input
    grads = jnp.stack(
        [gain_zero, gain_one, gain_two, gain_three, bias_zero, bias_one, bias_two, bias_three]
    )
    grads = grads.reshape(8, size, w_rows).transpose(1, 0, 2)
    grads = jnp.pad(grads, ((0, 0), (0, 8), (0, 128 - w_rows))).astype(low)
    head_all, grads_all = exchange(
        (grad_head.T.reshape(size, w_rows, 3 * HEAD_DIM), grads), 12
    )
    grad_qkv = head_all.reshape(HEADS, w_rows, 3, HEAD_DIM).transpose(1, 2, 0, 3)
    grad_qkv = grad_qkv.reshape(w_rows, 3 * width)
    grad_up = grad_up_all.transpose(1, 0, 2).reshape(w_rows, size * hidden_units)
    grads = jnp.sum(grads_all[:, :8, :w_rows].astype(jnp.float32), 0)

    def swap(value):
        mine = value.astype(low)
        other = lax.ppermute(mine, "dp", [(0, 1), (1, 0)])
        return mine.astype(jnp.float32) + other.astype(jnp.float32)

    grads = swap(grads)
    return (
        output[None],
        grad_tokens[None],
        swap(grad_qkv),
        swap(grad_out),
        swap(grad_up),
        swap(grad_down),
        grads[:4],
        grads[4:],
    )


def shifted(x, axis, by):
    size = lax.axis_size(axis)
    return lax.ppermute(x, axis, [(i, (i + by) % size) for i in range(size)])


def passed_along(value, axis, steps):
    count = lax.axis_size(axis)
    first, last = (max(0, -steps), min(count, count - steps))
    return lax.ppermute(value, axis, [(source, source + steps) for source in range(first, last)])


def rotate(values, position, direction):
    half_size = values.shape[-1] // 2
    freq = jnp.exp(
        jnp.arange(half_size).astype(jnp.float32) * (-2.0 * math.log(10000.0) / values.shape[-1])
    )
    angle = position[:, None] * freq[None, :]
    cosine = jnp.cos(angle)[:, None, :]
    sine = direction * jnp.sin(angle)[:, None, :]
    first = values[..., :half_size]
    second = values[..., half_size:]
    return jnp.concatenate([first * cosine - second * sine, first * sine + second * cosine], -1)


def per_device(
    tokens, w_qkv, w_out, w_up, w_down, norm_gains, norm_biases, corpus_id, corpus_weight, cotangent
):
    full_qkv, full_out, full_up, full_down, gains_low, biases_low = (
        lax.all_gather(w_qkv, "seq", axis=0, tiled=True),
        lax.all_gather(w_out, "seq", axis=0, tiled=True),
        lax.all_gather(w_up, "seq", axis=0, tiled=True),
        lax.all_gather(w_down, "seq", axis=0, tiled=True),
        lax.all_gather(norm_gains, "seq", axis=1, tiled=True),
        lax.all_gather(norm_biases, "seq", axis=1, tiled=True),
    )
    gains = gains_low.astype(jnp.float32)
    biases = biases_low.astype(jnp.float32)
    seq_count, row_count, model_width = tokens.shape
    shape_heads = (seq_count, row_count, HEADS, HEAD_DIM)
    scale = HEAD_DIM ** (-0.5)
    cycle_size = lax.axis_size("seq")
    cycle_index = lax.axis_index("seq")
    query_pos = cycle_index * row_count + jnp.arange(row_count)
    position = query_pos.astype(jnp.float32)
    x_float = tokens.astype(jnp.float32)
    normed_low = layer_norm(x_float, gains[0], biases[0]).astype(jnp.bfloat16)
    qkv = jnp.einsum("std,de->ste", normed_low, full_qkv, preferred_element_type=jnp.float32)
    query_low = rotate(qkv[..., :model_width].reshape(shape_heads), position, 1.0).astype(
        jnp.bfloat16
    )
    key_low = rotate(
        qkv[..., model_width : 2 * model_width].reshape(shape_heads), position, 1.0
    ).astype(jnp.bfloat16)
    value_low = qkv[..., 2 * model_width :].reshape(shape_heads).astype(jnp.bfloat16)

    def block_scores(key_piece, key_pos):
        scores = (
            jnp.einsum("sqhd,skhd->shqk", query_low, key_piece, preferred_element_type=jnp.float32)
            * scale
        )
        allowed = query_pos[:, None] >= key_pos[None, :]
        return (scores, allowed)

    stat_shape = (seq_count, HEADS, row_count)
    key_piece = lax.all_gather(key_low, "seq", axis=1, tiled=True)
    value_piece = lax.all_gather(value_low, "seq", axis=1, tiled=True)
    key_pos = jnp.arange(key_piece.shape[1])
    run_max = jnp.full(stat_shape, -1e30, jnp.float32)
    scores, allowed = block_scores(key_piece, key_pos)
    new_max = jnp.maximum(run_max, jnp.max(jnp.where(allowed, scores, -1e30), -1))
    weights = jnp.where(allowed, jnp.exp(scores - new_max[..., None]), 0.0)
    run_sum = jnp.sum(weights, -1)
    total = jnp.einsum(
        "shqk,skhd->sqhd",
        weights.astype(jnp.bfloat16),
        value_piece,
        preferred_element_type=jnp.float32,
    )
    run_max, run_sum, total = (new_max, run_sum, total)
    log_sum = run_max + jnp.log(run_sum)
    attended = total / jnp.transpose(run_sum, (0, 2, 1))[..., None]
    attended_low = attended.reshape(seq_count, row_count, model_width).astype(jnp.bfloat16)
    proj = jnp.einsum("std,de->ste", attended_low, full_out, preferred_element_type=jnp.float32)
    hidden = x_float + layer_norm(proj, gains[1], biases[1])
    mid_low = layer_norm(hidden, gains[2], biases[2]).astype(jnp.bfloat16)
    up_proj = jnp.einsum("std,df->stf", mid_low, full_up, preferred_element_type=jnp.float32)
    act_low = gelu_tanh(up_proj).astype(jnp.bfloat16)
    down = jnp.einsum("stf,fd->std", act_low, full_down, preferred_element_type=jnp.float32)
    output = (hidden + layer_norm(down, gains[3], biases[3])).astype(jnp.bfloat16)
    matches = (corpus_id[..., None] == jnp.arange(corpus_weight.shape[0])).astype(jnp.float32)
    row_weight = jnp.sum(matches * corpus_weight, -1)
    grad_y = cotangent.astype(jnp.float32) * row_weight[..., None]
    _, down_back = jax.vjp(layer_norm, down, gains[3], biases[3])
    d_down, gain_three, bias_three = down_back(grad_y)
    d_down_low = d_down.astype(jnp.bfloat16)
    grad_down = jnp.einsum("stf,std->fd", act_low, d_down_low, preferred_element_type=jnp.float32)
    d_act = jnp.einsum("std,fd->stf", d_down_low, full_down, preferred_element_type=jnp.float32)
    _, gelu_back = jax.vjp(gelu_tanh, up_proj)
    d_up_low = gelu_back(d_act)[0].astype(jnp.bfloat16)
    grad_up = jnp.einsum("std,stf->df", mid_low, d_up_low, preferred_element_type=jnp.float32)
    d_mid = jnp.einsum("stf,df->std", d_up_low, full_up, preferred_element_type=jnp.float32)
    _, mid_back = jax.vjp(layer_norm, hidden, gains[2], biases[2])
    d_hidden_mid, gain_two, bias_two = mid_back(d_mid)
    d_hidden = grad_y + d_hidden_mid
    _, proj_back = jax.vjp(layer_norm, proj, gains[1], biases[1])
    d_proj, gain_one, bias_one = proj_back(d_hidden)
    d_proj_low = d_proj.astype(jnp.bfloat16)
    grad_out = jnp.einsum(
        "std,ste->de", attended_low, d_proj_low, preferred_element_type=jnp.float32
    )
    d_att_low = (
        jnp.einsum("ste,de->std", d_proj_low, full_out, preferred_element_type=jnp.float32)
        .astype(jnp.bfloat16)
        .reshape(shape_heads)
    )
    delta = jnp.transpose(jnp.sum(d_att_low.astype(jnp.float32) * attended, -1), (0, 2, 1))

    def contribute(d_query, key_piece, value_piece, d_key, d_value, owner):
        key_pos = owner * row_count + jnp.arange(row_count)
        query_sum = d_query
        key_sum = d_key
        value_sum = d_value
        scores, allowed = block_scores(key_piece, key_pos)
        probs = jnp.where(allowed, jnp.exp(scores - log_sum[..., None]), 0.0)
        value_sum = value_sum + jnp.einsum(
            "shqk,sqhd->skhd",
            probs.astype(jnp.bfloat16),
            d_att_low,
            preferred_element_type=jnp.float32,
        )
        d_probs = jnp.einsum(
            "sqhd,skhd->shqk", d_att_low, value_piece, preferred_element_type=jnp.float32
        )
        d_scores = (probs * (d_probs - delta[..., None]) * scale).astype(jnp.bfloat16)
        query_sum = query_sum + jnp.einsum(
            "shqk,skhd->sqhd", d_scores, key_piece, preferred_element_type=jnp.float32
        )
        key_sum = key_sum + jnp.einsum(
            "shqk,sqhd->skhd", d_scores, query_low, preferred_element_type=jnp.float32
        )
        return (query_sum, key_sum, value_sum)

    zeros_heads = jnp.zeros(shape_heads, jnp.float32)

    def pass_grads(d_key, d_value):
        return (
            shifted(d_key.astype(jnp.bfloat16), "seq", 1).astype(d_key.dtype),
            shifted(d_value.astype(jnp.bfloat16), "seq", 1).astype(d_value.dtype),
        )

    def cycle_turn(turn_index, state):
        d_query, key_piece, value_piece, d_key, d_value = state
        owner = (cycle_index - turn_index) % cycle_size
        d_query, d_key, d_value = contribute(d_query, key_piece, value_piece, d_key, d_value, owner)
        d_key, d_value = pass_grads(d_key, d_value)
        key_piece, value_piece = passed_along((key_piece, value_piece), "seq", 1)
        return (d_query, key_piece, value_piece, d_key, d_value)

    d_query, key_piece, value_piece, d_key, d_value = lax.fori_loop(
        0, cycle_size - 1, cycle_turn, (zeros_heads, key_low, value_low, zeros_heads, zeros_heads)
    )
    last_owner = (cycle_index + 1) % cycle_size
    d_query, d_key, d_value = contribute(
        d_query, key_piece, value_piece, d_key, d_value, last_owner
    )
    d_key, d_value = pass_grads(d_key, d_value)
    flat_shape = (seq_count, row_count, model_width)
    d_qkv_low = jnp.concatenate(
        [
            rotate(d_query, position, -1.0).reshape(flat_shape),
            rotate(d_key, position, -1.0).reshape(flat_shape),
            d_value.reshape(flat_shape),
        ],
        -1,
    ).astype(jnp.bfloat16)
    grad_qkv = jnp.einsum("std,ste->de", normed_low, d_qkv_low, preferred_element_type=jnp.float32)
    d_normed = jnp.einsum("ste,de->std", d_qkv_low, full_qkv, preferred_element_type=jnp.float32)
    _, input_back = jax.vjp(layer_norm, x_float, gains[0], biases[0])
    d_input, gain_zero, bias_zero = input_back(d_normed)
    grad_tokens = d_hidden + d_input
    grad_gains = jnp.stack([gain_zero, gain_one, gain_two, gain_three])
    grad_biases = jnp.stack([bias_zero, bias_one, bias_two, bias_three])
    all_grads = (grad_qkv, grad_out, grad_up, grad_down, grad_gains, grad_biases)
    pieces = (
        lax.psum_scatter(
            all_grads[0].astype(jnp.bfloat16), "seq", scatter_dimension=0, tiled=True
        ).astype(jnp.float32),
        lax.psum_scatter(
            all_grads[1].astype(jnp.bfloat16), "seq", scatter_dimension=0, tiled=True
        ).astype(jnp.float32),
        lax.psum_scatter(
            all_grads[2].astype(jnp.bfloat16), "seq", scatter_dimension=0, tiled=True
        ).astype(jnp.float32),
        lax.psum_scatter(
            all_grads[3].astype(jnp.bfloat16), "seq", scatter_dimension=0, tiled=True
        ).astype(jnp.float32),
        lax.psum_scatter(
            all_grads[4].astype(jnp.bfloat16), "seq", scatter_dimension=1, tiled=True
        ).astype(jnp.float32),
        lax.psum_scatter(
            all_grads[5].astype(jnp.bfloat16), "seq", scatter_dimension=1, tiled=True
        ).astype(jnp.float32),
    )
    shards = (
        lax.psum(pieces[0].astype(jnp.bfloat16), "dp").astype(jnp.float32),
        lax.psum(pieces[1].astype(jnp.bfloat16), "dp").astype(jnp.float32),
        lax.psum(pieces[2].astype(jnp.bfloat16), "dp").astype(jnp.float32),
        lax.psum(pieces[3].astype(jnp.bfloat16), "dp").astype(jnp.float32),
        lax.psum(pieces[4].astype(jnp.bfloat16), "dp").astype(jnp.float32),
        lax.psum(pieces[5].astype(jnp.bfloat16), "dp").astype(jnp.float32),
    )
    return (output, grad_tokens, shards[0], shards[1], shards[2], shards[3], shards[4], shards[5])


def solution(mesh):
    placed = (
        P("dp", "seq", None),
        P("seq", None),
        P("seq", None),
        P("seq", None),
        P("seq", None),
        P(None, "seq"),
        P(None, "seq"),
        P("dp", "seq"),
        P(),
        P("dp", "seq", None),
    )
    fits = mesh.shape["seq"] == HEADS and mesh.shape["dp"] == 2
    return jax.shard_map(
        split_heads if fits else per_device,
        mesh=mesh,
        in_specs=placed,
        out_specs=(
            P("dp", "seq", None),
            P("dp", "seq", None),
            P("seq", None),
            P("seq", None),
            P("seq", None),
            P("seq", None),
            P(None, "seq"),
            P(None, "seq"),
        ),
        check_vma=False,
    )
```

```python
import functools
import math

import jax
import jax.numpy as jnp
import numpy as np
from jax import lax
from jax.experimental import pallas as pl
from jax.experimental.pallas import tpu as pltpu
from jax.sharding import PartitionSpec as P

HEADS = 16
HEAD_DIM = 64
MESH = pl.DeviceIdType.MESH
ANY = pl.BlockSpec(memory_space=pl.ANY)
VMEM = pl.BlockSpec(memory_space=pltpu.VMEM)
DMA = pltpu.SemaphoreType.DMA
TILE = 256


def ring_place():
    me = lax.axis_index("seq")
    chips = lax.axis_size("seq") // 2
    core = me % 2
    column = (me // 2) % 2
    row = me // 4
    place = row + column * (chips - 1 - 2 * row)
    return me, core, place, chips


def ring_device(place, core, chips):
    place = (place + 2 * chips) % chips
    column = place // (chips // 2)
    row = place + column * (chips - 1 - 2 * place)
    return row * 4 + column * 2 + core


def greet(devices):
    barrier = pltpu.get_barrier_semaphore()
    for device in devices:
        pl.semaphore_signal(barrier, inc=1, device_id={"seq": device}, device_id_type=MESH)
    pl.semaphore_wait(barrier, len(devices))


def remote(source, target, send, recv, device):
    return pltpu.make_async_remote_copy(
        src_ref=source,
        dst_ref=target,
        send_sem=send,
        recv_sem=recv,
        device_id={"seq": device},
        device_id_type=MESH,
    )


def gather_kernel(count, *refs):
    ins, outs = refs[:count], refs[count : 2 * count]
    send, recv, side_send, side_recv, local = refs[2 * count :]
    me, core, place, chips = ring_place()
    right = ring_device(place + 1, core, chips)
    left = ring_device(place - 1, core, chips)
    sibling = ring_device(place, 1 - core, chips)
    messages = chips - 1
    greet((left, right, sibling))

    def part(ref, device, half):
        rows = ref.shape[1] // 2
        return ref.at[device, pl.ds(half * rows, rows)]

    def hop(a, way, j):
        half = j % 2 if way == 0 else 1 - j % 2
        step = 1 if way == 0 else -1
        owner = ring_device(place - step * (j // 2), core, chips)
        if j < 2:
            rows = ins[a].shape[0] // 2
            source = ins[a].at[pl.ds(half * rows, rows)]
        else:
            source = part(outs[a], owner, half)
        return remote(
            source,
            part(outs[a], owner, half),
            send.at[a, way, j],
            recv.at[a, way, j],
            right if way == 0 else left,
        )

    def landed(a, way, j):
        half = j % 2 if way == 0 else 1 - j % 2
        step = 1 if way == 0 else -1
        owner = ring_device(place - step * (1 + j // 2), core, chips)
        return part(outs[a], owner, half)

    def across(a, way, j):
        if j < 0:
            return remote(
                ins[a], outs[a].at[me], side_send.at[a, 0, 0], side_recv.at[a, 0, 0], sibling
            )
        ref = landed(a, way, j)
        return remote(
            ref, ref, side_send.at[a, way, j + 1], side_recv.at[a, way, j + 1], sibling
        )

    for a in range(count):
        for j in range(2):
            for way in range(2):
                hop(a, way, j).start()
    for a in range(count):
        across(a, 0, -1).start()
        pltpu.make_async_copy(ins[a], outs[a].at[me], local.at[a]).start()
    for a in range(count):
        for j in range(messages):
            for way in range(2):
                hop(a, way, j).wait_recv()
                if j + 2 < messages:
                    hop(a, way, j + 2).start()
                across(a, way, j).start()
    for a in range(count):
        pltpu.make_async_copy(ins[a], outs[a].at[me], local.at[a]).wait()
        across(a, 0, -1).wait()
        for way in range(2):
            for j in range(messages):
                hop(a, way, j).wait_send()
                across(a, way, j).wait()


def gather(arrays, number):
    size = lax.axis_size("seq")
    count = len(arrays)
    messages = size // 2 - 1
    return pl.pallas_call(
        functools.partial(gather_kernel, count),
        out_shape=[jax.ShapeDtypeStruct((size,) + a.shape, a.dtype) for a in arrays],
        in_specs=[ANY] * count,
        out_specs=[ANY] * count,
        scratch_shapes=[
            DMA((count, 2, messages)),
            DMA((count, 2, messages)),
            DMA((count, 2, messages + 1)),
            DMA((count, 2, messages + 1)),
            DMA((count,)),
        ],
        compiler_params=pltpu.CompilerParams(collective_id=number, has_side_effects=True),
    )(*arrays)


def scatter_kernel(x, out, side, inbox, outbox, send, recv, side_send, side_recv):
    me, core, place, chips = ring_place()
    right = ring_device(place + 1, core, chips)
    left = ring_device(place - 1, core, chips)
    sibling = ring_device(place, 1 - core, chips)
    messages = chips - 1
    rows = x.shape[1] // 2
    greet((left, right, sibling))
    order = [chips // 2]
    for k in range(chips // 2 - 1, 0, -1):
        order += [k, -k]
    order.append(0)

    def chip(k):
        return (place + k + chips) % chips

    def across(k):
        p = chip(k)
        return remote(
            x.at[ring_device(p, 1 - core, chips)],
            side.at[p],
            side_send.at[order.index(k)],
            side_recv.at[order.index(k)],
            sibling,
        )

    def own(k, half):
        p = chip(k)
        span = pl.ds(half * rows, rows)
        mine = x[ring_device(p, core, chips), span].astype(jnp.float32)
        return mine + side[p, span].astype(jnp.float32)

    def hop(way, j):
        return remote(
            outbox.at[way, j],
            inbox.at[way, j],
            send.at[way, j],
            recv.at[way, j],
            right if way == 0 else left,
        )

    for k in order:
        across(k).start()
    waited = set()
    for j in range(messages):
        far = chips // 2 - (j + 1) // 2
        for way in range(2):
            half = j % 2 if way == 0 else 1 - j % 2
            k = far if way == 0 or far == chips // 2 else -far
            if k not in waited:
                across(k).wait_recv()
                waited.add(k)
            total = own(k, half)
            if j >= 2:
                hop(way, j - 2).wait_recv()
                total += inbox[way, j - 2].astype(jnp.float32)
            outbox[way, j] = total.astype(outbox.dtype)
            hop(way, j).start()
    across(0).wait_recv()
    for half in range(2):
        total = own(0, half)
        for way in range(2):
            last = messages - 1 if (half == 0) == (way == 0) else messages - 2
            hop(way, last).wait_recv()
            total += inbox[way, last].astype(jnp.float32)
        out[pl.ds(half * rows, rows)] = total
    for k in order:
        across(k).wait_send()
    for way in range(2):
        for j in range(messages):
            hop(way, j).wait_send()


def scatter(x, number):
    size, rows, columns = x.shape
    chips = size // 2
    messages = chips - 1
    return pl.pallas_call(
        scatter_kernel,
        out_shape=jax.ShapeDtypeStruct((rows, columns), jnp.float32),
        in_specs=[VMEM],
        out_specs=VMEM,
        scratch_shapes=[
            pltpu.VMEM((chips, rows, columns), x.dtype),
            pltpu.VMEM((2, messages, rows // 2, columns), x.dtype),
            pltpu.VMEM((2, messages, rows // 2, columns), x.dtype),
            DMA((2, messages)),
            DMA((2, messages)),
            DMA((chips,)),
            DMA((chips,)),
        ],
        compiler_params=pltpu.CompilerParams(
            collective_id=number, has_side_effects=True, vmem_limit_bytes=48 * 2**20
        ),
    )(x)


def exchange_kernel(count, *refs):
    ins, outs = refs[:count], refs[count : 2 * count]
    send, recv, local = refs[2 * count :]
    me = lax.axis_index("seq")
    size = lax.axis_size("seq")
    greet([(me + i) % size for i in range(1, size)])

    def copy(a, i):
        target = (me + i) % size
        return remote(
            ins[a].at[target], outs[a].at[me], send.at[a, i], recv.at[a, i], target
        )

    def arrival(a, i):
        source = (me + size - i) % size
        return remote(
            ins[a].at[source], outs[a].at[source], send.at[a, i], recv.at[a, i], source
        )

    for a in range(count):
        for i in range(1, size):
            copy(a, i).start()
        pltpu.make_async_copy(ins[a].at[me], outs[a].at[me], local.at[a]).start()
    for a in range(count):
        for i in range(1, size):
            arrival(a, i).wait_recv()
            copy(a, i).wait_send()
        pltpu.make_async_copy(ins[a].at[me], outs[a].at[me], local.at[a]).wait()


def exchange(arrays, number):
    size = lax.axis_size("seq")
    count = len(arrays)
    return pl.pallas_call(
        functools.partial(exchange_kernel, count),
        out_shape=[jax.ShapeDtypeStruct(a.shape, a.dtype) for a in arrays],
        in_specs=[ANY] * count,
        out_specs=[ANY] * count,
        scratch_shapes=[DMA((count, size)), DMA((count, size)), DMA((count,))],
        compiler_params=pltpu.CompilerParams(collective_id=number, has_side_effects=True),
    )(*arrays)


def dot(left, right, contract=((1,), (0,))):
    return lax.dot_general(
        left, right, (contract, ((), ())), preferred_element_type=jnp.float32
    )


NT = ((1,), (1,))
TN = ((0,), (0,))


def attend_kernel(x, w, cos, sin, q_t, k_t, v_t, total, lse, send, k_nat, scores):
    length = x.shape[0]
    half = HEAD_DIM // 2
    tiles = length // TILE
    for t in range(tiles):
        span = pl.ds(t * TILE, TILE)
        qkv = dot(w[...], x[span, :], NT)
        c, s = cos[:, span], sin[:, span]
        for i, (ref, scale) in enumerate(((q_t, HEAD_DIM**-0.5), (k_t, 1.0))):
            first = qkv[i * HEAD_DIM : i * HEAD_DIM + half]
            second = qkv[i * HEAD_DIM + half : (i + 1) * HEAD_DIM]
            turned = jnp.concatenate([first * c - second * s, first * s + second * c], 0)
            ref[:, span] = (turned * scale).astype(jnp.bfloat16)
            if i == 1:
                k_nat[span, :] = turned.T.astype(jnp.bfloat16)
        v_t[:, span] = qkv[2 * HEAD_DIM :].astype(jnp.bfloat16)
    for t in range(tiles):
        span = pl.ds(t * TILE, TILE)
        query = q_t[:, span]
        top = None
        for j in range(t + 1):
            keys = pl.ds(j * TILE, TILE)
            s = dot(k_nat[keys, :], query)
            if j == t:
                key_pos = lax.broadcasted_iota(jnp.int32, s.shape, 0)
                query_pos = lax.broadcasted_iota(jnp.int32, s.shape, 1)
                s = jnp.where(key_pos <= query_pos, s, -1e30)
            scores[keys, :] = s
            here = jnp.max(s, 0, keepdims=True)
            top = here if top is None else jnp.maximum(top, here)
        acc, norm = None, None
        for j in range(t + 1):
            keys = pl.ds(j * TILE, TILE)
            p = jnp.exp(scores[keys, :] - top)
            here = jnp.sum(p, 0, keepdims=True)
            add = dot(v_t[:, keys], p.astype(jnp.bfloat16))
            acc = add if acc is None else acc + add
            norm = here if norm is None else norm + here
        acc = acc / norm
        total[:, span] = acc
        lse[:, span] = top + jnp.log(norm)
        for b in range(TILE // 128):
            send[t * (TILE // 128) + b] = acc[:, b * 128 : (b + 1) * 128].astype(jnp.bfloat16)


def attend(x, w, cos, sin):
    length, width = x.shape
    low = jax.ShapeDtypeStruct((HEAD_DIM, length), jnp.bfloat16)
    return pl.pallas_call(
        attend_kernel,
        out_shape=[
            low,
            low,
            low,
            jax.ShapeDtypeStruct((HEAD_DIM, length), jnp.float32),
            jax.ShapeDtypeStruct((1, length), jnp.float32),
            jax.ShapeDtypeStruct((length // 128, HEAD_DIM, 128), jnp.bfloat16),
        ],
        in_specs=[VMEM] * 4,
        out_specs=[VMEM] * 6,
        scratch_shapes=[
            pltpu.VMEM((length, HEAD_DIM), jnp.bfloat16),
            pltpu.VMEM((length, TILE), jnp.float32),
        ],
        compiler_params=pltpu.CompilerParams(vmem_limit_bytes=48 * 2**20),
    )(x, w, cos, sin)


def attend_back_kernel(
    x, w, cos, sin, q_t, k_t, v_t, total, lse, d_att, d_x, d_w, d_t, q_nat, k_nat, v_nat, do_nat, do_t, dq, delta
):
    length = x.shape[0]
    half = HEAD_DIM // 2
    tiles = length // TILE
    for b in range(length // 128):
        do_t[:, pl.ds(b * 128, 128)] = d_att[b]
    for t in range(tiles):
        span = pl.ds(t * TILE, TILE)
        for ref, nat in ((q_t, q_nat), (k_t, k_nat), (v_t, v_nat), (do_t, do_nat)):
            nat[span, :] = ref[:, span].astype(jnp.float32).T.astype(jnp.bfloat16)
        delta[:, span] = jnp.sum(
            do_t[:, span].astype(jnp.float32) * total[:, span], 0, keepdims=True
        )
    dq[...] = jnp.zeros_like(dq)

    def turned_back(u, span, base):
        c, s = cos[:, span], sin[:, span]
        first, second = u[:half], u[half:]
        d_t[base : base + half, span] = (first * c + second * s).astype(jnp.bfloat16)
        d_t[base + half : base + 2 * half, span] = (second * c - first * s).astype(jnp.bfloat16)

    for j in range(tiles):
        keys = pl.ds(j * TILE, TILE)
        dk, dv = None, None
        for t in range(j, tiles):
            span = pl.ds(t * TILE, TILE)
            s = dot(k_nat[keys, :], q_t[:, span])
            p = jnp.exp(s - lse[:, span])
            if j == t:
                key_pos = lax.broadcasted_iota(jnp.int32, s.shape, 0)
                query_pos = lax.broadcasted_iota(jnp.int32, s.shape, 1)
                p = jnp.where(key_pos <= query_pos, p, 0.0)
            dp = dot(v_nat[keys, :], do_t[:, span])
            ds = (p * (dp - delta[:, span])).astype(jnp.bfloat16)
            dv_add = dot(p.astype(jnp.bfloat16), do_nat[span, :])
            dk_add = dot(ds, q_nat[span, :])
            dv = dv_add if dv is None else dv + dv_add
            dk = dk_add if dk is None else dk + dk_add
            dq[:, span] += dot(k_t[:, keys], ds)
        turned_back(dk.T, keys, HEAD_DIM)
        d_t[2 * HEAD_DIM :, keys] = dv.T.astype(jnp.bfloat16)
    for t in range(tiles):
        span = pl.ds(t * TILE, TILE)
        turned_back(dq[:, span] * HEAD_DIM**-0.5, span, 0)
    for t in range(tiles):
        span = pl.ds(t * TILE, TILE)
        d_x[span, :] = dot(d_t[:, span], w[...], TN).astype(jnp.bfloat16)
    for t in range(x.shape[1] // TILE):
        span = pl.ds(t * TILE, TILE)
        d_w[:, span] = dot(d_t[...], x[:, span]).astype(jnp.bfloat16)


def attend_back(x, w, cos, sin, q_t, k_t, v_t, total, lse, d_att):
    length, width = x.shape
    nat = pltpu.VMEM((length, HEAD_DIM), jnp.bfloat16)
    return pl.pallas_call(
        attend_back_kernel,
        out_shape=[
            jax.ShapeDtypeStruct((length, width), jnp.bfloat16),
            jax.ShapeDtypeStruct((3 * HEAD_DIM, width), jnp.bfloat16),
        ],
        in_specs=[VMEM] * 10,
        out_specs=[VMEM] * 2,
        scratch_shapes=[
            pltpu.VMEM((3 * HEAD_DIM, length), jnp.bfloat16),
            nat,
            nat,
            nat,
            nat,
            pltpu.VMEM((HEAD_DIM, length), jnp.bfloat16),
            pltpu.VMEM((HEAD_DIM, length), jnp.float32),
            pltpu.VMEM((1, length), jnp.float32),
        ],
        compiler_params=pltpu.CompilerParams(vmem_limit_bytes=48 * 2**20),
    )(x, w, cos, sin, q_t, k_t, v_t, total, lse, d_att)


class Ring:
    def __init__(self):
        self.me, self.core, self.place, self.chips = ring_place()
        self.right = self.device(1, self.core)
        self.left = self.device(-1, self.core)
        self.sibling = self.device(0, 1 - self.core)
        self.steps = self.chips // 2

    def chip(self, ahead):
        return (self.place + ahead + self.chips) % self.chips

    def device(self, ahead, core):
        return ring_device(self.chip(ahead), core, self.chips)


class Gather:
    def __init__(self, ring, everyone, sems):
        self.ring, self.everyone = ring, everyone
        self.send, self.recv, self.side_send, self.side_recv = sems
        self.messages = ring.chips - 1
        self.rows = everyone.shape[1] // 2

    def piece(self, device, half):
        return self.everyone.at[device, pl.ds(half * self.rows, self.rows)]

    def half(self, way, j):
        return j % 2 if way == 0 else 1 - j % 2

    def owner(self, way, j, core):
        return self.ring.device(-(j // 2) if way == 0 else j // 2, core)

    def hop(self, way, j):
        ref = self.piece(self.owner(way, j, self.ring.core), self.half(way, j))
        target = self.ring.right if way == 0 else self.ring.left
        return remote(ref, ref, self.send.at[way, j], self.recv.at[way, j], target)

    def across(self, way, j):
        if j < 0:
            ref = self.piece(self.ring.me, -j - 1)
            slot = self.messages
        else:
            ref = self.piece(self.owner(way, j + 2, self.ring.core), self.half(way, j))
            slot = j
        if j < 0:
            way = -j - 1
        return remote(
            ref, ref, self.side_send.at[way, slot], self.side_recv.at[way, slot], self.ring.sibling
        )

    def start(self):
        for j in range(2):
            for way in range(2):
                self.hop(way, j).start()
        for j in range(2):
            self.across(0, -1 - j).start()

    def wait_sibling(self):
        for j in range(2):
            self.across(0, -1 - j).wait_recv()

    def pass_on(self, j):
        for way in range(2):
            self.hop(way, j).wait_recv()
            if j + 2 < self.messages:
                self.hop(way, j + 2).start()
            self.across(way, j).start()

    def wait_across(self, j):
        for way in range(2):
            self.across(way, j).wait_recv()

    def finish(self):
        for way in range(2):
            self.across(0, -1 - way).wait_send()
            for j in range(self.messages):
                self.hop(way, j).wait_send()
                self.across(way, j).wait_send()

    @staticmethod
    def scratch(chips):
        return [DMA((2, chips - 1)), DMA((2, chips - 1)), DMA((2, chips)), DMA((2, chips))]


class Scatter:
    def __init__(self, ring, parts, side, inbox, outbox, sems):
        self.ring, self.parts, self.side, self.inbox, self.outbox = ring, parts, side, inbox, outbox
        self.send, self.recv, self.side_send, self.side_recv = sems
        self.messages = ring.chips - 1
        self.rows = parts.shape[1] // 2
        self.waited = set()

    def across(self, ahead):
        slot = ahead % self.ring.chips
        return remote(
            self.parts.at[self.ring.device(ahead, 1 - self.ring.core)],
            self.side.at[slot],
            self.side_send.at[slot],
            self.side_recv.at[slot],
            self.ring.sibling,
        )

    def hop(self, way, j):
        target = self.ring.right if way == 0 else self.ring.left
        return remote(
            self.outbox.at[way, j],
            self.inbox.at[way, j],
            self.send.at[way, j],
            self.recv.at[way, j],
            target,
        )

    def own(self, ahead, half):
        if ahead % self.ring.chips not in self.waited:
            self.waited.add(ahead % self.ring.chips)
            self.across(ahead).wait_recv()
        span = pl.ds(half * self.rows, self.rows)
        mine = self.parts[self.ring.device(ahead, self.ring.core), span].astype(jnp.float32)
        return mine + self.side[ahead % self.ring.chips, span].astype(jnp.float32)

    def step(self, j):
        for way in range(2):
            half = j % 2 if way == 0 else 1 - j % 2
            ahead = self.ring.steps - (j + 1) // 2
            total = self.own(ahead if way == 0 else -ahead, half)
            if j >= 2:
                self.hop(way, j - 2).wait_recv()
                total += self.inbox[way, j - 2].astype(jnp.float32)
            self.outbox[way, j] = total.astype(self.outbox.dtype)
            self.hop(way, j).start()

    def result(self, half):
        total = self.own(0, half)
        for way in range(2):
            last = self.messages - 1 if half == way else self.messages - 2
            self.hop(way, last).wait_recv()
            total += self.inbox[way, last].astype(jnp.float32)
        return total

    def finish(self):
        for ahead in range(self.ring.chips):
            self.across(ahead).wait_send()
        for way in range(2):
            for j in range(self.messages):
                self.hop(way, j).wait_send()

    @staticmethod
    def scratch(chips, rows, columns, dtype):
        box = pltpu.VMEM((2, chips - 1, rows // 2, columns), dtype)
        return [pltpu.VMEM((chips, rows, columns), dtype), box, box] + [
            DMA((2, chips - 1)),
            DMA((2, chips - 1)),
            DMA((chips,)),
            DMA((chips,)),
        ]


def normalized(values):
    center = values - jnp.mean(values, -1, keepdims=True)
    scale = lax.rsqrt(jnp.mean(center * center, -1, keepdims=True) + 1e-05)
    return center * scale, scale


def norm_back(grad, hat, scale, gain):
    d_hat = grad * gain
    mean = jnp.mean(d_hat, -1, keepdims=True)
    along = jnp.mean(d_hat * hat, -1, keepdims=True)
    return scale * (d_hat - mean - hat * along)


def gelu_and_slope(u):
    c = math.sqrt(2.0 / math.pi)
    square = u * u
    t = jnp.tanh(c * u * (1.0 + 0.044715 * square))
    act = 0.5 * u * (1.0 + t)
    slope = 0.5 * (1.0 + t) + 0.5 * u * (1.0 - t * t) * (c * (1.0 + 3 * 0.044715 * square))
    return act, slope


def mlp_kernel(
    tokens, att_t, w_out, w_up, w_down, norms, corpus, weight, cotangent,
    output, d_hidden_out, d_att, grad_up, grad_down, grad_out, norm_grads,
    mid_all, dd_all, parts1, parts2, act_all, slope_all, d_up_all, hidden_s, proj_s, *rest
):
    sems = list(rest)
    ring = Ring()
    gather1 = Gather(ring, mid_all, sems[0:4])
    gather2 = Gather(ring, dd_all, sems[4:8])
    scatter1 = Scatter(ring, parts1, *sems[8:11], sems[11:15])
    scatter2 = Scatter(ring, parts2, *sems[15:18], sems[18:22])
    greet((ring.left, ring.right, ring.sibling))
    low = jnp.bfloat16
    rows = tokens.shape[0]
    width = tokens.shape[1]
    steps = ring.steps

    def gain(i):
        return norms[i : i + 1, :]

    def bias(i):
        return norms[4 + i : 5 + i, :]

    proj = dot(att_t[...], w_out[...], TN)
    proj_s[...] = proj
    hat1, _ = normalized(proj)
    hidden = tokens[...].astype(jnp.float32) + hat1 * gain(1) + bias(1)
    hidden_s[...] = hidden
    hat2, _ = normalized(hidden)
    mid_all[ring.me] = (hat2 * gain(2) + bias(2)).astype(low)
    gather1.start()

    def chip_rows(ahead):
        return ring.device(ahead, 0)

    def forward(ahead):
        base = chip_rows(ahead)
        x = mid_all[pl.ds(base, 2)].reshape(2 * rows, width)
        act, slope = gelu_and_slope(dot(x, w_up[...]))
        act = act.astype(low)
        act_all[pl.ds(base, 2)] = act.reshape(2, rows, act.shape[1])
        slope_all[pl.ds(base, 2)] = slope.reshape(2, rows, act.shape[1])
        part = dot(act, w_down[...]).astype(low)
        parts1[pl.ds(base, 2)] = part.reshape(2, rows, width)
        scatter1.across(ahead).start()

    def backward(ahead):
        base = chip_rows(ahead)
        x = dd_all[pl.ds(base, 2)].reshape(2 * rows, width)
        d_act = dot(x, w_down[...], NT)
        slope = slope_all[pl.ds(base, 2)].reshape(2 * rows, d_act.shape[1])
        d_up = (d_act * slope).astype(low)
        d_up_all[pl.ds(base, 2)] = d_up.reshape(2, rows, d_up.shape[1])
        part = dot(d_up, w_up[...], NT).astype(low)
        parts2[pl.ds(base, 2)] = part.reshape(2, rows, width)
        scatter2.across(ahead).start()

    def there_and_back(gather, scatter, work, fill):
        gather.wait_sibling()
        work(0)
        for k in range(1, steps):
            for j in (2 * k - 2, 2 * k - 1):
                gather.pass_on(j)
            for j in (2 * k - 2, 2 * k - 1):
                gather.wait_across(j)
            work(-k)
            work(k)
        scatter.step(1)
        gather.pass_on(2 * steps - 2)
        gather.wait_across(2 * steps - 2)
        work(steps)
        scatter.step(0)
        for j in range(2, scatter.messages):
            fill(j)
            scatter.step(j)
        fill(scatter.messages)

    there_and_back(gather1, scatter1, forward, lambda j: None)

    row_weight = jnp.zeros((rows, 1), jnp.float32)
    for c in range(weight.shape[0]):
        row_weight += jnp.where(corpus[...] == c, weight[c], 0.0)
    for half in range(2):
        span = pl.ds(half * (rows // 2), rows // 2)
        down = scatter1.result(half)
        hat3, scale3 = normalized(down)
        hidden = hidden_s[span, :]
        output[span, :] = (hidden + hat3 * gain(3) + bias(3)).astype(low)
        grad_y = cotangent[span, :].astype(jnp.float32) * row_weight[half * (rows // 2) : (half + 1) * (rows // 2)]
        d_hidden_out[span, :] = grad_y
        dd_all[ring.me, span] = norm_back(grad_y, hat3, scale3, gain(3)).astype(low)
        g3 = jnp.sum(grad_y * hat3, 0, keepdims=True)
        b3 = jnp.sum(grad_y, 0, keepdims=True)
        if half == 0:
            norm_grads[3:4, :] = g3
            norm_grads[7:8, :] = b3
        else:
            norm_grads[3:4, :] += g3
            norm_grads[7:8, :] += b3
    gather2.start()

    units = w_up.shape[1]
    length = rows * 2 * ring.chips

    def fill(j):
        for i in (j - 2, j - 2 + 6) if j - 2 < 2 else (j - 2,):
            if i >= 8:
                continue
            span = pl.ds((i % 4) * (width // 4), width // 4)
            if i < 4:
                dd = dd_all[:, :, span].reshape(length, width // 4)
                act = act_all[...].reshape(length, units)
                grad_down[:, span] = dot(act, dd, TN).astype(low)
            else:
                x = mid_all[:, :, span].reshape(length, width // 4)
                d_up = d_up_all[...].reshape(length, units)
                grad_up[span, :] = dot(d_up, x, TN).T.astype(low)

    there_and_back(gather2, scatter2, backward, fill)

    hat1, scale1 = normalized(proj_s[...])
    hat2, scale2 = normalized(hidden_s[...])
    d_mid = jnp.concatenate([scatter2.result(0), scatter2.result(1)], 0)
    norm_grads[2:3, :] = jnp.sum(d_mid * hat2, 0, keepdims=True)
    norm_grads[6:7, :] = jnp.sum(d_mid, 0, keepdims=True)
    d_hidden = d_hidden_out[...] + norm_back(d_mid, hat2, scale2, gain(2))
    d_hidden_out[...] = d_hidden
    norm_grads[1:2, :] = jnp.sum(d_hidden * hat1, 0, keepdims=True)
    norm_grads[5:6, :] = jnp.sum(d_hidden, 0, keepdims=True)
    d_proj = norm_back(d_hidden, hat1, scale1, gain(1)).astype(low)
    d_att[...] = dot(w_out[...], d_proj, NT).astype(low)
    grad_out[...] = dot(att_t[...], d_proj).astype(low)
    norm_grads[0:1, :] = jnp.zeros((1, width), jnp.float32)
    norm_grads[4:5, :] = jnp.zeros((1, width), jnp.float32)
    gather1.finish()
    gather2.finish()
    scatter1.finish()
    scatter2.finish()


def mlp(tokens, att_t, w_out, w_up, w_down, norms, corpus, weight, cotangent, number):
    size = lax.axis_size("seq")
    chips = size // 2
    rows, width = tokens.shape
    units = w_down.shape[0]
    low, full = jnp.bfloat16, jnp.float32
    shape = jax.ShapeDtypeStruct
    blocks = pltpu.VMEM((size, rows, width), low)
    return pl.pallas_call(
        mlp_kernel,
        out_shape=[
            shape((rows, width), low),
            shape((rows, width), full),
            shape((width, rows), low),
            shape((width, units), low),
            shape((units, width), low),
            shape((width, width), low),
            shape((8, width), full),
        ],
        in_specs=[VMEM] * 7 + [pl.BlockSpec(memory_space=pltpu.SMEM), VMEM],
        out_specs=[VMEM] * 7,
        scratch_shapes=[blocks] * 4
        + [
            pltpu.VMEM((size, rows, units), low),
            pltpu.VMEM((size, rows, units), full),
            pltpu.VMEM((size, rows, units), low),
            pltpu.VMEM((rows, width), full),
            pltpu.VMEM((rows, width), full),
        ]
        + Gather.scratch(chips) * 2
        + Scatter.scratch(chips, rows, width, low) * 2,
        compiler_params=pltpu.CompilerParams(
            collective_id=number, has_side_effects=True, vmem_limit_bytes=58 * 2**20
        ),
    )(tokens, att_t, w_out, w_up, w_down, norms, corpus, weight, cotangent)


def layer_norm(values, gain, bias):
    center = values - jnp.mean(values, -1, keepdims=True)
    variance = jnp.mean(center * center, -1, keepdims=True)
    return center * lax.rsqrt(variance + 1e-05) * gain + bias


def gelu_tanh(values):
    return jax.nn.gelu(values, approximate=True)


def turn_tables(length):
    half = HEAD_DIM // 2
    freq = np.exp(
        np.arange(half, dtype=np.float32) * np.float32(-2.0 * math.log(10000.0) / HEAD_DIM)
    )
    angle = freq[:, None] * np.arange(length, dtype=np.float32)[None, :]
    return jnp.asarray(np.cos(angle)), jnp.asarray(np.sin(angle))


def split_heads(
    tokens, w_qkv, w_out, w_up, w_down, norm_gains, norm_biases, corpus_id, corpus_weight, cotangent
):
    size = lax.axis_size("seq")
    _, rows, width = tokens.shape
    length = rows * size
    low = jnp.bfloat16
    w_rows = w_qkv.shape[0]
    hidden_units = w_down.shape[0]

    qkv_blocks = w_qkv.reshape(w_rows, 3, HEADS, HEAD_DIM).transpose(2, 0, 1, 3)
    qkv_blocks = qkv_blocks.reshape(HEADS, w_rows, 3 * HEAD_DIM)
    up_blocks = w_up.reshape(w_rows, size, hidden_units).transpose(1, 0, 2)
    norms = jnp.concatenate([norm_gains, norm_biases, norm_gains, norm_biases], 0)
    norms = jnp.concatenate([norms, norms], 1)
    qkv_all, up_all = exchange((qkv_blocks, up_blocks), 1)
    out_all, norms_all = gather((w_out, jnp.concatenate([norms, norms], 0)), 2)
    w_head = qkv_all.reshape(width, 3 * HEAD_DIM).T
    w_up_own = up_all.reshape(width, hidden_units)
    w_out_all = out_all.reshape(width, width)
    norms_all = norms_all[:, :8, :w_rows].transpose(1, 0, 2).reshape(8, width).astype(jnp.float32)
    gains, biases = norms_all[:4], norms_all[4:]

    cos, sin = turn_tables(length)
    x_float = tokens[0].astype(jnp.float32)
    normed_low, input_back = jax.vjp(layer_norm, x_float, gains[0], biases[0])
    normed_low = normed_low.astype(low)
    (normed_all,) = gather((normed_low,), 3)
    normed_all = normed_all.reshape(length, width)
    q_t, k_t, v_t, total, lse, att_blocks = attend(normed_all, w_head, cos, sin)
    (att_t,) = exchange((att_blocks,), 4)
    att_t = att_t.reshape(width, rows)
    output, d_hidden, d_att_t, grad_up, grad_down, grad_out, norm_grads = mlp(
        tokens[0],
        att_t,
        w_out_all,
        w_up_own,
        w_down,
        norms_all,
        corpus_id.reshape(rows, 1),
        corpus_weight,
        cotangent[0],
        5,
    )
    d_att_blocks, grad_up_all = exchange(
        (d_att_t.reshape(HEADS, HEAD_DIM, rows), grad_up.reshape(size, w_rows, hidden_units)), 9
    )
    d_normed_part, grad_head = attend_back(
        normed_all, w_head, cos, sin, q_t, k_t, v_t, total, lse, d_att_blocks
    )
    d_normed = scatter(d_normed_part.reshape(size, rows, width), 10)
    grad_out = scatter(grad_out.reshape(size, w_rows, width), 11)
    d_input, gain_zero, bias_zero = input_back(d_normed)
    grad_tokens = d_hidden + d_input
    grads = norm_grads.at[0].set(gain_zero).at[4].set(bias_zero)
    grads = grads.reshape(8, size, w_rows).transpose(1, 0, 2)
    grads = jnp.pad(grads, ((0, 0), (0, 8), (0, 128 - w_rows))).astype(low)
    head_all, grads_all = exchange(
        (grad_head.T.reshape(size, w_rows, 3 * HEAD_DIM), grads), 12
    )
    grad_qkv = head_all.reshape(HEADS, w_rows, 3, HEAD_DIM).transpose(1, 2, 0, 3)
    grad_qkv = grad_qkv.reshape(w_rows, 3 * width)
    grad_up = grad_up_all.transpose(1, 0, 2).reshape(w_rows, size * hidden_units)
    grads = jnp.sum(grads_all[:, :8, :w_rows].astype(jnp.float32), 0)

    def swap(value):
        mine = value.astype(low)
        other = lax.ppermute(mine, "dp", [(0, 1), (1, 0)])
        return mine.astype(jnp.float32) + other.astype(jnp.float32)

    grads = swap(grads)
    return (
        output[None],
        grad_tokens[None],
        swap(grad_qkv),
        swap(grad_out),
        swap(grad_up),
        swap(grad_down),
        grads[:4],
        grads[4:],
    )


def shifted(x, axis, by):
    size = lax.axis_size(axis)
    return lax.ppermute(x, axis, [(i, (i + by) % size) for i in range(size)])


def passed_along(value, axis, steps):
    count = lax.axis_size(axis)
    first, last = (max(0, -steps), min(count, count - steps))
    return lax.ppermute(value, axis, [(source, source + steps) for source in range(first, last)])


def rotate(values, position, direction):
    half_size = values.shape[-1] // 2
    freq = jnp.exp(
        jnp.arange(half_size).astype(jnp.float32) * (-2.0 * math.log(10000.0) / values.shape[-1])
    )
    angle = position[:, None] * freq[None, :]
    cosine = jnp.cos(angle)[:, None, :]
    sine = direction * jnp.sin(angle)[:, None, :]
    first = values[..., :half_size]
    second = values[..., half_size:]
    return jnp.concatenate([first * cosine - second * sine, first * sine + second * cosine], -1)


def per_device(
    tokens, w_qkv, w_out, w_up, w_down, norm_gains, norm_biases, corpus_id, corpus_weight, cotangent
):
    full_qkv, full_out, full_up, full_down, gains_low, biases_low = (
        lax.all_gather(w_qkv, "seq", axis=0, tiled=True),
        lax.all_gather(w_out, "seq", axis=0, tiled=True),
        lax.all_gather(w_up, "seq", axis=0, tiled=True),
        lax.all_gather(w_down, "seq", axis=0, tiled=True),
        lax.all_gather(norm_gains, "seq", axis=1, tiled=True),
        lax.all_gather(norm_biases, "seq", axis=1, tiled=True),
    )
    gains = gains_low.astype(jnp.float32)
    biases = biases_low.astype(jnp.float32)
    seq_count, row_count, model_width = tokens.shape
    shape_heads = (seq_count, row_count, HEADS, HEAD_DIM)
    scale = HEAD_DIM ** (-0.5)
    cycle_size = lax.axis_size("seq")
    cycle_index = lax.axis_index("seq")
    query_pos = cycle_index * row_count + jnp.arange(row_count)
    position = query_pos.astype(jnp.float32)
    x_float = tokens.astype(jnp.float32)
    normed_low = layer_norm(x_float, gains[0], biases[0]).astype(jnp.bfloat16)
    qkv = jnp.einsum("std,de->ste", normed_low, full_qkv, preferred_element_type=jnp.float32)
    query_low = rotate(qkv[..., :model_width].reshape(shape_heads), position, 1.0).astype(
        jnp.bfloat16
    )
    key_low = rotate(
        qkv[..., model_width : 2 * model_width].reshape(shape_heads), position, 1.0
    ).astype(jnp.bfloat16)
    value_low = qkv[..., 2 * model_width :].reshape(shape_heads).astype(jnp.bfloat16)

    def block_scores(key_piece, key_pos):
        scores = (
            jnp.einsum("sqhd,skhd->shqk", query_low, key_piece, preferred_element_type=jnp.float32)
            * scale
        )
        allowed = query_pos[:, None] >= key_pos[None, :]
        return (scores, allowed)

    stat_shape = (seq_count, HEADS, row_count)
    key_piece = lax.all_gather(key_low, "seq", axis=1, tiled=True)
    value_piece = lax.all_gather(value_low, "seq", axis=1, tiled=True)
    key_pos = jnp.arange(key_piece.shape[1])
    run_max = jnp.full(stat_shape, -1e30, jnp.float32)
    scores, allowed = block_scores(key_piece, key_pos)
    new_max = jnp.maximum(run_max, jnp.max(jnp.where(allowed, scores, -1e30), -1))
    weights = jnp.where(allowed, jnp.exp(scores - new_max[..., None]), 0.0)
    run_sum = jnp.sum(weights, -1)
    total = jnp.einsum(
        "shqk,skhd->sqhd",
        weights.astype(jnp.bfloat16),
        value_piece,
        preferred_element_type=jnp.float32,
    )
    run_max, run_sum, total = (new_max, run_sum, total)
    log_sum = run_max + jnp.log(run_sum)
    attended = total / jnp.transpose(run_sum, (0, 2, 1))[..., None]
    attended_low = attended.reshape(seq_count, row_count, model_width).astype(jnp.bfloat16)
    proj = jnp.einsum("std,de->ste", attended_low, full_out, preferred_element_type=jnp.float32)
    hidden = x_float + layer_norm(proj, gains[1], biases[1])
    mid_low = layer_norm(hidden, gains[2], biases[2]).astype(jnp.bfloat16)
    up_proj = jnp.einsum("std,df->stf", mid_low, full_up, preferred_element_type=jnp.float32)
    act_low = gelu_tanh(up_proj).astype(jnp.bfloat16)
    down = jnp.einsum("stf,fd->std", act_low, full_down, preferred_element_type=jnp.float32)
    output = (hidden + layer_norm(down, gains[3], biases[3])).astype(jnp.bfloat16)
    matches = (corpus_id[..., None] == jnp.arange(corpus_weight.shape[0])).astype(jnp.float32)
    row_weight = jnp.sum(matches * corpus_weight, -1)
    grad_y = cotangent.astype(jnp.float32) * row_weight[..., None]
    _, down_back = jax.vjp(layer_norm, down, gains[3], biases[3])
    d_down, gain_three, bias_three = down_back(grad_y)
    d_down_low = d_down.astype(jnp.bfloat16)
    grad_down = jnp.einsum("stf,std->fd", act_low, d_down_low, preferred_element_type=jnp.float32)
    d_act = jnp.einsum("std,fd->stf", d_down_low, full_down, preferred_element_type=jnp.float32)
    _, gelu_back = jax.vjp(gelu_tanh, up_proj)
    d_up_low = gelu_back(d_act)[0].astype(jnp.bfloat16)
    grad_up = jnp.einsum("std,stf->df", mid_low, d_up_low, preferred_element_type=jnp.float32)
    d_mid = jnp.einsum("stf,df->std", d_up_low, full_up, preferred_element_type=jnp.float32)
    _, mid_back = jax.vjp(layer_norm, hidden, gains[2], biases[2])
    d_hidden_mid, gain_two, bias_two = mid_back(d_mid)
    d_hidden = grad_y + d_hidden_mid
    _, proj_back = jax.vjp(layer_norm, proj, gains[1], biases[1])
    d_proj, gain_one, bias_one = proj_back(d_hidden)
    d_proj_low = d_proj.astype(jnp.bfloat16)
    grad_out = jnp.einsum(
        "std,ste->de", attended_low, d_proj_low, preferred_element_type=jnp.float32
    )
    d_att_low = (
        jnp.einsum("ste,de->std", d_proj_low, full_out, preferred_element_type=jnp.float32)
        .astype(jnp.bfloat16)
        .reshape(shape_heads)
    )
    delta = jnp.transpose(jnp.sum(d_att_low.astype(jnp.float32) * attended, -1), (0, 2, 1))

    def contribute(d_query, key_piece, value_piece, d_key, d_value, owner):
        key_pos = owner * row_count + jnp.arange(row_count)
        query_sum = d_query
        key_sum = d_key
        value_sum = d_value
        scores, allowed = block_scores(key_piece, key_pos)
        probs = jnp.where(allowed, jnp.exp(scores - log_sum[..., None]), 0.0)
        value_sum = value_sum + jnp.einsum(
            "shqk,sqhd->skhd",
            probs.astype(jnp.bfloat16),
            d_att_low,
            preferred_element_type=jnp.float32,
        )
        d_probs = jnp.einsum(
            "sqhd,skhd->shqk", d_att_low, value_piece, preferred_element_type=jnp.float32
        )
        d_scores = (probs * (d_probs - delta[..., None]) * scale).astype(jnp.bfloat16)
        query_sum = query_sum + jnp.einsum(
            "shqk,skhd->sqhd", d_scores, key_piece, preferred_element_type=jnp.float32
        )
        key_sum = key_sum + jnp.einsum(
            "shqk,sqhd->skhd", d_scores, query_low, preferred_element_type=jnp.float32
        )
        return (query_sum, key_sum, value_sum)

    zeros_heads = jnp.zeros(shape_heads, jnp.float32)

    def pass_grads(d_key, d_value):
        return (
            shifted(d_key.astype(jnp.bfloat16), "seq", 1).astype(d_key.dtype),
            shifted(d_value.astype(jnp.bfloat16), "seq", 1).astype(d_value.dtype),
        )

    def cycle_turn(turn_index, state):
        d_query, key_piece, value_piece, d_key, d_value = state
        owner = (cycle_index - turn_index) % cycle_size
        d_query, d_key, d_value = contribute(d_query, key_piece, value_piece, d_key, d_value, owner)
        d_key, d_value = pass_grads(d_key, d_value)
        key_piece, value_piece = passed_along((key_piece, value_piece), "seq", 1)
        return (d_query, key_piece, value_piece, d_key, d_value)

    d_query, key_piece, value_piece, d_key, d_value = lax.fori_loop(
        0, cycle_size - 1, cycle_turn, (zeros_heads, key_low, value_low, zeros_heads, zeros_heads)
    )
    last_owner = (cycle_index + 1) % cycle_size
    d_query, d_key, d_value = contribute(
        d_query, key_piece, value_piece, d_key, d_value, last_owner
    )
    d_key, d_value = pass_grads(d_key, d_value)
    flat_shape = (seq_count, row_count, model_width)
    d_qkv_low = jnp.concatenate(
        [
            rotate(d_query, position, -1.0).reshape(flat_shape),
            rotate(d_key, position, -1.0).reshape(flat_shape),
            d_value.reshape(flat_shape),
        ],
        -1,
    ).astype(jnp.bfloat16)
    grad_qkv = jnp.einsum("std,ste->de", normed_low, d_qkv_low, preferred_element_type=jnp.float32)
    d_normed = jnp.einsum("ste,de->std", d_qkv_low, full_qkv, preferred_element_type=jnp.float32)
    _, input_back = jax.vjp(layer_norm, x_float, gains[0], biases[0])
    d_input, gain_zero, bias_zero = input_back(d_normed)
    grad_tokens = d_hidden + d_input
    grad_gains = jnp.stack([gain_zero, gain_one, gain_two, gain_three])
    grad_biases = jnp.stack([bias_zero, bias_one, bias_two, bias_three])
    all_grads = (grad_qkv, grad_out, grad_up, grad_down, grad_gains, grad_biases)
    pieces = (
        lax.psum_scatter(
            all_grads[0].astype(jnp.bfloat16), "seq", scatter_dimension=0, tiled=True
        ).astype(jnp.float32),
        lax.psum_scatter(
            all_grads[1].astype(jnp.bfloat16), "seq", scatter_dimension=0, tiled=True
        ).astype(jnp.float32),
        lax.psum_scatter(
            all_grads[2].astype(jnp.bfloat16), "seq", scatter_dimension=0, tiled=True
        ).astype(jnp.float32),
        lax.psum_scatter(
            all_grads[3].astype(jnp.bfloat16), "seq", scatter_dimension=0, tiled=True
        ).astype(jnp.float32),
        lax.psum_scatter(
            all_grads[4].astype(jnp.bfloat16), "seq", scatter_dimension=1, tiled=True
        ).astype(jnp.float32),
        lax.psum_scatter(
            all_grads[5].astype(jnp.bfloat16), "seq", scatter_dimension=1, tiled=True
        ).astype(jnp.float32),
    )
    shards = (
        lax.psum(pieces[0].astype(jnp.bfloat16), "dp").astype(jnp.float32),
        lax.psum(pieces[1].astype(jnp.bfloat16), "dp").astype(jnp.float32),
        lax.psum(pieces[2].astype(jnp.bfloat16), "dp").astype(jnp.float32),
        lax.psum(pieces[3].astype(jnp.bfloat16), "dp").astype(jnp.float32),
        lax.psum(pieces[4].astype(jnp.bfloat16), "dp").astype(jnp.float32),
        lax.psum(pieces[5].astype(jnp.bfloat16), "dp").astype(jnp.float32),
    )
    return (output, grad_tokens, shards[0], shards[1], shards[2], shards[3], shards[4], shards[5])


def solution(mesh):
    placed = (
        P("dp", "seq", None),
        P("seq", None),
        P("seq", None),
        P("seq", None),
        P("seq", None),
        P(None, "seq"),
        P(None, "seq"),
        P("dp", "seq"),
        P(),
        P("dp", "seq", None),
    )
    fits = mesh.shape["seq"] == HEADS and mesh.shape["dp"] == 2
    return jax.shard_map(
        split_heads if fits else per_device,
        mesh=mesh,
        in_specs=placed,
        out_specs=(
            P("dp", "seq", None),
            P("dp", "seq", None),
            P("seq", None),
            P("seq", None),
            P("seq", None),
            P("seq", None),
            P(None, "seq"),
            P(None, "seq"),
        ),
        check_vma=False,
    )
```

```python
import functools
import math

import jax
import jax.numpy as jnp
import numpy as np
from jax import lax
from jax.experimental import pallas as pl
from jax.experimental.pallas import tpu as pltpu
from jax.sharding import PartitionSpec as P

HEADS = 16
HEAD_DIM = 64
MESH = pl.DeviceIdType.MESH
ANY = pl.BlockSpec(memory_space=pl.ANY)
VMEM = pl.BlockSpec(memory_space=pltpu.VMEM)
DMA = pltpu.SemaphoreType.DMA
TILE = 256


def ring_place():
    me = lax.axis_index("seq")
    chips = lax.axis_size("seq") // 2
    core = me % 2
    column = (me // 2) % 2
    row = me // 4
    place = row + column * (chips - 1 - 2 * row)
    return me, core, place, chips


def ring_device(place, core, chips):
    place = (place + 2 * chips) % chips
    column = place // (chips // 2)
    row = place + column * (chips - 1 - 2 * place)
    return row * 4 + column * 2 + core


def greet(devices):
    barrier = pltpu.get_barrier_semaphore()
    for device in devices:
        pl.semaphore_signal(barrier, inc=1, device_id={"seq": device}, device_id_type=MESH)
    pl.semaphore_wait(barrier, len(devices))


def remote(source, target, send, recv, device):
    return pltpu.make_async_remote_copy(
        src_ref=source,
        dst_ref=target,
        send_sem=send,
        recv_sem=recv,
        device_id={"seq": device},
        device_id_type=MESH,
    )


def dot(left, right, contract=((1,), (0,))):
    return lax.dot_general(
        left, right, (contract, ((), ())), preferred_element_type=jnp.float32
    )


NT = ((1,), (1,))
TN = ((0,), (0,))


class Ring:
    def __init__(self):
        self.me, self.core, self.place, self.chips = ring_place()
        self.right = self.device(1, self.core)
        self.left = self.device(-1, self.core)
        self.sibling = self.device(0, 1 - self.core)
        self.steps = self.chips // 2

    def chip(self, ahead):
        return (self.place + ahead + self.chips) % self.chips

    def device(self, ahead, core):
        return ring_device(self.chip(ahead), core, self.chips)


class Gather:
    def __init__(self, ring, everyone, sems):
        self.ring, self.everyone = ring, everyone
        self.send, self.recv, self.side_send, self.side_recv = sems
        self.messages = ring.chips - 1
        self.rows = everyone.shape[1] // 2

    def piece(self, device, half):
        return self.everyone.at[device, pl.ds(half * self.rows, self.rows)]

    def half(self, way, j):
        return j % 2 if way == 0 else 1 - j % 2

    def owner(self, way, j, core):
        return self.ring.device(-(j // 2) if way == 0 else j // 2, core)

    def hop(self, way, j):
        ref = self.piece(self.owner(way, j, self.ring.core), self.half(way, j))
        target = self.ring.right if way == 0 else self.ring.left
        return remote(ref, ref, self.send.at[way, j], self.recv.at[way, j], target)

    def across(self, way, j):
        if j < 0:
            ref = self.piece(self.ring.me, -j - 1)
            slot = self.messages
        else:
            ref = self.piece(self.owner(way, j + 2, self.ring.core), self.half(way, j))
            slot = j
        if j < 0:
            way = -j - 1
        return remote(
            ref, ref, self.side_send.at[way, slot], self.side_recv.at[way, slot], self.ring.sibling
        )

    def start(self):
        for j in range(2):
            for way in range(2):
                self.hop(way, j).start()
        for j in range(2):
            self.across(0, -1 - j).start()

    def wait_sibling(self):
        for j in range(2):
            self.across(0, -1 - j).wait_recv()

    def pass_on(self, j):
        for way in range(2):
            self.hop(way, j).wait_recv()
            if j + 2 < self.messages:
                self.hop(way, j + 2).start()
            self.across(way, j).start()

    def wait_across(self, j):
        for way in range(2):
            self.across(way, j).wait_recv()

    def finish(self):
        for way in range(2):
            self.across(0, -1 - way).wait_send()
            for j in range(self.messages):
                self.hop(way, j).wait_send()
                self.across(way, j).wait_send()

    @staticmethod
    def scratch(chips):
        return [DMA((2, chips - 1)), DMA((2, chips - 1)), DMA((2, chips)), DMA((2, chips))]


class Scatter:
    def __init__(self, ring, parts, side, inbox, outbox, sems):
        self.ring, self.parts, self.side, self.inbox, self.outbox = ring, parts, side, inbox, outbox
        self.send, self.recv, self.side_send, self.side_recv = sems
        self.messages = ring.chips - 1
        self.rows = parts.shape[1] // 2
        self.waited = set()

    def across(self, ahead):
        slot = ahead % self.ring.chips
        return remote(
            self.parts.at[self.ring.device(ahead, 1 - self.ring.core)],
            self.side.at[slot],
            self.side_send.at[slot],
            self.side_recv.at[slot],
            self.ring.sibling,
        )

    def hop(self, way, j):
        target = self.ring.right if way == 0 else self.ring.left
        return remote(
            self.outbox.at[way, j],
            self.inbox.at[way, j],
            self.send.at[way, j],
            self.recv.at[way, j],
            target,
        )

    def own(self, ahead, half):
        if ahead % self.ring.chips not in self.waited:
            self.waited.add(ahead % self.ring.chips)
            self.across(ahead).wait_recv()
        span = pl.ds(half * self.rows, self.rows)
        mine = self.parts[self.ring.device(ahead, self.ring.core), span].astype(jnp.float32)
        return mine + self.side[ahead % self.ring.chips, span].astype(jnp.float32)

    def step(self, j):
        for way in range(2):
            half = j % 2 if way == 0 else 1 - j % 2
            ahead = self.ring.steps - (j + 1) // 2
            total = self.own(ahead if way == 0 else -ahead, half)
            if j >= 2:
                self.hop(way, j - 2).wait_recv()
                total += self.inbox[way, j - 2].astype(jnp.float32)
            self.outbox[way, j] = total.astype(self.outbox.dtype)
            self.hop(way, j).start()

    def result(self, half):
        total = self.own(0, half)
        for way in range(2):
            last = self.messages - 1 if half == way else self.messages - 2
            self.hop(way, last).wait_recv()
            total += self.inbox[way, last].astype(jnp.float32)
        return total

    def finish(self):
        for ahead in range(self.ring.chips):
            self.across(ahead).wait_send()
        for way in range(2):
            for j in range(self.messages):
                self.hop(way, j).wait_send()

    @staticmethod
    def scratch(chips, rows, columns, dtype):
        box = pltpu.VMEM((2, chips - 1, rows // 2, columns), dtype)
        return [pltpu.VMEM((chips, rows, columns), dtype), box, box] + [
            DMA((2, chips - 1)),
            DMA((2, chips - 1)),
            DMA((chips,)),
            DMA((chips,)),
        ]


def normalized(values):
    center = values - jnp.mean(values, -1, keepdims=True)
    scale = lax.rsqrt(jnp.mean(center * center, -1, keepdims=True) + 1e-05)
    return center * scale, scale


def norm_back(grad, hat, scale, gain):
    d_hat = grad * gain
    mean = jnp.mean(d_hat, -1, keepdims=True)
    along = jnp.mean(d_hat * hat, -1, keepdims=True)
    return scale * (d_hat - mean - hat * along)


def gelu_and_slope(u):
    c = math.sqrt(2.0 / math.pi)
    square = u * u
    t = jnp.tanh(c * u * (1.0 + 0.044715 * square))
    act = 0.5 * u * (1.0 + t)
    slope = 0.5 * (1.0 + t) + 0.5 * u * (1.0 - t * t) * (c * (1.0 + 3 * 0.044715 * square))
    return act, slope


def mlp_kernel(
    tokens, att_t, w_out, w_up, w_down, norms, corpus, weight, cotangent,
    output, d_hidden_out, d_att, grad_up, grad_down, grad_out, norm_grads,
    mid_all, dd_all, parts1, parts2, act_all, slope_all, d_up_all, hidden_s, proj_s, *rest
):
    sems = list(rest)
    ring = Ring()
    gather1 = Gather(ring, mid_all, sems[0:4])
    gather2 = Gather(ring, dd_all, sems[4:8])
    scatter1 = Scatter(ring, parts1, *sems[8:11], sems[11:15])
    scatter2 = Scatter(ring, parts2, *sems[15:18], sems[18:22])
    greet((ring.left, ring.right, ring.sibling))
    low = jnp.bfloat16
    rows = tokens.shape[0]
    width = tokens.shape[1]
    steps = ring.steps

    def gain(i):
        return norms[i : i + 1, :]

    def bias(i):
        return norms[4 + i : 5 + i, :]

    proj = dot(att_t[...], w_out[...], TN)
    proj_s[...] = proj
    hat1, _ = normalized(proj)
    hidden = tokens[...].astype(jnp.float32) + hat1 * gain(1) + bias(1)
    hidden_s[...] = hidden
    hat2, _ = normalized(hidden)
    mid_all[ring.me] = (hat2 * gain(2) + bias(2)).astype(low)
    gather1.start()

    def chip_rows(ahead):
        return ring.device(ahead, 0)

    def forward(ahead):
        base = chip_rows(ahead)
        x = mid_all[pl.ds(base, 2)].reshape(2 * rows, width)
        act, slope = gelu_and_slope(dot(x, w_up[...]))
        act = act.astype(low)
        act_all[pl.ds(base, 2)] = act.reshape(2, rows, act.shape[1])
        slope_all[pl.ds(base, 2)] = slope.reshape(2, rows, act.shape[1])
        part = dot(act, w_down[...]).astype(low)
        parts1[pl.ds(base, 2)] = part.reshape(2, rows, width)
        scatter1.across(ahead).start()

    def backward(ahead):
        base = chip_rows(ahead)
        x = dd_all[pl.ds(base, 2)].reshape(2 * rows, width)
        d_act = dot(x, w_down[...], NT)
        slope = slope_all[pl.ds(base, 2)].reshape(2 * rows, d_act.shape[1])
        d_up = (d_act * slope).astype(low)
        d_up_all[pl.ds(base, 2)] = d_up.reshape(2, rows, d_up.shape[1])
        part = dot(d_up, w_up[...], NT).astype(low)
        parts2[pl.ds(base, 2)] = part.reshape(2, rows, width)
        scatter2.across(ahead).start()

    def there_and_back(gather, scatter, work, fill):
        gather.wait_sibling()
        work(0)
        for k in range(1, steps):
            for j in (2 * k - 2, 2 * k - 1):
                gather.pass_on(j)
            for j in (2 * k - 2, 2 * k - 1):
                gather.wait_across(j)
            work(-k)
            work(k)
        scatter.step(1)
        gather.pass_on(2 * steps - 2)
        gather.wait_across(2 * steps - 2)
        work(steps)
        scatter.step(0)
        for j in range(2, scatter.messages):
            fill(j)
            scatter.step(j)
        fill(scatter.messages)

    there_and_back(gather1, scatter1, forward, lambda j: None)

    row_weight = jnp.zeros((rows, 1), jnp.float32)
    for c in range(weight.shape[0]):
        row_weight += jnp.where(corpus[...] == c, weight[c], 0.0)
    for half in range(2):
        span = pl.ds(half * (rows // 2), rows // 2)
        down = scatter1.result(half)
        hat3, scale3 = normalized(down)
        hidden = hidden_s[span, :]
        output[span, :] = (hidden + hat3 * gain(3) + bias(3)).astype(low)
        grad_y = cotangent[span, :].astype(jnp.float32) * row_weight[half * (rows // 2) : (half + 1) * (rows // 2)]
        d_hidden_out[span, :] = grad_y
        dd_all[ring.me, span] = norm_back(grad_y, hat3, scale3, gain(3)).astype(low)
        g3 = jnp.sum(grad_y * hat3, 0, keepdims=True)
        b3 = jnp.sum(grad_y, 0, keepdims=True)
        if half == 0:
            norm_grads[3:4, :] = g3
            norm_grads[7:8, :] = b3
        else:
            norm_grads[3:4, :] += g3
            norm_grads[7:8, :] += b3
    gather2.start()

    units = w_up.shape[1]
    length = rows * 2 * ring.chips

    def fill(j):
        for i in (j - 2, j - 2 + 6) if j - 2 < 2 else (j - 2,):
            if i >= 8:
                continue
            span = pl.ds((i % 4) * (width // 4), width // 4)
            if i < 4:
                dd = dd_all[:, :, span].reshape(length, width // 4)
                act = act_all[...].reshape(length, units)
                grad_down[:, span] = dot(act, dd, TN).astype(low)
            else:
                x = mid_all[:, :, span].reshape(length, width // 4)
                d_up = d_up_all[...].reshape(length, units)
                grad_up[span, :] = dot(d_up, x, TN).T.astype(low)

    there_and_back(gather2, scatter2, backward, fill)

    hat1, scale1 = normalized(proj_s[...])
    hat2, scale2 = normalized(hidden_s[...])
    d_mid = jnp.concatenate([scatter2.result(0), scatter2.result(1)], 0)
    norm_grads[2:3, :] = jnp.sum(d_mid * hat2, 0, keepdims=True)
    norm_grads[6:7, :] = jnp.sum(d_mid, 0, keepdims=True)
    d_hidden = d_hidden_out[...] + norm_back(d_mid, hat2, scale2, gain(2))
    d_hidden_out[...] = d_hidden
    norm_grads[1:2, :] = jnp.sum(d_hidden * hat1, 0, keepdims=True)
    norm_grads[5:6, :] = jnp.sum(d_hidden, 0, keepdims=True)
    d_proj = norm_back(d_hidden, hat1, scale1, gain(1)).astype(low)
    d_att[...] = dot(w_out[...], d_proj, NT).astype(low)
    grad_out[...] = dot(att_t[...], d_proj).astype(low)
    norm_grads[0:1, :] = jnp.zeros((1, width), jnp.float32)
    norm_grads[4:5, :] = jnp.zeros((1, width), jnp.float32)
    gather1.finish()
    gather2.finish()
    scatter1.finish()
    scatter2.finish()


def mlp(tokens, att_t, w_out, w_up, w_down, norms, corpus, weight, cotangent, number):
    size = lax.axis_size("seq")
    chips = size // 2
    rows, width = tokens.shape
    units = w_down.shape[0]
    low, full = jnp.bfloat16, jnp.float32
    shape = jax.ShapeDtypeStruct
    blocks = pltpu.VMEM((size, rows, width), low)
    return pl.pallas_call(
        mlp_kernel,
        out_shape=[
            shape((rows, width), low),
            shape((rows, width), full),
            shape((width, rows), low),
            shape((width, units), low),
            shape((units, width), low),
            shape((width, width), low),
            shape((8, width), full),
        ],
        in_specs=[VMEM] * 7 + [pl.BlockSpec(memory_space=pltpu.SMEM), VMEM],
        out_specs=[VMEM] * 7,
        scratch_shapes=[blocks] * 4
        + [
            pltpu.VMEM((size, rows, units), low),
            pltpu.VMEM((size, rows, units), full),
            pltpu.VMEM((size, rows, units), low),
            pltpu.VMEM((rows, width), full),
            pltpu.VMEM((rows, width), full),
        ]
        + Gather.scratch(chips) * 2
        + Scatter.scratch(chips, rows, width, low) * 2,
        compiler_params=pltpu.CompilerParams(
            collective_id=number, has_side_effects=True, vmem_limit_bytes=58 * 2**20
        ),
    )(tokens, att_t, w_out, w_up, w_down, norms, corpus, weight, cotangent)


def signal_all(devices):
    barrier = pltpu.get_barrier_semaphore()
    for device in devices:
        pl.semaphore_signal(barrier, inc=1, device_id={"seq": device}, device_id_type=MESH)


class Exchange:
    def __init__(self, source, target, send, recv):
        self.source, self.target, self.send, self.recv = source, target, send, recv
        self.me, self.size = lax.axis_index("seq"), lax.axis_size("seq")

    def copy(self, i):
        to = (self.me + i) % self.size
        return remote(self.source(to), self.target(self.me), self.send.at[i], self.recv.at[i], to)

    def start(self):
        for i in range(1, self.size):
            self.copy(i).start()

    def wait(self):
        for i in range(1, self.size):
            came = (self.me + self.size - i) % self.size
            ref = self.target(came)
            remote(ref, ref, self.send.at[i], self.recv.at[i], came).wait_recv()

    def finish(self):
        for i in range(1, self.size):
            self.copy(i).wait_send()


def front_kernel(
    tokens, w_qkv, w_out, w_up, gains, biases, cos, sin,
    q_t, k_t, v_t, total, lse, att_t, normed_all, w_t, w_out_all, w_up_all, norms,
    tokens_all, k_nat, scores, head_send, head_recv, norm_send, norm_recv, att_send_buf, *sems
):
    ring = Ring()
    me, size = ring.me, 2 * ring.chips
    low = jnp.bfloat16
    rows, width = tokens.shape
    w_rows = w_qkv.shape[0]
    units = w_up_all.shape[1]
    half = HEAD_DIM // 2
    others = [(me + i) % size for i in range(1, size)]
    signal_all(others)

    gather = Gather(ring, tokens_all, sems[0:4])
    gather_out = Gather(ring, w_out_all, sems[4:8])
    heads = Exchange(lambda d: head_send.at[d], lambda s: head_recv.at[s], sems[8], sems[9])
    norm_sums = Exchange(lambda d: norm_send, lambda s: norm_recv.at[s], sems[10], sems[11])
    ups = Exchange(
        lambda d: w_up.at[:, pl.ds(pl.multiple_of(d * units, units), units)],
        lambda s: w_up_all.at[pl.ds(pl.multiple_of(s * w_rows, w_rows), w_rows)],
        sems[12],
        sems[13],
    )
    att_send, att_recv = sems[14], sems[15]

    tokens_all[me] = tokens[...]
    norm_send[...] = jnp.zeros_like(norm_send)
    norm_send[0:4, 0:w_rows] = gains[...].astype(jnp.float32)
    norm_send[4:8, 0:w_rows] = biases[...].astype(jnp.float32)
    for h in range(HEADS):
        q, k, v = (
            w_qkv[:, i * width + h * HEAD_DIM : i * width + (h + 1) * HEAD_DIM] for i in range(3)
        )
        head_send[h, 0:w_rows] = jnp.concatenate([q, k], 1)
        head_send[h, w_rows : 3 * w_rows // 2] = jnp.concatenate(
            [v[: w_rows // 2], v[w_rows // 2 :]], 1
        )
    pl.semaphore_wait(pltpu.get_barrier_semaphore(), size - 1)
    gather.start()
    norm_sums.start()
    heads.start()
    head_recv[me] = head_send[me]
    norm_recv[me] = norm_send[...]
    w_up_all[pl.ds(pl.multiple_of(me * w_rows, w_rows), w_rows)] = w_up[
        :, pl.ds(pl.multiple_of(me * units, units), units)
    ]
    w_out_all[me] = w_out[...]

    norm_sums.wait()
    for j in range(size // 2):
        norms[:, j * 128 : (j + 1) * 128] = jnp.concatenate(
            [norm_recv[2 * j][:, :w_rows], norm_recv[2 * j + 1][:, :w_rows]], 1
        )
    gain, bias = norms[0:1, :], norms[4:5, :]
    heads.wait()
    for j in range(size // 2):
        span = pl.ds(j * 2 * w_rows, 2 * w_rows)
        pair = [head_recv[2 * j], head_recv[2 * j + 1]]
        qk = jnp.concatenate([p[:w_rows] for p in pair], 0)
        v = jnp.concatenate(
            [p[w_rows:, s] for p in pair for s in (slice(0, HEAD_DIM), slice(HEAD_DIM, None))], 0
        )
        w_t[0 : 2 * HEAD_DIM, span] = qk.astype(jnp.float32).T.astype(low)
        w_t[2 * HEAD_DIM :, span] = v.astype(jnp.float32).T.astype(low)

    def work(ahead):
        base = ring.device(ahead, 0)
        x = tokens_all[pl.ds(base, 2)].reshape(2 * rows, width).astype(jnp.float32)
        hat, _ = normalized(x)
        normed = (hat * gain + bias).astype(low)
        normed_all[pl.ds(base, 2)] = normed.reshape(2, rows, width)
        qkv = dot(w_t[...], normed, NT)
        span = pl.ds(pl.multiple_of(base * rows, 2 * rows), 2 * rows)
        c, s = cos[:, span], sin[:, span]
        for i, (ref, scale) in enumerate(((q_t, HEAD_DIM**-0.5), (k_t, 1.0))):
            first = qkv[i * HEAD_DIM : i * HEAD_DIM + half]
            second = qkv[i * HEAD_DIM + half : (i + 1) * HEAD_DIM]
            turned = jnp.concatenate([first * c - second * s, first * s + second * c], 0)
            ref[:, span] = (turned * scale).astype(low)
            if i == 1:
                k_nat[span, :] = turned.T.astype(low)
        v_t[:, span] = qkv[2 * HEAD_DIM :].astype(low)

    gather.wait_sibling()
    work(0)
    for k in range(1, ring.steps):
        for j in (2 * k - 2, 2 * k - 1):
            gather.pass_on(j)
        if k == ring.steps - 1:
            gather_out.start()
            ups.start()
        for j in (2 * k - 2, 2 * k - 1):
            gather.wait_across(j)
        work(-k)
        work(k)
    gather.pass_on(2 * ring.steps - 2)
    gather.wait_across(2 * ring.steps - 2)
    work(ring.steps)

    length = rows * size
    tiles = length // TILE
    passed = 0
    for t in range(tiles):
        span = pl.ds(t * TILE, TILE)
        query = q_t[:, span]
        top = None
        for j in range(t + 1):
            keys = pl.ds(j * TILE, TILE)
            s = dot(k_nat[keys, :], query)
            if j == t:
                key_pos = lax.broadcasted_iota(jnp.int32, s.shape, 0)
                query_pos = lax.broadcasted_iota(jnp.int32, s.shape, 1)
                s = jnp.where(key_pos <= query_pos, s, -1e30)
            scores[keys, :] = s
            here = jnp.max(s, 0, keepdims=True)
            top = here if top is None else jnp.maximum(top, here)
        acc, norm = None, None
        for j in range(t + 1):
            keys = pl.ds(j * TILE, TILE)
            p = jnp.exp(scores[keys, :] - top)
            here = jnp.sum(p, 0, keepdims=True)
            add = dot(v_t[:, keys], p.astype(low))
            acc = add if acc is None else acc + add
            norm = here if norm is None else norm + here
        acc = acc / norm
        total[:, span] = acc
        lse[:, span] = top + jnp.log(norm)
        for b in range(TILE // rows):
            to = t * (TILE // rows) + b
            block = acc[:, b * rows : (b + 1) * rows].astype(low)
            att_send_buf[to] = block

            @pl.when(me != to)
            def _(to=to):
                remote(
                    att_send_buf.at[to], att_t.at[me], att_send.at[to], att_recv.at[me], to
                ).start()

            @pl.when(me == to)
            def _(to=to, block=block):
                att_t[me] = block

        if t >= tiles - gather_out.messages and passed < gather_out.messages:
            gather_out.pass_on(passed)
            passed += 1
    for j in range(passed, gather_out.messages):
        gather_out.pass_on(j)
    gather_out.wait_sibling()
    for j in range(gather_out.messages):
        gather_out.wait_across(j)
    ups.wait()
    for source in range(size):

        @pl.when(me != source)
        def _(source=source):
            remote(
                att_t.at[source], att_t.at[source], att_send.at[source], att_recv.at[source], source
            ).wait()

    gather.finish()
    gather_out.finish()
    heads.finish()
    norm_sums.finish()
    ups.finish()


def front(tokens, w_qkv, w_out, w_up, gains, biases, cos, sin, number):
    size = lax.axis_size("seq")
    chips = size // 2
    rows, width = tokens.shape
    w_rows = w_qkv.shape[0]
    units = w_up.shape[1] // size
    length = rows * size
    low, full = jnp.bfloat16, jnp.float32
    shape = jax.ShapeDtypeStruct
    head = shape((HEAD_DIM, length), low)
    packed = pltpu.VMEM((size, 3 * w_rows // 2, 2 * HEAD_DIM), low)
    return pl.pallas_call(
        front_kernel,
        out_shape=[
            head,
            head,
            head,
            shape((HEAD_DIM, length), full),
            shape((1, length), full),
            shape((size, HEAD_DIM, rows), low),
            shape((size, rows, width), low),
            shape((3 * HEAD_DIM, width), low),
            shape((size, w_rows, width), low),
            shape((width, units), low),
            shape((8, width), full),
        ],
        in_specs=[VMEM] * 8,
        out_specs=[VMEM] * 11,
        scratch_shapes=[
            pltpu.VMEM((size, rows, width), low),
            pltpu.VMEM((length, HEAD_DIM), low),
            pltpu.VMEM((length, TILE), full),
            packed,
            packed,
            pltpu.VMEM((8, 128), full),
            pltpu.VMEM((size, 8, 128), full),
            pltpu.VMEM((size, HEAD_DIM, rows), low),
        ]
        + Gather.scratch(chips) * 2
        + [DMA((size,))] * 8,
        compiler_params=pltpu.CompilerParams(
            collective_id=number, has_side_effects=True, vmem_limit_bytes=50 * 2**20
        ),
    )(tokens, w_qkv, w_out, w_up, gains, biases, cos, sin)


def swap(source, target, send, recv):
    return pltpu.make_async_remote_copy(
        src_ref=source,
        dst_ref=target,
        send_sem=send,
        recv_sem=recv,
        device_id={"dp": 1 - lax.axis_index("dp")},
        device_id_type=MESH,
    )


def back_kernel(
    d_att, up_in, down_in, out_in, norm_in, d_hidden, tokens, normed_all, w_t, cos, sin,
    q_t, k_t, v_t, total, lse, norms,
    grad_tokens, grad_qkv, grad_out, grad_up, grad_down, grad_gains, grad_biases,
    att_recv, q_nat, k_nat, v_nat, do_nat, do_t, dq, delta, d_t, d_parts,
    up_peer, up_send, up_all, down_peer, out_mine, out_peer,
    head_parts, head_peer, head_send, head_all, norm_send, norm_recv, *rest
):
    ring = Ring()
    me, dp, chips = ring.me, lax.axis_index("dp"), ring.chips
    size = 2 * chips
    low, full = jnp.bfloat16, jnp.float32
    rows, width = tokens.shape
    w_rows = out_in.shape[1]
    units = up_in.shape[2]
    half = HEAD_DIM // 2
    length = rows * size
    tiles = length // TILE
    rest = list(rest)
    scatter = Scatter(ring, d_parts, *rest[0:3], rest[3:7])
    scatter_out = Scatter(ring, out_in, *rest[7:10], rest[10:14])
    swap_send, swap_recv, norm_ssem, norm_rsem = rest[14:18]
    atts = Exchange(lambda d: d_att.at[d], lambda s: att_recv.at[s], rest[18], rest[19])
    kept = w_rows // 2
    ups = Exchange(
        lambda d: up_send.at[d], lambda s: up_all.at[s, pl.ds(dp * kept, kept)], rest[20], rest[21]
    )
    packed = head_send.shape[1]
    heads = Exchange(
        lambda d: head_send.at[d],
        lambda s: head_all.at[s, pl.ds(dp * packed, packed)],
        rest[22],
        rest[23],
    )
    up_half = swap(
        up_in.at[:, pl.ds((1 - dp) * kept, kept)], up_peer, swap_send.at[0], swap_recv.at[0]
    )
    down_whole = swap(down_in, down_peer, swap_send.at[1], swap_recv.at[1])
    out_whole = swap(out_mine, out_peer, swap_send.at[2], swap_recv.at[2])
    up_mine = up_all.at[:, pl.ds(dp * kept, kept)]
    up_back = swap(up_mine, up_mine, swap_send.at[3], swap_recv.at[3])
    head_half = swap(
        head_parts.at[:, pl.ds((1 - dp) * packed, packed)],
        head_peer,
        swap_send.at[4],
        swap_recv.at[4],
    )
    head_mine = head_all.at[:, pl.ds(dp * packed, packed)]
    head_back = swap(head_mine, head_mine, swap_send.at[5], swap_recv.at[5])

    barrier = pltpu.get_barrier_semaphore()
    for i in range(1, size):
        pl.semaphore_signal(
            barrier, inc=1, device_id={"seq": (me + i) % size}, device_id_type=MESH
        )
    for i in range(size):
        pl.semaphore_signal(
            barrier,
            inc=1,
            device_id={"seq": (me + i) % size, "dp": 1 - dp},
            device_id_type=MESH,
        )

    def natural(ref, nat, t):
        span = pl.ds(t * TILE, TILE)
        nat[span, :] = ref[:, span].astype(full).T.astype(low)

    for t in range(tiles):
        for ref, nat in ((q_t, q_nat), (k_t, k_nat), (v_t, v_nat)):
            natural(ref, nat, t)
    pl.semaphore_wait(barrier, 2 * size - 1)
    atts.start()
    up_half.start()
    down_whole.start()
    for ahead in range(chips):
        scatter_out.across(ahead).start()
    att_recv[me] = d_att[me]
    hat0, scale0 = normalized(tokens[...].astype(full))
    dq[...] = jnp.zeros_like(dq)
    scatter_out.step(0)
    scatter_out.step(1)
    atts.wait()
    for b in range(size):
        do_t[:, b * rows : (b + 1) * rows] = att_recv[b]
    for t in range(tiles):
        natural(do_t, do_nat, t)
        span = pl.ds(t * TILE, TILE)
        delta[:, span] = jnp.sum(do_t[:, span].astype(full) * total[:, span], 0, keepdims=True)

    def turned_back(u, span, base):
        c, s = cos[:, span], sin[:, span]
        first, second = u[:half], u[half:]
        d_t[base : base + half, span] = (first * c + second * s).astype(low)
        d_t[base + half : base + 2 * half, span] = (second * c - first * s).astype(low)

    def beside_attention(j):
        if j == 0:
            up_half.wait_recv()
            mine = up_in[:, pl.ds(dp * kept, kept)].astype(full)
            up_send[...] = (mine + up_peer[...].astype(full)).astype(low)
            ups.start()
            up_all[me, pl.ds(dp * kept, kept)] = up_send[me]
        if 1 <= j <= 5:
            scatter_out.step(j + 1)
        if j == 6:
            out_mine[...] = jnp.concatenate(
                [scatter_out.result(0), scatter_out.result(1)], 0
            ).astype(low)
            out_whole.start()
            ups.wait()
            up_back.start()

    for j in range(tiles):
        keys = pl.ds(j * TILE, TILE)
        dk, dv = None, None
        for t in range(j, tiles):
            span = pl.ds(t * TILE, TILE)
            s = dot(k_nat[keys, :], q_t[:, span])
            p = jnp.exp(s - lse[:, span])
            if j == t:
                key_pos = lax.broadcasted_iota(jnp.int32, s.shape, 0)
                query_pos = lax.broadcasted_iota(jnp.int32, s.shape, 1)
                p = jnp.where(key_pos <= query_pos, p, 0.0)
            dp_ = dot(v_nat[keys, :], do_t[:, span])
            ds = (p * (dp_ - delta[:, span])).astype(low)
            dv_add = dot(p.astype(low), do_nat[span, :])
            dk_add = dot(ds, q_nat[span, :])
            dv = dv_add if dv is None else dv + dv_add
            dk = dk_add if dk is None else dk + dk_add
            dq[:, span] += dot(k_t[:, keys], ds)
        turned_back(dk.T, keys, HEAD_DIM)
        d_t[2 * HEAD_DIM :, keys] = dv.T.astype(low)
        turned_back(dq[:, keys] * HEAD_DIM**-0.5, keys, 0)
        beside_attention(j)

    def part(ahead):
        base = ring.device(ahead, 0)
        span = pl.ds(pl.multiple_of(base * rows, 2 * rows), 2 * rows)
        d_x = dot(d_t[:, span], w_t[...], TN).astype(low)
        d_parts[pl.ds(base, 2)] = d_x.reshape(2, rows, width)
        scatter.across(ahead).start()

    def head_gradient(j):
        x = normed_all[:, :, j * 128 : (j + 1) * 128].reshape(length, 128)
        d_w = dot(d_t[...], x).T
        for i in range(2):
            for h in range(2):
                base = i * w_rows + h * kept
                v = d_w[base : base + kept, 2 * HEAD_DIM :]
                head_parts[2 * j + i, h * packed : h * packed + kept] = d_w[
                    base : base + kept, : 2 * HEAD_DIM
                ].astype(low)
                head_parts[2 * j + i, h * packed + kept : (h + 1) * packed] = jnp.concatenate(
                    [v[: kept // 2], v[kept // 2 :]], 1
                ).astype(low)

    steps = ring.steps
    part(steps)
    part(steps - 1)
    part(1 - steps)
    scatter.step(0)
    scatter.step(1)
    for k in range(steps - 2, 0, -1):
        part(k)
        part(-k)
    part(0)
    for j in range(size // 2):
        head_gradient(j)
    head_half.start()
    scatter.step(2)
    scatter.step(3)
    head_half.wait_recv()
    mine = head_parts[:, pl.ds(dp * packed, packed)].astype(full)
    head_send[...] = (mine + head_peer[...].astype(full)).astype(low)
    heads.start()
    head_all[me, pl.ds(dp * packed, packed)] = head_send[me]
    scatter.step(4)
    scatter.step(5)
    down_whole.wait_recv()
    grad_down[...] = down_in[...].astype(full) + down_peer[...].astype(full)
    out_whole.wait_recv()
    grad_out[...] = out_mine[...].astype(full) + out_peer[...].astype(full)
    scatter.step(6)
    heads.wait()
    head_back.start()
    up_back.wait_recv()
    for h in range(size):
        grad_up[:, h * units : (h + 1) * units] = up_all[h].astype(full)

    d_normed = jnp.concatenate([scatter.result(0), scatter.result(1)], 0)
    norm_send[1:4, :] = norm_in[1:4, :]
    norm_send[5:8, :] = norm_in[5:8, :]
    norm_send[0:1, :] = jnp.sum(d_normed * hat0, 0, keepdims=True)
    norm_send[4:5, :] = jnp.sum(d_normed, 0, keepdims=True)

    def norm_copy(i, other):
        to = (me + i) % size
        columns = pl.ds(pl.multiple_of((to // 2) * 128, 128), 128)
        return pltpu.make_async_remote_copy(
            src_ref=norm_send.at[:, columns],
            dst_ref=norm_recv.at[other, i],
            send_sem=norm_ssem.at[other, i],
            recv_sem=norm_rsem.at[other, i],
            device_id={"seq": to, "dp": (dp + other) % 2},
            device_id_type=MESH,
        )

    pairs = [(i, other) for i in range(size) for other in range(2) if i or other]
    for i, other in pairs:
        norm_copy(i, other).start()
    norm_recv[0, 0] = norm_send[:, pl.ds(pl.multiple_of((me // 2) * 128, 128), 128)]
    grad_tokens[...] = d_hidden[...] + norm_back(d_normed, hat0, scale0, norms[0:1, :])
    head_back.wait_recv()
    for h in range(2):
        for j in range(size // 2):
            pair = [head_all[2 * j + i, h * packed : (h + 1) * packed].astype(full) for i in range(2)]
            columns = slice(j * 128, (j + 1) * 128)
            for b in range(2):
                grad_qkv[h * kept : (h + 1) * kept, b * width + j * 128 : b * width + (j + 1) * 128] = (
                    jnp.concatenate(
                        [p[:kept, b * HEAD_DIM : (b + 1) * HEAD_DIM] for p in pair], 1
                    )
                )
            v = [jnp.concatenate([p[kept:, :HEAD_DIM], p[kept:, HEAD_DIM:]], 0) for p in pair]
            grad_qkv[
                h * kept : (h + 1) * kept, 2 * width + j * 128 : 2 * width + (j + 1) * 128
            ] = jnp.concatenate(v, 1)
    for i, other in pairs:
        norm_copy(i, other).wait_recv()
    sums = jnp.sum(norm_recv[...].reshape(2 * size, 8, 128), 0)
    sums = jnp.where(ring.core == 0, sums[:, :w_rows], sums[:, w_rows:])
    grad_gains[...] = sums[0:4]
    grad_biases[...] = sums[4:8]
    for i, other in pairs:
        norm_copy(i, other).wait_send()
    scatter.finish()
    scatter_out.finish()
    atts.finish()
    ups.finish()
    heads.finish()
    for copy in (up_half, down_whole, out_whole, up_back, head_half, head_back):
        copy.wait_send()


def back(
    d_att, up, down, out, norm_grads, d_hidden, tokens, normed_all, w_t, cos, sin,
    q_t, k_t, v_t, total, lse, norms, number
):
    size = lax.axis_size("seq")
    chips = size // 2
    rows, width = tokens.shape
    w_rows = out.shape[1]
    units = up.shape[2]
    length = rows * size
    low, full = jnp.bfloat16, jnp.float32
    shape = jax.ShapeDtypeStruct
    vmem = pltpu.VMEM
    nat = vmem((length, HEAD_DIM), low)
    head_shape = (size, 3 * w_rows // 2, 2 * HEAD_DIM)
    half_shape = (size, 3 * w_rows // 4, 2 * HEAD_DIM)
    return pl.pallas_call(
        back_kernel,
        out_shape=[
            shape((rows, width), full),
            shape((w_rows, 3 * width), full),
            shape((w_rows, width), full),
            shape((w_rows, size * units), full),
            shape(down.shape, full),
            shape((4, w_rows), full),
            shape((4, w_rows), full),
        ],
        in_specs=[VMEM] * 17,
        out_specs=[VMEM] * 7,
        scratch_shapes=[
            vmem((size, HEAD_DIM, rows), low),
            nat,
            nat,
            nat,
            nat,
            vmem((HEAD_DIM, length), low),
            vmem((HEAD_DIM, length), full),
            vmem((1, length), full),
            vmem((3 * HEAD_DIM, length), low),
            vmem((size, rows, width), low),
            vmem((size, w_rows // 2, units), low),
            vmem((size, w_rows // 2, units), low),
            vmem((size, w_rows, units), low),
            vmem(down.shape, low),
            vmem((w_rows, width), low),
            vmem((w_rows, width), low),
            vmem(head_shape, low),
            vmem(half_shape, low),
            vmem(half_shape, low),
            vmem(head_shape, low),
            vmem((8, width), full),
            vmem((2, size, 8, 128), full),
        ]
        + Scatter.scratch(chips, rows, width, low)
        + Scatter.scratch(chips, w_rows, width, low)
        + [DMA((6,)), DMA((6,)), DMA((2, size)), DMA((2, size))]
        + [DMA((size,))] * 6,
        compiler_params=pltpu.CompilerParams(
            collective_id=number, has_side_effects=True, vmem_limit_bytes=58 * 2**20
        ),
    )(
        d_att, up, down, out, norm_grads, d_hidden, tokens, normed_all, w_t, cos, sin,
        q_t, k_t, v_t, total, lse, norms,
    )


def layer_norm(values, gain, bias):
    center = values - jnp.mean(values, -1, keepdims=True)
    variance = jnp.mean(center * center, -1, keepdims=True)
    return center * lax.rsqrt(variance + 1e-05) * gain + bias


def gelu_tanh(values):
    return jax.nn.gelu(values, approximate=True)


def turn_tables(length):
    half = HEAD_DIM // 2
    freq = np.exp(
        np.arange(half, dtype=np.float32) * np.float32(-2.0 * math.log(10000.0) / HEAD_DIM)
    )
    angle = freq[:, None] * np.arange(length, dtype=np.float32)[None, :]
    return jnp.asarray(np.cos(angle)), jnp.asarray(np.sin(angle))


def split_heads(
    tokens, w_qkv, w_out, w_up, w_down, norm_gains, norm_biases, corpus_id, corpus_weight, cotangent
):
    size = lax.axis_size("seq")
    _, rows, width = tokens.shape
    length = rows * size
    low = jnp.bfloat16
    w_rows = w_qkv.shape[0]
    hidden_units = w_down.shape[0]

    cos, sin = turn_tables(length)
    q_t, k_t, v_t, total, lse, att_t, normed_all, w_head, w_out_all, w_up_own, norms_all = front(
        tokens[0], w_qkv, w_out, w_up, norm_gains, norm_biases, cos, sin, 1
    )
    att_t = att_t.reshape(width, rows)
    w_out_all = w_out_all.reshape(width, width)
    output, d_hidden, d_att_t, grad_up, grad_down, grad_out, norm_grads = mlp(
        tokens[0],
        att_t,
        w_out_all,
        w_up_own,
        w_down,
        norms_all,
        corpus_id.reshape(rows, 1),
        corpus_weight,
        cotangent[0],
        5,
    )
    grad_tokens, grad_qkv, grad_out, grad_up, grad_down, grad_gains, grad_biases = back(
        d_att_t.reshape(HEADS, HEAD_DIM, rows),
        grad_up.reshape(size, w_rows, hidden_units),
        grad_down,
        grad_out.reshape(size, w_rows, width),
        norm_grads,
        d_hidden,
        tokens[0],
        normed_all,
        w_head,
        cos,
        sin,
        q_t,
        k_t,
        v_t,
        total,
        lse,
        norms_all,
        9,
    )
    return (
        output[None],
        grad_tokens[None],
        grad_qkv,
        grad_out,
        grad_up,
        grad_down,
        grad_gains,
        grad_biases,
    )


def shifted(x, axis, by):
    size = lax.axis_size(axis)
    return lax.ppermute(x, axis, [(i, (i + by) % size) for i in range(size)])


def passed_along(value, axis, steps):
    count = lax.axis_size(axis)
    first, last = (max(0, -steps), min(count, count - steps))
    return lax.ppermute(value, axis, [(source, source + steps) for source in range(first, last)])


def rotate(values, position, direction):
    half_size = values.shape[-1] // 2
    freq = jnp.exp(
        jnp.arange(half_size).astype(jnp.float32) * (-2.0 * math.log(10000.0) / values.shape[-1])
    )
    angle = position[:, None] * freq[None, :]
    cosine = jnp.cos(angle)[:, None, :]
    sine = direction * jnp.sin(angle)[:, None, :]
    first = values[..., :half_size]
    second = values[..., half_size:]
    return jnp.concatenate([first * cosine - second * sine, first * sine + second * cosine], -1)


def per_device(
    tokens, w_qkv, w_out, w_up, w_down, norm_gains, norm_biases, corpus_id, corpus_weight, cotangent
):
    full_qkv, full_out, full_up, full_down, gains_low, biases_low = (
        lax.all_gather(w_qkv, "seq", axis=0, tiled=True),
        lax.all_gather(w_out, "seq", axis=0, tiled=True),
        lax.all_gather(w_up, "seq", axis=0, tiled=True),
        lax.all_gather(w_down, "seq", axis=0, tiled=True),
        lax.all_gather(norm_gains, "seq", axis=1, tiled=True),
        lax.all_gather(norm_biases, "seq", axis=1, tiled=True),
    )
    gains = gains_low.astype(jnp.float32)
    biases = biases_low.astype(jnp.float32)
    seq_count, row_count, model_width = tokens.shape
    shape_heads = (seq_count, row_count, HEADS, HEAD_DIM)
    scale = HEAD_DIM ** (-0.5)
    cycle_size = lax.axis_size("seq")
    cycle_index = lax.axis_index("seq")
    query_pos = cycle_index * row_count + jnp.arange(row_count)
    position = query_pos.astype(jnp.float32)
    x_float = tokens.astype(jnp.float32)
    normed_low = layer_norm(x_float, gains[0], biases[0]).astype(jnp.bfloat16)
    qkv = jnp.einsum("std,de->ste", normed_low, full_qkv, preferred_element_type=jnp.float32)
    query_low = rotate(qkv[..., :model_width].reshape(shape_heads), position, 1.0).astype(
        jnp.bfloat16
    )
    key_low = rotate(
        qkv[..., model_width : 2 * model_width].reshape(shape_heads), position, 1.0
    ).astype(jnp.bfloat16)
    value_low = qkv[..., 2 * model_width :].reshape(shape_heads).astype(jnp.bfloat16)

    def block_scores(key_piece, key_pos):
        scores = (
            jnp.einsum("sqhd,skhd->shqk", query_low, key_piece, preferred_element_type=jnp.float32)
            * scale
        )
        allowed = query_pos[:, None] >= key_pos[None, :]
        return (scores, allowed)

    stat_shape = (seq_count, HEADS, row_count)
    key_piece = lax.all_gather(key_low, "seq", axis=1, tiled=True)
    value_piece = lax.all_gather(value_low, "seq", axis=1, tiled=True)
    key_pos = jnp.arange(key_piece.shape[1])
    run_max = jnp.full(stat_shape, -1e30, jnp.float32)
    scores, allowed = block_scores(key_piece, key_pos)
    new_max = jnp.maximum(run_max, jnp.max(jnp.where(allowed, scores, -1e30), -1))
    weights = jnp.where(allowed, jnp.exp(scores - new_max[..., None]), 0.0)
    run_sum = jnp.sum(weights, -1)
    total = jnp.einsum(
        "shqk,skhd->sqhd",
        weights.astype(jnp.bfloat16),
        value_piece,
        preferred_element_type=jnp.float32,
    )
    run_max, run_sum, total = (new_max, run_sum, total)
    log_sum = run_max + jnp.log(run_sum)
    attended = total / jnp.transpose(run_sum, (0, 2, 1))[..., None]
    attended_low = attended.reshape(seq_count, row_count, model_width).astype(jnp.bfloat16)
    proj = jnp.einsum("std,de->ste", attended_low, full_out, preferred_element_type=jnp.float32)
    hidden = x_float + layer_norm(proj, gains[1], biases[1])
    mid_low = layer_norm(hidden, gains[2], biases[2]).astype(jnp.bfloat16)
    up_proj = jnp.einsum("std,df->stf", mid_low, full_up, preferred_element_type=jnp.float32)
    act_low = gelu_tanh(up_proj).astype(jnp.bfloat16)
    down = jnp.einsum("stf,fd->std", act_low, full_down, preferred_element_type=jnp.float32)
    output = (hidden + layer_norm(down, gains[3], biases[3])).astype(jnp.bfloat16)
    matches = (corpus_id[..., None] == jnp.arange(corpus_weight.shape[0])).astype(jnp.float32)
    row_weight = jnp.sum(matches * corpus_weight, -1)
    grad_y = cotangent.astype(jnp.float32) * row_weight[..., None]
    _, down_back = jax.vjp(layer_norm, down, gains[3], biases[3])
    d_down, gain_three, bias_three = down_back(grad_y)
    d_down_low = d_down.astype(jnp.bfloat16)
    grad_down = jnp.einsum("stf,std->fd", act_low, d_down_low, preferred_element_type=jnp.float32)
    d_act = jnp.einsum("std,fd->stf", d_down_low, full_down, preferred_element_type=jnp.float32)
    _, gelu_back = jax.vjp(gelu_tanh, up_proj)
    d_up_low = gelu_back(d_act)[0].astype(jnp.bfloat16)
    grad_up = jnp.einsum("std,stf->df", mid_low, d_up_low, preferred_element_type=jnp.float32)
    d_mid = jnp.einsum("stf,df->std", d_up_low, full_up, preferred_element_type=jnp.float32)
    _, mid_back = jax.vjp(layer_norm, hidden, gains[2], biases[2])
    d_hidden_mid, gain_two, bias_two = mid_back(d_mid)
    d_hidden = grad_y + d_hidden_mid
    _, proj_back = jax.vjp(layer_norm, proj, gains[1], biases[1])
    d_proj, gain_one, bias_one = proj_back(d_hidden)
    d_proj_low = d_proj.astype(jnp.bfloat16)
    grad_out = jnp.einsum(
        "std,ste->de", attended_low, d_proj_low, preferred_element_type=jnp.float32
    )
    d_att_low = (
        jnp.einsum("ste,de->std", d_proj_low, full_out, preferred_element_type=jnp.float32)
        .astype(jnp.bfloat16)
        .reshape(shape_heads)
    )
    delta = jnp.transpose(jnp.sum(d_att_low.astype(jnp.float32) * attended, -1), (0, 2, 1))

    def contribute(d_query, key_piece, value_piece, d_key, d_value, owner):
        key_pos = owner * row_count + jnp.arange(row_count)
        query_sum = d_query
        key_sum = d_key
        value_sum = d_value
        scores, allowed = block_scores(key_piece, key_pos)
        probs = jnp.where(allowed, jnp.exp(scores - log_sum[..., None]), 0.0)
        value_sum = value_sum + jnp.einsum(
            "shqk,sqhd->skhd",
            probs.astype(jnp.bfloat16),
            d_att_low,
            preferred_element_type=jnp.float32,
        )
        d_probs = jnp.einsum(
            "sqhd,skhd->shqk", d_att_low, value_piece, preferred_element_type=jnp.float32
        )
        d_scores = (probs * (d_probs - delta[..., None]) * scale).astype(jnp.bfloat16)
        query_sum = query_sum + jnp.einsum(
            "shqk,skhd->sqhd", d_scores, key_piece, preferred_element_type=jnp.float32
        )
        key_sum = key_sum + jnp.einsum(
            "shqk,sqhd->skhd", d_scores, query_low, preferred_element_type=jnp.float32
        )
        return (query_sum, key_sum, value_sum)

    zeros_heads = jnp.zeros(shape_heads, jnp.float32)

    def pass_grads(d_key, d_value):
        return (
            shifted(d_key.astype(jnp.bfloat16), "seq", 1).astype(d_key.dtype),
            shifted(d_value.astype(jnp.bfloat16), "seq", 1).astype(d_value.dtype),
        )

    def cycle_turn(turn_index, state):
        d_query, key_piece, value_piece, d_key, d_value = state
        owner = (cycle_index - turn_index) % cycle_size
        d_query, d_key, d_value = contribute(d_query, key_piece, value_piece, d_key, d_value, owner)
        d_key, d_value = pass_grads(d_key, d_value)
        key_piece, value_piece = passed_along((key_piece, value_piece), "seq", 1)
        return (d_query, key_piece, value_piece, d_key, d_value)

    d_query, key_piece, value_piece, d_key, d_value = lax.fori_loop(
        0, cycle_size - 1, cycle_turn, (zeros_heads, key_low, value_low, zeros_heads, zeros_heads)
    )
    last_owner = (cycle_index + 1) % cycle_size
    d_query, d_key, d_value = contribute(
        d_query, key_piece, value_piece, d_key, d_value, last_owner
    )
    d_key, d_value = pass_grads(d_key, d_value)
    flat_shape = (seq_count, row_count, model_width)
    d_qkv_low = jnp.concatenate(
        [
            rotate(d_query, position, -1.0).reshape(flat_shape),
            rotate(d_key, position, -1.0).reshape(flat_shape),
            d_value.reshape(flat_shape),
        ],
        -1,
    ).astype(jnp.bfloat16)
    grad_qkv = jnp.einsum("std,ste->de", normed_low, d_qkv_low, preferred_element_type=jnp.float32)
    d_normed = jnp.einsum("ste,de->std", d_qkv_low, full_qkv, preferred_element_type=jnp.float32)
    _, input_back = jax.vjp(layer_norm, x_float, gains[0], biases[0])
    d_input, gain_zero, bias_zero = input_back(d_normed)
    grad_tokens = d_hidden + d_input
    grad_gains = jnp.stack([gain_zero, gain_one, gain_two, gain_three])
    grad_biases = jnp.stack([bias_zero, bias_one, bias_two, bias_three])
    all_grads = (grad_qkv, grad_out, grad_up, grad_down, grad_gains, grad_biases)
    pieces = (
        lax.psum_scatter(
            all_grads[0].astype(jnp.bfloat16), "seq", scatter_dimension=0, tiled=True
        ).astype(jnp.float32),
        lax.psum_scatter(
            all_grads[1].astype(jnp.bfloat16), "seq", scatter_dimension=0, tiled=True
        ).astype(jnp.float32),
        lax.psum_scatter(
            all_grads[2].astype(jnp.bfloat16), "seq", scatter_dimension=0, tiled=True
        ).astype(jnp.float32),
        lax.psum_scatter(
            all_grads[3].astype(jnp.bfloat16), "seq", scatter_dimension=0, tiled=True
        ).astype(jnp.float32),
        lax.psum_scatter(
            all_grads[4].astype(jnp.bfloat16), "seq", scatter_dimension=1, tiled=True
        ).astype(jnp.float32),
        lax.psum_scatter(
            all_grads[5].astype(jnp.bfloat16), "seq", scatter_dimension=1, tiled=True
        ).astype(jnp.float32),
    )
    shards = (
        lax.psum(pieces[0].astype(jnp.bfloat16), "dp").astype(jnp.float32),
        lax.psum(pieces[1].astype(jnp.bfloat16), "dp").astype(jnp.float32),
        lax.psum(pieces[2].astype(jnp.bfloat16), "dp").astype(jnp.float32),
        lax.psum(pieces[3].astype(jnp.bfloat16), "dp").astype(jnp.float32),
        lax.psum(pieces[4].astype(jnp.bfloat16), "dp").astype(jnp.float32),
        lax.psum(pieces[5].astype(jnp.bfloat16), "dp").astype(jnp.float32),
    )
    return (output, grad_tokens, shards[0], shards[1], shards[2], shards[3], shards[4], shards[5])


def solution(mesh):
    placed = (
        P("dp", "seq", None),
        P("seq", None),
        P("seq", None),
        P("seq", None),
        P("seq", None),
        P(None, "seq"),
        P(None, "seq"),
        P("dp", "seq"),
        P(),
        P("dp", "seq", None),
    )
    fits = mesh.shape["seq"] == HEADS and mesh.shape["dp"] == 2
    return jax.shard_map(
        split_heads if fits else per_device,
        mesh=mesh,
        in_specs=placed,
        out_specs=(
            P("dp", "seq", None),
            P("dp", "seq", None),
            P("seq", None),
            P("seq", None),
            P("seq", None),
            P("seq", None),
            P(None, "seq"),
            P(None, "seq"),
        ),
        check_vma=False,
    )
```

```python
import functools
import math
import types

import jax
import jax.numpy as jnp
import numpy as np
from jax import lax
from jax.experimental import pallas as pl
from jax.experimental.pallas import tpu as pltpu
from jax.sharding import PartitionSpec as P

HEADS = 16
HEAD_DIM = 64
TILE = 256
MESH = pl.DeviceIdType.MESH
ANY = pl.BlockSpec(memory_space=pl.ANY)
DMA = pltpu.SemaphoreType.DMA
NT = ((1,), (1,))
TN = ((0,), (0,))
low, full = jnp.bfloat16, jnp.float32


def dot(left, right, contract=((1,), (0,))):
    return lax.dot_general(left, right, (contract, ((), ())), preferred_element_type=full)


def remote(source, target, send, recv, device):
    return pltpu.make_async_remote_copy(
        src_ref=source,
        dst_ref=target,
        send_sem=send,
        recv_sem=recv,
        device_id={"seq": device},
        device_id_type=MESH,
    )


def swap(source, target, send, recv):
    return pltpu.make_async_remote_copy(
        src_ref=source,
        dst_ref=target,
        send_sem=send,
        recv_sem=recv,
        device_id={"dp": 1 - lax.axis_index("dp")},
        device_id_type=MESH,
    )


class Ring:
    def __init__(self):
        self.me = lax.axis_index("seq")
        self.size = lax.axis_size("seq")
        self.chips = self.size // 2
        self.steps = self.chips // 2
        self.core = self.me % 2
        column, row = (self.me // 2) % 2, self.me // 4
        self.place = row + column * (self.chips - 1 - 2 * row)
        self.right = self.device(1, self.core)
        self.left = self.device(-1, self.core)
        self.sibling = self.device(0, 1 - self.core)

    def device(self, ahead, core):
        place = (self.place + ahead + self.chips) % self.chips
        column = place // (self.chips // 2)
        row = place + column * (self.chips - 1 - 2 * place)
        return row * 4 + column * 2 + core


class Gather:
    def __init__(self, ring, piece, block, blocks, pieces, sems):
        self.ring, self.piece, self.block, self.blocks = ring, piece, block, blocks
        self.pieces = pieces
        self.send, self.recv, self.side_send, self.side_recv = sems
        self.messages = self.count(ring.chips, pieces)

    @staticmethod
    def count(chips, pieces):
        return pieces * (chips // 2) - pieces // 2

    def ref(self, way, j, ahead):
        k, q = j // self.pieces + ahead, j % self.pieces
        q = q if way == 0 else self.pieces - 1 - q
        return self.piece(self.ring.device(-k if way == 0 else k, self.ring.core), q)

    def hop(self, way, j):
        ref = self.ref(way, j, 0)
        target = self.ring.right if way == 0 else self.ring.left
        return remote(ref, ref, self.send.at[0], self.recv.at[way, j], target)

    def landed(self, way, j):
        return self.ref(way, j, 1)

    def side(self, ref, slot):
        return remote(ref, ref, self.side_send.at[0], self.side_recv.at[slot], self.ring.sibling)

    def start(self):
        for j in range(self.pieces):
            for way in range(2):
                self.hop(way, j).start()
        self.side(self.block(self.ring.me), 0).start()

    def pass_on(self, j):
        k = j // self.pieces + 1
        for way in range(2):
            self.hop(way, j).wait_recv()
            if j + self.pieces < self.messages:
                self.hop(way, j + self.pieces).start()
            slot = (-k if way == 0 else k) % self.ring.chips
            self.side(self.landed(way, j), slot).start()

    def wait_chip(self, ahead):
        block = self.block(self.ring.device(ahead, 1 - self.ring.core))
        self.side(block, ahead % self.ring.chips).wait_recv()

    def finish(self):
        count = self.ring.chips - 1
        everything = self.blocks(count)
        remote(everything, everything, self.send.at[0], self.recv.at[0, 0], self.ring.right).wait_send()
        self.side(self.blocks(count + 1), 0).wait_send()

    @staticmethod
    def sems(chips, pieces):
        return [DMA((1,)), DMA((2, Gather.count(chips, pieces))), DMA((1,)), DMA((chips,))]


class Scatter:
    def __init__(self, ring, parts, pieces, side, inbox, outbox, sems):
        self.ring, self.parts, self.pieces = ring, parts, pieces
        self.side, self.inbox, self.outbox = side, inbox, outbox
        self.send, self.recv, self.side_send, self.side_recv = sems
        self.messages = Gather.count(ring.chips, pieces)
        self.rows = parts.shape[1] // pieces
        self.waited = set()

    def across(self, ahead):
        slot = ahead % self.ring.chips
        return remote(
            self.parts.at[self.ring.device(ahead, 1 - self.ring.core)],
            self.side.at[slot],
            self.side_send.at[0],
            self.side_recv.at[slot],
            self.ring.sibling,
        )

    def hop(self, way, j):
        target = self.ring.right if way == 0 else self.ring.left
        return remote(
            self.outbox.at[way, j],
            self.inbox.at[way, j],
            self.send.at[0],
            self.recv.at[way, j],
            target,
        )

    def own(self, ahead, q):
        slot = ahead % self.ring.chips
        if slot not in self.waited:
            self.waited.add(slot)
            self.across(ahead).wait_recv()
        span = pl.ds(q * self.rows, self.rows)
        mine = self.parts[self.ring.device(ahead, self.ring.core), span].astype(full)
        return mine + self.side[slot, span].astype(full)

    def ahead(self, j):
        return self.ring.steps - (j + self.pieces // 2) // self.pieces

    def step(self, j):
        for way in range(2):
            q = j % self.pieces if way == 0 else self.pieces - 1 - j % self.pieces
            total = self.own(self.ahead(j) if way == 0 else -self.ahead(j), q)
            if j >= self.pieces:
                self.hop(way, j - self.pieces).wait_recv()
                total += self.inbox[way, j - self.pieces].astype(full)
            self.outbox[way, j] = total.astype(self.outbox.dtype)
            self.hop(way, j).start()

    def result(self, q):
        total = self.own(0, q)
        for way in range(2):
            k = q if way == 0 else self.pieces - 1 - q
            last = max(j for j in range(self.messages) if j % self.pieces == k)
            self.hop(way, last).wait_recv()
            total += self.inbox[way, last].astype(full)
        return total

    def whole(self):
        return jnp.concatenate([self.result(q) for q in range(self.pieces)], 0)

    def finish(self):
        everything = self.parts.at[pl.ds(0, self.ring.chips)]
        side = self.side_send.at[0], self.side_recv.at[0]
        remote(everything, self.side, *side, self.ring.sibling).wait_send()
        hops = self.send.at[0], self.recv.at[0, 0]
        remote(self.outbox, self.inbox, *hops, self.ring.right).wait_send()

    @staticmethod
    def buffers(chips, rows, columns, pieces):
        box = pltpu.VMEM((2, Gather.count(chips, pieces), rows // pieces, columns), low)
        return [pltpu.VMEM((chips, rows, columns), low), box, box]

    @staticmethod
    def sems(chips, pieces):
        return [DMA((1,)), DMA((2, Gather.count(chips, pieces))), DMA((1,)), DMA((chips,))]


class Exchange:
    def __init__(self, source, target, blocks, sems):
        self.source, self.target, self.blocks = source, target, blocks
        self.send, self.recv = sems
        self.me, self.size = lax.axis_index("seq"), lax.axis_size("seq")

    def start(self):
        for i in range(1, self.size):
            to = (self.me + i) % self.size
            remote(
                self.source(to), self.target(self.me), self.send.at[0], self.recv.at[0], to
            ).start()

    def all(self):
        ref = self.blocks(self.size - 1)
        to = (self.me + 1) % self.size
        return remote(ref, ref, self.send.at[0], self.recv.at[0], to)

    def wait(self):
        self.all().wait_recv()

    def finish(self):
        self.all().wait_send()


def normalized(values):
    center = values - jnp.mean(values, -1, keepdims=True)
    scale = lax.rsqrt(jnp.mean(center * center, -1, keepdims=True) + 1e-05)
    return center * scale, scale


def norm_back(grad, hat, scale, gain):
    d_hat = grad * gain
    mean = jnp.mean(d_hat, -1, keepdims=True)
    along = jnp.mean(d_hat * hat, -1, keepdims=True)
    return scale * (d_hat - mean - hat * along)


def gelu_and_slope(u):
    c = math.sqrt(2.0 / math.pi)
    square = u * u
    t = jnp.tanh(c * u * (1.0 + 0.044715 * square))
    act = 0.5 * u * (1.0 + t)
    slope = 0.5 * (1.0 + t) + 0.5 * u * (1.0 - t * t) * (c * (1.0 + 3 * 0.044715 * square))
    return act, slope


def causal(shape):
    key_pos = lax.broadcasted_iota(jnp.int32, shape, 0)
    query_pos = lax.broadcasted_iota(jnp.int32, shape, 1)
    return key_pos <= query_pos


def turn_tables(length):
    half = HEAD_DIM // 2
    freq = np.exp(
        np.arange(half, dtype=np.float32) * np.float32(-2.0 * math.log(10000.0) / HEAD_DIM)
    )
    angle = freq[:, None] * np.arange(length, dtype=np.float32)[None, :]
    return jnp.asarray(np.cos(angle)), jnp.asarray(np.sin(angle))


INPUTS = (
    "tokens",
    "w_qkv",
    "gains",
    "biases",
    "w_out",
    "w_up",
    "cos",
    "sin",
    "w_down",
    "cotangent",
    "corpus",
)
OUTPUTS = (
    "output",
    "grad_tokens",
    "grad_qkv",
    "grad_out",
    "grad_up",
    "grad_down",
    "grad_gains",
    "grad_biases",
)


def layer_kernel(names, *refs):
    r = types.SimpleNamespace(**dict(zip(names, refs, strict=True)))
    ring = Ring()
    me, core, size, chips, steps = ring.me, ring.core, ring.size, ring.chips, ring.steps
    dp = lax.axis_index("dp")
    rows, width = r.tokens.shape
    w_rows = r.w_out.shape[0]
    units = r.w_down.shape[0]
    length = rows * size
    tiles = length // TILE
    half = HEAD_DIM // 2
    kept = w_rows // 2
    packed = 3 * kept // 2
    pair = 2 * rows

    def mine(ref):
        return ref.at[:, pl.ds(dp * (ref.shape[1] // 2), ref.shape[1] // 2)]

    def theirs(ref):
        return ref.at[:, pl.ds((1 - dp) * (ref.shape[1] // 2), ref.shape[1] // 2)]

    def columns(device, count):
        return pl.ds(pl.multiple_of(device * count, count), count)

    loads = {
        name: pltpu.make_async_copy(getattr(r, name), getattr(r, name + "_v"), r.load_sem.at[i])
        for i, name in enumerate(INPUTS)
    }
    for name in INPUTS:
        loads[name].start()
    barrier = pltpu.get_barrier_semaphore()
    for i in range(1, size):
        pl.semaphore_signal(barrier, inc=1, device_id={"seq": (me + i) % size}, device_id_type=MESH)
    pl.semaphore_signal(barrier, inc=1, device_id={"dp": 1 - dp}, device_id_type=MESH)

    quarter = rows // 4

    def gather(ref, count, sems, first=0):
        pieces = 4 if ref.shape[1] == rows else 2
        return Gather(
            ring,
            lambda d, q: ref.at[d, pl.ds(first + q * (count // pieces), count // pieces)],
            lambda d: ref.at[d, pl.ds(first, count)],
            lambda n: ref.at[pl.ds(0, n), pl.ds(0, count)],
            pieces,
            sems,
        )

    tokens_in = gather(r.big, rows, r.gather0)
    mids = gather(r.mid_all, rows, r.gather0)
    d_downs = gather(r.big, rows, r.gather0)
    w_outs = gather(r.w_out_all, kept, r.gather1, dp * kept)
    sum_down = Scatter(ring, r.parts, 4, r.side, r.inbox, r.outbox, r.scatter0)
    sum_mid = Scatter(ring, r.parts, 4, r.side, r.inbox, r.outbox, r.scatter0)
    sum_in = Scatter(ring, r.parts, 4, r.side, r.inbox, r.outbox, r.scatter0)
    sum_out = Scatter(ring, r.out_parts, 2, r.out_side, r.out_inbox, r.out_outbox, r.scatter1)

    def exchange(source, ref, sems, count):
        return Exchange(
            source,
            lambda d: ref.at[d, pl.ds(dp * count if count < ref.shape[1] else 0, count)],
            lambda n: ref.at[pl.ds(0, n), pl.ds(0, count)],
            sems,
        )

    head_weights = exchange(lambda d: r.head_send.at[d], r.head_recv, r.exchange0, packed)
    norm_rows = exchange(lambda d: r.norm_send, r.norm_recv, r.exchange1, 8)
    up_weights = exchange(
        lambda d: r.w_up_v.at[pl.ds(dp * kept, kept), columns(d, units)],
        r.w_up_all,
        r.exchange2,
        kept,
    )
    d_atts = exchange(lambda d: r.d_att.at[d], r.att_recv, r.exchange3, HEAD_DIM)
    up_grads = exchange(lambda d: r.up_send.at[d], r.up_all, r.exchange4, kept)
    head_grads = exchange(lambda d: r.head_send.at[d], r.head_all, r.exchange5, packed)

    def swapped(source, target, slot):
        return swap(source, target, r.swap_send.at[slot], r.swap_recv.at[slot])

    head_other = swapped(mine(r.head_recv), mine(r.head_recv), 0)
    up_other = swapped(mine(r.w_up_all), mine(r.w_up_all), 1)
    up_half = swapped(theirs(r.up_grad), r.up_peer, 2)
    down_whole = swapped(r.down_grad, r.down_peer, 3)
    out_whole = swapped(r.out_mine, r.out_peer, 4)
    up_back = swapped(mine(r.up_all), mine(r.up_all), 5)
    head_half = swapped(theirs(r.head_parts), r.head_peer, 6)
    head_back = swapped(mine(r.head_all), mine(r.head_all), 7)

    loads["w_qkv"].wait()
    rows_mine = pl.ds(dp * kept, kept)
    for h in range(HEADS):
        q, k, v = (
            r.w_qkv_v[rows_mine, i * width + h * HEAD_DIM : i * width + (h + 1) * HEAD_DIM]
            for i in range(3)
        )
        r.head_send[h, 0:kept] = jnp.concatenate([q, k], 1)
        r.head_send[h, kept:packed] = jnp.concatenate([v[: kept // 2], v[kept // 2 :]], 1)
    r.head_recv[me, pl.ds(dp * packed, packed)] = r.head_send[me]
    loads["gains"].wait()
    loads["biases"].wait()
    r.norm_send[...] = jnp.zeros_like(r.norm_send)
    r.norm_send[0:4, 0:w_rows] = r.gains_v[...].astype(full)
    r.norm_send[4:8, 0:w_rows] = r.biases_v[...].astype(full)
    r.norm_recv[me] = r.norm_send[...]
    loads["tokens"].wait()
    r.big[me] = r.tokens_v[...]
    pl.semaphore_wait(barrier, size)
    tokens_in.start()
    norm_rows.start()
    head_weights.start()

    def gain(i):
        return r.norms[i : i + 1, :]

    def bias(i):
        return r.norms[4 + i : 5 + i, :]

    loads["w_out"].wait()
    r.w_out_all[me] = r.w_out_v[...]
    loads["w_up"].wait()
    r.w_up_all[me, rows_mine] = r.w_up_v[rows_mine, columns(me, units)]
    loads["cos"].wait()
    loads["sin"].wait()
    for name in ("w_down", "cotangent", "corpus"):
        loads[name].wait()

    def unpack_heads():
        head_other.wait_recv()
        for j in range(size // 2):
            span = pl.ds(j * 2 * w_rows, 2 * w_rows)
            qk, v = [], []
            for d in (2 * j, 2 * j + 1):
                for h in range(2):
                    p = r.head_recv[d, h * packed : (h + 1) * packed]
                    qk.append(p[:kept])
                    v += [p[kept:, :HEAD_DIM], p[kept:, HEAD_DIM:]]
            r.w_t[0 : 2 * HEAD_DIM, span] = jnp.concatenate(qk, 0).astype(full).T.astype(low)
            r.w_t[2 * HEAD_DIM :, span] = jnp.concatenate(v, 0).astype(full).T.astype(low)

    def project(ahead):
        base = ring.device(ahead, 0)
        x = r.big[pl.ds(base, 2)].reshape(pair, width).astype(full)
        hat, _ = normalized(x)
        normed = (hat * gain(0) + bias(0)).astype(low)
        r.normed_all[pl.ds(base, 2)] = normed.reshape(2, rows, width)
        qkv = dot(r.w_t[...], normed, NT)
        span = pl.ds(pl.multiple_of(base * rows, pair), pair)
        c, s = r.cos_v[:, span], r.sin_v[:, span]
        for i, (ref, nat, scale) in enumerate(
            ((r.q_t, r.q_nat, HEAD_DIM**-0.5), (r.k_t, r.k_nat, 1.0))
        ):
            first = qkv[i * HEAD_DIM : i * HEAD_DIM + half]
            second = qkv[i * HEAD_DIM + half : (i + 1) * HEAD_DIM]
            turned = jnp.concatenate([first * c - second * s, first * s + second * c], 0) * scale
            ref[:, span] = turned.astype(low)
            nat[span, :] = turned.T.astype(low)
        v = qkv[2 * HEAD_DIM :]
        r.v_t[:, span] = v.astype(low)
        r.v_nat[span, :] = v.T.astype(low)

    def out_swap(ref, way, j):
        return swap(ref, ref, r.out_swap_send.at[0], r.out_swap_recv.at[way, j])

    def out_other(way, j):
        k, q = j // 2 + 1, j % 2
        q = q if way == 0 else 1 - q
        device = ring.device(-k if way == 0 else k, core)
        return r.w_out_all.at[device, pl.ds((1 - dp) * kept + q * (kept // 2), kept // 2)]

    def out_side(ref, slot):
        send, recv = r.out_side_send.at[slot], r.out_side_recv.at[slot]
        return remote(ref, ref, send, recv, ring.sibling)

    def out_own():
        return out_side(r.w_out_all.at[me, pl.ds((1 - dp) * kept, kept)], 0)

    def out_others():
        return out_side(w_outs.blocks(chips - 1), 1)

    def pass_out(j):
        w_outs.pass_on(j)
        for way in range(2):
            out_swap(w_outs.landed(way, j), way, j).start()

    def pass_other(j):
        for way in range(2):
            ref = out_other(way, j)
            out_swap(ref, way, j).wait_recv()
            out_side(ref, 1).start()

    for j in range(4):
        tokens_in.pass_on(j)
    norm_rows.wait()
    for j in range(size // 2):
        r.norms[:, j * 128 : (j + 1) * 128] = jnp.concatenate(
            [r.norm_recv[2 * j][:, :w_rows], r.norm_recv[2 * j + 1][:, :w_rows]], 1
        )
    head_weights.wait()
    head_other.start()
    for j in range(4, 8):
        tokens_in.pass_on(j)
    unpack_heads()
    for ahead in (0, 1, -1):
        tokens_in.wait_chip(ahead)
        project(ahead)
    for j in range(8, 12):
        tokens_in.pass_on(j)
    w_outs.start()
    out_own().start()
    for ahead in (2, -2):
        tokens_in.wait_chip(ahead)
        project(ahead)
    for j in range(12, 14):
        tokens_in.pass_on(j)
    up_weights.start()
    pass_out(0)
    pass_out(1)
    for ahead in (3, -3, 4):
        tokens_in.wait_chip(ahead)
        project(ahead)

    for t in range(tiles):
        span = pl.ds(t * TILE, TILE)
        query = r.q_t[:, span]
        top = None
        for j in range(t + 1):
            keys = pl.ds(j * TILE, TILE)
            s = dot(r.k_nat[keys, :], query)
            if j == t:
                s = jnp.where(causal(s.shape), s, -1e30)
            r.scores[keys, :] = s
            here = jnp.max(s, 0, keepdims=True)
            top = here if top is None else jnp.maximum(top, here)
        acc, norm = None, None
        for j in range(t + 1):
            keys = pl.ds(j * TILE, TILE)
            p = jnp.exp(r.scores[keys, :] - top)
            here = jnp.sum(p, 0, keepdims=True)
            add = dot(r.v_t[:, keys], p.astype(low))
            acc = add if acc is None else acc + add
            norm = here if norm is None else norm + here
        acc = acc / norm
        r.total[:, span] = acc
        r.lse[:, span] = top + jnp.log(norm)
        for b in range(TILE // rows):
            to = t * (TILE // rows) + b
            block = acc[:, b * rows : (b + 1) * rows].astype(low)
            r.att_send[to] = block

            @pl.when(me != to)
            def _(to=to):
                remote(
                    r.att_send.at[to], r.att_t.at[me], r.att_ssem.at[0], r.att_rsem.at[0], to
                ).start()

            @pl.when(me == to)
            def _(block=block):
                r.att_t[me] = block

        if t in (2, 4):
            pass_out(t)
            pass_out(t + 1)
            pass_other(t - 2)
            pass_other(t - 1)
        if t == 6:
            pass_out(6)
            pass_other(4)
            pass_other(5)
    pass_other(6)
    up_weights.wait()
    up_other.start()
    for ahead in range(chips):
        w_outs.wait_chip(ahead)
    out_own().wait_recv()
    out_others().wait_recv()
    attended = r.att_t.at[pl.ds(0, size - 1)]
    attended = remote(attended, attended, r.att_ssem.at[0], r.att_rsem.at[0], ring.right)
    attended.wait()
    tokens_in.finish()

    att_t = r.att_t[...].reshape(width, rows)
    w_out_all = r.w_out_all
    proj = dot(att_t, w_out_all[...].reshape(width, width), TN)
    r.proj[...] = proj
    hat1, _ = normalized(proj)
    hidden = r.tokens_v[...].astype(full) + hat1 * gain(1) + bias(1)
    r.hidden[...] = hidden
    hat2, _ = normalized(hidden)
    r.mid_all[me] = (hat2 * gain(2) + bias(2)).astype(low)
    mids.start()
    up_other.wait_recv()
    w_outs.finish()

    def w_up():
        return r.w_up_all[...].reshape(width, units)

    def forward(ahead):
        base = ring.device(ahead, 0)
        x = r.mid_all[pl.ds(base, 2)].reshape(pair, width)
        act, slope = gelu_and_slope(dot(x, w_up()))
        act = act.astype(low)
        r.act_all[pl.ds(base, 2)] = act.reshape(2, rows, units)
        r.slope_all[pl.ds(base, 2)] = slope.reshape(2, rows, units)
        part = dot(act, r.w_down_v[...]).astype(low)
        r.parts[pl.ds(base, 2)] = part.reshape(2, rows, width)
        sum_down.across(ahead).start()

    def backward(ahead):
        base = ring.device(ahead, 0)
        x = r.big[pl.ds(base, 2)].reshape(pair, width)
        d_act = dot(x, r.w_down_v[...], NT)
        slope = r.slope_all[pl.ds(base, 2)].reshape(pair, units)
        d_up = (d_act * slope).astype(low)
        r.d_up_all[pl.ds(base, 2)] = d_up.reshape(2, rows, units)
        part = dot(d_up, w_up(), NT).astype(low)
        r.parts[pl.ds(base, 2)] = part.reshape(2, rows, width)
        sum_mid.across(ahead).start()

    def there_and_back(gather, scatter, work, fill):
        gather.wait_chip(0)
        work(0)
        for k in range(1, steps + 1):
            arrivals = range(4 * (k - 1), min(4 * k, gather.messages))
            if k == steps:
                scatter.step(2)
                scatter.step(3)
            for j in arrivals:
                gather.pass_on(j)
            for ahead in (k, -k) if k < steps else (k,):
                gather.wait_chip(ahead)
                work(ahead)
        scatter.step(0)
        scatter.step(1)
        for j in range(4, scatter.messages):
            fill(j)
            scatter.step(j)
        fill(scatter.messages)

    there_and_back(mids, sum_down, forward, lambda j: None)

    weight_row = jnp.zeros((1, rows), full)
    for c in range(r.weight.shape[0]):
        weight_row += jnp.where(r.corpus_v[...] == c, r.weight[c], 0.0)
    row_weight = jnp.broadcast_to(weight_row, (rows, rows)).T[:, 0:1]
    for q in range(4):
        span = pl.ds(q * quarter, quarter)
        down = sum_down.result(q)
        hat3, scale3 = normalized(down)
        r.output_v[span, :] = (r.hidden[span, :] + hat3 * gain(3) + bias(3)).astype(low)
        grad_y = r.cotangent_v[span, :].astype(full) * row_weight[q * quarter : (q + 1) * quarter]
        r.d_hidden[span, :] = grad_y
        r.big[me, span] = norm_back(grad_y, hat3, scale3, gain(3)).astype(low)
        g3 = jnp.sum(grad_y * hat3, 0, keepdims=True)
        b3 = jnp.sum(grad_y, 0, keepdims=True)
        r.norm_grads[3:4, :] = g3 if q == 0 else r.norm_grads[3:4, :] + g3
        r.norm_grads[7:8, :] = b3 if q == 0 else r.norm_grads[7:8, :] + b3
    mids.finish()
    sum_down.finish()
    d_downs.start()
    saves = {}

    def save(name):
        i = OUTPUTS.index(name)
        saves[name] = pltpu.make_async_copy(
            getattr(r, name + "_v"), getattr(r, name), r.save_sem.at[i]
        )
        saves[name].start()

    save("output")

    def fill(j):
        i = j - 4
        if i >= 8:
            return
        slice_width = width // 4
        span = pl.ds((i % 4) * slice_width, slice_width)
        if i < 4:
            x = r.mid_all[:, :, span].reshape(length, slice_width)
            d_up = r.d_up_all[...].reshape(length, units)
            grad = dot(d_up, x, TN).T.astype(low)
            blocks = slice_width // w_rows
            r.up_grad[(i % 4) * blocks : (i % 4 + 1) * blocks] = grad.reshape(blocks, w_rows, units)
            if i == 3:
                up_half.start()
        else:
            dd = r.big[:, :, span].reshape(length, slice_width)
            act = r.act_all[...].reshape(length, units)
            r.down_grad[:, span] = dot(act, dd, TN).astype(low)
            if i == 7:
                down_whole.start()

    there_and_back(d_downs, sum_mid, backward, fill)

    hat1, scale1 = normalized(r.proj[...])
    hat2, scale2 = normalized(r.hidden[...])
    hat0, scale0 = normalized(r.tokens_v[...].astype(full))
    r.hat0[...] = hat0
    d_mid = sum_mid.whole()
    r.norm_grads[2:3, :] = jnp.sum(d_mid * hat2, 0, keepdims=True)
    r.norm_grads[6:7, :] = jnp.sum(d_mid, 0, keepdims=True)
    d_hidden = r.d_hidden[...] + norm_back(d_mid, hat2, scale2, gain(2))
    r.d_hidden[...] = d_hidden
    r.norm_grads[1:2, :] = jnp.sum(d_hidden * hat1, 0, keepdims=True)
    r.norm_grads[5:6, :] = jnp.sum(d_hidden, 0, keepdims=True)
    d_proj = norm_back(d_hidden, hat1, scale1, gain(1)).astype(low)
    d_att = dot(w_out_all[...].reshape(width, width), d_proj, NT).astype(low)
    r.d_att[...] = d_att.reshape(HEADS, HEAD_DIM, rows)
    d_atts.start()

    r.out_parts[...] = dot(att_t, d_proj).astype(low).reshape(size, w_rows, width)
    for ahead in range(chips):
        sum_out.across(ahead).start()
    r.att_recv[me] = r.d_att[me]
    d_downs.finish()
    sum_mid.finish()
    r.dq[...] = jnp.zeros_like(r.dq)
    up_half.wait_recv()
    up_mine = r.up_grad[:, rows_mine].astype(full)
    r.up_send[...] = (up_mine + r.up_peer[...].astype(full)).astype(low)
    r.up_all[me, rows_mine] = r.up_send[me]
    d_atts.wait()
    sum_out.step(0)
    sum_out.step(1)
    up_grads.start()
    for b in range(size):
        r.do_t[:, b * rows : (b + 1) * rows] = r.att_recv[b]
    for t in range(tiles):
        span = pl.ds(t * TILE, TILE)
        do = r.do_t[:, span].astype(full)
        r.do_nat[span, :] = do.T.astype(low)
        r.delta[:, span] = jnp.sum(do * r.total[:, span], 0, keepdims=True)

    def turned_back(u, span, base):
        c, s = r.cos_v[:, span], r.sin_v[:, span]
        first, second = u[:half], u[half:]
        r.d_t[base : base + half, span] = (first * c + second * s).astype(low)
        r.d_t[base + half : base + 2 * half, span] = (second * c - first * s).astype(low)

    def beside_attention(j):
        if 1 <= j <= 5:
            sum_out.step(j + 1)
        if j == 6:
            r.out_mine[...] = sum_out.whole().astype(low)
            out_whole.start()
            up_grads.wait()
            up_back.start()

    for j in range(tiles):
        keys = pl.ds(j * TILE, TILE)
        dk, dv = None, None
        for t in range(j, tiles):
            span = pl.ds(t * TILE, TILE)
            s = dot(r.k_nat[keys, :], r.q_t[:, span])
            p = jnp.exp(s - r.lse[:, span])
            if j == t:
                p = jnp.where(causal(p.shape), p, 0.0)
            d_p = dot(r.v_nat[keys, :], r.do_t[:, span])
            d_s = (p * (d_p - r.delta[:, span])).astype(low)
            dv_add = dot(p.astype(low), r.do_nat[span, :])
            dk_add = dot(d_s, r.q_nat[span, :])
            dv = dv_add if dv is None else dv + dv_add
            dk = dk_add if dk is None else dk + dk_add
            r.dq[:, span] += dot(r.k_t[:, keys], d_s)
        turned_back(dk.T, keys, HEAD_DIM)
        r.d_t[2 * HEAD_DIM :, keys] = dv.T.astype(low)
        turned_back(r.dq[:, keys] * HEAD_DIM**-0.5, keys, 0)
        beside_attention(j)

    def part(ahead):
        base = ring.device(ahead, 0)
        span = pl.ds(pl.multiple_of(base * rows, pair), pair)
        d_x = dot(r.d_t[:, span], r.w_t[...], TN).astype(low)
        r.parts[pl.ds(base, 2)] = d_x.reshape(2, rows, width)
        sum_in.across(ahead).start()

    def head_gradient(j):
        x = r.normed_all[:, :, j * 128 : (j + 1) * 128].reshape(length, 128)
        d_w = dot(r.d_t[...], x).T
        for i in range(2):
            for h in range(2):
                base = i * w_rows + h * kept
                block = d_w[base : base + kept]
                v = block[:, 2 * HEAD_DIM :]
                v = jnp.concatenate([v[: kept // 2], v[kept // 2 :]], 1)
                at = h * packed
                r.head_parts[2 * j + i, at : at + kept] = block[:, : 2 * HEAD_DIM].astype(low)
                r.head_parts[2 * j + i, at + kept : at + packed] = v.astype(low)

    part(steps)
    part(steps - 1)
    part(1 - steps)
    for j in range(4):
        sum_in.step(j)
    for k in range(steps - 2, 0, -1):
        part(k)
        part(-k)
    part(0)
    sum_in.step(4)
    sum_in.step(5)
    for j in range(size // 2):
        head_gradient(j)
    head_weights.finish()
    head_half.start()
    for j in range(6, 10):
        sum_in.step(j)
    head_half.wait_recv()
    own_half = r.head_parts[:, pl.ds(dp * packed, packed)].astype(full)
    r.head_send[...] = (own_half + r.head_peer[...].astype(full)).astype(low)
    r.head_all[me, pl.ds(dp * packed, packed)] = r.head_send[me]
    head_grads.start()
    for j in range(10, 12):
        sum_in.step(j)
    down_whole.wait_recv()
    r.grad_down_v[...] = r.down_grad[...].astype(full) + r.down_peer[...].astype(full)
    save("grad_down")
    for j in range(12, 14):
        sum_in.step(j)
    out_whole.wait_recv()
    r.grad_out_v[...] = r.out_mine[...].astype(full) + r.out_peer[...].astype(full)
    save("grad_out")
    up_back.wait_recv()
    for h in range(size):
        r.grad_up_v[:, h * units : (h + 1) * units] = r.up_all[h].astype(full)
    save("grad_up")
    head_grads.wait()
    head_back.start()

    d_normed = sum_in.whole()
    hat0 = r.hat0[...]
    r.norm_grads[0:1, :] = jnp.sum(d_normed * hat0, 0, keepdims=True)
    r.norm_grads[4:5, :] = jnp.sum(d_normed, 0, keepdims=True)

    def norm_copy(i, other):
        to = (me + i) % size
        return pltpu.make_async_remote_copy(
            src_ref=r.norm_grads.at[:, columns(to // 2, 128)],
            dst_ref=r.norm_sums.at[2 * i + other],
            send_sem=r.norm_ssem.at[0],
            recv_sem=r.norm_rsem.at[0],
            device_id={"seq": to, "dp": (dp + other) % 2},
            device_id_type=MESH,
        )

    partners = [(i, other) for i in range(size) for other in range(2) if i or other]
    for i, other in partners:
        norm_copy(i, other).start()
    r.norm_sums[0] = r.norm_grads[:, columns(me // 2, 128)]
    _, scale0 = normalized(r.tokens_v[...].astype(full))
    r.grad_tokens_v[...] = r.d_hidden[...] + norm_back(d_normed, hat0, scale0, gain(0))
    save("grad_tokens")
    head_back.wait_recv()
    for h in range(2):
        for j in range(size // 2):
            blocks = [
                r.head_all[2 * j + i, h * packed : (h + 1) * packed].astype(full) for i in range(2)
            ]
            span = slice(h * kept, (h + 1) * kept)
            for b in range(2):
                place = slice(b * width + j * 128, b * width + (j + 1) * 128)
                r.grad_qkv_v[span, place] = jnp.concatenate(
                    [p[:kept, b * HEAD_DIM : (b + 1) * HEAD_DIM] for p in blocks], 1
                )
            v = [jnp.concatenate([p[kept:, :HEAD_DIM], p[kept:, HEAD_DIM:]], 0) for p in blocks]
            place = slice(2 * width + j * 128, 2 * width + (j + 1) * 128)
            r.grad_qkv_v[span, place] = jnp.concatenate(v, 1)
    save("grad_qkv")
    norm_all = r.norm_sums.at[pl.ds(1, 2 * size - 1)]
    norm_all = swap(norm_all, norm_all, r.norm_ssem.at[0], r.norm_rsem.at[0])
    norm_all.wait_recv()
    sums = jnp.sum(r.norm_sums[...], 0)
    sums = jnp.where(core == 0, sums[:, :w_rows], sums[:, w_rows:])
    r.grad_gains_v[...] = sums[0:4]
    r.grad_biases_v[...] = sums[4:8]
    save("grad_gains")
    save("grad_biases")

    norm_all.wait_send()
    sum_in.finish()
    sum_out.finish()
    for exchange in (norm_rows, up_weights, d_atts, up_grads, head_grads):
        exchange.finish()
    for copy in (
        head_other, up_other, up_half, down_whole, out_whole, up_back, head_half, head_back
    ):
        copy.wait_send()
    out_own().wait_send()
    out_others().wait_send()
    out_swap(w_outs.blocks(chips - 1), 0, 0).wait_send()
    for copy in saves.values():
        copy.wait()


def hand_over_kernel(count, *refs):
    ins, outs, held = (refs[i * count : (i + 1) * count] for i in range(3))
    sems = refs[-1]
    loads = [pltpu.make_async_copy(ins[i], held[i], sems.at[0, i]) for i in range(count)]
    saves = [pltpu.make_async_copy(held[i], outs[i], sems.at[1, i]) for i in range(count)]
    for copy in loads:
        copy.start()
    for load, copy in zip(loads, saves):
        load.wait()
        copy.start()
    for copy in saves:
        copy.wait()


def hand_over(arrays):
    count = len(arrays)
    return pl.pallas_call(
        functools.partial(hand_over_kernel, count),
        out_shape=[jax.ShapeDtypeStruct(a.shape, a.dtype) for a in arrays],
        in_specs=[ANY] * count,
        out_specs=[ANY] * count,
        scratch_shapes=[pltpu.VMEM(a.shape, a.dtype) for a in arrays] + [DMA((2, count))],
    )(*arrays)


def split_heads(
    tokens, w_qkv, w_out, w_up, w_down, norm_gains, norm_biases, corpus_id, corpus_weight, cotangent
):
    size = lax.axis_size("seq")
    chips = size // 2
    _, rows, width = tokens.shape
    w_rows = w_out.shape[0]
    units = w_down.shape[0]
    length = rows * size
    shape = jax.ShapeDtypeStruct
    cos, sin = turn_tables(length)
    inputs = dict(
        tokens=tokens[0],
        w_qkv=w_qkv,
        w_out=w_out,
        w_up=w_up,
        w_down=w_down,
        gains=norm_gains,
        biases=norm_biases,
        corpus=corpus_id,
        cotangent=cotangent[0],
        cos=cos,
        sin=sin,
    )
    outputs = dict(
        output=shape((rows, width), low),
        grad_tokens=shape((rows, width), full),
        grad_qkv=shape((w_rows, 3 * width), full),
        grad_out=shape((w_rows, width), full),
        grad_up=shape((w_rows, size * units), full),
        grad_down=shape((units, width), full),
        grad_gains=shape((4, w_rows), full),
        grad_biases=shape((4, w_rows), full),
    )

    def vmem(*dims, kind=low):
        return pltpu.VMEM(dims, kind)

    head_rows = 3 * w_rows // 2
    blocks = vmem(size, rows, width)
    nat, turned = vmem(length, HEAD_DIM), vmem(HEAD_DIM, length)
    side, inbox, outbox = Scatter.buffers(chips, rows, width, 4)
    out_side, out_inbox, out_outbox = Scatter.buffers(chips, w_rows, width, 2)
    scratch = {name + "_v": vmem(*a.shape, kind=a.dtype) for name, a in inputs.items()}
    scratch |= {name + "_v": vmem(*a.shape, kind=a.dtype) for name, a in outputs.items()}
    scratch |= dict(
        big=blocks,
        normed_all=blocks,
        mid_all=blocks,
        parts=blocks,
        side=side,
        inbox=inbox,
        outbox=outbox,
        out_parts=vmem(size, w_rows, width),
        out_side=out_side,
        out_inbox=out_inbox,
        out_outbox=out_outbox,
        out_mine=vmem(w_rows, width),
        out_peer=vmem(w_rows, width),
        w_out_all=vmem(size, w_rows, width),
        w_up_all=vmem(size, w_rows, units),
        w_t=vmem(3 * HEAD_DIM, width),
        head_send=vmem(size, head_rows // 2, 128),
        head_recv=vmem(size, head_rows, 128),
        head_parts=vmem(size, head_rows, 128),
        head_peer=vmem(size, head_rows // 2, 128),
        head_all=vmem(size, head_rows, 128),
        norm_send=vmem(8, 128, kind=full),
        norm_recv=vmem(size, 8, 128, kind=full),
        norms=vmem(8, width, kind=full),
        norm_grads=vmem(8, width, kind=full),
        norm_sums=vmem(2 * size, 8, 128, kind=full),
        q_t=turned,
        k_t=turned,
        v_t=turned,
        do_t=turned,
        q_nat=nat,
        k_nat=nat,
        v_nat=nat,
        do_nat=nat,
        total=vmem(HEAD_DIM, length, kind=full),
        dq=vmem(HEAD_DIM, length, kind=full),
        d_t=vmem(3 * HEAD_DIM, length),
        lse=vmem(1, length, kind=full),
        delta=vmem(1, length, kind=full),
        scores=vmem(length, TILE, kind=full),
        att_send=vmem(size, HEAD_DIM, rows),
        att_t=vmem(size, HEAD_DIM, rows),
        d_att=vmem(size, HEAD_DIM, rows),
        att_recv=vmem(size, HEAD_DIM, rows),
        proj=vmem(rows, width, kind=full),
        hidden=vmem(rows, width, kind=full),
        d_hidden=vmem(rows, width, kind=full),
        hat0=vmem(rows, width, kind=full),
        act_all=vmem(size, rows, units),
        slope_all=vmem(size, rows, units, kind=full),
        d_up_all=vmem(size, rows, units),
        up_grad=vmem(size, w_rows, units),
        up_peer=vmem(size, w_rows // 2, units),
        up_send=vmem(size, w_rows // 2, units),
        up_all=vmem(size, w_rows, units),
        down_grad=vmem(units, width),
        down_peer=vmem(units, width),
        load_sem=DMA((len(inputs),)),
        save_sem=DMA((len(outputs),)),
        swap_send=DMA((8,)),
        swap_recv=DMA((8,)),
        out_side_send=DMA((2,)),
        out_side_recv=DMA((2,)),
        out_swap_send=DMA((1,)),
        out_swap_recv=DMA((2, Gather.count(chips, 2))),
        att_ssem=DMA((1,)),
        att_rsem=DMA((1,)),
        norm_ssem=DMA((1,)),
        norm_rsem=DMA((1,)),
    )
    for i, pieces in enumerate((4, 2)):
        scratch[f"gather{i}"] = Gather.sems(chips, pieces)
        scratch[f"scatter{i}"] = Scatter.sems(chips, pieces)
    for i in range(6):
        scratch[f"exchange{i}"] = [DMA((1,)), DMA((1,))]
    flat, groups = [], []
    for name, entry in scratch.items():
        entries = entry if isinstance(entry, list) else [entry]
        groups.append((name, len(entries) if isinstance(entry, list) else 0))
        flat += entries

    def kernel(*refs):
        count = len(inputs) + 1 + len(outputs)
        names = [*inputs, "weight", *outputs]
        values = list(refs[:count])
        rest = list(refs[count:])
        for name, many in groups:
            names.append(name)
            if many:
                values.append(tuple(rest[:many]))
                rest = rest[many:]
            else:
                values.append(rest.pop(0))
        layer_kernel(names, *values)

    results = pl.pallas_call(
        kernel,
        out_shape=list(outputs.values()),
        in_specs=[ANY] * len(inputs) + [pl.BlockSpec(memory_space=pltpu.SMEM)],
        out_specs=[ANY] * len(outputs),
        scratch_shapes=flat,
        compiler_params=pltpu.CompilerParams(
            collective_id=1, has_side_effects=True, vmem_limit_bytes=61 * 2**20
        ),
    )(*inputs.values(), corpus_weight)
    results = hand_over(results)
    return (results[0][None], results[1][None], *results[2:])


def shifted(x, axis, by):
    size = lax.axis_size(axis)
    return lax.ppermute(x, axis, [(i, (i + by) % size) for i in range(size)])


def passed_along(value, axis, steps):
    count = lax.axis_size(axis)
    first, last = (max(0, -steps), min(count, count - steps))
    return lax.ppermute(value, axis, [(source, source + steps) for source in range(first, last)])


def layer_norm(values, gain, bias):
    center = values - jnp.mean(values, -1, keepdims=True)
    variance = jnp.mean(center * center, -1, keepdims=True)
    return center * lax.rsqrt(variance + 1e-05) * gain + bias


def rotate(values, position, direction):
    half_size = values.shape[-1] // 2
    freq = jnp.exp(
        jnp.arange(half_size).astype(jnp.float32) * (-2.0 * math.log(10000.0) / values.shape[-1])
    )
    angle = position[:, None] * freq[None, :]
    cosine = jnp.cos(angle)[:, None, :]
    sine = direction * jnp.sin(angle)[:, None, :]
    first = values[..., :half_size]
    second = values[..., half_size:]
    return jnp.concatenate([first * cosine - second * sine, first * sine + second * cosine], -1)


def gelu_tanh(values):
    return jax.nn.gelu(values, approximate=True)


def per_device(
    tokens, w_qkv, w_out, w_up, w_down, norm_gains, norm_biases, corpus_id, corpus_weight, cotangent
):
    full_qkv, full_out, full_up, full_down, gains_low, biases_low = (
        lax.all_gather(w_qkv, "seq", axis=0, tiled=True),
        lax.all_gather(w_out, "seq", axis=0, tiled=True),
        lax.all_gather(w_up, "seq", axis=0, tiled=True),
        lax.all_gather(w_down, "seq", axis=0, tiled=True),
        lax.all_gather(norm_gains, "seq", axis=1, tiled=True),
        lax.all_gather(norm_biases, "seq", axis=1, tiled=True),
    )
    gains = gains_low.astype(jnp.float32)
    biases = biases_low.astype(jnp.float32)
    seq_count, row_count, model_width = tokens.shape
    shape_heads = (seq_count, row_count, HEADS, HEAD_DIM)
    scale = HEAD_DIM ** (-0.5)
    cycle_size = lax.axis_size("seq")
    cycle_index = lax.axis_index("seq")
    query_pos = cycle_index * row_count + jnp.arange(row_count)
    position = query_pos.astype(jnp.float32)
    x_float = tokens.astype(jnp.float32)
    normed_low = layer_norm(x_float, gains[0], biases[0]).astype(jnp.bfloat16)
    qkv = jnp.einsum("std,de->ste", normed_low, full_qkv, preferred_element_type=jnp.float32)
    query_low = rotate(qkv[..., :model_width].reshape(shape_heads), position, 1.0).astype(
        jnp.bfloat16
    )
    key_low = rotate(
        qkv[..., model_width : 2 * model_width].reshape(shape_heads), position, 1.0
    ).astype(jnp.bfloat16)
    value_low = qkv[..., 2 * model_width :].reshape(shape_heads).astype(jnp.bfloat16)

    def block_scores(key_piece, key_pos):
        scores = (
            jnp.einsum("sqhd,skhd->shqk", query_low, key_piece, preferred_element_type=jnp.float32)
            * scale
        )
        allowed = query_pos[:, None] >= key_pos[None, :]
        return (scores, allowed)

    stat_shape = (seq_count, HEADS, row_count)
    key_piece = lax.all_gather(key_low, "seq", axis=1, tiled=True)
    value_piece = lax.all_gather(value_low, "seq", axis=1, tiled=True)
    key_pos = jnp.arange(key_piece.shape[1])
    run_max = jnp.full(stat_shape, -1e30, jnp.float32)
    scores, allowed = block_scores(key_piece, key_pos)
    new_max = jnp.maximum(run_max, jnp.max(jnp.where(allowed, scores, -1e30), -1))
    weights = jnp.where(allowed, jnp.exp(scores - new_max[..., None]), 0.0)
    run_sum = jnp.sum(weights, -1)
    total = jnp.einsum(
        "shqk,skhd->sqhd",
        weights.astype(jnp.bfloat16),
        value_piece,
        preferred_element_type=jnp.float32,
    )
    run_max, run_sum, total = (new_max, run_sum, total)
    log_sum = run_max + jnp.log(run_sum)
    attended = total / jnp.transpose(run_sum, (0, 2, 1))[..., None]
    attended_low = attended.reshape(seq_count, row_count, model_width).astype(jnp.bfloat16)
    proj = jnp.einsum("std,de->ste", attended_low, full_out, preferred_element_type=jnp.float32)
    hidden = x_float + layer_norm(proj, gains[1], biases[1])
    mid_low = layer_norm(hidden, gains[2], biases[2]).astype(jnp.bfloat16)
    up_proj = jnp.einsum("std,df->stf", mid_low, full_up, preferred_element_type=jnp.float32)
    act_low = gelu_tanh(up_proj).astype(jnp.bfloat16)
    down = jnp.einsum("stf,fd->std", act_low, full_down, preferred_element_type=jnp.float32)
    output = (hidden + layer_norm(down, gains[3], biases[3])).astype(jnp.bfloat16)
    matches = (corpus_id[..., None] == jnp.arange(corpus_weight.shape[0])).astype(jnp.float32)
    row_weight = jnp.sum(matches * corpus_weight, -1)
    grad_y = cotangent.astype(jnp.float32) * row_weight[..., None]
    _, down_back = jax.vjp(layer_norm, down, gains[3], biases[3])
    d_down, gain_three, bias_three = down_back(grad_y)
    d_down_low = d_down.astype(jnp.bfloat16)
    grad_down = jnp.einsum("stf,std->fd", act_low, d_down_low, preferred_element_type=jnp.float32)
    d_act = jnp.einsum("std,fd->stf", d_down_low, full_down, preferred_element_type=jnp.float32)
    _, gelu_back = jax.vjp(gelu_tanh, up_proj)
    d_up_low = gelu_back(d_act)[0].astype(jnp.bfloat16)
    grad_up = jnp.einsum("std,stf->df", mid_low, d_up_low, preferred_element_type=jnp.float32)
    d_mid = jnp.einsum("stf,df->std", d_up_low, full_up, preferred_element_type=jnp.float32)
    _, mid_back = jax.vjp(layer_norm, hidden, gains[2], biases[2])
    d_hidden_mid, gain_two, bias_two = mid_back(d_mid)
    d_hidden = grad_y + d_hidden_mid
    _, proj_back = jax.vjp(layer_norm, proj, gains[1], biases[1])
    d_proj, gain_one, bias_one = proj_back(d_hidden)
    d_proj_low = d_proj.astype(jnp.bfloat16)
    grad_out = jnp.einsum(
        "std,ste->de", attended_low, d_proj_low, preferred_element_type=jnp.float32
    )
    d_att_low = (
        jnp.einsum("ste,de->std", d_proj_low, full_out, preferred_element_type=jnp.float32)
        .astype(jnp.bfloat16)
        .reshape(shape_heads)
    )
    delta = jnp.transpose(jnp.sum(d_att_low.astype(jnp.float32) * attended, -1), (0, 2, 1))

    def contribute(d_query, key_piece, value_piece, d_key, d_value, owner):
        key_pos = owner * row_count + jnp.arange(row_count)
        query_sum = d_query
        key_sum = d_key
        value_sum = d_value
        scores, allowed = block_scores(key_piece, key_pos)
        probs = jnp.where(allowed, jnp.exp(scores - log_sum[..., None]), 0.0)
        value_sum = value_sum + jnp.einsum(
            "shqk,sqhd->skhd",
            probs.astype(jnp.bfloat16),
            d_att_low,
            preferred_element_type=jnp.float32,
        )
        d_probs = jnp.einsum(
            "sqhd,skhd->shqk", d_att_low, value_piece, preferred_element_type=jnp.float32
        )
        d_scores = (probs * (d_probs - delta[..., None]) * scale).astype(jnp.bfloat16)
        query_sum = query_sum + jnp.einsum(
            "shqk,skhd->sqhd", d_scores, key_piece, preferred_element_type=jnp.float32
        )
        key_sum = key_sum + jnp.einsum(
            "shqk,sqhd->skhd", d_scores, query_low, preferred_element_type=jnp.float32
        )
        return (query_sum, key_sum, value_sum)

    zeros_heads = jnp.zeros(shape_heads, jnp.float32)

    def pass_grads(d_key, d_value):
        return (
            shifted(d_key.astype(jnp.bfloat16), "seq", 1).astype(d_key.dtype),
            shifted(d_value.astype(jnp.bfloat16), "seq", 1).astype(d_value.dtype),
        )

    def cycle_turn(turn_index, state):
        d_query, key_piece, value_piece, d_key, d_value = state
        owner = (cycle_index - turn_index) % cycle_size
        d_query, d_key, d_value = contribute(d_query, key_piece, value_piece, d_key, d_value, owner)
        d_key, d_value = pass_grads(d_key, d_value)
        key_piece, value_piece = passed_along((key_piece, value_piece), "seq", 1)
        return (d_query, key_piece, value_piece, d_key, d_value)

    d_query, key_piece, value_piece, d_key, d_value = lax.fori_loop(
        0, cycle_size - 1, cycle_turn, (zeros_heads, key_low, value_low, zeros_heads, zeros_heads)
    )
    last_owner = (cycle_index + 1) % cycle_size
    d_query, d_key, d_value = contribute(
        d_query, key_piece, value_piece, d_key, d_value, last_owner
    )
    d_key, d_value = pass_grads(d_key, d_value)
    flat_shape = (seq_count, row_count, model_width)
    d_qkv_low = jnp.concatenate(
        [
            rotate(d_query, position, -1.0).reshape(flat_shape),
            rotate(d_key, position, -1.0).reshape(flat_shape),
            d_value.reshape(flat_shape),
        ],
        -1,
    ).astype(jnp.bfloat16)
    grad_qkv = jnp.einsum("std,ste->de", normed_low, d_qkv_low, preferred_element_type=jnp.float32)
    d_normed = jnp.einsum("ste,de->std", d_qkv_low, full_qkv, preferred_element_type=jnp.float32)
    _, input_back = jax.vjp(layer_norm, x_float, gains[0], biases[0])
    d_input, gain_zero, bias_zero = input_back(d_normed)
    grad_tokens = d_hidden + d_input
    grad_gains = jnp.stack([gain_zero, gain_one, gain_two, gain_three])
    grad_biases = jnp.stack([bias_zero, bias_one, bias_two, bias_three])
    all_grads = (grad_qkv, grad_out, grad_up, grad_down, grad_gains, grad_biases)
    pieces = (
        lax.psum_scatter(
            all_grads[0].astype(jnp.bfloat16), "seq", scatter_dimension=0, tiled=True
        ).astype(jnp.float32),
        lax.psum_scatter(
            all_grads[1].astype(jnp.bfloat16), "seq", scatter_dimension=0, tiled=True
        ).astype(jnp.float32),
        lax.psum_scatter(
            all_grads[2].astype(jnp.bfloat16), "seq", scatter_dimension=0, tiled=True
        ).astype(jnp.float32),
        lax.psum_scatter(
            all_grads[3].astype(jnp.bfloat16), "seq", scatter_dimension=0, tiled=True
        ).astype(jnp.float32),
        lax.psum_scatter(
            all_grads[4].astype(jnp.bfloat16), "seq", scatter_dimension=1, tiled=True
        ).astype(jnp.float32),
        lax.psum_scatter(
            all_grads[5].astype(jnp.bfloat16), "seq", scatter_dimension=1, tiled=True
        ).astype(jnp.float32),
    )
    shards = (
        lax.psum(pieces[0].astype(jnp.bfloat16), "dp").astype(jnp.float32),
        lax.psum(pieces[1].astype(jnp.bfloat16), "dp").astype(jnp.float32),
        lax.psum(pieces[2].astype(jnp.bfloat16), "dp").astype(jnp.float32),
        lax.psum(pieces[3].astype(jnp.bfloat16), "dp").astype(jnp.float32),
        lax.psum(pieces[4].astype(jnp.bfloat16), "dp").astype(jnp.float32),
        lax.psum(pieces[5].astype(jnp.bfloat16), "dp").astype(jnp.float32),
    )
    return (output, grad_tokens, shards[0], shards[1], shards[2], shards[3], shards[4], shards[5])


def solution(mesh):
    placed = (
        P("dp", "seq", None),
        P("seq", None),
        P("seq", None),
        P("seq", None),
        P("seq", None),
        P(None, "seq"),
        P(None, "seq"),
        P("dp", "seq"),
        P(),
        P("dp", "seq", None),
    )
    fits = mesh.shape["seq"] == HEADS and mesh.shape["dp"] == 2
    return jax.shard_map(
        split_heads if fits else per_device,
        mesh=mesh,
        in_specs=placed,
        out_specs=(
            P("dp", "seq", None),
            P("dp", "seq", None),
            P("seq", None),
            P("seq", None),
            P("seq", None),
            P("seq", None),
            P(None, "seq"),
            P(None, "seq"),
        ),
        check_vma=False,
    )
```

```python
import functools
import math
import types

import jax
import jax.numpy as jnp
import numpy as np
from jax import lax
from jax.experimental import pallas as pl
from jax.experimental.pallas import tpu as pltpu
from jax.sharding import PartitionSpec as P

HEADS = 16
HEAD_DIM = 64
TILE = 256
MESH = pl.DeviceIdType.MESH
ANY = pl.BlockSpec(memory_space=pl.ANY)
DMA = pltpu.SemaphoreType.DMA
NT = ((1,), (1,))
TN = ((0,), (0,))
low, full = jnp.bfloat16, jnp.float32


def dot(left, right, contract=((1,), (0,))):
    return lax.dot_general(left, right, (contract, ((), ())), preferred_element_type=full)


def remote(source, target, send, recv, device):
    return pltpu.make_async_remote_copy(
        src_ref=source,
        dst_ref=target,
        send_sem=send,
        recv_sem=recv,
        device_id={"seq": device},
        device_id_type=MESH,
    )


def swap(source, target, send, recv):
    return pltpu.make_async_remote_copy(
        src_ref=source,
        dst_ref=target,
        send_sem=send,
        recv_sem=recv,
        device_id={"dp": 1 - lax.axis_index("dp")},
        device_id_type=MESH,
    )


class Ring:
    def __init__(self, length):
        self.me = lax.axis_index("seq")
        self.length = length
        self.chips = 2 * length
        self.steps = length
        self.core = self.me % 2
        column, row = (self.me // 2) % 2, self.me // 4
        self.first = (row // length) * length
        row = row - self.first
        self.base = self.first * 4
        self.place = row + column * (self.chips - 1 - 2 * row)
        self.right = self.device(1, self.core)
        self.left = self.device(-1, self.core)
        self.sibling = self.device(0, 1 - self.core)

    def device(self, ahead, core):
        place = (self.place + ahead + self.chips) % self.chips
        column = place // self.length
        row = place + column * (self.chips - 1 - 2 * place)
        return (self.first + row) * 4 + column * 2 + core


class Gather:
    def __init__(self, ring, piece, block, blocks, pieces, sems):
        self.ring, self.piece, self.block, self.blocks = ring, piece, block, blocks
        self.pieces = pieces
        self.send, self.recv, self.side_send, self.side_recv = sems
        self.messages = self.count(ring.chips, pieces)

    @staticmethod
    def count(chips, pieces):
        return pieces * (chips // 2) - pieces // 2

    def ref(self, way, j, ahead):
        k, q = j // self.pieces + ahead, j % self.pieces
        q = q if way == 0 else self.pieces - 1 - q
        return self.piece(self.ring.device(-k if way == 0 else k, self.ring.core), q)

    def hop(self, way, j):
        ref = self.ref(way, j, 0)
        target = self.ring.right if way == 0 else self.ring.left
        return remote(ref, ref, self.send.at[0], self.recv.at[way, j], target)

    def landed(self, way, j):
        return self.ref(way, j, 1)

    def side(self, ref, slot):
        return remote(ref, ref, self.side_send.at[0], self.side_recv.at[slot], self.ring.sibling)

    def start(self):
        for j in range(self.pieces):
            for way in range(2):
                self.hop(way, j).start()
        self.side(self.block(self.ring.me), 0).start()

    def pass_on(self, j):
        k = j // self.pieces + 1
        for way in range(2):
            self.hop(way, j).wait_recv()
            if j + self.pieces < self.messages:
                self.hop(way, j + self.pieces).start()
            slot = (-k if way == 0 else k) % self.ring.chips
            self.side(self.landed(way, j), slot).start()

    def wait_chip(self, ahead):
        block = self.block(self.ring.device(ahead, 1 - self.ring.core))
        self.side(block, ahead % self.ring.chips).wait_recv()

    def finish(self):
        count = self.ring.chips - 1
        everything = self.blocks(count)
        remote(everything, everything, self.send.at[0], self.recv.at[0, 0], self.ring.right).wait_send()
        self.side(self.blocks(count + 1), 0).wait_send()

    @staticmethod
    def sems(chips, pieces):
        return [DMA((1,)), DMA((2, Gather.count(chips, pieces))), DMA((1,)), DMA((chips,))]


class Scatter:
    def __init__(self, ring, parts, pieces, side, inbox, outbox, sems, shift=0):
        self.ring, self.parts, self.pieces = ring, parts, pieces
        self.base = ring.base - shift
        self.side, self.inbox, self.outbox = side, inbox, outbox
        self.send, self.recv, self.side_send, self.side_recv = sems
        self.messages = Gather.count(ring.chips, pieces)
        self.rows = parts.shape[1] // pieces
        self.waited = set()

    def across(self, ahead):
        slot = ahead % self.ring.chips
        return remote(
            self.parts.at[self.ring.device(ahead, 1 - self.ring.core) - self.base],
            self.side.at[slot],
            self.side_send.at[0],
            self.side_recv.at[slot],
            self.ring.sibling,
        )

    def hop(self, way, j):
        target = self.ring.right if way == 0 else self.ring.left
        return remote(
            self.outbox.at[way, j],
            self.inbox.at[way, j],
            self.send.at[0],
            self.recv.at[way, j],
            target,
        )

    def own(self, ahead, q):
        slot = ahead % self.ring.chips
        if slot not in self.waited:
            self.waited.add(slot)
            self.across(ahead).wait_recv()
        span = pl.ds(q * self.rows, self.rows)
        mine = self.parts[self.ring.device(ahead, self.ring.core) - self.base, span].astype(full)
        return mine + self.side[slot, span].astype(full)

    def ahead(self, j):
        return self.ring.steps - (j + self.pieces // 2) // self.pieces

    def step(self, j):
        for way in range(2):
            q = j % self.pieces if way == 0 else self.pieces - 1 - j % self.pieces
            total = self.own(self.ahead(j) if way == 0 else -self.ahead(j), q)
            if j >= self.pieces:
                self.hop(way, j - self.pieces).wait_recv()
                total += self.inbox[way, j - self.pieces].astype(full)
            self.outbox[way, j] = total.astype(self.outbox.dtype)
            self.hop(way, j).start()

    def result(self, q):
        total = self.own(0, q)
        for way in range(2):
            k = q if way == 0 else self.pieces - 1 - q
            last = max(j for j in range(self.messages) if j % self.pieces == k)
            self.hop(way, last).wait_recv()
            total += self.inbox[way, last].astype(full)
        return total

    def whole(self):
        return jnp.concatenate([self.result(q) for q in range(self.pieces)], 0)

    def finish(self):
        everything = self.parts.at[pl.ds(0, self.ring.chips)]
        side = self.side_send.at[0], self.side_recv.at[0]
        remote(everything, self.side, *side, self.ring.sibling).wait_send()
        hops = self.send.at[0], self.recv.at[0, 0]
        remote(self.outbox, self.inbox, *hops, self.ring.right).wait_send()

    @staticmethod
    def buffers(chips, rows, columns, pieces):
        box = pltpu.VMEM((2, Gather.count(chips, pieces), rows // pieces, columns), low)
        return [pltpu.VMEM((chips, rows, columns), low), box, box]

    @staticmethod
    def sems(chips, pieces):
        return [DMA((1,)), DMA((2, Gather.count(chips, pieces))), DMA((1,)), DMA((chips,))]


class Exchange:
    def __init__(self, source, target, blocks, sems):
        self.source, self.target, self.blocks = source, target, blocks
        self.send, self.recv = sems
        self.me, self.size = lax.axis_index("seq"), lax.axis_size("seq")

    def start(self):
        for i in range(1, self.size):
            to = (self.me + i) % self.size
            remote(
                self.source(to), self.target(self.me), self.send.at[0], self.recv.at[0], to
            ).start()

    def all(self):
        ref = self.blocks(self.size - 1)
        to = (self.me + 1) % self.size
        return remote(ref, ref, self.send.at[0], self.recv.at[0], to)

    def wait(self):
        self.all().wait_recv()

    def finish(self):
        self.all().wait_send()


def normalized(values):
    center = values - jnp.mean(values, -1, keepdims=True)
    scale = lax.rsqrt(jnp.mean(center * center, -1, keepdims=True) + 1e-05)
    return center * scale, scale


def norm_back(grad, hat, scale, gain):
    d_hat = grad * gain
    mean = jnp.mean(d_hat, -1, keepdims=True)
    along = jnp.mean(d_hat * hat, -1, keepdims=True)
    return scale * (d_hat - mean - hat * along)


def gelu_and_slope(u):
    c = math.sqrt(2.0 / math.pi)
    square = u * u
    t = jnp.tanh(c * u * (1.0 + 0.044715 * square))
    act = 0.5 * u * (1.0 + t)
    slope = 0.5 * (1.0 + t) + 0.5 * u * (1.0 - t * t) * (c * (1.0 + 3 * 0.044715 * square))
    return act, slope


def causal(shape):
    key_pos = lax.broadcasted_iota(jnp.int32, shape, 0)
    query_pos = lax.broadcasted_iota(jnp.int32, shape, 1)
    return key_pos <= query_pos


def turn_tables(length):
    half = HEAD_DIM // 2
    freq = np.exp(
        np.arange(half, dtype=np.float32) * np.float32(-2.0 * math.log(10000.0) / HEAD_DIM)
    )
    angle = freq[:, None] * np.arange(length, dtype=np.float32)[None, :]
    return jnp.asarray(np.cos(angle)), jnp.asarray(np.sin(angle))


INPUTS = (
    "tokens",
    "w_qkv",
    "gains",
    "biases",
    "w_out",
    "w_up",
    "cos",
    "sin",
    "w_down",
    "cotangent",
    "corpus",
)
OUTPUTS = (
    "output",
    "grad_tokens",
    "grad_qkv",
    "grad_out",
    "grad_up",
    "grad_down",
    "grad_gains",
    "grad_biases",
)


def layer_kernel(names, *refs):
    r = types.SimpleNamespace(**dict(zip(names, refs, strict=True)))
    size = lax.axis_size("seq")
    ring, near = Ring(size // 4), Ring(size // 8)
    me, core, chips, steps = ring.me, ring.core, ring.chips, ring.steps
    far = (me + size // 2) % size
    close = size // 2
    dp = lax.axis_index("dp")
    rows, width = r.tokens.shape
    w_rows = r.w_out.shape[0]
    units = r.w_down.shape[0]
    length = rows * size
    near_length = rows * close
    tiles = length // TILE
    half = HEAD_DIM // 2
    kept = w_rows // 2
    packed = 3 * kept // 2
    pair = 2 * rows

    def mine(ref):
        return ref.at[:, pl.ds(dp * (ref.shape[1] // 2), ref.shape[1] // 2)]

    def theirs(ref):
        return ref.at[:, pl.ds((1 - dp) * (ref.shape[1] // 2), ref.shape[1] // 2)]

    def columns(device, count):
        return pl.ds(pl.multiple_of(device * count, count), count)

    loads = {
        name: pltpu.make_async_copy(getattr(r, name), getattr(r, name + "_v"), r.load_sem.at[i])
        for i, name in enumerate(INPUTS)
    }
    for name in INPUTS:
        loads[name].start()
    barrier = pltpu.get_barrier_semaphore()
    for i in range(1, size):
        pl.semaphore_signal(barrier, inc=1, device_id={"seq": (me + i) % size}, device_id_type=MESH)
    pl.semaphore_signal(barrier, inc=1, device_id={"dp": 1 - dp}, device_id_type=MESH)

    quarter = rows // 4

    def gather(ring, ref, count, sems, first=0, shift=0):
        pieces = 4 if ref.shape[1] == rows else 2
        shift = shift - ring.base
        return Gather(
            ring,
            lambda d, q: ref.at[d + shift, pl.ds(first + q * (count // pieces), count // pieces)],
            lambda d: ref.at[d + shift, pl.ds(first, count)],
            lambda n: ref.at[pl.ds(0, n), pl.ds(0, count)],
            pieces,
            sems,
        )

    mid_place, dd_place = me - near.base, me - near.base + close
    other = close - near.base
    tokens_in = gather(near, r.big, rows, r.gather2, shift=near.base)
    tokens_far = gather(near, r.big, rows, r.gather0, shift=other)

    def over(q):
        ref = r.big.at[me, pl.ds(q * (rows // 4), rows // 4)]
        return remote(ref, ref, r.over_send.at[q], r.over_recv.at[q], far)

    def over_again(q):
        over(q).wait_recv()
        tokens_far.hop(0, q).start()
        tokens_far.hop(1, 3 - q).start()

    mids = gather(near, r.big, rows, r.gather2)
    d_downs = gather(near, r.big, rows, r.gather2, shift=close)
    w_outs = gather(ring, r.w_out_all, kept, r.gather1, dp * kept)
    boxes = [(r.side[i], r.inbox[i], r.outbox[i], (r.scatter0, r.scatter1)[i]) for i in range(2)]
    sum_down = Scatter(near, r.parts, 4, *boxes[0])
    sum_mid = Scatter(near, r.parts, 4, *boxes[0])
    sum_out = Scatter(near, r.out_parts, 4, *boxes[1])
    sum_in = Scatter(ring, r.parts, 4, r.in_side, r.in_inbox, r.in_outbox, r.scatter2)
    out_over = remote(r.out_send, r.out_recv, r.far_sems.at[8], r.far_sems.at[9], far)

    def exchange(source, ref, sems, count):
        return Exchange(
            source,
            lambda d: ref.at[d, pl.ds(dp * count if count < ref.shape[1] else 0, count)],
            lambda n: ref.at[pl.ds(0, n), pl.ds(0, count)],
            sems,
        )

    head_weights = exchange(lambda d: r.head_send.at[d], r.head_recv, r.exchange0, packed)
    norm_rows = exchange(lambda d: r.norm_send, r.norm_recv, r.exchange1, 8)

    def up_exchange(ref, sems, shift):
        return exchange(
            lambda d: r.w_up_v.at[pl.ds(dp * kept, kept), columns((d + shift) % size, units)],
            ref,
            sems,
            kept,
        )

    up_weights = up_exchange(r.w_up_all, r.exchange2, 0)
    up_weights_far = up_exchange(r.w_up_far, r.exchange6, size // 2)
    d_atts = exchange(lambda d: r.d_att.at[d], r.att_recv, r.exchange3, HEAD_DIM)
    up_grads = exchange(lambda d: r.up_send[0].at[d], r.up_recv[0], r.exchange4, kept)
    up_grads_far = exchange(lambda d: r.up_send[1].at[d], r.up_recv[1], r.exchange7, kept)
    head_grads = exchange(lambda d: r.head_send.at[d], r.head_all, r.exchange5, packed)

    def swapped(source, target, slot):
        return swap(source, target, r.swap_send.at[slot], r.swap_recv.at[slot])

    head_other = swapped(mine(r.head_recv), mine(r.head_recv), 0)
    up_other = swapped(mine(r.w_up_all), mine(r.w_up_all), 1)
    up_other_far = swapped(mine(r.w_up_far), mine(r.w_up_far), 8)
    units_mine = pl.ds(dp * (units // 2), units // 2)
    units_theirs = pl.ds((1 - dp) * (units // 2), units // 2)
    down_far = remote(
        r.w_down_v.at[units_mine],
        r.w_down_far.at[units_mine],
        r.far_sems.at[0],
        r.far_sems.at[1],
        far,
    )
    down_other_far = swapped(r.w_down_far.at[units_mine], r.w_down_far.at[units_mine], 9)
    up_half = [swapped(theirs(r.up_grad[b]), r.up_peer[b], 2 + 8 * b) for b in range(2)]
    down_half = [
        swapped(r.down_grad[b].at[units_theirs], r.down_peer[b], 3 + 8 * b) for b in range(2)
    ]
    down_back_far = remote(r.down_send, r.down_recv, r.far_sems.at[2], r.far_sems.at[3], far)
    down_back = swapped(r.down_sum.at[units_mine], r.down_sum.at[units_mine], 12)
    out_whole = swapped(r.out_mine, r.out_peer, 4)
    up_back = swapped(mine(r.up_all), mine(r.up_all), 5)
    head_half = swapped(theirs(r.head_parts), r.head_peer, 6)
    head_back = swapped(mine(r.head_all), mine(r.head_all), 7)

    loads["w_qkv"].wait()
    rows_mine = pl.ds(dp * kept, kept)
    for h in range(HEADS):
        q, k, v = (
            r.w_qkv_v[rows_mine, i * width + h * HEAD_DIM : i * width + (h + 1) * HEAD_DIM]
            for i in range(3)
        )
        r.head_send[h, 0:kept] = jnp.concatenate([q, k], 1)
        r.head_send[h, kept:packed] = jnp.concatenate([v[: kept // 2], v[kept // 2 :]], 1)
    r.head_recv[me, pl.ds(dp * packed, packed)] = r.head_send[me]
    loads["gains"].wait()
    loads["biases"].wait()
    r.norm_send[...] = jnp.zeros_like(r.norm_send)
    r.norm_send[0:4, 0:w_rows] = r.gains_v[...].astype(full)
    r.norm_send[4:8, 0:w_rows] = r.biases_v[...].astype(full)
    r.norm_recv[me] = r.norm_send[...]
    loads["tokens"].wait()
    r.big[me] = r.tokens_v[...]
    pl.semaphore_wait(barrier, size)
    tokens_in.start()
    for q in (0, 3, 1, 2):
        over(q).start()
    norm_rows.start()
    head_weights.start()

    def gain(i):
        return r.norms[i : i + 1, :]

    def bias(i):
        return r.norms[4 + i : 5 + i, :]

    loads["w_out"].wait()
    r.w_out_all[me] = r.w_out_v[...]
    loads["w_up"].wait()
    r.w_up_all[me, rows_mine] = r.w_up_v[rows_mine, columns(me, units)]
    r.w_up_far[me, rows_mine] = r.w_up_v[rows_mine, columns(far, units)]
    loads["cos"].wait()
    loads["sin"].wait()
    for name in ("w_down", "cotangent", "corpus"):
        loads[name].wait()

    def unpack_heads():
        head_other.wait_recv()
        for j in range(size // 2):
            span = pl.ds(j * 2 * w_rows, 2 * w_rows)
            qk, v = [], []
            for d in (2 * j, 2 * j + 1):
                for h in range(2):
                    p = r.head_recv[d, h * packed : (h + 1) * packed]
                    qk.append(p[:kept])
                    v += [p[kept:, :HEAD_DIM], p[kept:, HEAD_DIM:]]
            r.w_t[0 : 2 * HEAD_DIM, span] = jnp.concatenate(qk, 0).astype(full).T.astype(low)
            r.w_t[2 * HEAD_DIM :, span] = jnp.concatenate(v, 0).astype(full).T.astype(low)

    def project(ahead, shift=0):
        base = near.device(ahead, 0) + shift
        x = r.big[pl.ds(base, 2)].reshape(pair, width).astype(full)
        hat, _ = normalized(x)
        normed = (hat * gain(0) + bias(0)).astype(low)
        r.normed_all[pl.ds(base, 2)] = normed.reshape(2, rows, width)
        qkv = dot(r.w_t[...], normed, NT)
        span = pl.ds(pl.multiple_of(base * rows, pair), pair)
        c, s = r.cos_v[:, span], r.sin_v[:, span]
        for i, (ref, nat, scale) in enumerate(
            ((r.q_t, r.q_nat, HEAD_DIM**-0.5), (r.k_t, r.k_nat, 1.0))
        ):
            first = qkv[i * HEAD_DIM : i * HEAD_DIM + half]
            second = qkv[i * HEAD_DIM + half : (i + 1) * HEAD_DIM]
            turned = jnp.concatenate([first * c - second * s, first * s + second * c], 0) * scale
            ref[:, span] = turned.astype(low)
            nat[span, :] = turned.T.astype(low)
        v = qkv[2 * HEAD_DIM :]
        r.v_t[:, span] = v.astype(low)
        r.v_nat[span, :] = v.T.astype(low)

    def out_swap(ref, way, j):
        return swap(ref, ref, r.out_swap_send.at[0], r.out_swap_recv.at[way, j])

    def out_other(way, j):
        k, q = j // 2 + 1, j % 2
        q = q if way == 0 else 1 - q
        device = ring.device(-k if way == 0 else k, core)
        return r.w_out_all.at[device, pl.ds((1 - dp) * kept + q * (kept // 2), kept // 2)]

    def out_side(ref, slot):
        send, recv = r.out_side_send.at[slot], r.out_side_recv.at[slot]
        return remote(ref, ref, send, recv, ring.sibling)

    def out_own():
        return out_side(r.w_out_all.at[me, pl.ds((1 - dp) * kept, kept)], 0)

    def out_others():
        return out_side(w_outs.blocks(chips - 1), 1)

    def pass_out(j):
        w_outs.pass_on(j)
        for way in range(2):
            out_swap(w_outs.landed(way, j), way, j).start()

    def pass_other(j):
        for way in range(2):
            ref = out_other(way, j)
            out_swap(ref, way, j).wait_recv()
            out_side(ref, 1).start()

    tokens_in.pass_on(0)
    tokens_in.pass_on(1)
    over_again(0)
    tokens_in.pass_on(2)
    tokens_in.pass_on(3)
    norm_rows.wait()
    for j in range(size // 2):
        r.norms[:, j * 128 : (j + 1) * 128] = jnp.concatenate(
            [r.norm_recv[2 * j][:, :w_rows], r.norm_recv[2 * j + 1][:, :w_rows]], 1
        )
    head_weights.wait()
    head_other.start()
    over_again(3)
    for j in range(4, 6):
        tokens_in.pass_on(j)
    over_again(1)
    over_again(2)
    tokens_far.side(tokens_far.block(me), 0).start()
    w_outs.start()
    out_own().start()
    down_far.start()
    tokens_far.pass_on(0)
    tokens_far.pass_on(1)
    unpack_heads()
    for ahead in (0, 1, -1):
        tokens_in.wait_chip(ahead)
        project(ahead)
    tokens_far.pass_on(2)
    tokens_far.pass_on(3)
    pass_out(0)
    pass_out(1)
    tokens_in.wait_chip(2)
    project(2)
    for ahead in (0, 1, -1):
        tokens_far.wait_chip(ahead)
        project(ahead, other - near.base)
    for j in range(4, 6):
        tokens_far.pass_on(j)
    tokens_far.wait_chip(2)
    project(2, other - near.base)
    tokens_in.finish()
    tokens_far.finish()
    for q in range(4):
        over(q).wait_send()
    pass_out(2)
    pass_out(3)
    pass_other(0)
    pass_other(1)

    for t in range(tiles):
        span = pl.ds(t * TILE, TILE)
        query = r.q_t[:, span]
        top = None
        for j in range(t + 1):
            keys = pl.ds(j * TILE, TILE)
            s = dot(r.k_nat[keys, :], query)
            if j == t:
                s = jnp.where(causal(s.shape), s, -1e30)
            r.scores[keys, :] = s
            here = jnp.max(s, 0, keepdims=True)
            top = here if top is None else jnp.maximum(top, here)
        acc, norm = None, None
        for j in range(t + 1):
            keys = pl.ds(j * TILE, TILE)
            p = jnp.exp(r.scores[keys, :] - top)
            here = jnp.sum(p, 0, keepdims=True)
            add = dot(r.v_t[:, keys], p.astype(low))
            acc = add if acc is None else acc + add
            norm = here if norm is None else norm + here
        acc = acc / norm
        r.total[:, span] = acc
        r.lse[:, span] = top + jnp.log(norm)
        for b in range(TILE // rows):
            to = t * (TILE // rows) + b
            block = acc[:, b * rows : (b + 1) * rows].astype(low)
            r.att_send[to] = block

            @pl.when(me != to)
            def _(to=to):
                remote(
                    r.att_send.at[to], r.att_t.at[me], r.att_ssem.at[0], r.att_rsem.at[0], to
                ).start()

            @pl.when(me == to)
            def _(block=block):
                r.att_t[me] = block

        if t == 4:
            pass_out(4)
            pass_out(5)
            pass_other(2)
            pass_other(3)
        if t == 6:
            pass_out(6)
            pass_other(4)
            pass_other(5)
    up_weights.start()
    up_weights_far.start()
    pass_other(6)
    for ahead in range(chips):
        w_outs.wait_chip(ahead)
    out_own().wait_recv()
    out_others().wait_recv()
    attended = r.att_t.at[pl.ds(0, size - 1)]
    attended = remote(attended, attended, r.att_ssem.at[0], r.att_rsem.at[0], ring.right)
    down_far.wait_recv()
    down_other_far.start()
    attended.wait()

    att_t = r.att_t[...].reshape(width, rows)
    w_out_all = r.w_out_all
    proj = dot(att_t, w_out_all[...].reshape(width, width), TN)
    r.proj[...] = proj
    hat1, _ = normalized(proj)
    hidden = r.tokens_v[...].astype(full) + hat1 * gain(1) + bias(1)
    r.hidden[...] = hidden
    hat2, _ = normalized(hidden)
    r.big[mid_place] = (hat2 * gain(2) + bias(2)).astype(low)
    mids.start()
    w_outs.finish()

    def weights(b):
        up, down = ((r.w_up_all, r.w_down_v), (r.w_up_far, r.w_down_far))[b]
        return up[...].reshape(width, units), down[...]

    def forward(ahead):
        place = pl.ds(near.device(ahead, 0) - near.base, 2)
        x = r.big[place].reshape(pair, width)
        part = None
        for b in range(2):
            w_up, w_down = weights(b)
            act, slope = gelu_and_slope(dot(x, w_up))
            act = act.astype(low)
            r.act_all[b, place] = act.reshape(2, rows, units)
            r.slope_all[b, place] = slope.reshape(2, rows, units)
            add = dot(act, w_down)
            part = add if part is None else part + add
        r.parts[place] = part.astype(low).reshape(2, rows, width)
        sum_down.across(ahead).start()

    def backward(ahead):
        place = pl.ds(near.device(ahead, 0) - near.base, 2)
        x = r.big[pl.ds(near.device(ahead, 0) - near.base + close, 2)].reshape(pair, width)
        part = None
        for b in range(2):
            w_up, w_down = weights(b)
            d_act = dot(x, w_down, NT)
            d_up = (d_act * r.slope_all[b, place].reshape(pair, units)).astype(low)
            r.d_up_all[b, place] = d_up.reshape(2, rows, units)
            add = dot(d_up, w_up, NT)
            part = add if part is None else part + add
        r.parts[place] = part.astype(low).reshape(2, rows, width)
        sum_mid.across(ahead).start()

    def there_and_back(gather, scatter, ready, work, fill):
        last = near.steps
        for k in range(1, last + 1):
            if k == last:
                ready()
                gather.wait_chip(0)
                work(0)
                for ahead in range(1, last):
                    for chip in (ahead, -ahead):
                        gather.wait_chip(chip)
                        work(chip)
                scatter.step(2)
                scatter.step(3)
            for j in range(4 * (k - 1), min(4 * k, gather.messages)):
                gather.pass_on(j)
        gather.wait_chip(last)
        work(last)
        scatter.step(0)
        scatter.step(1)
        for j in range(4, scatter.messages):
            fill(j)
            scatter.step(j)
        fill(scatter.messages)

    def weights_here():
        up_weights.wait()
        up_other.start()
        up_weights_far.wait()
        up_other_far.start()
        up_other.wait_recv()
        up_other_far.wait_recv()
        down_other_far.wait_recv()

    there_and_back(mids, sum_down, weights_here, forward, lambda j: None)

    weight_row = jnp.zeros((1, rows), full)
    for c in range(r.weight.shape[0]):
        weight_row += jnp.where(r.corpus_v[...] == c, r.weight[c], 0.0)
    row_weight = jnp.broadcast_to(weight_row, (rows, rows)).T[:, 0:1]
    for q in range(4):
        span = pl.ds(q * quarter, quarter)
        down = sum_down.result(q)
        hat3, scale3 = normalized(down)
        r.output_v[span, :] = (r.hidden[span, :] + hat3 * gain(3) + bias(3)).astype(low)
        grad_y = r.cotangent_v[span, :].astype(full) * row_weight[q * quarter : (q + 1) * quarter]
        r.d_hidden[span, :] = grad_y
        r.big[dd_place, span] = norm_back(grad_y, hat3, scale3, gain(3)).astype(low)
        g3 = jnp.sum(grad_y * hat3, 0, keepdims=True)
        b3 = jnp.sum(grad_y, 0, keepdims=True)
        r.norm_grads[3:4, :] = g3 if q == 0 else r.norm_grads[3:4, :] + g3
        r.norm_grads[7:8, :] = b3 if q == 0 else r.norm_grads[7:8, :] + b3
    mids.finish()
    sum_down.finish()
    d_downs.start()
    saves = {}

    def save(name):
        i = OUTPUTS.index(name)
        saves[name] = pltpu.make_async_copy(
            getattr(r, name + "_v"), getattr(r, name), r.save_sem.at[i]
        )
        saves[name].start()

    save("output")

    def up_gradient(b):
        d_up = r.d_up_all[b].reshape(near_length, units)
        blocks = size // 4
        for i in range(4):
            span = pl.ds(i * (width // 4), width // 4)
            x = r.big[:close, :, span].reshape(near_length, width // 4)
            grad = dot(d_up, x, TN).T.astype(low)
            r.up_grad[b][i * blocks : (i + 1) * blocks] = grad.reshape(blocks, w_rows, units)
        up_half[b].start()

    def down_gradient(b):
        act = r.act_all[b].reshape(near_length, units)
        for i in range(4):
            span = pl.ds(i * (width // 4), width // 4)
            dd = r.big[close:, :, span].reshape(near_length, width // 4)
            r.down_grad[b][:, span] = dot(act, dd, TN).astype(low)
        down_half[b].start()

    def fill(j):
        if j < 6:
            up_gradient(j - 4)

    there_and_back(d_downs, sum_mid, lambda: None, backward, fill)

    hat1, scale1 = normalized(r.proj[...])
    hat2, scale2 = normalized(r.hidden[...])
    hat0, scale0 = normalized(r.tokens_v[...].astype(full))
    r.hat0[...] = hat0
    d_mid = sum_mid.whole()
    r.norm_grads[2:3, :] = jnp.sum(d_mid * hat2, 0, keepdims=True)
    r.norm_grads[6:7, :] = jnp.sum(d_mid, 0, keepdims=True)
    d_hidden = r.d_hidden[...] + norm_back(d_mid, hat2, scale2, gain(2))
    r.d_hidden[...] = d_hidden
    r.norm_grads[1:2, :] = jnp.sum(d_hidden * hat1, 0, keepdims=True)
    r.norm_grads[5:6, :] = jnp.sum(d_hidden, 0, keepdims=True)
    d_proj = norm_back(d_hidden, hat1, scale1, gain(1)).astype(low)
    d_att = dot(w_out_all[...].reshape(width, width), d_proj, NT).astype(low)
    r.d_att[...] = d_att.reshape(HEADS, HEAD_DIM, rows)
    d_atts.start()

    out = dot(att_t, d_proj).astype(low).reshape(size, w_rows, width)
    r.out_parts[:, :w_rows] = out[:close]
    r.out_parts[:, w_rows:] = out[close:]
    for ahead in range(near.chips):
        sum_out.across(ahead).start()
    r.att_recv[me] = r.d_att[me]
    d_downs.finish()
    sum_mid.finish()
    r.dq[...] = jnp.zeros_like(r.dq)
    for b in range(2):
        down_gradient(b)
    for b in range(2):
        up_half[b].wait_recv()
        up_mine = r.up_grad[b][:, rows_mine].astype(full)
        r.up_send[b][...] = (up_mine + r.up_peer[b][...].astype(full)).astype(low)
        r.up_recv[b][me] = r.up_send[b][me]
    up_grads.start()
    up_grads_far.start()
    for j in range(4):
        sum_out.step(j)
    d_atts.wait()
    for b in range(size):
        r.do_t[:, b * rows : (b + 1) * rows] = r.att_recv[b]
    for t in range(tiles):
        span = pl.ds(t * TILE, TILE)
        do = r.do_t[:, span].astype(full)
        r.do_nat[span, :] = do.T.astype(low)
        r.delta[:, span] = jnp.sum(do * r.total[:, span], 0, keepdims=True)

    def turned_back(u, span, base):
        c, s = r.cos_v[:, span], r.sin_v[:, span]
        first, second = u[:half], u[half:]
        r.d_t[base : base + half, span] = (first * c + second * s).astype(low)
        r.d_t[base + half : base + 2 * half, span] = (second * c - first * s).astype(low)

    high = near.base // close
    out_own_rows, out_far_rows = pl.ds(high * w_rows, w_rows), pl.ds((1 - high) * w_rows, w_rows)

    def beside_attention(j):
        if j in (0, 1):
            sum_out.step(4 + j)
        if j == 2:
            for b in range(2):
                down_half[b].wait_recv()
            down_mine = r.down_grad[1][units_mine].astype(full)
            r.down_send[...] = (down_mine + r.down_peer[1][...].astype(full)).astype(low)
            down_back_far.start()
        if j == 3:
            r.out_sum[...] = sum_out.whole()
            r.out_send[...] = r.out_sum[out_far_rows].astype(low)
            out_over.start()

    def collect_up():
        up_grads.wait()
        up_grads_far.wait()
        for h in range(size):
            both = r.up_recv[0][h].astype(full) + r.up_recv[1][(h + close) % size].astype(full)
            r.up_all[h, rows_mine] = both.astype(low)
        up_back.start()

    def collect_out():
        out_over.wait_recv()
        r.out_mine[...] = (r.out_sum[out_own_rows] + r.out_recv[...].astype(full)).astype(low)
        out_whole.start()

    def collect_down():
        down_back_far.wait_recv()
        both = r.down_grad[0][units_mine].astype(full) + r.down_peer[0][...].astype(full)
        r.down_sum[units_mine] = (both + r.down_recv[...].astype(full)).astype(low)
        down_back.start()

    for j in range(tiles):
        keys = pl.ds(j * TILE, TILE)
        dk, dv = None, None
        for t in range(j, tiles):
            span = pl.ds(t * TILE, TILE)
            s = dot(r.k_nat[keys, :], r.q_t[:, span])
            p = jnp.exp(s - r.lse[:, span])
            if j == t:
                p = jnp.where(causal(p.shape), p, 0.0)
            d_p = dot(r.v_nat[keys, :], r.do_t[:, span])
            d_s = (p * (d_p - r.delta[:, span])).astype(low)
            dv_add = dot(p.astype(low), r.do_nat[span, :])
            dk_add = dot(d_s, r.q_nat[span, :])
            dv = dv_add if dv is None else dv + dv_add
            dk = dk_add if dk is None else dk + dk_add
            r.dq[:, span] += dot(r.k_t[:, keys], d_s)
        turned_back(dk.T, keys, HEAD_DIM)
        r.d_t[2 * HEAD_DIM :, keys] = dv.T.astype(low)
        turned_back(r.dq[:, keys] * HEAD_DIM**-0.5, keys, 0)
        beside_attention(j)

    def part(ahead):
        base = ring.device(ahead, 0)
        span = pl.ds(pl.multiple_of(base * rows, pair), pair)
        d_x = dot(r.d_t[:, span], r.w_t[...], TN).astype(low)
        r.parts[pl.ds(base, 2)] = d_x.reshape(2, rows, width)
        sum_in.across(ahead).start()

    def head_gradient(j):
        x = r.normed_all[:, :, j * 128 : (j + 1) * 128].reshape(length, 128)
        d_w = dot(r.d_t[...], x).T
        for i in range(2):
            for h in range(2):
                base = i * w_rows + h * kept
                block = d_w[base : base + kept]
                v = block[:, 2 * HEAD_DIM :]
                v = jnp.concatenate([v[: kept // 2], v[kept // 2 :]], 1)
                at = h * packed
                r.head_parts[2 * j + i, at : at + kept] = block[:, : 2 * HEAD_DIM].astype(low)
                r.head_parts[2 * j + i, at + kept : at + packed] = v.astype(low)

    part(steps)
    part(steps - 1)
    part(1 - steps)
    for j in range(4):
        sum_in.step(j)
    for k in range(steps - 2, 0, -1):
        part(k)
        part(-k)
    part(0)
    sum_in.step(4)
    sum_in.step(5)
    for j in range(size // 2):
        head_gradient(j)
    head_weights.finish()
    head_half.start()
    for j in range(6, 8):
        sum_in.step(j)
    collect_out()
    for j in range(8, 10):
        sum_in.step(j)
    collect_up()
    head_half.wait_recv()
    own_half = r.head_parts[:, pl.ds(dp * packed, packed)].astype(full)
    r.head_send[...] = (own_half + r.head_peer[...].astype(full)).astype(low)
    r.head_all[me, pl.ds(dp * packed, packed)] = r.head_send[me]
    head_grads.start()
    for j in range(10, 12):
        sum_in.step(j)
    collect_down()
    for j in range(12, 14):
        sum_in.step(j)
    out_whole.wait_recv()
    r.grad_out_v[...] = r.out_mine[...].astype(full) + r.out_peer[...].astype(full)
    save("grad_out")
    d_normed = sum_in.whole()
    up_back.wait_recv()
    for h in range(size):
        r.grad_up_v[:, h * units : (h + 1) * units] = r.up_all[h].astype(full)
    save("grad_up")
    down_back.wait_recv()
    r.grad_down_v[...] = r.down_sum[...].astype(full)
    save("grad_down")
    head_grads.wait()
    head_back.start()

    hat0 = r.hat0[...]
    r.norm_grads[0:1, :] = jnp.sum(d_normed * hat0, 0, keepdims=True)
    r.norm_grads[4:5, :] = jnp.sum(d_normed, 0, keepdims=True)

    def norm_copy(i, other):
        to = (me + i) % size
        return pltpu.make_async_remote_copy(
            src_ref=r.norm_grads.at[:, columns(to // 2, 128)],
            dst_ref=r.norm_sums.at[2 * i + other],
            send_sem=r.norm_ssem.at[0],
            recv_sem=r.norm_rsem.at[0],
            device_id={"seq": to, "dp": (dp + other) % 2},
            device_id_type=MESH,
        )

    partners = [(i, other) for i in range(size) for other in range(2) if i or other]
    for i, other in partners:
        norm_copy(i, other).start()
    r.norm_sums[0] = r.norm_grads[:, columns(me // 2, 128)]
    _, scale0 = normalized(r.tokens_v[...].astype(full))
    r.grad_tokens_v[...] = r.d_hidden[...] + norm_back(d_normed, hat0, scale0, gain(0))
    save("grad_tokens")
    head_back.wait_recv()
    for h in range(2):
        for j in range(size // 2):
            blocks = [
                r.head_all[2 * j + i, h * packed : (h + 1) * packed].astype(full) for i in range(2)
            ]
            span = slice(h * kept, (h + 1) * kept)
            for b in range(2):
                place = slice(b * width + j * 128, b * width + (j + 1) * 128)
                r.grad_qkv_v[span, place] = jnp.concatenate(
                    [p[:kept, b * HEAD_DIM : (b + 1) * HEAD_DIM] for p in blocks], 1
                )
            v = [jnp.concatenate([p[kept:, :HEAD_DIM], p[kept:, HEAD_DIM:]], 0) for p in blocks]
            place = slice(2 * width + j * 128, 2 * width + (j + 1) * 128)
            r.grad_qkv_v[span, place] = jnp.concatenate(v, 1)
    save("grad_qkv")
    norm_all = r.norm_sums.at[pl.ds(1, 2 * size - 1)]
    norm_all = swap(norm_all, norm_all, r.norm_ssem.at[0], r.norm_rsem.at[0])
    norm_all.wait_recv()
    sums = jnp.sum(r.norm_sums[...], 0)
    sums = jnp.where(core == 0, sums[:, :w_rows], sums[:, w_rows:])
    r.grad_gains_v[...] = sums[0:4]
    r.grad_biases_v[...] = sums[4:8]
    save("grad_gains")
    save("grad_biases")

    norm_all.wait_send()
    sum_in.finish()
    sum_out.finish()
    for moved in (
        norm_rows, up_weights, up_weights_far, d_atts, up_grads, up_grads_far, head_grads
    ):
        moved.finish()
    for copy in (
        head_other,
        up_other,
        up_other_far,
        down_far,
        down_other_far,
        *up_half,
        *down_half,
        down_back_far,
        down_back,
        out_over,
        out_whole,
        up_back,
        head_half,
        head_back,
    ):
        copy.wait_send()
    out_own().wait_send()
    out_others().wait_send()
    out_swap(w_outs.blocks(chips - 1), 0, 0).wait_send()
    for copy in saves.values():
        copy.wait()


def hand_over_kernel(count, *refs):
    ins, outs, held = (refs[i * count : (i + 1) * count] for i in range(3))
    sems = refs[-1]
    loads = [pltpu.make_async_copy(ins[i], held[i], sems.at[0, i]) for i in range(count)]
    saves = [pltpu.make_async_copy(held[i], outs[i], sems.at[1, i]) for i in range(count)]
    for copy in loads:
        copy.start()
    for load, copy in zip(loads, saves):
        load.wait()
        copy.start()
    for copy in saves:
        copy.wait()


def hand_over(arrays):
    count = len(arrays)
    return pl.pallas_call(
        functools.partial(hand_over_kernel, count),
        out_shape=[jax.ShapeDtypeStruct(a.shape, a.dtype) for a in arrays],
        in_specs=[ANY] * count,
        out_specs=[ANY] * count,
        scratch_shapes=[pltpu.VMEM(a.shape, a.dtype) for a in arrays] + [DMA((2, count))],
    )(*arrays)


def split_heads(
    tokens, w_qkv, w_out, w_up, w_down, norm_gains, norm_biases, corpus_id, corpus_weight, cotangent
):
    size = lax.axis_size("seq")
    chips = size // 2
    _, rows, width = tokens.shape
    w_rows = w_out.shape[0]
    units = w_down.shape[0]
    length = rows * size
    shape = jax.ShapeDtypeStruct
    cos, sin = turn_tables(length)
    inputs = dict(
        tokens=tokens[0],
        w_qkv=w_qkv,
        w_out=w_out,
        w_up=w_up,
        w_down=w_down,
        gains=norm_gains,
        biases=norm_biases,
        corpus=corpus_id,
        cotangent=cotangent[0],
        cos=cos,
        sin=sin,
    )
    outputs = dict(
        output=shape((rows, width), low),
        grad_tokens=shape((rows, width), full),
        grad_qkv=shape((w_rows, 3 * width), full),
        grad_out=shape((w_rows, width), full),
        grad_up=shape((w_rows, size * units), full),
        grad_down=shape((units, width), full),
        grad_gains=shape((4, w_rows), full),
        grad_biases=shape((4, w_rows), full),
    )

    def vmem(*dims, kind=low):
        return pltpu.VMEM(dims, kind)

    head_rows = 3 * w_rows // 2
    blocks = vmem(size, rows, width)
    nat, turned = vmem(length, HEAD_DIM), vmem(HEAD_DIM, length)
    side, inbox, outbox = Scatter.buffers(chips, rows, width, 4)
    side, inbox, outbox = Scatter.buffers(chips // 2, rows, width, 4)
    in_side, in_inbox, in_outbox = Scatter.buffers(chips, rows, width, 4)
    scratch = {name + "_v": vmem(*a.shape, kind=a.dtype) for name, a in inputs.items()}
    scratch |= {name + "_v": vmem(*a.shape, kind=a.dtype) for name, a in outputs.items()}
    scratch |= dict(
        big=blocks,
        normed_all=blocks,
        parts=blocks,
        side=[side] * 2,
        inbox=[inbox] * 2,
        outbox=[outbox] * 2,
        in_side=in_side,
        in_inbox=in_inbox,
        in_outbox=in_outbox,
        out_parts=vmem(size // 2, 2 * w_rows, width),
        out_sum=vmem(2 * w_rows, width, kind=full),
        out_send=vmem(w_rows, width),
        out_recv=vmem(w_rows, width),
        out_mine=vmem(w_rows, width),
        out_peer=vmem(w_rows, width),
        w_out_all=vmem(size, w_rows, width),
        w_up_all=vmem(size, w_rows, units),
        w_up_far=vmem(size, w_rows, units),
        w_down_far=vmem(units, width),
        w_t=vmem(3 * HEAD_DIM, width),
        head_send=vmem(size, head_rows // 2, 128),
        head_recv=vmem(size, head_rows, 128),
        head_parts=vmem(size, head_rows, 128),
        head_peer=vmem(size, head_rows // 2, 128),
        head_all=vmem(size, head_rows, 128),
        norm_send=vmem(8, 128, kind=full),
        norm_recv=vmem(size, 8, 128, kind=full),
        norms=vmem(8, width, kind=full),
        norm_grads=vmem(8, width, kind=full),
        norm_sums=vmem(2 * size, 8, 128, kind=full),
        q_t=turned,
        k_t=turned,
        v_t=turned,
        do_t=turned,
        q_nat=nat,
        k_nat=nat,
        v_nat=nat,
        do_nat=nat,
        total=vmem(HEAD_DIM, length, kind=full),
        dq=vmem(HEAD_DIM, length, kind=full),
        d_t=vmem(3 * HEAD_DIM, length),
        lse=vmem(1, length, kind=full),
        delta=vmem(1, length, kind=full),
        scores=vmem(length, TILE, kind=full),
        att_send=vmem(size, HEAD_DIM, rows),
        att_t=vmem(size, HEAD_DIM, rows),
        d_att=vmem(size, HEAD_DIM, rows),
        att_recv=vmem(size, HEAD_DIM, rows),
        proj=vmem(rows, width, kind=full),
        hidden=vmem(rows, width, kind=full),
        d_hidden=vmem(rows, width, kind=full),
        hat0=vmem(rows, width, kind=full),
        act_all=vmem(2, size // 2, rows, units),
        slope_all=vmem(2, size // 2, rows, units, kind=full),
        d_up_all=vmem(2, size // 2, rows, units),
        up_grad=[vmem(size, w_rows, units)] * 2,
        up_peer=[vmem(size, w_rows // 2, units)] * 2,
        up_send=[vmem(size, w_rows // 2, units)] * 2,
        up_recv=[vmem(size, w_rows // 2, units)] * 2,
        up_all=vmem(size, w_rows, units),
        down_grad=[vmem(units, width)] * 2,
        down_peer=[vmem(units // 2, width)] * 2,
        down_send=vmem(units // 2, width),
        down_recv=vmem(units // 2, width),
        down_sum=vmem(units, width),
        far_sems=DMA((10,)),
        over_send=DMA((4,)),
        over_recv=DMA((4,)),
        load_sem=DMA((len(inputs),)),
        save_sem=DMA((len(outputs),)),
        swap_send=DMA((13,)),
        swap_recv=DMA((13,)),
        out_side_send=DMA((2,)),
        out_side_recv=DMA((2,)),
        out_swap_send=DMA((1,)),
        out_swap_recv=DMA((2, Gather.count(chips, 2))),
        att_ssem=DMA((1,)),
        att_rsem=DMA((1,)),
        norm_ssem=DMA((1,)),
        norm_rsem=DMA((1,)),
    )
    for i, (count, pieces) in enumerate(((chips // 2, 4), (chips, 2), (chips // 2, 4))):
        scratch[f"gather{i}"] = Gather.sems(count, pieces)
    for i in range(3):
        scratch[f"scatter{i}"] = Scatter.sems(chips if i == 2 else chips // 2, 4)
    for i in range(8):
        scratch[f"exchange{i}"] = [DMA((1,)), DMA((1,))]
    flat, groups = [], []
    for name, entry in scratch.items():
        entries = entry if isinstance(entry, list) else [entry]
        groups.append((name, len(entries) if isinstance(entry, list) else 0))
        flat += entries

    def kernel(*refs):
        count = len(inputs) + 1 + len(outputs)
        names = [*inputs, "weight", *outputs]
        values = list(refs[:count])
        rest = list(refs[count:])
        for name, many in groups:
            names.append(name)
            if many:
                values.append(tuple(rest[:many]))
                rest = rest[many:]
            else:
                values.append(rest.pop(0))
        layer_kernel(names, *values)

    results = pl.pallas_call(
        kernel,
        out_shape=list(outputs.values()),
        in_specs=[ANY] * len(inputs) + [pl.BlockSpec(memory_space=pltpu.SMEM)],
        out_specs=[ANY] * len(outputs),
        scratch_shapes=flat,
        compiler_params=pltpu.CompilerParams(
            collective_id=1, has_side_effects=True, vmem_limit_bytes=61 * 2**20
        ),
    )(*inputs.values(), corpus_weight)
    results = hand_over(results)
    return (results[0][None], results[1][None], *results[2:])


def shifted(x, axis, by):
    size = lax.axis_size(axis)
    return lax.ppermute(x, axis, [(i, (i + by) % size) for i in range(size)])


def passed_along(value, axis, steps):
    count = lax.axis_size(axis)
    first, last = (max(0, -steps), min(count, count - steps))
    return lax.ppermute(value, axis, [(source, source + steps) for source in range(first, last)])


def layer_norm(values, gain, bias):
    center = values - jnp.mean(values, -1, keepdims=True)
    variance = jnp.mean(center * center, -1, keepdims=True)
    return center * lax.rsqrt(variance + 1e-05) * gain + bias


def rotate(values, position, direction):
    half_size = values.shape[-1] // 2
    freq = jnp.exp(
        jnp.arange(half_size).astype(jnp.float32) * (-2.0 * math.log(10000.0) / values.shape[-1])
    )
    angle = position[:, None] * freq[None, :]
    cosine = jnp.cos(angle)[:, None, :]
    sine = direction * jnp.sin(angle)[:, None, :]
    first = values[..., :half_size]
    second = values[..., half_size:]
    return jnp.concatenate([first * cosine - second * sine, first * sine + second * cosine], -1)


def gelu_tanh(values):
    return jax.nn.gelu(values, approximate=True)


def per_device(
    tokens, w_qkv, w_out, w_up, w_down, norm_gains, norm_biases, corpus_id, corpus_weight, cotangent
):
    full_qkv, full_out, full_up, full_down, gains_low, biases_low = (
        lax.all_gather(w_qkv, "seq", axis=0, tiled=True),
        lax.all_gather(w_out, "seq", axis=0, tiled=True),
        lax.all_gather(w_up, "seq", axis=0, tiled=True),
        lax.all_gather(w_down, "seq", axis=0, tiled=True),
        lax.all_gather(norm_gains, "seq", axis=1, tiled=True),
        lax.all_gather(norm_biases, "seq", axis=1, tiled=True),
    )
    gains = gains_low.astype(jnp.float32)
    biases = biases_low.astype(jnp.float32)
    seq_count, row_count, model_width = tokens.shape
    shape_heads = (seq_count, row_count, HEADS, HEAD_DIM)
    scale = HEAD_DIM ** (-0.5)
    cycle_size = lax.axis_size("seq")
    cycle_index = lax.axis_index("seq")
    query_pos = cycle_index * row_count + jnp.arange(row_count)
    position = query_pos.astype(jnp.float32)
    x_float = tokens.astype(jnp.float32)
    normed_low = layer_norm(x_float, gains[0], biases[0]).astype(jnp.bfloat16)
    qkv = jnp.einsum("std,de->ste", normed_low, full_qkv, preferred_element_type=jnp.float32)
    query_low = rotate(qkv[..., :model_width].reshape(shape_heads), position, 1.0).astype(
        jnp.bfloat16
    )
    key_low = rotate(
        qkv[..., model_width : 2 * model_width].reshape(shape_heads), position, 1.0
    ).astype(jnp.bfloat16)
    value_low = qkv[..., 2 * model_width :].reshape(shape_heads).astype(jnp.bfloat16)

    def block_scores(key_piece, key_pos):
        scores = (
            jnp.einsum("sqhd,skhd->shqk", query_low, key_piece, preferred_element_type=jnp.float32)
            * scale
        )
        allowed = query_pos[:, None] >= key_pos[None, :]
        return (scores, allowed)

    stat_shape = (seq_count, HEADS, row_count)
    key_piece = lax.all_gather(key_low, "seq", axis=1, tiled=True)
    value_piece = lax.all_gather(value_low, "seq", axis=1, tiled=True)
    key_pos = jnp.arange(key_piece.shape[1])
    run_max = jnp.full(stat_shape, -1e30, jnp.float32)
    scores, allowed = block_scores(key_piece, key_pos)
    new_max = jnp.maximum(run_max, jnp.max(jnp.where(allowed, scores, -1e30), -1))
    weights = jnp.where(allowed, jnp.exp(scores - new_max[..., None]), 0.0)
    run_sum = jnp.sum(weights, -1)
    total = jnp.einsum(
        "shqk,skhd->sqhd",
        weights.astype(jnp.bfloat16),
        value_piece,
        preferred_element_type=jnp.float32,
    )
    run_max, run_sum, total = (new_max, run_sum, total)
    log_sum = run_max + jnp.log(run_sum)
    attended = total / jnp.transpose(run_sum, (0, 2, 1))[..., None]
    attended_low = attended.reshape(seq_count, row_count, model_width).astype(jnp.bfloat16)
    proj = jnp.einsum("std,de->ste", attended_low, full_out, preferred_element_type=jnp.float32)
    hidden = x_float + layer_norm(proj, gains[1], biases[1])
    mid_low = layer_norm(hidden, gains[2], biases[2]).astype(jnp.bfloat16)
    up_proj = jnp.einsum("std,df->stf", mid_low, full_up, preferred_element_type=jnp.float32)
    act_low = gelu_tanh(up_proj).astype(jnp.bfloat16)
    down = jnp.einsum("stf,fd->std", act_low, full_down, preferred_element_type=jnp.float32)
    output = (hidden + layer_norm(down, gains[3], biases[3])).astype(jnp.bfloat16)
    matches = (corpus_id[..., None] == jnp.arange(corpus_weight.shape[0])).astype(jnp.float32)
    row_weight = jnp.sum(matches * corpus_weight, -1)
    grad_y = cotangent.astype(jnp.float32) * row_weight[..., None]
    _, down_back = jax.vjp(layer_norm, down, gains[3], biases[3])
    d_down, gain_three, bias_three = down_back(grad_y)
    d_down_low = d_down.astype(jnp.bfloat16)
    grad_down = jnp.einsum("stf,std->fd", act_low, d_down_low, preferred_element_type=jnp.float32)
    d_act = jnp.einsum("std,fd->stf", d_down_low, full_down, preferred_element_type=jnp.float32)
    _, gelu_back = jax.vjp(gelu_tanh, up_proj)
    d_up_low = gelu_back(d_act)[0].astype(jnp.bfloat16)
    grad_up = jnp.einsum("std,stf->df", mid_low, d_up_low, preferred_element_type=jnp.float32)
    d_mid = jnp.einsum("stf,df->std", d_up_low, full_up, preferred_element_type=jnp.float32)
    _, mid_back = jax.vjp(layer_norm, hidden, gains[2], biases[2])
    d_hidden_mid, gain_two, bias_two = mid_back(d_mid)
    d_hidden = grad_y + d_hidden_mid
    _, proj_back = jax.vjp(layer_norm, proj, gains[1], biases[1])
    d_proj, gain_one, bias_one = proj_back(d_hidden)
    d_proj_low = d_proj.astype(jnp.bfloat16)
    grad_out = jnp.einsum(
        "std,ste->de", attended_low, d_proj_low, preferred_element_type=jnp.float32
    )
    d_att_low = (
        jnp.einsum("ste,de->std", d_proj_low, full_out, preferred_element_type=jnp.float32)
        .astype(jnp.bfloat16)
        .reshape(shape_heads)
    )
    delta = jnp.transpose(jnp.sum(d_att_low.astype(jnp.float32) * attended, -1), (0, 2, 1))

    def contribute(d_query, key_piece, value_piece, d_key, d_value, owner):
        key_pos = owner * row_count + jnp.arange(row_count)
        query_sum = d_query
        key_sum = d_key
        value_sum = d_value
        scores, allowed = block_scores(key_piece, key_pos)
        probs = jnp.where(allowed, jnp.exp(scores - log_sum[..., None]), 0.0)
        value_sum = value_sum + jnp.einsum(
            "shqk,sqhd->skhd",
            probs.astype(jnp.bfloat16),
            d_att_low,
            preferred_element_type=jnp.float32,
        )
        d_probs = jnp.einsum(
            "sqhd,skhd->shqk", d_att_low, value_piece, preferred_element_type=jnp.float32
        )
        d_scores = (probs * (d_probs - delta[..., None]) * scale).astype(jnp.bfloat16)
        query_sum = query_sum + jnp.einsum(
            "shqk,skhd->sqhd", d_scores, key_piece, preferred_element_type=jnp.float32
        )
        key_sum = key_sum + jnp.einsum(
            "shqk,sqhd->skhd", d_scores, query_low, preferred_element_type=jnp.float32
        )
        return (query_sum, key_sum, value_sum)

    zeros_heads = jnp.zeros(shape_heads, jnp.float32)

    def pass_grads(d_key, d_value):
        return (
            shifted(d_key.astype(jnp.bfloat16), "seq", 1).astype(d_key.dtype),
            shifted(d_value.astype(jnp.bfloat16), "seq", 1).astype(d_value.dtype),
        )

    def cycle_turn(turn_index, state):
        d_query, key_piece, value_piece, d_key, d_value = state
        owner = (cycle_index - turn_index) % cycle_size
        d_query, d_key, d_value = contribute(d_query, key_piece, value_piece, d_key, d_value, owner)
        d_key, d_value = pass_grads(d_key, d_value)
        key_piece, value_piece = passed_along((key_piece, value_piece), "seq", 1)
        return (d_query, key_piece, value_piece, d_key, d_value)

    d_query, key_piece, value_piece, d_key, d_value = lax.fori_loop(
        0, cycle_size - 1, cycle_turn, (zeros_heads, key_low, value_low, zeros_heads, zeros_heads)
    )
    last_owner = (cycle_index + 1) % cycle_size
    d_query, d_key, d_value = contribute(
        d_query, key_piece, value_piece, d_key, d_value, last_owner
    )
    d_key, d_value = pass_grads(d_key, d_value)
    flat_shape = (seq_count, row_count, model_width)
    d_qkv_low = jnp.concatenate(
        [
            rotate(d_query, position, -1.0).reshape(flat_shape),
            rotate(d_key, position, -1.0).reshape(flat_shape),
            d_value.reshape(flat_shape),
        ],
        -1,
    ).astype(jnp.bfloat16)
    grad_qkv = jnp.einsum("std,ste->de", normed_low, d_qkv_low, preferred_element_type=jnp.float32)
    d_normed = jnp.einsum("ste,de->std", d_qkv_low, full_qkv, preferred_element_type=jnp.float32)
    _, input_back = jax.vjp(layer_norm, x_float, gains[0], biases[0])
    d_input, gain_zero, bias_zero = input_back(d_normed)
    grad_tokens = d_hidden + d_input
    grad_gains = jnp.stack([gain_zero, gain_one, gain_two, gain_three])
    grad_biases = jnp.stack([bias_zero, bias_one, bias_two, bias_three])
    all_grads = (grad_qkv, grad_out, grad_up, grad_down, grad_gains, grad_biases)
    pieces = (
        lax.psum_scatter(
            all_grads[0].astype(jnp.bfloat16), "seq", scatter_dimension=0, tiled=True
        ).astype(jnp.float32),
        lax.psum_scatter(
            all_grads[1].astype(jnp.bfloat16), "seq", scatter_dimension=0, tiled=True
        ).astype(jnp.float32),
        lax.psum_scatter(
            all_grads[2].astype(jnp.bfloat16), "seq", scatter_dimension=0, tiled=True
        ).astype(jnp.float32),
        lax.psum_scatter(
            all_grads[3].astype(jnp.bfloat16), "seq", scatter_dimension=0, tiled=True
        ).astype(jnp.float32),
        lax.psum_scatter(
            all_grads[4].astype(jnp.bfloat16), "seq", scatter_dimension=1, tiled=True
        ).astype(jnp.float32),
        lax.psum_scatter(
            all_grads[5].astype(jnp.bfloat16), "seq", scatter_dimension=1, tiled=True
        ).astype(jnp.float32),
    )
    shards = (
        lax.psum(pieces[0].astype(jnp.bfloat16), "dp").astype(jnp.float32),
        lax.psum(pieces[1].astype(jnp.bfloat16), "dp").astype(jnp.float32),
        lax.psum(pieces[2].astype(jnp.bfloat16), "dp").astype(jnp.float32),
        lax.psum(pieces[3].astype(jnp.bfloat16), "dp").astype(jnp.float32),
        lax.psum(pieces[4].astype(jnp.bfloat16), "dp").astype(jnp.float32),
        lax.psum(pieces[5].astype(jnp.bfloat16), "dp").astype(jnp.float32),
    )
    return (output, grad_tokens, shards[0], shards[1], shards[2], shards[3], shards[4], shards[5])


def solution(mesh):
    placed = (
        P("dp", "seq", None),
        P("seq", None),
        P("seq", None),
        P("seq", None),
        P("seq", None),
        P(None, "seq"),
        P(None, "seq"),
        P("dp", "seq"),
        P(),
        P("dp", "seq", None),
    )
    fits = mesh.shape["seq"] == HEADS and mesh.shape["dp"] == 2
    return jax.shard_map(
        split_heads if fits else per_device,
        mesh=mesh,
        in_specs=placed,
        out_specs=(
            P("dp", "seq", None),
            P("dp", "seq", None),
            P("seq", None),
            P("seq", None),
            P("seq", None),
            P("seq", None),
            P(None, "seq"),
            P(None, "seq"),
        ),
        check_vma=False,
    )
```

```python
import functools
import math
import types

import jax
import jax.numpy as jnp
import numpy as np
from jax import lax
from jax.experimental import pallas as pl
from jax.experimental.pallas import tpu as pltpu
from jax.sharding import PartitionSpec as P

HEADS = 16
HEAD_DIM = 64
TILE = 256
MESH = pl.DeviceIdType.MESH
ANY = pl.BlockSpec(memory_space=pl.ANY)
DMA = pltpu.SemaphoreType.DMA
NT = ((1,), (1,))
TN = ((0,), (0,))
low, full = jnp.bfloat16, jnp.float32


def dot(left, right, contract=((1,), (0,))):
    return lax.dot_general(left, right, (contract, ((), ())), preferred_element_type=full)


def remote(source, target, send, recv, device):
    return pltpu.make_async_remote_copy(
        src_ref=source,
        dst_ref=target,
        send_sem=send,
        recv_sem=recv,
        device_id={"seq": device},
        device_id_type=MESH,
    )


def swap(source, target, send, recv):
    return pltpu.make_async_remote_copy(
        src_ref=source,
        dst_ref=target,
        send_sem=send,
        recv_sem=recv,
        device_id={"dp": 1 - lax.axis_index("dp")},
        device_id_type=MESH,
    )


class Ring:
    def __init__(self, length):
        self.me = lax.axis_index("seq")
        self.length = length
        self.chips = 2 * length
        self.steps = length
        self.core = self.me % 2
        column, row = (self.me // 2) % 2, self.me // 4
        self.first = (row // length) * length
        row = row - self.first
        self.base = self.first * 4
        self.place = row + column * (self.chips - 1 - 2 * row)
        self.right = self.device(1, self.core)
        self.left = self.device(-1, self.core)
        self.sibling = self.device(0, 1 - self.core)

    def device(self, ahead, core):
        place = (self.place + ahead + self.chips) % self.chips
        column = place // self.length
        row = place + column * (self.chips - 1 - 2 * place)
        return (self.first + row) * 4 + column * 2 + core


class Gather:
    def __init__(self, ring, piece, block, blocks, pieces, sems):
        self.ring, self.piece, self.block, self.blocks = ring, piece, block, blocks
        self.pieces = pieces
        self.send, self.recv, self.side_send, self.side_recv = sems
        self.messages = self.count(ring.chips, pieces)

    @staticmethod
    def count(chips, pieces):
        return pieces * (chips // 2) - pieces // 2

    def ref(self, way, j, ahead):
        k, q = j // self.pieces + ahead, j % self.pieces
        q = q if way == 0 else self.pieces - 1 - q
        return self.piece(self.ring.device(-k if way == 0 else k, self.ring.core), q)

    def hop(self, way, j):
        ref = self.ref(way, j, 0)
        target = self.ring.right if way == 0 else self.ring.left
        return remote(ref, ref, self.send.at[0], self.recv.at[way, j], target)

    def landed(self, way, j):
        return self.ref(way, j, 1)

    def side(self, ref, slot):
        return remote(ref, ref, self.side_send.at[0], self.side_recv.at[slot], self.ring.sibling)

    def start(self):
        for j in range(self.pieces):
            for way in range(2):
                self.hop(way, j).start()
        self.side(self.block(self.ring.me), 0).start()

    def pass_on(self, j):
        k = j // self.pieces + 1
        for way in range(2):
            self.hop(way, j).wait_recv()
            if j + self.pieces < self.messages:
                self.hop(way, j + self.pieces).start()
            slot = (-k if way == 0 else k) % self.ring.chips
            self.side(self.landed(way, j), slot).start()

    def wait_chip(self, ahead):
        block = self.block(self.ring.device(ahead, 1 - self.ring.core))
        self.side(block, ahead % self.ring.chips).wait_recv()

    def finish(self):
        count = self.ring.chips - 1
        everything = self.blocks(count)
        remote(everything, everything, self.send.at[0], self.recv.at[0, 0], self.ring.right).wait_send()
        self.side(self.blocks(count + 1), 0).wait_send()

    @staticmethod
    def sems(chips, pieces):
        return [DMA((1,)), DMA((2, Gather.count(chips, pieces))), DMA((1,)), DMA((chips,))]


class Scatter:
    def __init__(self, ring, parts, pieces, side, inbox, outbox, sems, shift=0):
        self.ring, self.parts, self.pieces = ring, parts, pieces
        self.base = ring.base - shift
        self.side, self.inbox, self.outbox = side, inbox, outbox
        self.send, self.recv, self.side_send, self.side_recv = sems
        self.messages = Gather.count(ring.chips, pieces)
        self.rows = parts.shape[1] // pieces
        self.waited = set()

    def across(self, ahead):
        slot = ahead % self.ring.chips
        return remote(
            self.parts.at[self.ring.device(ahead, 1 - self.ring.core) - self.base],
            self.side.at[slot],
            self.side_send.at[0],
            self.side_recv.at[slot],
            self.ring.sibling,
        )

    def hop(self, way, j):
        target = self.ring.right if way == 0 else self.ring.left
        return remote(
            self.outbox.at[way, j],
            self.inbox.at[way, j],
            self.send.at[0],
            self.recv.at[way, j],
            target,
        )

    def own(self, ahead, q):
        slot = ahead % self.ring.chips
        if slot not in self.waited:
            self.waited.add(slot)
            self.across(ahead).wait_recv()
        span = pl.ds(q * self.rows, self.rows)
        mine = self.parts[self.ring.device(ahead, self.ring.core) - self.base, span].astype(full)
        return mine + self.side[slot, span].astype(full)

    def ahead(self, j):
        return self.ring.steps - (j + self.pieces // 2) // self.pieces

    def step(self, j):
        for way in range(2):
            q = j % self.pieces if way == 0 else self.pieces - 1 - j % self.pieces
            total = self.own(self.ahead(j) if way == 0 else -self.ahead(j), q)
            if j >= self.pieces:
                self.hop(way, j - self.pieces).wait_recv()
                total += self.inbox[way, j - self.pieces].astype(full)
            self.outbox[way, j] = total.astype(self.outbox.dtype)
            self.hop(way, j).start()

    def result(self, q):
        total = self.own(0, q)
        for way in range(2):
            k = q if way == 0 else self.pieces - 1 - q
            last = max(j for j in range(self.messages) if j % self.pieces == k)
            self.hop(way, last).wait_recv()
            total += self.inbox[way, last].astype(full)
        return total

    def whole(self):
        return jnp.concatenate([self.result(q) for q in range(self.pieces)], 0)

    def finish(self):
        everything = self.parts.at[pl.ds(0, self.ring.chips)]
        side = self.side_send.at[0], self.side_recv.at[0]
        remote(everything, self.side, *side, self.ring.sibling).wait_send()
        hops = self.send.at[0], self.recv.at[0, 0]
        remote(self.outbox, self.inbox, *hops, self.ring.right).wait_send()

    @staticmethod
    def buffers(chips, rows, columns, pieces):
        box = pltpu.VMEM((2, Gather.count(chips, pieces), rows // pieces, columns), low)
        return [pltpu.VMEM((chips, rows, columns), low), box, box]

    @staticmethod
    def sems(chips, pieces):
        return [DMA((1,)), DMA((2, Gather.count(chips, pieces))), DMA((1,)), DMA((chips,))]


class Exchange:
    def __init__(self, source, target, blocks, sems):
        self.source, self.target, self.blocks = source, target, blocks
        self.send, self.recv = sems
        self.me, self.size = lax.axis_index("seq"), lax.axis_size("seq")

    def start(self):
        for i in range(1, self.size):
            to = (self.me + i) % self.size
            remote(
                self.source(to), self.target(self.me), self.send.at[0], self.recv.at[0], to
            ).start()

    def all(self):
        ref = self.blocks(self.size - 1)
        to = (self.me + 1) % self.size
        return remote(ref, ref, self.send.at[0], self.recv.at[0], to)

    def wait(self):
        self.all().wait_recv()

    def finish(self):
        self.all().wait_send()


def normalized(values):
    center = values - jnp.mean(values, -1, keepdims=True)
    scale = lax.rsqrt(jnp.mean(center * center, -1, keepdims=True) + 1e-05)
    return center * scale, scale


def norm_back(grad, hat, scale, gain):
    d_hat = grad * gain
    mean = jnp.mean(d_hat, -1, keepdims=True)
    along = jnp.mean(d_hat * hat, -1, keepdims=True)
    return scale * (d_hat - mean - hat * along)


def gelu_and_slope(u):
    c = math.sqrt(2.0 / math.pi)
    square = u * u
    t = jnp.tanh(c * u * (1.0 + 0.044715 * square))
    act = 0.5 * u * (1.0 + t)
    slope = 0.5 * (1.0 + t) + 0.5 * u * (1.0 - t * t) * (c * (1.0 + 3 * 0.044715 * square))
    return act, slope


def causal(shape):
    key_pos = lax.broadcasted_iota(jnp.int32, shape, 0)
    query_pos = lax.broadcasted_iota(jnp.int32, shape, 1)
    return key_pos <= query_pos


def turn_tables(length):
    half = HEAD_DIM // 2
    freq = np.exp(
        np.arange(half, dtype=np.float32) * np.float32(-2.0 * math.log(10000.0) / HEAD_DIM)
    )
    angle = freq[:, None] * np.arange(length, dtype=np.float32)[None, :]
    return jnp.asarray(np.cos(angle)), jnp.asarray(np.sin(angle))


INPUTS = (
    "tokens",
    "w_qkv",
    "gains",
    "biases",
    "w_out",
    "w_up",
    "cos",
    "sin",
    "w_down",
    "cotangent",
    "corpus",
)
OUTPUTS = (
    "output",
    "grad_tokens",
    "grad_qkv",
    "grad_out",
    "grad_up",
    "grad_down",
    "grad_gains",
    "grad_biases",
)


def layer_kernel(names, *refs):
    r = types.SimpleNamespace(**dict(zip(names, refs, strict=True)))
    size = lax.axis_size("seq")
    ring, near = Ring(size // 4), Ring(size // 8)
    me, core, chips, steps = ring.me, ring.core, ring.chips, ring.steps
    far = (me + size // 2) % size
    close = size // 2
    dp = lax.axis_index("dp")
    rows, width = r.tokens.shape
    w_rows = r.w_out.shape[0]
    units = r.w_down.shape[0]
    length = rows * size
    near_length = rows * close
    tiles = length // TILE
    half = HEAD_DIM // 2
    kept = w_rows // 2
    packed = 3 * kept // 2
    pair = 2 * rows

    def mine(ref):
        return ref.at[:, pl.ds(dp * (ref.shape[1] // 2), ref.shape[1] // 2)]

    def theirs(ref):
        return ref.at[:, pl.ds((1 - dp) * (ref.shape[1] // 2), ref.shape[1] // 2)]

    def columns(device, count):
        return pl.ds(pl.multiple_of(device * count, count), count)

    loads = {
        name: pltpu.make_async_copy(getattr(r, name), getattr(r, name + "_v"), r.load_sem.at[i])
        for i, name in enumerate(INPUTS)
    }
    for name in INPUTS:
        loads[name].start()
    barrier = pltpu.get_barrier_semaphore()
    for i in range(1, size):
        pl.semaphore_signal(barrier, inc=1, device_id={"seq": (me + i) % size}, device_id_type=MESH)
    pl.semaphore_signal(barrier, inc=1, device_id={"dp": 1 - dp}, device_id_type=MESH)

    quarter = rows // 4

    def gather(ring, ref, count, sems, first=0, shift=0):
        pieces = 4 if ref.shape[1] == rows else 2
        shift = shift - ring.base
        return Gather(
            ring,
            lambda d, q: ref.at[d + shift, pl.ds(first + q * (count // pieces), count // pieces)],
            lambda d: ref.at[d + shift, pl.ds(first, count)],
            lambda n: ref.at[pl.ds(0, n), pl.ds(0, count)],
            pieces,
            sems,
        )

    mid_place, dd_place = me - near.base, me - near.base + close
    other = close - near.base
    tokens_in = gather(near, r.big, rows, r.gather2, shift=near.base)
    tokens_far = gather(near, r.big, rows, r.gather0, shift=other)

    def over(q):
        ref = r.big.at[me, pl.ds(q * (rows // 4), rows // 4)]
        return remote(ref, ref, r.over_send.at[q], r.over_recv.at[q], far)

    def over_again(q):
        over(q).wait_recv()
        tokens_far.hop(0, q).start()
        tokens_far.hop(1, 3 - q).start()

    mids = gather(near, r.big, rows, r.gather2)
    d_downs = gather(near, r.big, rows, r.gather2, shift=close)
    w_outs = gather(ring, r.w_out_all, kept, r.gather1, dp * kept)
    boxes = [(r.side[i], r.inbox[i], r.outbox[i], (r.scatter0, r.scatter1)[i]) for i in range(2)]
    sum_down = Scatter(near, r.parts, 4, *boxes[0])
    sum_mid = Scatter(near, r.parts, 4, *boxes[0])
    sum_out = Scatter(near, r.out_parts, 4, *boxes[1])
    sum_in = Scatter(ring, r.parts, 4, r.in_side, r.in_inbox, r.in_outbox, r.scatter2)
    out_over = remote(r.out_send, r.out_recv, r.far_sems.at[8], r.far_sems.at[9], far)

    def exchange(source, ref, sems, count):
        return Exchange(
            source,
            lambda d: ref.at[d, pl.ds(dp * count if count < ref.shape[1] else 0, count)],
            lambda n: ref.at[pl.ds(0, n), pl.ds(0, count)],
            sems,
        )

    head_weights = exchange(lambda d: r.head_send.at[d], r.head_recv, r.exchange0, packed)
    norm_rows = exchange(lambda d: r.norm_send, r.norm_recv, r.exchange1, 8)

    def up_exchange(ref, sems, shift):
        return exchange(
            lambda d: r.w_up_v.at[pl.ds(dp * kept, kept), columns((d + shift) % size, units)],
            ref,
            sems,
            kept,
        )

    up_weights = up_exchange(r.w_up_all, r.exchange2, 0)
    up_weights_far = up_exchange(r.w_up_far, r.exchange6, size // 2)
    d_atts = exchange(lambda d: r.d_att.at[d], r.att_recv, r.exchange3, HEAD_DIM)
    up_grads = exchange(lambda d: r.up_send[0].at[d], r.up_recv[0], r.exchange4, kept)
    up_grads_far = exchange(lambda d: r.up_send[1].at[d], r.up_recv[1], r.exchange7, kept)
    head_grads = exchange(lambda d: r.head_send.at[d], r.head_all, r.exchange5, packed)

    def swapped(source, target, slot):
        return swap(source, target, r.swap_send.at[slot], r.swap_recv.at[slot])

    head_other = swapped(mine(r.head_recv), mine(r.head_recv), 0)
    up_other = swapped(mine(r.w_up_all), mine(r.w_up_all), 1)
    up_other_far = swapped(mine(r.w_up_far), mine(r.w_up_far), 8)
    units_mine = pl.ds(dp * (units // 2), units // 2)
    units_theirs = pl.ds((1 - dp) * (units // 2), units // 2)
    down_far = remote(
        r.w_down_v.at[units_mine],
        r.w_down_far.at[units_mine],
        r.far_sems.at[0],
        r.far_sems.at[1],
        far,
    )
    down_other_far = swapped(r.w_down_far.at[units_mine], r.w_down_far.at[units_mine], 9)
    up_half = [swapped(theirs(r.up_grad[b]), r.up_peer[b], 2 + 8 * b) for b in range(2)]
    down_half = [
        swapped(r.down_grad[b].at[units_theirs], r.down_peer[b], 3 + 8 * b) for b in range(2)
    ]
    down_back_far = remote(r.down_send, r.down_recv, r.far_sems.at[2], r.far_sems.at[3], far)
    down_back = swapped(r.down_sum.at[units_mine], r.down_sum.at[units_mine], 12)
    out_whole = swapped(r.out_mine, r.out_peer, 4)
    up_back = swapped(mine(r.up_all), mine(r.up_all), 5)
    head_half = swapped(theirs(r.head_parts), r.head_peer, 6)
    head_back = swapped(mine(r.head_all), mine(r.head_all), 7)

    loads["w_qkv"].wait()
    rows_mine = pl.ds(dp * kept, kept)
    for h in range(HEADS):
        q, k, v = (
            r.w_qkv_v[rows_mine, i * width + h * HEAD_DIM : i * width + (h + 1) * HEAD_DIM]
            for i in range(3)
        )
        r.head_send[h, 0:kept] = jnp.concatenate([q, k], 1)
        r.head_send[h, kept:packed] = jnp.concatenate([v[: kept // 2], v[kept // 2 :]], 1)
    r.head_recv[me, pl.ds(dp * packed, packed)] = r.head_send[me]
    loads["gains"].wait()
    loads["biases"].wait()
    r.norm_send[...] = jnp.zeros_like(r.norm_send)
    r.norm_send[0:4, 0:w_rows] = r.gains_v[...].astype(full)
    r.norm_send[4:8, 0:w_rows] = r.biases_v[...].astype(full)
    r.norm_recv[me] = r.norm_send[...]
    loads["tokens"].wait()
    r.big[me] = r.tokens_v[...]
    pl.semaphore_wait(barrier, size)
    tokens_in.start()
    for q in (0, 3, 1, 2):
        over(q).start()
    norm_rows.start()
    head_weights.start()

    def gain(i):
        return r.norms[i : i + 1, :]

    def bias(i):
        return r.norms[4 + i : 5 + i, :]

    loads["w_out"].wait()
    r.w_out_all[me] = r.w_out_v[...]
    loads["w_up"].wait()
    r.w_up_all[me, rows_mine] = r.w_up_v[rows_mine, columns(me, units)]
    r.w_up_far[me, rows_mine] = r.w_up_v[rows_mine, columns(far, units)]
    loads["cos"].wait()
    loads["sin"].wait()
    for name in ("w_down", "cotangent", "corpus"):
        loads[name].wait()

    def unpack_heads():
        head_other.wait_recv()
        for j in range(size // 2):
            span = pl.ds(j * 2 * w_rows, 2 * w_rows)
            qk, v = [], []
            for d in (2 * j, 2 * j + 1):
                for h in range(2):
                    p = r.head_recv[d, h * packed : (h + 1) * packed]
                    qk.append(p[:kept])
                    v += [p[kept:, :HEAD_DIM], p[kept:, HEAD_DIM:]]
            r.w_t[0 : 2 * HEAD_DIM, span] = jnp.concatenate(qk, 0).astype(full).T.astype(low)
            r.w_t[2 * HEAD_DIM :, span] = jnp.concatenate(v, 0).astype(full).T.astype(low)

    def project(ahead, shift=0):
        base = near.device(ahead, 0) + shift
        x = r.big[pl.ds(base, 2)].reshape(pair, width).astype(full)
        hat, _ = normalized(x)
        normed = (hat * gain(0) + bias(0)).astype(low)
        r.normed_all[pl.ds(base, 2)] = normed.reshape(2, rows, width)
        qkv = dot(r.w_t[...], normed, NT)
        span = pl.ds(pl.multiple_of(base * rows, pair), pair)
        c, s = r.cos_v[:, span], r.sin_v[:, span]
        for i, (ref, nat, scale) in enumerate(
            ((r.q_t, r.q_nat, HEAD_DIM**-0.5), (r.k_t, r.k_nat, 1.0))
        ):
            first = qkv[i * HEAD_DIM : i * HEAD_DIM + half]
            second = qkv[i * HEAD_DIM + half : (i + 1) * HEAD_DIM]
            turned = jnp.concatenate([first * c - second * s, first * s + second * c], 0) * scale
            ref[:, span] = turned.astype(low)
            nat[span, :] = turned.T.astype(low)
        v = qkv[2 * HEAD_DIM :]
        r.v_t[:, span] = v.astype(low)
        r.v_nat[span, :] = v.T.astype(low)

    def out_swap(ref, way, j):
        return swap(ref, ref, r.out_swap_send.at[0], r.out_swap_recv.at[way, j])

    def out_other(way, j):
        k, q = j // 2 + 1, j % 2
        q = q if way == 0 else 1 - q
        device = ring.device(-k if way == 0 else k, core)
        return r.w_out_all.at[device, pl.ds((1 - dp) * kept + q * (kept // 2), kept // 2)]

    def out_side(ref, slot):
        send, recv = r.out_side_send.at[slot], r.out_side_recv.at[slot]
        return remote(ref, ref, send, recv, ring.sibling)

    def out_own():
        return out_side(r.w_out_all.at[me, pl.ds((1 - dp) * kept, kept)], 0)

    def out_others():
        return out_side(w_outs.blocks(chips - 1), 1)

    def pass_out(j):
        w_outs.pass_on(j)
        for way in range(2):
            out_swap(w_outs.landed(way, j), way, j).start()

    def pass_other(j):
        for way in range(2):
            ref = out_other(way, j)
            out_swap(ref, way, j).wait_recv()
            out_side(ref, 1).start()

    tokens_in.pass_on(0)
    tokens_in.pass_on(1)
    over_again(0)
    tokens_in.pass_on(2)
    tokens_in.pass_on(3)
    norm_rows.wait()
    for j in range(size // 2):
        r.norms[:, j * 128 : (j + 1) * 128] = jnp.concatenate(
            [r.norm_recv[2 * j][:, :w_rows], r.norm_recv[2 * j + 1][:, :w_rows]], 1
        )
    head_weights.wait()
    head_other.start()
    over_again(3)
    for j in range(4, 6):
        tokens_in.pass_on(j)
    over_again(1)
    over_again(2)
    tokens_far.side(tokens_far.block(me), 0).start()
    w_outs.start()
    out_own().start()
    down_far.start()
    up_weights.start()
    up_weights_far.start()
    tokens_far.pass_on(0)
    tokens_far.pass_on(1)
    unpack_heads()
    for ahead in (0, 1, -1):
        tokens_in.wait_chip(ahead)
        project(ahead)
    tokens_far.pass_on(2)
    tokens_far.pass_on(3)
    pass_out(0)
    pass_out(1)
    tokens_in.wait_chip(2)
    project(2)
    for ahead in (0, 1, -1):
        tokens_far.wait_chip(ahead)
        project(ahead, other - near.base)
    for j in range(4, 6):
        tokens_far.pass_on(j)
    tokens_far.wait_chip(2)
    project(2, other - near.base)
    tokens_in.finish()
    tokens_far.finish()
    for q in range(4):
        over(q).wait_send()
    pass_out(2)
    pass_out(3)
    pass_other(0)
    pass_other(1)

    for t in range(tiles):
        span = pl.ds(t * TILE, TILE)
        query = r.q_t[:, span]
        top = None
        for j in range(t + 1):
            keys = pl.ds(j * TILE, TILE)
            s = dot(r.k_nat[keys, :], query)
            if j == t:
                s = jnp.where(causal(s.shape), s, -1e30)
            r.scores[keys, :] = s
            here = jnp.max(s, 0, keepdims=True)
            top = here if top is None else jnp.maximum(top, here)
        acc, norm = None, None
        for j in range(t + 1):
            keys = pl.ds(j * TILE, TILE)
            p = jnp.exp(r.scores[keys, :] - top)
            here = jnp.sum(p, 0, keepdims=True)
            add = dot(r.v_t[:, keys], p.astype(low))
            acc = add if acc is None else acc + add
            norm = here if norm is None else norm + here
        acc = acc / norm
        r.total[:, span] = acc
        r.lse[:, span] = top + jnp.log(norm)
        for b in range(TILE // rows):
            to = t * (TILE // rows) + b
            block = acc[:, b * rows : (b + 1) * rows].astype(low)
            r.att_send[to] = block

            @pl.when(me != to)
            def _(to=to):
                remote(
                    r.att_send.at[to], r.att_t.at[me], r.att_ssem.at[0], r.att_rsem.at[0], to
                ).start()

            @pl.when(me == to)
            def _(block=block):
                r.att_t[me] = block

        if t == 4:
            pass_out(4)
            pass_out(5)
            up_weights.wait()
            up_other.start()
            pass_other(2)
            pass_other(3)
        if t == 6:
            pass_out(6)
            up_weights_far.wait()
            up_other_far.start()
            pass_other(4)
            pass_other(5)
    pass_other(6)
    for ahead in range(chips):
        w_outs.wait_chip(ahead)
    out_own().wait_recv()
    out_others().wait_recv()
    attended = r.att_t.at[pl.ds(0, size - 1)]
    attended = remote(attended, attended, r.att_ssem.at[0], r.att_rsem.at[0], ring.right)
    down_far.wait_recv()
    down_other_far.start()
    attended.wait()

    att_t = r.att_t[...].reshape(width, rows)
    w_out_all = r.w_out_all
    proj = dot(att_t, w_out_all[...].reshape(width, width), TN)
    r.proj[...] = proj
    hat1, _ = normalized(proj)
    hidden = r.tokens_v[...].astype(full) + hat1 * gain(1) + bias(1)
    r.hidden[...] = hidden
    hat2, _ = normalized(hidden)
    r.big[mid_place] = (hat2 * gain(2) + bias(2)).astype(low)
    mids.start()
    w_outs.finish()

    def weights(b):
        up, down = ((r.w_up_all, r.w_down_v), (r.w_up_far, r.w_down_far))[b]
        return up[...].reshape(width, units), down[...]

    def forward(ahead):
        place = pl.ds(near.device(ahead, 0) - near.base, 2)
        x = r.big[place].reshape(pair, width)
        part = None
        for b in range(2):
            w_up, w_down = weights(b)
            act, slope = gelu_and_slope(dot(x, w_up))
            act = act.astype(low)
            r.act_all[b, place] = act.reshape(2, rows, units)
            r.slope_all[b, place] = slope.reshape(2, rows, units)
            add = dot(act, w_down)
            part = add if part is None else part + add
        r.parts[place] = part.astype(low).reshape(2, rows, width)
        sum_down.across(ahead).start()

    def backward(ahead):
        place = pl.ds(near.device(ahead, 0) - near.base, 2)
        x = r.big[pl.ds(near.device(ahead, 0) - near.base + close, 2)].reshape(pair, width)
        part = None
        for b in range(2):
            w_up, w_down = weights(b)
            d_act = dot(x, w_down, NT)
            d_up = (d_act * r.slope_all[b, place].reshape(pair, units)).astype(low)
            r.d_up_all[b, place] = d_up.reshape(2, rows, units)
            add = dot(d_up, w_up, NT)
            part = add if part is None else part + add
        r.parts[place] = part.astype(low).reshape(2, rows, width)
        sum_mid.across(ahead).start()

    def there_and_back(gather, scatter, ready, work, fill):
        last = near.steps
        for k in range(1, last + 1):
            if k == last:
                ready()
                gather.wait_chip(0)
                work(0)
                for ahead in range(1, last):
                    for chip in (ahead, -ahead):
                        gather.wait_chip(chip)
                        work(chip)
                scatter.step(2)
                scatter.step(3)
            for j in range(4 * (k - 1), min(4 * k, gather.messages)):
                gather.pass_on(j)
        gather.wait_chip(last)
        work(last)
        scatter.step(0)
        scatter.step(1)
        for j in range(4, scatter.messages):
            fill(j)
            scatter.step(j)
        fill(scatter.messages)

    def weights_here():
        up_other.wait_recv()
        up_other_far.wait_recv()
        down_other_far.wait_recv()

    there_and_back(mids, sum_down, weights_here, forward, lambda j: None)

    weight_row = jnp.zeros((1, rows), full)
    for c in range(r.weight.shape[0]):
        weight_row += jnp.where(r.corpus_v[...] == c, r.weight[c], 0.0)
    row_weight = jnp.broadcast_to(weight_row, (rows, rows)).T[:, 0:1]
    for q in range(4):
        span = pl.ds(q * quarter, quarter)
        down = sum_down.result(q)
        hat3, scale3 = normalized(down)
        r.output_v[span, :] = (r.hidden[span, :] + hat3 * gain(3) + bias(3)).astype(low)
        grad_y = r.cotangent_v[span, :].astype(full) * row_weight[q * quarter : (q + 1) * quarter]
        r.d_hidden[span, :] = grad_y
        r.big[dd_place, span] = norm_back(grad_y, hat3, scale3, gain(3)).astype(low)
        g3 = jnp.sum(grad_y * hat3, 0, keepdims=True)
        b3 = jnp.sum(grad_y, 0, keepdims=True)
        r.norm_grads[3:4, :] = g3 if q == 0 else r.norm_grads[3:4, :] + g3
        r.norm_grads[7:8, :] = b3 if q == 0 else r.norm_grads[7:8, :] + b3
    mids.finish()
    sum_down.finish()
    d_downs.start()
    saves = {}

    def save(name):
        i = OUTPUTS.index(name)
        saves[name] = pltpu.make_async_copy(
            getattr(r, name + "_v"), getattr(r, name), r.save_sem.at[i]
        )
        saves[name].start()

    save("output")

    def up_gradient(b):
        d_up = r.d_up_all[b].reshape(near_length, units)
        blocks = size // 4
        for i in range(4):
            span = pl.ds(i * (width // 4), width // 4)
            x = r.big[:close, :, span].reshape(near_length, width // 4)
            grad = dot(d_up, x, TN).T.astype(low)
            r.up_grad[b][i * blocks : (i + 1) * blocks] = grad.reshape(blocks, w_rows, units)
        up_half[b].start()

    def down_gradient(b):
        act = r.act_all[b].reshape(near_length, units)
        for i in range(4):
            span = pl.ds(i * (width // 4), width // 4)
            dd = r.big[close:, :, span].reshape(near_length, width // 4)
            r.down_grad[b][:, span] = dot(act, dd, TN).astype(low)
        down_half[b].start()

    def fill(j):
        if j < 6:
            up_gradient(j - 4)

    there_and_back(d_downs, sum_mid, lambda: None, backward, fill)

    hat1, scale1 = normalized(r.proj[...])
    hat2, scale2 = normalized(r.hidden[...])
    hat0, scale0 = normalized(r.tokens_v[...].astype(full))
    r.hat0[...] = hat0
    d_mid = sum_mid.whole()
    r.norm_grads[2:3, :] = jnp.sum(d_mid * hat2, 0, keepdims=True)
    r.norm_grads[6:7, :] = jnp.sum(d_mid, 0, keepdims=True)
    d_hidden = r.d_hidden[...] + norm_back(d_mid, hat2, scale2, gain(2))
    r.d_hidden[...] = d_hidden
    r.norm_grads[1:2, :] = jnp.sum(d_hidden * hat1, 0, keepdims=True)
    r.norm_grads[5:6, :] = jnp.sum(d_hidden, 0, keepdims=True)
    d_proj = norm_back(d_hidden, hat1, scale1, gain(1)).astype(low)
    d_att = dot(w_out_all[...].reshape(width, width), d_proj, NT).astype(low)
    r.d_att[...] = d_att.reshape(HEADS, HEAD_DIM, rows)
    d_atts.start()

    out = dot(att_t, d_proj).astype(low).reshape(size, w_rows, width)
    r.out_parts[:, :w_rows] = out[:close]
    r.out_parts[:, w_rows:] = out[close:]
    for ahead in range(near.chips):
        sum_out.across(ahead).start()
    r.att_recv[me] = r.d_att[me]
    d_downs.finish()
    sum_mid.finish()
    r.dq[...] = jnp.zeros_like(r.dq)
    for b in range(2):
        down_gradient(b)
    for b in range(2):
        up_half[b].wait_recv()
        up_mine = r.up_grad[b][:, rows_mine].astype(full)
        r.up_send[b][...] = (up_mine + r.up_peer[b][...].astype(full)).astype(low)
        r.up_recv[b][me] = r.up_send[b][me]
    up_grads.start()
    up_grads_far.start()
    for j in range(4):
        sum_out.step(j)
    d_atts.wait()
    for b in range(size):
        r.do_t[:, b * rows : (b + 1) * rows] = r.att_recv[b]
    for t in range(tiles):
        span = pl.ds(t * TILE, TILE)
        do = r.do_t[:, span].astype(full)
        r.do_nat[span, :] = do.T.astype(low)
        r.delta[:, span] = jnp.sum(do * r.total[:, span], 0, keepdims=True)

    def turned_back(u, span, base):
        c, s = r.cos_v[:, span], r.sin_v[:, span]
        first, second = u[:half], u[half:]
        r.d_t[base : base + half, span] = (first * c + second * s).astype(low)
        r.d_t[base + half : base + 2 * half, span] = (second * c - first * s).astype(low)

    high = near.base // close
    out_own_rows, out_far_rows = pl.ds(high * w_rows, w_rows), pl.ds((1 - high) * w_rows, w_rows)

    def beside_attention(j):
        if j in (0, 1):
            sum_out.step(4 + j)
        if j == 1:
            for b in range(2):
                down_half[b].wait_recv()
            down_mine = r.down_grad[1][units_mine].astype(full)
            r.down_send[...] = (down_mine + r.down_peer[1][...].astype(full)).astype(low)
            down_back_far.start()
        if j == 3:
            r.out_sum[...] = sum_out.whole()
            r.out_send[...] = r.out_sum[out_far_rows].astype(low)
            out_over.start()

    def collect_up():
        up_grads.wait()
        up_grads_far.wait()
        for h in range(size):
            both = r.up_recv[0][h].astype(full) + r.up_recv[1][(h + close) % size].astype(full)
            r.up_all[h, rows_mine] = both.astype(low)
        up_back.start()

    def collect_out():
        out_over.wait_recv()
        r.out_mine[...] = (r.out_sum[out_own_rows] + r.out_recv[...].astype(full)).astype(low)
        out_whole.start()

    def collect_down():
        down_back_far.wait_recv()
        both = r.down_grad[0][units_mine].astype(full) + r.down_peer[0][...].astype(full)
        r.down_sum[units_mine] = (both + r.down_recv[...].astype(full)).astype(low)
        down_back.start()

    for j in range(tiles):
        keys = pl.ds(j * TILE, TILE)
        dk, dv = None, None
        for t in range(j, tiles):
            span = pl.ds(t * TILE, TILE)
            s = dot(r.k_nat[keys, :], r.q_t[:, span])
            p = jnp.exp(s - r.lse[:, span])
            if j == t:
                p = jnp.where(causal(p.shape), p, 0.0)
            d_p = dot(r.v_nat[keys, :], r.do_t[:, span])
            d_s = (p * (d_p - r.delta[:, span])).astype(low)
            dv_add = dot(p.astype(low), r.do_nat[span, :])
            dk_add = dot(d_s, r.q_nat[span, :])
            dv = dv_add if dv is None else dv + dv_add
            dk = dk_add if dk is None else dk + dk_add
            r.dq[:, span] += dot(r.k_t[:, keys], d_s)
        turned_back(dk.T, keys, HEAD_DIM)
        r.d_t[2 * HEAD_DIM :, keys] = dv.T.astype(low)
        turned_back(r.dq[:, keys] * HEAD_DIM**-0.5, keys, 0)
        beside_attention(j)

    def part(ahead):
        base = ring.device(ahead, 0)
        span = pl.ds(pl.multiple_of(base * rows, pair), pair)
        d_x = dot(r.d_t[:, span], r.w_t[...], TN).astype(low)
        r.parts[pl.ds(base, 2)] = d_x.reshape(2, rows, width)
        sum_in.across(ahead).start()

    def head_gradient(j):
        x = r.normed_all[:, :, j * 128 : (j + 1) * 128].reshape(length, 128)
        d_w = dot(r.d_t[...], x).T
        for i in range(2):
            for h in range(2):
                base = i * w_rows + h * kept
                block = d_w[base : base + kept]
                v = block[:, 2 * HEAD_DIM :]
                v = jnp.concatenate([v[: kept // 2], v[kept // 2 :]], 1)
                at = h * packed
                r.head_parts[2 * j + i, at : at + kept] = block[:, : 2 * HEAD_DIM].astype(low)
                r.head_parts[2 * j + i, at + kept : at + packed] = v.astype(low)

    part(steps)
    part(steps - 1)
    part(1 - steps)
    for j in range(4):
        sum_in.step(j)
    for k in range(steps - 2, 0, -1):
        part(k)
        part(-k)
    part(0)
    sum_in.step(4)
    sum_in.step(5)
    for j in range(size // 2):
        head_gradient(j)
    head_weights.finish()
    head_half.start()
    for j in range(6, 8):
        sum_in.step(j)
    collect_up()
    collect_out()
    for j in range(8, 10):
        sum_in.step(j)
    head_half.wait_recv()
    own_half = r.head_parts[:, pl.ds(dp * packed, packed)].astype(full)
    r.head_send[...] = (own_half + r.head_peer[...].astype(full)).astype(low)
    r.head_all[me, pl.ds(dp * packed, packed)] = r.head_send[me]
    head_grads.start()
    for j in range(10, 12):
        sum_in.step(j)
    collect_down()
    for j in range(12, 14):
        sum_in.step(j)
    out_whole.wait_recv()
    r.grad_out_v[...] = r.out_mine[...].astype(full) + r.out_peer[...].astype(full)
    save("grad_out")
    d_normed = sum_in.whole()
    up_back.wait_recv()
    for h in range(size):
        r.grad_up_v[:, h * units : (h + 1) * units] = r.up_all[h].astype(full)
    save("grad_up")
    down_back.wait_recv()
    r.grad_down_v[...] = r.down_sum[...].astype(full)
    save("grad_down")
    head_grads.wait()
    head_back.start()

    hat0 = r.hat0[...]
    r.norm_grads[0:1, :] = jnp.sum(d_normed * hat0, 0, keepdims=True)
    r.norm_grads[4:5, :] = jnp.sum(d_normed, 0, keepdims=True)

    def norm_copy(i, other):
        to = (me + i) % size
        return pltpu.make_async_remote_copy(
            src_ref=r.norm_grads.at[:, columns(to // 2, 128)],
            dst_ref=r.norm_sums.at[2 * i + other],
            send_sem=r.norm_ssem.at[0],
            recv_sem=r.norm_rsem.at[0],
            device_id={"seq": to, "dp": (dp + other) % 2},
            device_id_type=MESH,
        )

    partners = [(i, other) for i in range(size) for other in range(2) if i or other]
    for i, other in partners:
        norm_copy(i, other).start()
    r.norm_sums[0] = r.norm_grads[:, columns(me // 2, 128)]
    _, scale0 = normalized(r.tokens_v[...].astype(full))
    r.grad_tokens_v[...] = r.d_hidden[...] + norm_back(d_normed, hat0, scale0, gain(0))
    save("grad_tokens")
    head_back.wait_recv()
    for h in range(2):
        for j in range(size // 2):
            blocks = [
                r.head_all[2 * j + i, h * packed : (h + 1) * packed].astype(full) for i in range(2)
            ]
            span = slice(h * kept, (h + 1) * kept)
            for b in range(2):
                place = slice(b * width + j * 128, b * width + (j + 1) * 128)
                r.grad_qkv_v[span, place] = jnp.concatenate(
                    [p[:kept, b * HEAD_DIM : (b + 1) * HEAD_DIM] for p in blocks], 1
                )
            v = [jnp.concatenate([p[kept:, :HEAD_DIM], p[kept:, HEAD_DIM:]], 0) for p in blocks]
            place = slice(2 * width + j * 128, 2 * width + (j + 1) * 128)
            r.grad_qkv_v[span, place] = jnp.concatenate(v, 1)
    save("grad_qkv")
    norm_all = r.norm_sums.at[pl.ds(1, 2 * size - 1)]
    norm_all = swap(norm_all, norm_all, r.norm_ssem.at[0], r.norm_rsem.at[0])
    norm_all.wait_recv()
    sums = jnp.sum(r.norm_sums[...], 0)
    sums = jnp.where(core == 0, sums[:, :w_rows], sums[:, w_rows:])
    r.grad_gains_v[...] = sums[0:4]
    r.grad_biases_v[...] = sums[4:8]
    save("grad_gains")
    save("grad_biases")

    norm_all.wait_send()
    sum_in.finish()
    sum_out.finish()
    for moved in (
        norm_rows, up_weights, up_weights_far, d_atts, up_grads, up_grads_far, head_grads
    ):
        moved.finish()
    for copy in (
        head_other,
        up_other,
        up_other_far,
        down_far,
        down_other_far,
        *up_half,
        *down_half,
        down_back_far,
        down_back,
        out_over,
        out_whole,
        up_back,
        head_half,
        head_back,
    ):
        copy.wait_send()
    out_own().wait_send()
    out_others().wait_send()
    out_swap(w_outs.blocks(chips - 1), 0, 0).wait_send()
    for copy in saves.values():
        copy.wait()


def hand_over_kernel(count, *refs):
    ins, outs, held = (refs[i * count : (i + 1) * count] for i in range(3))
    sems = refs[-1]
    loads = [pltpu.make_async_copy(ins[i], held[i], sems.at[0, i]) for i in range(count)]
    saves = [pltpu.make_async_copy(held[i], outs[i], sems.at[1, i]) for i in range(count)]
    for copy in loads:
        copy.start()
    for load, copy in zip(loads, saves):
        load.wait()
        copy.start()
    for copy in saves:
        copy.wait()


def hand_over(arrays):
    count = len(arrays)
    return pl.pallas_call(
        functools.partial(hand_over_kernel, count),
        out_shape=[jax.ShapeDtypeStruct(a.shape, a.dtype) for a in arrays],
        in_specs=[ANY] * count,
        out_specs=[ANY] * count,
        scratch_shapes=[pltpu.VMEM(a.shape, a.dtype) for a in arrays] + [DMA((2, count))],
    )(*arrays)


def split_heads(
    tokens, w_qkv, w_out, w_up, w_down, norm_gains, norm_biases, corpus_id, corpus_weight, cotangent
):
    size = lax.axis_size("seq")
    chips = size // 2
    _, rows, width = tokens.shape
    w_rows = w_out.shape[0]
    units = w_down.shape[0]
    length = rows * size
    shape = jax.ShapeDtypeStruct
    cos, sin = turn_tables(length)
    inputs = dict(
        tokens=tokens[0],
        w_qkv=w_qkv,
        w_out=w_out,
        w_up=w_up,
        w_down=w_down,
        gains=norm_gains,
        biases=norm_biases,
        corpus=corpus_id,
        cotangent=cotangent[0],
        cos=cos,
        sin=sin,
    )
    outputs = dict(
        output=shape((rows, width), low),
        grad_tokens=shape((rows, width), full),
        grad_qkv=shape((w_rows, 3 * width), full),
        grad_out=shape((w_rows, width), full),
        grad_up=shape((w_rows, size * units), full),
        grad_down=shape((units, width), full),
        grad_gains=shape((4, w_rows), full),
        grad_biases=shape((4, w_rows), full),
    )

    def vmem(*dims, kind=low):
        return pltpu.VMEM(dims, kind)

    head_rows = 3 * w_rows // 2
    blocks = vmem(size, rows, width)
    nat, turned = vmem(length, HEAD_DIM), vmem(HEAD_DIM, length)
    side, inbox, outbox = Scatter.buffers(chips, rows, width, 4)
    side, inbox, outbox = Scatter.buffers(chips // 2, rows, width, 4)
    in_side, in_inbox, in_outbox = Scatter.buffers(chips, rows, width, 4)
    scratch = {name + "_v": vmem(*a.shape, kind=a.dtype) for name, a in inputs.items()}
    scratch |= {name + "_v": vmem(*a.shape, kind=a.dtype) for name, a in outputs.items()}
    scratch |= dict(
        big=blocks,
        normed_all=blocks,
        parts=blocks,
        side=[side] * 2,
        inbox=[inbox] * 2,
        outbox=[outbox] * 2,
        in_side=in_side,
        in_inbox=in_inbox,
        in_outbox=in_outbox,
        out_parts=vmem(size // 2, 2 * w_rows, width),
        out_sum=vmem(2 * w_rows, width, kind=full),
        out_send=vmem(w_rows, width),
        out_recv=vmem(w_rows, width),
        out_mine=vmem(w_rows, width),
        out_peer=vmem(w_rows, width),
        w_out_all=vmem(size, w_rows, width),
        w_up_all=vmem(size, w_rows, units),
        w_up_far=vmem(size, w_rows, units),
        w_down_far=vmem(units, width),
        w_t=vmem(3 * HEAD_DIM, width),
        head_send=vmem(size, head_rows // 2, 128),
        head_recv=vmem(size, head_rows, 128),
        head_parts=vmem(size, head_rows, 128),
        head_peer=vmem(size, head_rows // 2, 128),
        head_all=vmem(size, head_rows, 128),
        norm_send=vmem(8, 128, kind=full),
        norm_recv=vmem(size, 8, 128, kind=full),
        norms=vmem(8, width, kind=full),
        norm_grads=vmem(8, width, kind=full),
        norm_sums=vmem(2 * size, 8, 128, kind=full),
        q_t=turned,
        k_t=turned,
        v_t=turned,
        do_t=turned,
        q_nat=nat,
        k_nat=nat,
        v_nat=nat,
        do_nat=nat,
        total=vmem(HEAD_DIM, length, kind=full),
        dq=vmem(HEAD_DIM, length, kind=full),
        d_t=vmem(3 * HEAD_DIM, length),
        lse=vmem(1, length, kind=full),
        delta=vmem(1, length, kind=full),
        scores=vmem(length, TILE, kind=full),
        att_send=vmem(size, HEAD_DIM, rows),
        att_t=vmem(size, HEAD_DIM, rows),
        d_att=vmem(size, HEAD_DIM, rows),
        att_recv=vmem(size, HEAD_DIM, rows),
        proj=vmem(rows, width, kind=full),
        hidden=vmem(rows, width, kind=full),
        d_hidden=vmem(rows, width, kind=full),
        hat0=vmem(rows, width, kind=full),
        act_all=vmem(2, size // 2, rows, units),
        slope_all=vmem(2, size // 2, rows, units, kind=full),
        d_up_all=vmem(2, size // 2, rows, units),
        up_grad=[vmem(size, w_rows, units)] * 2,
        up_peer=[vmem(size, w_rows // 2, units)] * 2,
        up_send=[vmem(size, w_rows // 2, units)] * 2,
        up_recv=[vmem(size, w_rows // 2, units)] * 2,
        up_all=vmem(size, w_rows, units),
        down_grad=[vmem(units, width)] * 2,
        down_peer=[vmem(units // 2, width)] * 2,
        down_send=vmem(units // 2, width),
        down_recv=vmem(units // 2, width),
        down_sum=vmem(units, width),
        far_sems=DMA((10,)),
        over_send=DMA((4,)),
        over_recv=DMA((4,)),
        load_sem=DMA((len(inputs),)),
        save_sem=DMA((len(outputs),)),
        swap_send=DMA((13,)),
        swap_recv=DMA((13,)),
        out_side_send=DMA((2,)),
        out_side_recv=DMA((2,)),
        out_swap_send=DMA((1,)),
        out_swap_recv=DMA((2, Gather.count(chips, 2))),
        att_ssem=DMA((1,)),
        att_rsem=DMA((1,)),
        norm_ssem=DMA((1,)),
        norm_rsem=DMA((1,)),
    )
    for i, (count, pieces) in enumerate(((chips // 2, 4), (chips, 2), (chips // 2, 4))):
        scratch[f"gather{i}"] = Gather.sems(count, pieces)
    for i in range(3):
        scratch[f"scatter{i}"] = Scatter.sems(chips if i == 2 else chips // 2, 4)
    for i in range(8):
        scratch[f"exchange{i}"] = [DMA((1,)), DMA((1,))]
    flat, groups = [], []
    for name, entry in scratch.items():
        entries = entry if isinstance(entry, list) else [entry]
        groups.append((name, len(entries) if isinstance(entry, list) else 0))
        flat += entries

    def kernel(*refs):
        count = len(inputs) + 1 + len(outputs)
        names = [*inputs, "weight", *outputs]
        values = list(refs[:count])
        rest = list(refs[count:])
        for name, many in groups:
            names.append(name)
            if many:
                values.append(tuple(rest[:many]))
                rest = rest[many:]
            else:
                values.append(rest.pop(0))
        layer_kernel(names, *values)

    results = pl.pallas_call(
        kernel,
        out_shape=list(outputs.values()),
        in_specs=[ANY] * len(inputs) + [pl.BlockSpec(memory_space=pltpu.SMEM)],
        out_specs=[ANY] * len(outputs),
        scratch_shapes=flat,
        compiler_params=pltpu.CompilerParams(
            collective_id=1, has_side_effects=True, vmem_limit_bytes=61 * 2**20
        ),
    )(*inputs.values(), corpus_weight)
    results = hand_over(results)
    return (results[0][None], results[1][None], *results[2:])


def shifted(x, axis, by):
    size = lax.axis_size(axis)
    return lax.ppermute(x, axis, [(i, (i + by) % size) for i in range(size)])


def passed_along(value, axis, steps):
    count = lax.axis_size(axis)
    first, last = (max(0, -steps), min(count, count - steps))
    return lax.ppermute(value, axis, [(source, source + steps) for source in range(first, last)])


def layer_norm(values, gain, bias):
    center = values - jnp.mean(values, -1, keepdims=True)
    variance = jnp.mean(center * center, -1, keepdims=True)
    return center * lax.rsqrt(variance + 1e-05) * gain + bias


def rotate(values, position, direction):
    half_size = values.shape[-1] // 2
    freq = jnp.exp(
        jnp.arange(half_size).astype(jnp.float32) * (-2.0 * math.log(10000.0) / values.shape[-1])
    )
    angle = position[:, None] * freq[None, :]
    cosine = jnp.cos(angle)[:, None, :]
    sine = direction * jnp.sin(angle)[:, None, :]
    first = values[..., :half_size]
    second = values[..., half_size:]
    return jnp.concatenate([first * cosine - second * sine, first * sine + second * cosine], -1)


def gelu_tanh(values):
    return jax.nn.gelu(values, approximate=True)


def per_device(
    tokens, w_qkv, w_out, w_up, w_down, norm_gains, norm_biases, corpus_id, corpus_weight, cotangent
):
    full_qkv, full_out, full_up, full_down, gains_low, biases_low = (
        lax.all_gather(w_qkv, "seq", axis=0, tiled=True),
        lax.all_gather(w_out, "seq", axis=0, tiled=True),
        lax.all_gather(w_up, "seq", axis=0, tiled=True),
        lax.all_gather(w_down, "seq", axis=0, tiled=True),
        lax.all_gather(norm_gains, "seq", axis=1, tiled=True),
        lax.all_gather(norm_biases, "seq", axis=1, tiled=True),
    )
    gains = gains_low.astype(jnp.float32)
    biases = biases_low.astype(jnp.float32)
    seq_count, row_count, model_width = tokens.shape
    shape_heads = (seq_count, row_count, HEADS, HEAD_DIM)
    scale = HEAD_DIM ** (-0.5)
    cycle_size = lax.axis_size("seq")
    cycle_index = lax.axis_index("seq")
    query_pos = cycle_index * row_count + jnp.arange(row_count)
    position = query_pos.astype(jnp.float32)
    x_float = tokens.astype(jnp.float32)
    normed_low = layer_norm(x_float, gains[0], biases[0]).astype(jnp.bfloat16)
    qkv = jnp.einsum("std,de->ste", normed_low, full_qkv, preferred_element_type=jnp.float32)
    query_low = rotate(qkv[..., :model_width].reshape(shape_heads), position, 1.0).astype(
        jnp.bfloat16
    )
    key_low = rotate(
        qkv[..., model_width : 2 * model_width].reshape(shape_heads), position, 1.0
    ).astype(jnp.bfloat16)
    value_low = qkv[..., 2 * model_width :].reshape(shape_heads).astype(jnp.bfloat16)

    def block_scores(key_piece, key_pos):
        scores = (
            jnp.einsum("sqhd,skhd->shqk", query_low, key_piece, preferred_element_type=jnp.float32)
            * scale
        )
        allowed = query_pos[:, None] >= key_pos[None, :]
        return (scores, allowed)

    stat_shape = (seq_count, HEADS, row_count)
    key_piece = lax.all_gather(key_low, "seq", axis=1, tiled=True)
    value_piece = lax.all_gather(value_low, "seq", axis=1, tiled=True)
    key_pos = jnp.arange(key_piece.shape[1])
    run_max = jnp.full(stat_shape, -1e30, jnp.float32)
    scores, allowed = block_scores(key_piece, key_pos)
    new_max = jnp.maximum(run_max, jnp.max(jnp.where(allowed, scores, -1e30), -1))
    weights = jnp.where(allowed, jnp.exp(scores - new_max[..., None]), 0.0)
    run_sum = jnp.sum(weights, -1)
    total = jnp.einsum(
        "shqk,skhd->sqhd",
        weights.astype(jnp.bfloat16),
        value_piece,
        preferred_element_type=jnp.float32,
    )
    run_max, run_sum, total = (new_max, run_sum, total)
    log_sum = run_max + jnp.log(run_sum)
    attended = total / jnp.transpose(run_sum, (0, 2, 1))[..., None]
    attended_low = attended.reshape(seq_count, row_count, model_width).astype(jnp.bfloat16)
    proj = jnp.einsum("std,de->ste", attended_low, full_out, preferred_element_type=jnp.float32)
    hidden = x_float + layer_norm(proj, gains[1], biases[1])
    mid_low = layer_norm(hidden, gains[2], biases[2]).astype(jnp.bfloat16)
    up_proj = jnp.einsum("std,df->stf", mid_low, full_up, preferred_element_type=jnp.float32)
    act_low = gelu_tanh(up_proj).astype(jnp.bfloat16)
    down = jnp.einsum("stf,fd->std", act_low, full_down, preferred_element_type=jnp.float32)
    output = (hidden + layer_norm(down, gains[3], biases[3])).astype(jnp.bfloat16)
    matches = (corpus_id[..., None] == jnp.arange(corpus_weight.shape[0])).astype(jnp.float32)
    row_weight = jnp.sum(matches * corpus_weight, -1)
    grad_y = cotangent.astype(jnp.float32) * row_weight[..., None]
    _, down_back = jax.vjp(layer_norm, down, gains[3], biases[3])
    d_down, gain_three, bias_three = down_back(grad_y)
    d_down_low = d_down.astype(jnp.bfloat16)
    grad_down = jnp.einsum("stf,std->fd", act_low, d_down_low, preferred_element_type=jnp.float32)
    d_act = jnp.einsum("std,fd->stf", d_down_low, full_down, preferred_element_type=jnp.float32)
    _, gelu_back = jax.vjp(gelu_tanh, up_proj)
    d_up_low = gelu_back(d_act)[0].astype(jnp.bfloat16)
    grad_up = jnp.einsum("std,stf->df", mid_low, d_up_low, preferred_element_type=jnp.float32)
    d_mid = jnp.einsum("stf,df->std", d_up_low, full_up, preferred_element_type=jnp.float32)
    _, mid_back = jax.vjp(layer_norm, hidden, gains[2], biases[2])
    d_hidden_mid, gain_two, bias_two = mid_back(d_mid)
    d_hidden = grad_y + d_hidden_mid
    _, proj_back = jax.vjp(layer_norm, proj, gains[1], biases[1])
    d_proj, gain_one, bias_one = proj_back(d_hidden)
    d_proj_low = d_proj.astype(jnp.bfloat16)
    grad_out = jnp.einsum(
        "std,ste->de", attended_low, d_proj_low, preferred_element_type=jnp.float32
    )
    d_att_low = (
        jnp.einsum("ste,de->std", d_proj_low, full_out, preferred_element_type=jnp.float32)
        .astype(jnp.bfloat16)
        .reshape(shape_heads)
    )
    delta = jnp.transpose(jnp.sum(d_att_low.astype(jnp.float32) * attended, -1), (0, 2, 1))

    def contribute(d_query, key_piece, value_piece, d_key, d_value, owner):
        key_pos = owner * row_count + jnp.arange(row_count)
        query_sum = d_query
        key_sum = d_key
        value_sum = d_value
        scores, allowed = block_scores(key_piece, key_pos)
        probs = jnp.where(allowed, jnp.exp(scores - log_sum[..., None]), 0.0)
        value_sum = value_sum + jnp.einsum(
            "shqk,sqhd->skhd",
            probs.astype(jnp.bfloat16),
            d_att_low,
            preferred_element_type=jnp.float32,
        )
        d_probs = jnp.einsum(
            "sqhd,skhd->shqk", d_att_low, value_piece, preferred_element_type=jnp.float32
        )
        d_scores = (probs * (d_probs - delta[..., None]) * scale).astype(jnp.bfloat16)
        query_sum = query_sum + jnp.einsum(
            "shqk,skhd->sqhd", d_scores, key_piece, preferred_element_type=jnp.float32
        )
        key_sum = key_sum + jnp.einsum(
            "shqk,sqhd->skhd", d_scores, query_low, preferred_element_type=jnp.float32
        )
        return (query_sum, key_sum, value_sum)

    zeros_heads = jnp.zeros(shape_heads, jnp.float32)

    def pass_grads(d_key, d_value):
        return (
            shifted(d_key.astype(jnp.bfloat16), "seq", 1).astype(d_key.dtype),
            shifted(d_value.astype(jnp.bfloat16), "seq", 1).astype(d_value.dtype),
        )

    def cycle_turn(turn_index, state):
        d_query, key_piece, value_piece, d_key, d_value = state
        owner = (cycle_index - turn_index) % cycle_size
        d_query, d_key, d_value = contribute(d_query, key_piece, value_piece, d_key, d_value, owner)
        d_key, d_value = pass_grads(d_key, d_value)
        key_piece, value_piece = passed_along((key_piece, value_piece), "seq", 1)
        return (d_query, key_piece, value_piece, d_key, d_value)

    d_query, key_piece, value_piece, d_key, d_value = lax.fori_loop(
        0, cycle_size - 1, cycle_turn, (zeros_heads, key_low, value_low, zeros_heads, zeros_heads)
    )
    last_owner = (cycle_index + 1) % cycle_size
    d_query, d_key, d_value = contribute(
        d_query, key_piece, value_piece, d_key, d_value, last_owner
    )
    d_key, d_value = pass_grads(d_key, d_value)
    flat_shape = (seq_count, row_count, model_width)
    d_qkv_low = jnp.concatenate(
        [
            rotate(d_query, position, -1.0).reshape(flat_shape),
            rotate(d_key, position, -1.0).reshape(flat_shape),
            d_value.reshape(flat_shape),
        ],
        -1,
    ).astype(jnp.bfloat16)
    grad_qkv = jnp.einsum("std,ste->de", normed_low, d_qkv_low, preferred_element_type=jnp.float32)
    d_normed = jnp.einsum("ste,de->std", d_qkv_low, full_qkv, preferred_element_type=jnp.float32)
    _, input_back = jax.vjp(layer_norm, x_float, gains[0], biases[0])
    d_input, gain_zero, bias_zero = input_back(d_normed)
    grad_tokens = d_hidden + d_input
    grad_gains = jnp.stack([gain_zero, gain_one, gain_two, gain_three])
    grad_biases = jnp.stack([bias_zero, bias_one, bias_two, bias_three])
    all_grads = (grad_qkv, grad_out, grad_up, grad_down, grad_gains, grad_biases)
    pieces = (
        lax.psum_scatter(
            all_grads[0].astype(jnp.bfloat16), "seq", scatter_dimension=0, tiled=True
        ).astype(jnp.float32),
        lax.psum_scatter(
            all_grads[1].astype(jnp.bfloat16), "seq", scatter_dimension=0, tiled=True
        ).astype(jnp.float32),
        lax.psum_scatter(
            all_grads[2].astype(jnp.bfloat16), "seq", scatter_dimension=0, tiled=True
        ).astype(jnp.float32),
        lax.psum_scatter(
            all_grads[3].astype(jnp.bfloat16), "seq", scatter_dimension=0, tiled=True
        ).astype(jnp.float32),
        lax.psum_scatter(
            all_grads[4].astype(jnp.bfloat16), "seq", scatter_dimension=1, tiled=True
        ).astype(jnp.float32),
        lax.psum_scatter(
            all_grads[5].astype(jnp.bfloat16), "seq", scatter_dimension=1, tiled=True
        ).astype(jnp.float32),
    )
    shards = (
        lax.psum(pieces[0].astype(jnp.bfloat16), "dp").astype(jnp.float32),
        lax.psum(pieces[1].astype(jnp.bfloat16), "dp").astype(jnp.float32),
        lax.psum(pieces[2].astype(jnp.bfloat16), "dp").astype(jnp.float32),
        lax.psum(pieces[3].astype(jnp.bfloat16), "dp").astype(jnp.float32),
        lax.psum(pieces[4].astype(jnp.bfloat16), "dp").astype(jnp.float32),
        lax.psum(pieces[5].astype(jnp.bfloat16), "dp").astype(jnp.float32),
    )
    return (output, grad_tokens, shards[0], shards[1], shards[2], shards[3], shards[4], shards[5])


def solution(mesh):
    placed = (
        P("dp", "seq", None),
        P("seq", None),
        P("seq", None),
        P("seq", None),
        P("seq", None),
        P(None, "seq"),
        P(None, "seq"),
        P("dp", "seq"),
        P(),
        P("dp", "seq", None),
    )
    fits = mesh.shape["seq"] == HEADS and mesh.shape["dp"] == 2
    return jax.shard_map(
        split_heads if fits else per_device,
        mesh=mesh,
        in_specs=placed,
        out_specs=(
            P("dp", "seq", None),
            P("dp", "seq", None),
            P("seq", None),
            P("seq", None),
            P("seq", None),
            P("seq", None),
            P(None, "seq"),
            P(None, "seq"),
        ),
        check_vma=False,
    )
```

```python
import functools
import math
import types

import jax
import jax.numpy as jnp
import numpy as np
from jax import lax
from jax.experimental import pallas as pl
from jax.experimental.pallas import tpu as pltpu
from jax.sharding import PartitionSpec as P

HEADS = 16
HEAD_DIM = 64
TILE = 256
MESH = pl.DeviceIdType.MESH
ANY = pl.BlockSpec(memory_space=pl.ANY)
DMA = pltpu.SemaphoreType.DMA
NT = ((1,), (1,))
TN = ((0,), (0,))
low, full = jnp.bfloat16, jnp.float32


def dot(left, right, contract=((1,), (0,))):
    return lax.dot_general(left, right, (contract, ((), ())), preferred_element_type=full)


def remote(source, target, send, recv, device):
    return pltpu.make_async_remote_copy(
        src_ref=source,
        dst_ref=target,
        send_sem=send,
        recv_sem=recv,
        device_id={"seq": device},
        device_id_type=MESH,
    )


def swap(source, target, send, recv):
    return pltpu.make_async_remote_copy(
        src_ref=source,
        dst_ref=target,
        send_sem=send,
        recv_sem=recv,
        device_id={"dp": 1 - lax.axis_index("dp")},
        device_id_type=MESH,
    )


class Ring:
    def __init__(self, length):
        self.me = lax.axis_index("seq")
        self.length = length
        self.chips = 2 * length
        self.steps = length
        self.core = self.me % 2
        column, row = (self.me // 2) % 2, self.me // 4
        self.first = (row // length) * length
        row = row - self.first
        self.base = self.first * 4
        self.place = row + column * (self.chips - 1 - 2 * row)
        self.right = self.device(1, self.core)
        self.left = self.device(-1, self.core)
        self.sibling = self.device(0, 1 - self.core)

    def device(self, ahead, core):
        place = (self.place + ahead + self.chips) % self.chips
        column = place // self.length
        row = place + column * (self.chips - 1 - 2 * place)
        return (self.first + row) * 4 + column * 2 + core


class Gather:
    def __init__(self, ring, piece, block, blocks, pieces, sems):
        self.ring, self.piece, self.block, self.blocks = ring, piece, block, blocks
        self.pieces = pieces
        self.send, self.recv, self.side_send, self.side_recv = sems
        self.messages = self.count(ring.chips, pieces)

    @staticmethod
    def count(chips, pieces):
        return pieces * (chips // 2) - pieces // 2

    def ref(self, way, j, ahead):
        k, q = j // self.pieces + ahead, j % self.pieces
        q = q if way == 0 else self.pieces - 1 - q
        return self.piece(self.ring.device(-k if way == 0 else k, self.ring.core), q)

    def hop(self, way, j):
        ref = self.ref(way, j, 0)
        target = self.ring.right if way == 0 else self.ring.left
        return remote(ref, ref, self.send.at[0], self.recv.at[way, j], target)

    def landed(self, way, j):
        return self.ref(way, j, 1)

    def side(self, ref, slot):
        return remote(ref, ref, self.side_send.at[0], self.side_recv.at[slot], self.ring.sibling)

    def start(self):
        for j in range(self.pieces):
            for way in range(2):
                self.hop(way, j).start()
        self.side(self.block(self.ring.me), 0).start()

    def pass_on(self, j):
        k = j // self.pieces + 1
        for way in range(2):
            self.hop(way, j).wait_recv()
            if j + self.pieces < self.messages:
                self.hop(way, j + self.pieces).start()
            slot = (-k if way == 0 else k) % self.ring.chips
            self.side(self.landed(way, j), slot).start()

    def wait_chip(self, ahead):
        block = self.block(self.ring.device(ahead, 1 - self.ring.core))
        self.side(block, ahead % self.ring.chips).wait_recv()

    def finish(self):
        count = self.ring.chips - 1
        everything = self.blocks(count)
        remote(everything, everything, self.send.at[0], self.recv.at[0, 0], self.ring.right).wait_send()
        self.side(self.blocks(count + 1), 0).wait_send()

    @staticmethod
    def sems(chips, pieces):
        return [DMA((1,)), DMA((2, Gather.count(chips, pieces))), DMA((1,)), DMA((chips,))]


class Scatter:
    def __init__(self, ring, parts, pieces, side, inbox, outbox, sems, shift=0):
        self.ring, self.parts, self.pieces = ring, parts, pieces
        self.base = ring.base - shift
        self.side, self.inbox, self.outbox = side, inbox, outbox
        self.send, self.recv, self.side_send, self.side_recv = sems
        self.messages = Gather.count(ring.chips, pieces)
        self.rows = parts.shape[1] // pieces
        self.waited = set()

    def across(self, ahead):
        slot = ahead % self.ring.chips
        return remote(
            self.parts.at[self.ring.device(ahead, 1 - self.ring.core) - self.base],
            self.side.at[slot],
            self.side_send.at[0],
            self.side_recv.at[slot],
            self.ring.sibling,
        )

    def hop(self, way, j):
        target = self.ring.right if way == 0 else self.ring.left
        return remote(
            self.outbox.at[way, j],
            self.inbox.at[way, j],
            self.send.at[0],
            self.recv.at[way, j],
            target,
        )

    def own(self, ahead, q):
        slot = ahead % self.ring.chips
        if slot not in self.waited:
            self.waited.add(slot)
            self.across(ahead).wait_recv()
        span = pl.ds(q * self.rows, self.rows)
        mine = self.parts[self.ring.device(ahead, self.ring.core) - self.base, span].astype(full)
        return mine + self.side[slot, span].astype(full)

    def ahead(self, j):
        return self.ring.steps - (j + self.pieces // 2) // self.pieces

    def step(self, j):
        for way in range(2):
            q = j % self.pieces if way == 0 else self.pieces - 1 - j % self.pieces
            total = self.own(self.ahead(j) if way == 0 else -self.ahead(j), q)
            if j >= self.pieces:
                self.hop(way, j - self.pieces).wait_recv()
                total += self.inbox[way, j - self.pieces].astype(full)
            self.outbox[way, j] = total.astype(self.outbox.dtype)
            self.hop(way, j).start()

    def result(self, q):
        total = self.own(0, q)
        for way in range(2):
            k = q if way == 0 else self.pieces - 1 - q
            last = max(j for j in range(self.messages) if j % self.pieces == k)
            self.hop(way, last).wait_recv()
            total += self.inbox[way, last].astype(full)
        return total

    def whole(self):
        return jnp.concatenate([self.result(q) for q in range(self.pieces)], 0)

    def finish(self):
        everything = self.parts.at[pl.ds(0, self.ring.chips)]
        side = self.side_send.at[0], self.side_recv.at[0]
        remote(everything, self.side, *side, self.ring.sibling).wait_send()
        hops = self.send.at[0], self.recv.at[0, 0]
        remote(self.outbox, self.inbox, *hops, self.ring.right).wait_send()

    @staticmethod
    def buffers(chips, rows, columns, pieces):
        box = pltpu.VMEM((2, Gather.count(chips, pieces), rows // pieces, columns), low)
        return [pltpu.VMEM((chips, rows, columns), low), box, box]

    @staticmethod
    def sems(chips, pieces):
        return [DMA((1,)), DMA((2, Gather.count(chips, pieces))), DMA((1,)), DMA((chips,))]


class Exchange:
    def __init__(self, source, target, blocks, sems):
        self.source, self.target, self.blocks = source, target, blocks
        self.send, self.recv = sems
        self.me, self.size = lax.axis_index("seq"), lax.axis_size("seq")

    def start(self):
        for i in sorted(range(1, self.size), key=lambda i: -abs(i - self.size // 2)):
            to = (self.me + i) % self.size
            remote(
                self.source(to), self.target(self.me), self.send.at[0], self.recv.at[0], to
            ).start()

    def all(self):
        ref = self.blocks(self.size - 1)
        to = (self.me + 1) % self.size
        return remote(ref, ref, self.send.at[0], self.recv.at[0], to)

    def wait(self):
        self.all().wait_recv()

    def finish(self):
        self.all().wait_send()


def normalized(values):
    center = values - jnp.mean(values, -1, keepdims=True)
    scale = lax.rsqrt(jnp.mean(center * center, -1, keepdims=True) + 1e-05)
    return center * scale, scale


def norm_back(grad, hat, scale, gain):
    d_hat = grad * gain
    mean = jnp.mean(d_hat, -1, keepdims=True)
    along = jnp.mean(d_hat * hat, -1, keepdims=True)
    return scale * (d_hat - mean - hat * along)


def gelu_and_slope(u):
    c = math.sqrt(2.0 / math.pi)
    square = u * u
    t = jnp.tanh(c * u * (1.0 + 0.044715 * square))
    act = 0.5 * u * (1.0 + t)
    slope = 0.5 * (1.0 + t) + 0.5 * u * (1.0 - t * t) * (c * (1.0 + 3 * 0.044715 * square))
    return act, slope


def causal(shape):
    key_pos = lax.broadcasted_iota(jnp.int32, shape, 0)
    query_pos = lax.broadcasted_iota(jnp.int32, shape, 1)
    return key_pos <= query_pos


def turn_tables(length):
    half = HEAD_DIM // 2
    freq = np.exp(
        np.arange(half, dtype=np.float32) * np.float32(-2.0 * math.log(10000.0) / HEAD_DIM)
    )
    angle = freq[:, None] * np.arange(length, dtype=np.float32)[None, :]
    return jnp.asarray(np.cos(angle)), jnp.asarray(np.sin(angle))


INPUTS = (
    "tokens",
    "w_qkv",
    "gains",
    "biases",
    "w_out",
    "w_up",
    "cos",
    "sin",
    "w_down",
    "cotangent",
    "corpus",
)
OUTPUTS = (
    "output",
    "grad_tokens",
    "grad_qkv",
    "grad_out",
    "grad_up",
    "grad_down",
    "grad_gains",
    "grad_biases",
)


def layer_kernel(names, *refs):
    r = types.SimpleNamespace(**dict(zip(names, refs, strict=True)))
    size = lax.axis_size("seq")
    ring, near = Ring(size // 4), Ring(size // 8)
    me, core, chips, steps = ring.me, ring.core, ring.chips, ring.steps
    far = (me + size // 2) % size
    close = size // 2
    dp = lax.axis_index("dp")
    rows, width = r.tokens.shape
    w_rows = r.w_out.shape[0]
    units = r.w_down.shape[0]
    length = rows * size
    near_length = rows * close
    tiles = length // TILE
    half = HEAD_DIM // 2
    kept = w_rows // 2
    packed = 3 * kept // 2
    pair = 2 * rows

    def mine(ref):
        return ref.at[:, pl.ds(dp * (ref.shape[1] // 2), ref.shape[1] // 2)]

    def theirs(ref):
        return ref.at[:, pl.ds((1 - dp) * (ref.shape[1] // 2), ref.shape[1] // 2)]

    def columns(device, count):
        return pl.ds(pl.multiple_of(device * count, count), count)

    loads = {
        name: pltpu.make_async_copy(getattr(r, name), getattr(r, name + "_v"), r.load_sem.at[i])
        for i, name in enumerate(INPUTS)
    }
    for name in INPUTS:
        loads[name].start()
    barrier = pltpu.get_barrier_semaphore()
    for i in range(1, size):
        pl.semaphore_signal(barrier, inc=1, device_id={"seq": (me + i) % size}, device_id_type=MESH)
    pl.semaphore_signal(barrier, inc=1, device_id={"dp": 1 - dp}, device_id_type=MESH)

    quarter = rows // 4

    def gather(ring, ref, count, sems, first=0, shift=0):
        pieces = 4 if ref.shape[1] == rows else 2
        shift = shift - ring.base
        return Gather(
            ring,
            lambda d, q: ref.at[d + shift, pl.ds(first + q * (count // pieces), count // pieces)],
            lambda d: ref.at[d + shift, pl.ds(first, count)],
            lambda n: ref.at[pl.ds(0, n), pl.ds(0, count)],
            pieces,
            sems,
        )

    mid_place, dd_place = me - near.base, me - near.base + close
    other = close - near.base
    tokens_in = gather(near, r.big, rows, r.gather2, shift=near.base)
    tokens_far = gather(near, r.big, rows, r.gather0, shift=other)

    def over(q):
        ref = r.big.at[me, pl.ds(q * (rows // 4), rows // 4)]
        return remote(ref, ref, r.over_send.at[q], r.over_recv.at[q], far)

    def over_again(q):
        over(q).wait_recv()
        tokens_far.hop(0, q).start()
        tokens_far.hop(1, 3 - q).start()

    mids = gather(near, r.big, rows, r.gather2)
    d_downs = gather(near, r.big, rows, r.gather2, shift=close)
    w_outs = gather(ring, r.w_out_all, kept, r.gather1, dp * kept)
    boxes = [(r.side[i], r.inbox[i], r.outbox[i], (r.scatter0, r.scatter1)[i]) for i in range(2)]
    sum_down = Scatter(near, r.parts, 4, *boxes[0])
    sum_mid = Scatter(near, r.parts, 4, *boxes[0])
    sum_out = Scatter(near, r.out_parts, 4, *boxes[1])
    sum_in = Scatter(ring, r.parts, 4, r.in_side, r.in_inbox, r.in_outbox, r.scatter2)
    out_over = remote(r.out_send, r.out_recv, r.far_sems.at[8], r.far_sems.at[9], far)

    def exchange(source, ref, sems, count):
        return Exchange(
            source,
            lambda d: ref.at[d, pl.ds(dp * count if count < ref.shape[1] else 0, count)],
            lambda n: ref.at[pl.ds(0, n), pl.ds(0, count)],
            sems,
        )

    head_weights = exchange(lambda d: r.head_send.at[d], r.head_recv, r.exchange0, packed)
    norm_rows = exchange(lambda d: r.norm_send, r.norm_recv, r.exchange1, 8)

    def up_exchange(ref, sems, shift):
        return exchange(
            lambda d: r.w_up_v.at[pl.ds(dp * kept, kept), columns((d + shift) % size, units)],
            ref,
            sems,
            kept,
        )

    up_weights = up_exchange(r.w_up_all, r.exchange2, 0)
    up_weights_far = up_exchange(r.w_up_far, r.exchange6, size // 2)
    d_atts = exchange(lambda d: r.d_att.at[d], r.att_recv, r.exchange3, HEAD_DIM)
    up_grads = exchange(lambda d: r.up_send[0].at[d], r.up_recv[0], r.exchange4, kept)
    up_grads_far = exchange(lambda d: r.up_send[1].at[d], r.up_recv[1], r.exchange7, kept)
    head_grads = exchange(lambda d: r.head_send.at[d], r.head_all, r.exchange5, packed)

    def swapped(source, target, slot):
        return swap(source, target, r.swap_send.at[slot], r.swap_recv.at[slot])

    head_other = swapped(mine(r.head_recv), mine(r.head_recv), 0)
    up_other = swapped(mine(r.w_up_all), mine(r.w_up_all), 1)
    up_other_far = swapped(mine(r.w_up_far), mine(r.w_up_far), 8)
    units_mine = pl.ds(dp * (units // 2), units // 2)
    units_theirs = pl.ds((1 - dp) * (units // 2), units // 2)
    down_far = remote(
        r.w_down_v.at[units_mine],
        r.w_down_far.at[units_mine],
        r.far_sems.at[0],
        r.far_sems.at[1],
        far,
    )
    down_other_far = swapped(r.w_down_far.at[units_mine], r.w_down_far.at[units_mine], 9)
    up_half = [swapped(theirs(r.up_grad[b]), r.up_peer[b], 2 + 8 * b) for b in range(2)]
    down_half = [
        swapped(r.down_grad[b].at[units_theirs], r.down_peer[b], 3 + 8 * b) for b in range(2)
    ]
    down_back_far = remote(r.down_send, r.down_recv, r.far_sems.at[2], r.far_sems.at[3], far)
    down_back = swapped(r.down_sum.at[units_mine], r.down_sum.at[units_mine], 12)
    out_whole = swapped(r.out_mine, r.out_peer, 4)
    up_back = swapped(mine(r.up_all), mine(r.up_all), 5)
    head_half = swapped(theirs(r.head_parts), r.head_peer, 6)
    head_back = swapped(mine(r.head_all), mine(r.head_all), 7)

    loads["w_qkv"].wait()
    rows_mine = pl.ds(dp * kept, kept)
    for h in range(HEADS):
        q, k, v = (
            r.w_qkv_v[rows_mine, i * width + h * HEAD_DIM : i * width + (h + 1) * HEAD_DIM]
            for i in range(3)
        )
        r.head_send[h, 0:kept] = jnp.concatenate([q, k], 1)
        r.head_send[h, kept:packed] = jnp.concatenate([v[: kept // 2], v[kept // 2 :]], 1)
    r.head_recv[me, pl.ds(dp * packed, packed)] = r.head_send[me]
    loads["gains"].wait()
    loads["biases"].wait()
    r.norm_send[...] = jnp.zeros_like(r.norm_send)
    r.norm_send[0:4, 0:w_rows] = r.gains_v[...].astype(full)
    r.norm_send[4:8, 0:w_rows] = r.biases_v[...].astype(full)
    r.norm_recv[me] = r.norm_send[...]
    loads["tokens"].wait()
    r.big[me] = r.tokens_v[...]
    pl.semaphore_wait(barrier, size)
    tokens_in.start()
    for q in (0, 3, 1, 2):
        over(q).start()
    norm_rows.start()
    head_weights.start()

    def gain(i):
        return r.norms[i : i + 1, :]

    def bias(i):
        return r.norms[4 + i : 5 + i, :]

    loads["w_out"].wait()
    r.w_out_all[me] = r.w_out_v[...]
    loads["w_up"].wait()
    r.w_up_all[me, rows_mine] = r.w_up_v[rows_mine, columns(me, units)]
    r.w_up_far[me, rows_mine] = r.w_up_v[rows_mine, columns(far, units)]
    loads["cos"].wait()
    loads["sin"].wait()
    for name in ("w_down", "cotangent", "corpus"):
        loads[name].wait()

    def unpack_heads():
        head_other.wait_recv()
        for j in range(size // 2):
            span = pl.ds(j * 2 * w_rows, 2 * w_rows)
            qk, v = [], []
            for d in (2 * j, 2 * j + 1):
                for h in range(2):
                    p = r.head_recv[d, h * packed : (h + 1) * packed]
                    qk.append(p[:kept])
                    v += [p[kept:, :HEAD_DIM], p[kept:, HEAD_DIM:]]
            r.w_t[0 : 2 * HEAD_DIM, span] = jnp.concatenate(qk, 0).astype(full).T.astype(low)
            r.w_t[2 * HEAD_DIM :, span] = jnp.concatenate(v, 0).astype(full).T.astype(low)

    def project(ahead, shift=0):
        base = near.device(ahead, 0) + shift
        x = r.big[pl.ds(base, 2)].reshape(pair, width).astype(full)
        hat, _ = normalized(x)
        normed = (hat * gain(0) + bias(0)).astype(low)
        r.normed_all[pl.ds(base, 2)] = normed.reshape(2, rows, width)
        qkv = dot(r.w_t[...], normed, NT)
        span = pl.ds(pl.multiple_of(base * rows, pair), pair)
        c, s = r.cos_v[:, span], r.sin_v[:, span]
        for i, (ref, nat, scale) in enumerate(
            ((r.q_t, r.q_nat, HEAD_DIM**-0.5), (r.k_t, r.k_nat, 1.0))
        ):
            first = qkv[i * HEAD_DIM : i * HEAD_DIM + half]
            second = qkv[i * HEAD_DIM + half : (i + 1) * HEAD_DIM]
            turned = jnp.concatenate([first * c - second * s, first * s + second * c], 0) * scale
            ref[:, span] = turned.astype(low)
            nat[span, :] = turned.T.astype(low)
        v = qkv[2 * HEAD_DIM :]
        r.v_t[:, span] = v.astype(low)
        r.v_nat[span, :] = v.T.astype(low)

    def out_swap(ref, way, j):
        return swap(ref, ref, r.out_swap_send.at[0], r.out_swap_recv.at[way, j])

    def out_other(way, j):
        k, q = j // 2 + 1, j % 2
        q = q if way == 0 else 1 - q
        device = ring.device(-k if way == 0 else k, core)
        return r.w_out_all.at[device, pl.ds((1 - dp) * kept + q * (kept // 2), kept // 2)]

    def out_side(ref, slot):
        send, recv = r.out_side_send.at[slot], r.out_side_recv.at[slot]
        return remote(ref, ref, send, recv, ring.sibling)

    def out_own():
        return out_side(r.w_out_all.at[me, pl.ds((1 - dp) * kept, kept)], 0)

    def out_others():
        return out_side(w_outs.blocks(chips - 1), 1)

    def pass_out(j):
        w_outs.pass_on(j)
        for way in range(2):
            out_swap(w_outs.landed(way, j), way, j).start()

    def pass_other(j):
        for way in range(2):
            ref = out_other(way, j)
            out_swap(ref, way, j).wait_recv()
            out_side(ref, 1).start()

    tokens_in.pass_on(0)
    tokens_in.pass_on(1)
    over_again(0)
    tokens_in.pass_on(2)
    tokens_in.pass_on(3)
    norm_rows.wait()
    for j in range(size // 2):
        r.norms[:, j * 128 : (j + 1) * 128] = jnp.concatenate(
            [r.norm_recv[2 * j][:, :w_rows], r.norm_recv[2 * j + 1][:, :w_rows]], 1
        )
    head_weights.wait()
    head_other.start()
    over_again(3)
    for j in range(4, 6):
        tokens_in.pass_on(j)
    over_again(1)
    over_again(2)
    tokens_far.side(tokens_far.block(me), 0).start()
    w_outs.start()
    out_own().start()
    down_far.start()
    up_weights.start()
    up_weights_far.start()
    tokens_far.pass_on(0)
    tokens_far.pass_on(1)
    unpack_heads()
    for ahead in (0, 1, -1):
        tokens_in.wait_chip(ahead)
        project(ahead)
    tokens_far.pass_on(2)
    tokens_far.pass_on(3)
    pass_out(0)
    pass_out(1)
    tokens_in.wait_chip(2)
    project(2)
    for ahead in (0, 1, -1):
        tokens_far.wait_chip(ahead)
        project(ahead, other - near.base)
    for j in range(4, 6):
        tokens_far.pass_on(j)
    tokens_far.wait_chip(2)
    project(2, other - near.base)
    tokens_in.finish()
    tokens_far.finish()
    for q in range(4):
        over(q).wait_send()
    pass_out(2)
    pass_out(3)
    pass_other(0)
    pass_other(1)

    for t in range(tiles):
        span = pl.ds(t * TILE, TILE)
        query = r.q_t[:, span]
        top = None
        for j in range(t + 1):
            keys = pl.ds(j * TILE, TILE)
            s = dot(r.k_nat[keys, :], query)
            if j == t:
                s = jnp.where(causal(s.shape), s, -1e30)
            r.scores[keys, :] = s
            here = jnp.max(s, 0, keepdims=True)
            top = here if top is None else jnp.maximum(top, here)
        acc, norm = None, None
        for j in range(t + 1):
            keys = pl.ds(j * TILE, TILE)
            p = jnp.exp(r.scores[keys, :] - top)
            here = jnp.sum(p, 0, keepdims=True)
            add = dot(r.v_t[:, keys], p.astype(low))
            acc = add if acc is None else acc + add
            norm = here if norm is None else norm + here
        acc = acc / norm
        r.total[:, span] = acc
        r.lse[:, span] = top + jnp.log(norm)
        for b in range(TILE // rows):
            to = t * (TILE // rows) + b
            block = acc[:, b * rows : (b + 1) * rows].astype(low)
            r.att_send[to] = block

            @pl.when(me != to)
            def _(to=to):
                remote(
                    r.att_send.at[to], r.att_t.at[me], r.att_ssem.at[0], r.att_rsem.at[0], to
                ).start()

            @pl.when(me == to)
            def _(block=block):
                r.att_t[me] = block

        if t == 4:
            pass_out(4)
            pass_out(5)
            up_weights.wait()
            up_other.start()
            pass_other(2)
            pass_other(3)
        if t == 6:
            pass_out(6)
            up_weights_far.wait()
            up_other_far.start()
            pass_other(4)
            pass_other(5)
    pass_other(6)
    for ahead in range(chips):
        w_outs.wait_chip(ahead)
    out_own().wait_recv()
    out_others().wait_recv()
    attended = r.att_t.at[pl.ds(0, size - 1)]
    attended = remote(attended, attended, r.att_ssem.at[0], r.att_rsem.at[0], ring.right)
    down_far.wait_recv()
    down_other_far.start()
    attended.wait()

    att_t = r.att_t[...].reshape(width, rows)
    w_out_all = r.w_out_all
    proj = dot(att_t, w_out_all[...].reshape(width, width), TN)
    r.proj[...] = proj
    hat1, _ = normalized(proj)
    hidden = r.tokens_v[...].astype(full) + hat1 * gain(1) + bias(1)
    r.hidden[...] = hidden
    hat2, _ = normalized(hidden)
    r.big[mid_place] = (hat2 * gain(2) + bias(2)).astype(low)
    mids.start()
    w_outs.finish()

    def weights(b):
        up, down = ((r.w_up_all, r.w_down_v), (r.w_up_far, r.w_down_far))[b]
        return up[...].reshape(width, units), down[...]

    def forward(ahead):
        place = pl.ds(near.device(ahead, 0) - near.base, 2)
        x = r.big[place].reshape(pair, width)
        part = None
        for b in range(2):
            w_up, w_down = weights(b)
            act, slope = gelu_and_slope(dot(x, w_up))
            act = act.astype(low)
            r.act_all[b, place] = act.reshape(2, rows, units)
            r.slope_all[b, place] = slope.reshape(2, rows, units)
            add = dot(act, w_down)
            part = add if part is None else part + add
        r.parts[place] = part.astype(low).reshape(2, rows, width)
        sum_down.across(ahead).start()

    def backward(ahead):
        place = pl.ds(near.device(ahead, 0) - near.base, 2)
        x = r.big[pl.ds(near.device(ahead, 0) - near.base + close, 2)].reshape(pair, width)
        part = None
        for b in range(2):
            w_up, w_down = weights(b)
            d_act = dot(x, w_down, NT)
            d_up = (d_act * r.slope_all[b, place].reshape(pair, units)).astype(low)
            r.d_up_all[b, place] = d_up.reshape(2, rows, units)
            add = dot(d_up, w_up, NT)
            part = add if part is None else part + add
        r.parts[place] = part.astype(low).reshape(2, rows, width)
        sum_mid.across(ahead).start()

    def there_and_back(gather, scatter, ready, work, fill):
        last = near.steps
        for k in range(1, last + 1):
            if k == last:
                ready()
                gather.wait_chip(0)
                work(0)
                for ahead in range(1, last):
                    for chip in (ahead, -ahead):
                        gather.wait_chip(chip)
                        work(chip)
                scatter.step(2)
                scatter.step(3)
            for j in range(4 * (k - 1), min(4 * k, gather.messages)):
                gather.pass_on(j)
        gather.wait_chip(last)
        work(last)
        scatter.step(0)
        scatter.step(1)
        for j in range(4, scatter.messages):
            fill(j)
            scatter.step(j)
        fill(scatter.messages)

    def weights_here():
        up_other.wait_recv()
        up_other_far.wait_recv()
        down_other_far.wait_recv()

    there_and_back(mids, sum_down, weights_here, forward, lambda j: None)

    weight_row = jnp.zeros((1, rows), full)
    for c in range(r.weight.shape[0]):
        weight_row += jnp.where(r.corpus_v[...] == c, r.weight[c], 0.0)
    row_weight = jnp.broadcast_to(weight_row, (rows, rows)).T[:, 0:1]
    for q in range(4):
        span = pl.ds(q * quarter, quarter)
        down = sum_down.result(q)
        hat3, scale3 = normalized(down)
        r.output_v[span, :] = (r.hidden[span, :] + hat3 * gain(3) + bias(3)).astype(low)
        grad_y = r.cotangent_v[span, :].astype(full) * row_weight[q * quarter : (q + 1) * quarter]
        r.d_hidden[span, :] = grad_y
        r.big[dd_place, span] = norm_back(grad_y, hat3, scale3, gain(3)).astype(low)
        g3 = jnp.sum(grad_y * hat3, 0, keepdims=True)
        b3 = jnp.sum(grad_y, 0, keepdims=True)
        r.norm_grads[3:4, :] = g3 if q == 0 else r.norm_grads[3:4, :] + g3
        r.norm_grads[7:8, :] = b3 if q == 0 else r.norm_grads[7:8, :] + b3
    mids.finish()
    sum_down.finish()
    d_downs.start()
    saves = {}

    def save(name):
        i = OUTPUTS.index(name)
        saves[name] = pltpu.make_async_copy(
            getattr(r, name + "_v"), getattr(r, name), r.save_sem.at[i]
        )
        saves[name].start()

    save("output")

    def up_gradient(b):
        d_up = r.d_up_all[b].reshape(near_length, units)
        blocks = size // 4
        for i in range(4):
            span = pl.ds(i * (width // 4), width // 4)
            x = r.big[:close, :, span].reshape(near_length, width // 4)
            grad = dot(d_up, x, TN).T.astype(low)
            r.up_grad[b][i * blocks : (i + 1) * blocks] = grad.reshape(blocks, w_rows, units)
        up_half[b].start()

    def down_gradient(b):
        act = r.act_all[b].reshape(near_length, units)
        for i in range(4):
            span = pl.ds(i * (width // 4), width // 4)
            dd = r.big[close:, :, span].reshape(near_length, width // 4)
            r.down_grad[b][:, span] = dot(act, dd, TN).astype(low)
        down_half[b].start()

    def fill(j):
        if j < 6:
            up_gradient(j - 4)

    there_and_back(d_downs, sum_mid, lambda: None, backward, fill)

    hat1, scale1 = normalized(r.proj[...])
    hat2, scale2 = normalized(r.hidden[...])
    hat0, scale0 = normalized(r.tokens_v[...].astype(full))
    r.hat0[...] = hat0
    d_mid = sum_mid.whole()
    r.norm_grads[2:3, :] = jnp.sum(d_mid * hat2, 0, keepdims=True)
    r.norm_grads[6:7, :] = jnp.sum(d_mid, 0, keepdims=True)
    d_hidden = r.d_hidden[...] + norm_back(d_mid, hat2, scale2, gain(2))
    r.d_hidden[...] = d_hidden
    r.norm_grads[1:2, :] = jnp.sum(d_hidden * hat1, 0, keepdims=True)
    r.norm_grads[5:6, :] = jnp.sum(d_hidden, 0, keepdims=True)
    d_proj = norm_back(d_hidden, hat1, scale1, gain(1)).astype(low)
    d_att = dot(w_out_all[...].reshape(width, width), d_proj, NT).astype(low)
    r.d_att[...] = d_att.reshape(HEADS, HEAD_DIM, rows)
    d_atts.start()

    out = dot(att_t, d_proj).astype(low).reshape(size, w_rows, width)
    r.out_parts[:, :w_rows] = out[:close]
    r.out_parts[:, w_rows:] = out[close:]
    for ahead in range(near.chips):
        sum_out.across(ahead).start()
    r.att_recv[me] = r.d_att[me]
    d_downs.finish()
    sum_mid.finish()
    r.dq[...] = jnp.zeros_like(r.dq)
    for b in (1, 0):
        down_gradient(b)
    for b in range(2):
        up_half[b].wait_recv()
        up_mine = r.up_grad[b][:, rows_mine].astype(full)
        r.up_send[b][...] = (up_mine + r.up_peer[b][...].astype(full)).astype(low)
        r.up_recv[b][me] = r.up_send[b][me]
        (up_grads, up_grads_far)[b].start()
    for j in range(4):
        sum_out.step(j)
    d_atts.wait()
    for b in range(size):
        r.do_t[:, b * rows : (b + 1) * rows] = r.att_recv[b]
    for t in range(tiles):
        span = pl.ds(t * TILE, TILE)
        do = r.do_t[:, span].astype(full)
        r.do_nat[span, :] = do.T.astype(low)
        r.delta[:, span] = jnp.sum(do * r.total[:, span], 0, keepdims=True)

    def turned_back(u, span, base):
        c, s = r.cos_v[:, span], r.sin_v[:, span]
        first, second = u[:half], u[half:]
        r.d_t[base : base + half, span] = (first * c + second * s).astype(low)
        r.d_t[base + half : base + 2 * half, span] = (second * c - first * s).astype(low)

    high = near.base // close
    out_own_rows, out_far_rows = pl.ds(high * w_rows, w_rows), pl.ds((1 - high) * w_rows, w_rows)

    def beside_attention(j):
        if j in (0, 1):
            sum_out.step(4 + j)
        if j == 1:
            down_half[1].wait_recv()
            down_mine = r.down_grad[1][units_mine].astype(full)
            r.down_send[...] = (down_mine + r.down_peer[1][...].astype(full)).astype(low)
            down_back_far.start()
        if j == 3:
            r.out_sum[...] = sum_out.whole()
            r.out_send[...] = r.out_sum[out_far_rows].astype(low)
            out_over.start()

    def collect_up():
        up_grads.wait()
        up_grads_far.wait()
        for h in range(size):
            both = r.up_recv[0][h].astype(full) + r.up_recv[1][(h + close) % size].astype(full)
            r.up_all[h, rows_mine] = both.astype(low)
        up_back.start()

    def collect_out():
        out_over.wait_recv()
        r.out_mine[...] = (r.out_sum[out_own_rows] + r.out_recv[...].astype(full)).astype(low)
        out_whole.start()

    def collect_down():
        down_half[0].wait_recv()
        down_back_far.wait_recv()
        both = r.down_grad[0][units_mine].astype(full) + r.down_peer[0][...].astype(full)
        r.down_sum[units_mine] = (both + r.down_recv[...].astype(full)).astype(low)
        down_back.start()

    for j in range(tiles):
        keys = pl.ds(j * TILE, TILE)
        dk, dv = None, None
        for t in range(j, tiles):
            span = pl.ds(t * TILE, TILE)
            s = dot(r.k_nat[keys, :], r.q_t[:, span])
            p = jnp.exp(s - r.lse[:, span])
            if j == t:
                p = jnp.where(causal(p.shape), p, 0.0)
            d_p = dot(r.v_nat[keys, :], r.do_t[:, span])
            d_s = (p * (d_p - r.delta[:, span])).astype(low)
            dv_add = dot(p.astype(low), r.do_nat[span, :])
            dk_add = dot(d_s, r.q_nat[span, :])
            dv = dv_add if dv is None else dv + dv_add
            dk = dk_add if dk is None else dk + dk_add
            r.dq[:, span] += dot(r.k_t[:, keys], d_s)
        turned_back(dk.T, keys, HEAD_DIM)
        r.d_t[2 * HEAD_DIM :, keys] = dv.T.astype(low)
        turned_back(r.dq[:, keys] * HEAD_DIM**-0.5, keys, 0)
        beside_attention(j)

    def part(ahead):
        base = ring.device(ahead, 0)
        span = pl.ds(pl.multiple_of(base * rows, pair), pair)
        d_x = dot(r.d_t[:, span], r.w_t[...], TN).astype(low)
        r.parts[pl.ds(base, 2)] = d_x.reshape(2, rows, width)
        sum_in.across(ahead).start()

    def head_gradient(j):
        x = r.normed_all[:, :, j * 128 : (j + 1) * 128].reshape(length, 128)
        d_w = dot(r.d_t[...], x).T
        for i in range(2):
            for h in range(2):
                base = i * w_rows + h * kept
                block = d_w[base : base + kept]
                v = block[:, 2 * HEAD_DIM :]
                v = jnp.concatenate([v[: kept // 2], v[kept // 2 :]], 1)
                at = h * packed
                r.head_parts[2 * j + i, at : at + kept] = block[:, : 2 * HEAD_DIM].astype(low)
                r.head_parts[2 * j + i, at + kept : at + packed] = v.astype(low)

    part(steps)
    part(steps - 1)
    part(1 - steps)
    for j in range(4):
        sum_in.step(j)
    for j in range(size // 2):
        head_gradient(j)
    head_weights.finish()
    head_half.start()
    for k in range(steps - 2, 0, -1):
        part(k)
        part(-k)
    part(0)
    sum_in.step(4)
    sum_in.step(5)
    for j in range(6, 8):
        sum_in.step(j)
    head_half.wait_recv()
    own_half = r.head_parts[:, pl.ds(dp * packed, packed)].astype(full)
    r.head_send[...] = (own_half + r.head_peer[...].astype(full)).astype(low)
    r.head_all[me, pl.ds(dp * packed, packed)] = r.head_send[me]
    head_grads.start()
    collect_up()
    collect_out()
    for j in range(8, 10):
        sum_in.step(j)
    for j in range(10, 12):
        sum_in.step(j)
    collect_down()
    for j in range(12, 14):
        sum_in.step(j)
    out_whole.wait_recv()
    r.grad_out_v[...] = r.out_mine[...].astype(full) + r.out_peer[...].astype(full)
    save("grad_out")
    d_normed = sum_in.whole()
    up_back.wait_recv()
    for h in range(size):
        r.grad_up_v[:, h * units : (h + 1) * units] = r.up_all[h].astype(full)
    save("grad_up")
    down_back.wait_recv()
    r.grad_down_v[...] = r.down_sum[...].astype(full)
    save("grad_down")
    head_grads.wait()
    head_back.start()

    hat0 = r.hat0[...]
    r.norm_grads[0:1, :] = jnp.sum(d_normed * hat0, 0, keepdims=True)
    r.norm_grads[4:5, :] = jnp.sum(d_normed, 0, keepdims=True)

    def norm_copy(i, other):
        to = (me + i) % size
        return pltpu.make_async_remote_copy(
            src_ref=r.norm_grads.at[:, columns(to // 2, 128)],
            dst_ref=r.norm_sums.at[2 * i + other],
            send_sem=r.norm_ssem.at[0],
            recv_sem=r.norm_rsem.at[0],
            device_id={"seq": to, "dp": (dp + other) % 2},
            device_id_type=MESH,
        )

    partners = [(i, other) for i in range(size) for other in range(2) if i or other]
    for i, other in partners:
        norm_copy(i, other).start()
    r.norm_sums[0] = r.norm_grads[:, columns(me // 2, 128)]
    _, scale0 = normalized(r.tokens_v[...].astype(full))
    r.grad_tokens_v[...] = r.d_hidden[...] + norm_back(d_normed, hat0, scale0, gain(0))
    save("grad_tokens")
    head_back.wait_recv()
    for h in range(2):
        for j in range(size // 2):
            blocks = [
                r.head_all[2 * j + i, h * packed : (h + 1) * packed].astype(full) for i in range(2)
            ]
            span = slice(h * kept, (h + 1) * kept)
            for b in range(2):
                place = slice(b * width + j * 128, b * width + (j + 1) * 128)
                r.grad_qkv_v[span, place] = jnp.concatenate(
                    [p[:kept, b * HEAD_DIM : (b + 1) * HEAD_DIM] for p in blocks], 1
                )
            v = [jnp.concatenate([p[kept:, :HEAD_DIM], p[kept:, HEAD_DIM:]], 0) for p in blocks]
            place = slice(2 * width + j * 128, 2 * width + (j + 1) * 128)
            r.grad_qkv_v[span, place] = jnp.concatenate(v, 1)
    save("grad_qkv")
    norm_all = r.norm_sums.at[pl.ds(1, 2 * size - 1)]
    norm_all = swap(norm_all, norm_all, r.norm_ssem.at[0], r.norm_rsem.at[0])
    norm_all.wait_recv()
    sums = jnp.sum(r.norm_sums[...], 0)
    sums = jnp.where(core == 0, sums[:, :w_rows], sums[:, w_rows:])
    r.grad_gains_v[...] = sums[0:4]
    r.grad_biases_v[...] = sums[4:8]
    save("grad_gains")
    save("grad_biases")

    norm_all.wait_send()
    sum_in.finish()
    sum_out.finish()
    for moved in (
        norm_rows, up_weights, up_weights_far, d_atts, up_grads, up_grads_far, head_grads
    ):
        moved.finish()
    for copy in (
        head_other,
        up_other,
        up_other_far,
        down_far,
        down_other_far,
        *up_half,
        *down_half,
        down_back_far,
        down_back,
        out_over,
        out_whole,
        up_back,
        head_half,
        head_back,
    ):
        copy.wait_send()
    out_own().wait_send()
    out_others().wait_send()
    out_swap(w_outs.blocks(chips - 1), 0, 0).wait_send()
    for copy in saves.values():
        copy.wait()


def hand_over_kernel(count, *refs):
    ins, outs, held = (refs[i * count : (i + 1) * count] for i in range(3))
    sems = refs[-1]
    loads = [pltpu.make_async_copy(ins[i], held[i], sems.at[0, i]) for i in range(count)]
    saves = [pltpu.make_async_copy(held[i], outs[i], sems.at[1, i]) for i in range(count)]
    for copy in loads:
        copy.start()
    for load, copy in zip(loads, saves):
        load.wait()
        copy.start()
    for copy in saves:
        copy.wait()


def hand_over(arrays):
    count = len(arrays)
    return pl.pallas_call(
        functools.partial(hand_over_kernel, count),
        out_shape=[jax.ShapeDtypeStruct(a.shape, a.dtype) for a in arrays],
        in_specs=[ANY] * count,
        out_specs=[ANY] * count,
        scratch_shapes=[pltpu.VMEM(a.shape, a.dtype) for a in arrays] + [DMA((2, count))],
    )(*arrays)


def split_heads(
    tokens, w_qkv, w_out, w_up, w_down, norm_gains, norm_biases, corpus_id, corpus_weight, cotangent
):
    size = lax.axis_size("seq")
    chips = size // 2
    _, rows, width = tokens.shape
    w_rows = w_out.shape[0]
    units = w_down.shape[0]
    length = rows * size
    shape = jax.ShapeDtypeStruct
    cos, sin = turn_tables(length)
    inputs = dict(
        tokens=tokens[0],
        w_qkv=w_qkv,
        w_out=w_out,
        w_up=w_up,
        w_down=w_down,
        gains=norm_gains,
        biases=norm_biases,
        corpus=corpus_id,
        cotangent=cotangent[0],
        cos=cos,
        sin=sin,
    )
    outputs = dict(
        output=shape((rows, width), low),
        grad_tokens=shape((rows, width), full),
        grad_qkv=shape((w_rows, 3 * width), full),
        grad_out=shape((w_rows, width), full),
        grad_up=shape((w_rows, size * units), full),
        grad_down=shape((units, width), full),
        grad_gains=shape((4, w_rows), full),
        grad_biases=shape((4, w_rows), full),
    )

    def vmem(*dims, kind=low):
        return pltpu.VMEM(dims, kind)

    head_rows = 3 * w_rows // 2
    blocks = vmem(size, rows, width)
    nat, turned = vmem(length, HEAD_DIM), vmem(HEAD_DIM, length)
    side, inbox, outbox = Scatter.buffers(chips, rows, width, 4)
    side, inbox, outbox = Scatter.buffers(chips // 2, rows, width, 4)
    in_side, in_inbox, in_outbox = Scatter.buffers(chips, rows, width, 4)
    scratch = {name + "_v": vmem(*a.shape, kind=a.dtype) for name, a in inputs.items()}
    scratch |= {name + "_v": vmem(*a.shape, kind=a.dtype) for name, a in outputs.items()}
    scratch |= dict(
        big=blocks,
        normed_all=blocks,
        parts=blocks,
        side=[side] * 2,
        inbox=[inbox] * 2,
        outbox=[outbox] * 2,
        in_side=in_side,
        in_inbox=in_inbox,
        in_outbox=in_outbox,
        out_parts=vmem(size // 2, 2 * w_rows, width),
        out_sum=vmem(2 * w_rows, width, kind=full),
        out_send=vmem(w_rows, width),
        out_recv=vmem(w_rows, width),
        out_mine=vmem(w_rows, width),
        out_peer=vmem(w_rows, width),
        w_out_all=vmem(size, w_rows, width),
        w_up_all=vmem(size, w_rows, units),
        w_up_far=vmem(size, w_rows, units),
        w_down_far=vmem(units, width),
        w_t=vmem(3 * HEAD_DIM, width),
        head_send=vmem(size, head_rows // 2, 128),
        head_recv=vmem(size, head_rows, 128),
        head_parts=vmem(size, head_rows, 128),
        head_peer=vmem(size, head_rows // 2, 128),
        head_all=vmem(size, head_rows, 128),
        norm_send=vmem(8, 128, kind=full),
        norm_recv=vmem(size, 8, 128, kind=full),
        norms=vmem(8, width, kind=full),
        norm_grads=vmem(8, width, kind=full),
        norm_sums=vmem(2 * size, 8, 128, kind=full),
        q_t=turned,
        k_t=turned,
        v_t=turned,
        do_t=turned,
        q_nat=nat,
        k_nat=nat,
        v_nat=nat,
        do_nat=nat,
        total=vmem(HEAD_DIM, length, kind=full),
        dq=vmem(HEAD_DIM, length, kind=full),
        d_t=vmem(3 * HEAD_DIM, length),
        lse=vmem(1, length, kind=full),
        delta=vmem(1, length, kind=full),
        scores=vmem(length, TILE, kind=full),
        att_send=vmem(size, HEAD_DIM, rows),
        att_t=vmem(size, HEAD_DIM, rows),
        d_att=vmem(size, HEAD_DIM, rows),
        att_recv=vmem(size, HEAD_DIM, rows),
        proj=vmem(rows, width, kind=full),
        hidden=vmem(rows, width, kind=full),
        d_hidden=vmem(rows, width, kind=full),
        hat0=vmem(rows, width, kind=full),
        act_all=vmem(2, size // 2, rows, units),
        slope_all=vmem(2, size // 2, rows, units, kind=full),
        d_up_all=vmem(2, size // 2, rows, units),
        up_grad=[vmem(size, w_rows, units)] * 2,
        up_peer=[vmem(size, w_rows // 2, units)] * 2,
        up_send=[vmem(size, w_rows // 2, units)] * 2,
        up_recv=[vmem(size, w_rows // 2, units)] * 2,
        up_all=vmem(size, w_rows, units),
        down_grad=[vmem(units, width)] * 2,
        down_peer=[vmem(units // 2, width)] * 2,
        down_send=vmem(units // 2, width),
        down_recv=vmem(units // 2, width),
        down_sum=vmem(units, width),
        far_sems=DMA((10,)),
        over_send=DMA((4,)),
        over_recv=DMA((4,)),
        load_sem=DMA((len(inputs),)),
        save_sem=DMA((len(outputs),)),
        swap_send=DMA((13,)),
        swap_recv=DMA((13,)),
        out_side_send=DMA((2,)),
        out_side_recv=DMA((2,)),
        out_swap_send=DMA((1,)),
        out_swap_recv=DMA((2, Gather.count(chips, 2))),
        att_ssem=DMA((1,)),
        att_rsem=DMA((1,)),
        norm_ssem=DMA((1,)),
        norm_rsem=DMA((1,)),
    )
    for i, (count, pieces) in enumerate(((chips // 2, 4), (chips, 2), (chips // 2, 4))):
        scratch[f"gather{i}"] = Gather.sems(count, pieces)
    for i in range(3):
        scratch[f"scatter{i}"] = Scatter.sems(chips if i == 2 else chips // 2, 4)
    for i in range(8):
        scratch[f"exchange{i}"] = [DMA((1,)), DMA((1,))]
    flat, groups = [], []
    for name, entry in scratch.items():
        entries = entry if isinstance(entry, list) else [entry]
        groups.append((name, len(entries) if isinstance(entry, list) else 0))
        flat += entries

    def kernel(*refs):
        count = len(inputs) + 1 + len(outputs)
        names = [*inputs, "weight", *outputs]
        values = list(refs[:count])
        rest = list(refs[count:])
        for name, many in groups:
            names.append(name)
            if many:
                values.append(tuple(rest[:many]))
                rest = rest[many:]
            else:
                values.append(rest.pop(0))
        layer_kernel(names, *values)

    results = pl.pallas_call(
        kernel,
        out_shape=list(outputs.values()),
        in_specs=[ANY] * len(inputs) + [pl.BlockSpec(memory_space=pltpu.SMEM)],
        out_specs=[ANY] * len(outputs),
        scratch_shapes=flat,
        compiler_params=pltpu.CompilerParams(
            collective_id=1, has_side_effects=True, vmem_limit_bytes=61 * 2**20
        ),
    )(*inputs.values(), corpus_weight)
    results = hand_over(results)
    return (results[0][None], results[1][None], *results[2:])


def shifted(x, axis, by):
    size = lax.axis_size(axis)
    return lax.ppermute(x, axis, [(i, (i + by) % size) for i in range(size)])


def passed_along(value, axis, steps):
    count = lax.axis_size(axis)
    first, last = (max(0, -steps), min(count, count - steps))
    return lax.ppermute(value, axis, [(source, source + steps) for source in range(first, last)])


def layer_norm(values, gain, bias):
    center = values - jnp.mean(values, -1, keepdims=True)
    variance = jnp.mean(center * center, -1, keepdims=True)
    return center * lax.rsqrt(variance + 1e-05) * gain + bias


def rotate(values, position, direction):
    half_size = values.shape[-1] // 2
    freq = jnp.exp(
        jnp.arange(half_size).astype(jnp.float32) * (-2.0 * math.log(10000.0) / values.shape[-1])
    )
    angle = position[:, None] * freq[None, :]
    cosine = jnp.cos(angle)[:, None, :]
    sine = direction * jnp.sin(angle)[:, None, :]
    first = values[..., :half_size]
    second = values[..., half_size:]
    return jnp.concatenate([first * cosine - second * sine, first * sine + second * cosine], -1)


def gelu_tanh(values):
    return jax.nn.gelu(values, approximate=True)


def per_device(
    tokens, w_qkv, w_out, w_up, w_down, norm_gains, norm_biases, corpus_id, corpus_weight, cotangent
):
    full_qkv, full_out, full_up, full_down, gains_low, biases_low = (
        lax.all_gather(w_qkv, "seq", axis=0, tiled=True),
        lax.all_gather(w_out, "seq", axis=0, tiled=True),
        lax.all_gather(w_up, "seq", axis=0, tiled=True),
        lax.all_gather(w_down, "seq", axis=0, tiled=True),
        lax.all_gather(norm_gains, "seq", axis=1, tiled=True),
        lax.all_gather(norm_biases, "seq", axis=1, tiled=True),
    )
    gains = gains_low.astype(jnp.float32)
    biases = biases_low.astype(jnp.float32)
    seq_count, row_count, model_width = tokens.shape
    shape_heads = (seq_count, row_count, HEADS, HEAD_DIM)
    scale = HEAD_DIM ** (-0.5)
    cycle_size = lax.axis_size("seq")
    cycle_index = lax.axis_index("seq")
    query_pos = cycle_index * row_count + jnp.arange(row_count)
    position = query_pos.astype(jnp.float32)
    x_float = tokens.astype(jnp.float32)
    normed_low = layer_norm(x_float, gains[0], biases[0]).astype(jnp.bfloat16)
    qkv = jnp.einsum("std,de->ste", normed_low, full_qkv, preferred_element_type=jnp.float32)
    query_low = rotate(qkv[..., :model_width].reshape(shape_heads), position, 1.0).astype(
        jnp.bfloat16
    )
    key_low = rotate(
        qkv[..., model_width : 2 * model_width].reshape(shape_heads), position, 1.0
    ).astype(jnp.bfloat16)
    value_low = qkv[..., 2 * model_width :].reshape(shape_heads).astype(jnp.bfloat16)

    def block_scores(key_piece, key_pos):
        scores = (
            jnp.einsum("sqhd,skhd->shqk", query_low, key_piece, preferred_element_type=jnp.float32)
            * scale
        )
        allowed = query_pos[:, None] >= key_pos[None, :]
        return (scores, allowed)

    stat_shape = (seq_count, HEADS, row_count)
    key_piece = lax.all_gather(key_low, "seq", axis=1, tiled=True)
    value_piece = lax.all_gather(value_low, "seq", axis=1, tiled=True)
    key_pos = jnp.arange(key_piece.shape[1])
    run_max = jnp.full(stat_shape, -1e30, jnp.float32)
    scores, allowed = block_scores(key_piece, key_pos)
    new_max = jnp.maximum(run_max, jnp.max(jnp.where(allowed, scores, -1e30), -1))
    weights = jnp.where(allowed, jnp.exp(scores - new_max[..., None]), 0.0)
    run_sum = jnp.sum(weights, -1)
    total = jnp.einsum(
        "shqk,skhd->sqhd",
        weights.astype(jnp.bfloat16),
        value_piece,
        preferred_element_type=jnp.float32,
    )
    run_max, run_sum, total = (new_max, run_sum, total)
    log_sum = run_max + jnp.log(run_sum)
    attended = total / jnp.transpose(run_sum, (0, 2, 1))[..., None]
    attended_low = attended.reshape(seq_count, row_count, model_width).astype(jnp.bfloat16)
    proj = jnp.einsum("std,de->ste", attended_low, full_out, preferred_element_type=jnp.float32)
    hidden = x_float + layer_norm(proj, gains[1], biases[1])
    mid_low = layer_norm(hidden, gains[2], biases[2]).astype(jnp.bfloat16)
    up_proj = jnp.einsum("std,df->stf", mid_low, full_up, preferred_element_type=jnp.float32)
    act_low = gelu_tanh(up_proj).astype(jnp.bfloat16)
    down = jnp.einsum("stf,fd->std", act_low, full_down, preferred_element_type=jnp.float32)
    output = (hidden + layer_norm(down, gains[3], biases[3])).astype(jnp.bfloat16)
    matches = (corpus_id[..., None] == jnp.arange(corpus_weight.shape[0])).astype(jnp.float32)
    row_weight = jnp.sum(matches * corpus_weight, -1)
    grad_y = cotangent.astype(jnp.float32) * row_weight[..., None]
    _, down_back = jax.vjp(layer_norm, down, gains[3], biases[3])
    d_down, gain_three, bias_three = down_back(grad_y)
    d_down_low = d_down.astype(jnp.bfloat16)
    grad_down = jnp.einsum("stf,std->fd", act_low, d_down_low, preferred_element_type=jnp.float32)
    d_act = jnp.einsum("std,fd->stf", d_down_low, full_down, preferred_element_type=jnp.float32)
    _, gelu_back = jax.vjp(gelu_tanh, up_proj)
    d_up_low = gelu_back(d_act)[0].astype(jnp.bfloat16)
    grad_up = jnp.einsum("std,stf->df", mid_low, d_up_low, preferred_element_type=jnp.float32)
    d_mid = jnp.einsum("stf,df->std", d_up_low, full_up, preferred_element_type=jnp.float32)
    _, mid_back = jax.vjp(layer_norm, hidden, gains[2], biases[2])
    d_hidden_mid, gain_two, bias_two = mid_back(d_mid)
    d_hidden = grad_y + d_hidden_mid
    _, proj_back = jax.vjp(layer_norm, proj, gains[1], biases[1])
    d_proj, gain_one, bias_one = proj_back(d_hidden)
    d_proj_low = d_proj.astype(jnp.bfloat16)
    grad_out = jnp.einsum(
        "std,ste->de", attended_low, d_proj_low, preferred_element_type=jnp.float32
    )
    d_att_low = (
        jnp.einsum("ste,de->std", d_proj_low, full_out, preferred_element_type=jnp.float32)
        .astype(jnp.bfloat16)
        .reshape(shape_heads)
    )
    delta = jnp.transpose(jnp.sum(d_att_low.astype(jnp.float32) * attended, -1), (0, 2, 1))

    def contribute(d_query, key_piece, value_piece, d_key, d_value, owner):
        key_pos = owner * row_count + jnp.arange(row_count)
        query_sum = d_query
        key_sum = d_key
        value_sum = d_value
        scores, allowed = block_scores(key_piece, key_pos)
        probs = jnp.where(allowed, jnp.exp(scores - log_sum[..., None]), 0.0)
        value_sum = value_sum + jnp.einsum(
            "shqk,sqhd->skhd",
            probs.astype(jnp.bfloat16),
            d_att_low,
            preferred_element_type=jnp.float32,
        )
        d_probs = jnp.einsum(
            "sqhd,skhd->shqk", d_att_low, value_piece, preferred_element_type=jnp.float32
        )
        d_scores = (probs * (d_probs - delta[..., None]) * scale).astype(jnp.bfloat16)
        query_sum = query_sum + jnp.einsum(
            "shqk,skhd->sqhd", d_scores, key_piece, preferred_element_type=jnp.float32
        )
        key_sum = key_sum + jnp.einsum(
            "shqk,sqhd->skhd", d_scores, query_low, preferred_element_type=jnp.float32
        )
        return (query_sum, key_sum, value_sum)

    zeros_heads = jnp.zeros(shape_heads, jnp.float32)

    def pass_grads(d_key, d_value):
        return (
            shifted(d_key.astype(jnp.bfloat16), "seq", 1).astype(d_key.dtype),
            shifted(d_value.astype(jnp.bfloat16), "seq", 1).astype(d_value.dtype),
        )

    def cycle_turn(turn_index, state):
        d_query, key_piece, value_piece, d_key, d_value = state
        owner = (cycle_index - turn_index) % cycle_size
        d_query, d_key, d_value = contribute(d_query, key_piece, value_piece, d_key, d_value, owner)
        d_key, d_value = pass_grads(d_key, d_value)
        key_piece, value_piece = passed_along((key_piece, value_piece), "seq", 1)
        return (d_query, key_piece, value_piece, d_key, d_value)

    d_query, key_piece, value_piece, d_key, d_value = lax.fori_loop(
        0, cycle_size - 1, cycle_turn, (zeros_heads, key_low, value_low, zeros_heads, zeros_heads)
    )
    last_owner = (cycle_index + 1) % cycle_size
    d_query, d_key, d_value = contribute(
        d_query, key_piece, value_piece, d_key, d_value, last_owner
    )
    d_key, d_value = pass_grads(d_key, d_value)
    flat_shape = (seq_count, row_count, model_width)
    d_qkv_low = jnp.concatenate(
        [
            rotate(d_query, position, -1.0).reshape(flat_shape),
            rotate(d_key, position, -1.0).reshape(flat_shape),
            d_value.reshape(flat_shape),
        ],
        -1,
    ).astype(jnp.bfloat16)
    grad_qkv = jnp.einsum("std,ste->de", normed_low, d_qkv_low, preferred_element_type=jnp.float32)
    d_normed = jnp.einsum("ste,de->std", d_qkv_low, full_qkv, preferred_element_type=jnp.float32)
    _, input_back = jax.vjp(layer_norm, x_float, gains[0], biases[0])
    d_input, gain_zero, bias_zero = input_back(d_normed)
    grad_tokens = d_hidden + d_input
    grad_gains = jnp.stack([gain_zero, gain_one, gain_two, gain_three])
    grad_biases = jnp.stack([bias_zero, bias_one, bias_two, bias_three])
    all_grads = (grad_qkv, grad_out, grad_up, grad_down, grad_gains, grad_biases)
    pieces = (
        lax.psum_scatter(
            all_grads[0].astype(jnp.bfloat16), "seq", scatter_dimension=0, tiled=True
        ).astype(jnp.float32),
        lax.psum_scatter(
            all_grads[1].astype(jnp.bfloat16), "seq", scatter_dimension=0, tiled=True
        ).astype(jnp.float32),
        lax.psum_scatter(
            all_grads[2].astype(jnp.bfloat16), "seq", scatter_dimension=0, tiled=True
        ).astype(jnp.float32),
        lax.psum_scatter(
            all_grads[3].astype(jnp.bfloat16), "seq", scatter_dimension=0, tiled=True
        ).astype(jnp.float32),
        lax.psum_scatter(
            all_grads[4].astype(jnp.bfloat16), "seq", scatter_dimension=1, tiled=True
        ).astype(jnp.float32),
        lax.psum_scatter(
            all_grads[5].astype(jnp.bfloat16), "seq", scatter_dimension=1, tiled=True
        ).astype(jnp.float32),
    )
    shards = (
        lax.psum(pieces[0].astype(jnp.bfloat16), "dp").astype(jnp.float32),
        lax.psum(pieces[1].astype(jnp.bfloat16), "dp").astype(jnp.float32),
        lax.psum(pieces[2].astype(jnp.bfloat16), "dp").astype(jnp.float32),
        lax.psum(pieces[3].astype(jnp.bfloat16), "dp").astype(jnp.float32),
        lax.psum(pieces[4].astype(jnp.bfloat16), "dp").astype(jnp.float32),
        lax.psum(pieces[5].astype(jnp.bfloat16), "dp").astype(jnp.float32),
    )
    return (output, grad_tokens, shards[0], shards[1], shards[2], shards[3], shards[4], shards[5])


def solution(mesh):
    placed = (
        P("dp", "seq", None),
        P("seq", None),
        P("seq", None),
        P("seq", None),
        P("seq", None),
        P(None, "seq"),
        P(None, "seq"),
        P("dp", "seq"),
        P(),
        P("dp", "seq", None),
    )
    fits = mesh.shape["seq"] == HEADS and mesh.shape["dp"] == 2
    return jax.shard_map(
        split_heads if fits else per_device,
        mesh=mesh,
        in_specs=placed,
        out_specs=(
            P("dp", "seq", None),
            P("dp", "seq", None),
            P("seq", None),
            P("seq", None),
            P("seq", None),
            P("seq", None),
            P(None, "seq"),
            P(None, "seq"),
        ),
        check_vma=False,
    )
```

```python
import functools
import math
import types

import jax
import jax.numpy as jnp
import numpy as np
from jax import lax
from jax.experimental import pallas as pl
from jax.experimental.pallas import tpu as pltpu
from jax.sharding import PartitionSpec as P

HEADS = 16
HEAD_DIM = 64
TILE = 256
MESH = pl.DeviceIdType.MESH
ANY = pl.BlockSpec(memory_space=pl.ANY)
DMA = pltpu.SemaphoreType.DMA
NT = ((1,), (1,))
TN = ((0,), (0,))
low, full = jnp.bfloat16, jnp.float32


def dot(left, right, contract=((1,), (0,))):
    return lax.dot_general(left, right, (contract, ((), ())), preferred_element_type=full)


def remote(source, target, send, recv, device):
    return pltpu.make_async_remote_copy(
        src_ref=source,
        dst_ref=target,
        send_sem=send,
        recv_sem=recv,
        device_id={"seq": device},
        device_id_type=MESH,
    )


def swap(source, target, send, recv):
    return pltpu.make_async_remote_copy(
        src_ref=source,
        dst_ref=target,
        send_sem=send,
        recv_sem=recv,
        device_id={"dp": 1 - lax.axis_index("dp")},
        device_id_type=MESH,
    )


class Ring:
    def __init__(self, length):
        self.me = lax.axis_index("seq")
        self.length = length
        self.chips = 2 * length
        self.steps = length
        self.core = self.me % 2
        column, row = (self.me // 2) % 2, self.me // 4
        self.first = (row // length) * length
        row = row - self.first
        self.base = self.first * 4
        self.place = row + column * (self.chips - 1 - 2 * row)
        self.right = self.device(1, self.core)
        self.left = self.device(-1, self.core)
        self.sibling = self.device(0, 1 - self.core)

    def device(self, ahead, core):
        place = (self.place + ahead + self.chips) % self.chips
        column = place // self.length
        row = place + column * (self.chips - 1 - 2 * place)
        return (self.first + row) * 4 + column * 2 + core


class Gather:
    def __init__(self, ring, piece, block, blocks, pieces, sems):
        self.ring, self.piece, self.block, self.blocks = ring, piece, block, blocks
        self.pieces = pieces
        self.send, self.recv, self.side_send, self.side_recv = sems
        self.messages = self.count(ring.chips, pieces)

    @staticmethod
    def count(chips, pieces):
        return pieces * (chips // 2) - pieces // 2

    def ref(self, way, j, ahead):
        k, q = j // self.pieces + ahead, j % self.pieces
        q = q if way == 0 else self.pieces - 1 - q
        return self.piece(self.ring.device(-k if way == 0 else k, self.ring.core), q)

    def hop(self, way, j):
        ref = self.ref(way, j, 0)
        target = self.ring.right if way == 0 else self.ring.left
        return remote(ref, ref, self.send.at[0], self.recv.at[way, j], target)

    def landed(self, way, j):
        return self.ref(way, j, 1)

    def side(self, ref, slot):
        return remote(ref, ref, self.side_send.at[0], self.side_recv.at[slot], self.ring.sibling)

    def start(self):
        for j in range(self.pieces):
            for way in range(2):
                self.hop(way, j).start()
        self.side(self.block(self.ring.me), 0).start()

    def pass_on(self, j):
        k = j // self.pieces + 1
        for way in range(2):
            self.hop(way, j).wait_recv()
            if j + self.pieces < self.messages:
                self.hop(way, j + self.pieces).start()
            slot = (-k if way == 0 else k) % self.ring.chips
            self.side(self.landed(way, j), slot).start()

    def wait_chip(self, ahead):
        block = self.block(self.ring.device(ahead, 1 - self.ring.core))
        self.side(block, ahead % self.ring.chips).wait_recv()

    def finish(self):
        count = self.ring.chips - 1
        everything = self.blocks(count)
        remote(everything, everything, self.send.at[0], self.recv.at[0, 0], self.ring.right).wait_send()
        self.side(self.blocks(count + 1), 0).wait_send()

    @staticmethod
    def sems(chips, pieces):
        return [DMA((1,)), DMA((2, Gather.count(chips, pieces))), DMA((1,)), DMA((chips,))]


class Scatter:
    def __init__(self, ring, parts, pieces, side, inbox, outbox, sems, shift=0):
        self.ring, self.parts, self.pieces = ring, parts, pieces
        self.base = ring.base - shift
        self.side, self.inbox, self.outbox = side, inbox, outbox
        self.send, self.recv, self.side_send, self.side_recv = sems
        self.messages = Gather.count(ring.chips, pieces)
        self.rows = parts.shape[1] // pieces
        self.waited = set()

    def across(self, ahead):
        slot = ahead % self.ring.chips
        return remote(
            self.parts.at[self.ring.device(ahead, 1 - self.ring.core) - self.base],
            self.side.at[slot],
            self.side_send.at[0],
            self.side_recv.at[slot],
            self.ring.sibling,
        )

    def hop(self, way, j):
        target = self.ring.right if way == 0 else self.ring.left
        return remote(
            self.outbox.at[way, j],
            self.inbox.at[way, j],
            self.send.at[0],
            self.recv.at[way, j],
            target,
        )

    def own(self, ahead, q):
        slot = ahead % self.ring.chips
        if slot not in self.waited:
            self.waited.add(slot)
            self.across(ahead).wait_recv()
        span = pl.ds(q * self.rows, self.rows)
        mine = self.parts[self.ring.device(ahead, self.ring.core) - self.base, span].astype(full)
        return mine + self.side[slot, span].astype(full)

    def ahead(self, j):
        return self.ring.steps - (j + self.pieces // 2) // self.pieces

    def step(self, j):
        for way in range(2):
            q = j % self.pieces if way == 0 else self.pieces - 1 - j % self.pieces
            total = self.own(self.ahead(j) if way == 0 else -self.ahead(j), q)
            if j >= self.pieces:
                self.hop(way, j - self.pieces).wait_recv()
                total += self.inbox[way, j - self.pieces].astype(full)
            self.outbox[way, j] = total.astype(self.outbox.dtype)
            self.hop(way, j).start()

    def result(self, q):
        total = self.own(0, q)
        for way in range(2):
            k = q if way == 0 else self.pieces - 1 - q
            last = max(j for j in range(self.messages) if j % self.pieces == k)
            self.hop(way, last).wait_recv()
            total += self.inbox[way, last].astype(full)
        return total

    def whole(self):
        return jnp.concatenate([self.result(q) for q in range(self.pieces)], 0)

    def finish(self):
        everything = self.parts.at[pl.ds(0, self.ring.chips)]
        side = self.side_send.at[0], self.side_recv.at[0]
        remote(everything, self.side, *side, self.ring.sibling).wait_send()
        hops = self.send.at[0], self.recv.at[0, 0]
        remote(self.outbox, self.inbox, *hops, self.ring.right).wait_send()

    @staticmethod
    def buffers(chips, rows, columns, pieces):
        box = pltpu.VMEM((2, Gather.count(chips, pieces), rows // pieces, columns), low)
        return [pltpu.VMEM((chips, rows, columns), low), box, box]

    @staticmethod
    def sems(chips, pieces):
        return [DMA((1,)), DMA((2, Gather.count(chips, pieces))), DMA((1,)), DMA((chips,))]


class Exchange:
    def __init__(self, source, target, blocks, sems):
        self.source, self.target, self.blocks = source, target, blocks
        self.send, self.recv = sems
        self.me, self.size = lax.axis_index("seq"), lax.axis_size("seq")

    def start(self):
        for i in sorted(range(1, self.size), key=lambda i: -abs(i - self.size // 2)):
            to = (self.me + i) % self.size
            remote(
                self.source(to), self.target(self.me), self.send.at[0], self.recv.at[0], to
            ).start()

    def all(self):
        ref = self.blocks(self.size - 1)
        to = (self.me + 1) % self.size
        return remote(ref, ref, self.send.at[0], self.recv.at[0], to)

    def wait(self):
        self.all().wait_recv()

    def finish(self):
        self.all().wait_send()


def normalized(values):
    center = values - jnp.mean(values, -1, keepdims=True)
    scale = lax.rsqrt(jnp.mean(center * center, -1, keepdims=True) + 1e-05)
    return center * scale, scale


def norm_back(grad, hat, scale, gain):
    d_hat = grad * gain
    mean = jnp.mean(d_hat, -1, keepdims=True)
    along = jnp.mean(d_hat * hat, -1, keepdims=True)
    return scale * (d_hat - mean - hat * along)


def gelu_and_slope(u):
    c = math.sqrt(2.0 / math.pi)
    square = u * u
    t = jnp.tanh(c * u * (1.0 + 0.044715 * square))
    act = 0.5 * u * (1.0 + t)
    slope = 0.5 * (1.0 + t) + 0.5 * u * (1.0 - t * t) * (c * (1.0 + 3 * 0.044715 * square))
    return act, slope


def causal(shape):
    key_pos = lax.broadcasted_iota(jnp.int32, shape, 0)
    query_pos = lax.broadcasted_iota(jnp.int32, shape, 1)
    return key_pos <= query_pos


def turn_tables(length):
    half = HEAD_DIM // 2
    freq = np.exp(
        np.arange(half, dtype=np.float32) * np.float32(-2.0 * math.log(10000.0) / HEAD_DIM)
    )
    angle = freq[:, None] * np.arange(length, dtype=np.float32)[None, :]
    return jnp.asarray(np.cos(angle)), jnp.asarray(np.sin(angle))


INPUTS = (
    "tokens",
    "w_qkv",
    "gains",
    "biases",
    "w_out",
    "w_up",
    "cos",
    "sin",
    "w_down",
    "cotangent",
    "corpus",
)
OUTPUTS = (
    "output",
    "grad_tokens",
    "grad_qkv",
    "grad_out",
    "grad_up",
    "grad_down",
    "grad_gains",
    "grad_biases",
)


def layer_kernel(names, *refs):
    r = types.SimpleNamespace(**dict(zip(names, refs, strict=True)))
    size = lax.axis_size("seq")
    ring, near = Ring(size // 4), Ring(size // 8)
    me, core, chips, steps = ring.me, ring.core, ring.chips, ring.steps
    far = (me + size // 2) % size
    close = size // 2
    dp = lax.axis_index("dp")
    rows, width = r.tokens.shape
    w_rows = r.w_out.shape[0]
    units = r.w_down.shape[0]
    length = rows * size
    near_length = rows * close
    tiles = length // TILE
    half = HEAD_DIM // 2
    kept = w_rows // 2
    packed = 3 * kept // 2
    pair = 2 * rows

    def mine(ref):
        return ref.at[:, pl.ds(dp * (ref.shape[1] // 2), ref.shape[1] // 2)]

    def theirs(ref):
        return ref.at[:, pl.ds((1 - dp) * (ref.shape[1] // 2), ref.shape[1] // 2)]

    def columns(device, count):
        return pl.ds(pl.multiple_of(device * count, count), count)

    loads = {
        name: pltpu.make_async_copy(getattr(r, name), getattr(r, name + "_v"), r.load_sem.at[i])
        for i, name in enumerate(INPUTS)
    }
    for name in INPUTS:
        loads[name].start()
    barrier = pltpu.get_barrier_semaphore()
    for i in range(1, size):
        pl.semaphore_signal(barrier, inc=1, device_id={"seq": (me + i) % size}, device_id_type=MESH)
    pl.semaphore_signal(barrier, inc=1, device_id={"dp": 1 - dp}, device_id_type=MESH)

    quarter = rows // 4

    def gather(ring, ref, count, sems, first=0, shift=0):
        pieces = 4 if ref.shape[1] == rows else 2
        shift = shift - ring.base
        return Gather(
            ring,
            lambda d, q: ref.at[d + shift, pl.ds(first + q * (count // pieces), count // pieces)],
            lambda d: ref.at[d + shift, pl.ds(first, count)],
            lambda n: ref.at[pl.ds(0, n), pl.ds(0, count)],
            pieces,
            sems,
        )

    mid_place, dd_place = me - near.base, me - near.base + close
    other = close - near.base
    tokens_in = gather(near, r.big, rows, r.gather2, shift=near.base)
    tokens_far = gather(near, r.big, rows, r.gather0, shift=other)

    def over(q):
        ref = r.big.at[me, pl.ds(q * (rows // 4), rows // 4)]
        return remote(ref, ref, r.over_send.at[q], r.over_recv.at[q], far)

    def over_again(q):
        over(q).wait_recv()
        tokens_far.hop(0, q).start()
        tokens_far.hop(1, 3 - q).start()

    mids = gather(near, r.big, rows, r.gather2)
    d_downs = gather(near, r.big, rows, r.gather2, shift=close)
    w_outs = gather(ring, r.w_out_all, kept, r.gather1, dp * kept)
    boxes = [(r.side[i], r.inbox[i], r.outbox[i], (r.scatter0, r.scatter1)[i]) for i in range(2)]
    sum_down = Scatter(near, r.parts, 4, *boxes[0])
    sum_mid = Scatter(near, r.parts, 4, *boxes[0])
    sum_out = Scatter(near, r.out_parts, 4, *boxes[1])
    sum_in = Scatter(ring, r.parts, 4, r.in_side, r.in_inbox, r.in_outbox, r.scatter2)
    out_over = remote(r.out_send, r.out_recv, r.far_sems.at[8], r.far_sems.at[9], far)

    def exchange(source, ref, sems, count):
        return Exchange(
            source,
            lambda d: ref.at[d, pl.ds(dp * count if count < ref.shape[1] else 0, count)],
            lambda n: ref.at[pl.ds(0, n), pl.ds(0, count)],
            sems,
        )

    head_weights = exchange(lambda d: r.head_send.at[d], r.head_recv, r.exchange0, packed)
    norm_rows = exchange(lambda d: r.norm_send, r.norm_recv, r.exchange1, 8)

    def up_exchange(ref, sems, shift):
        return exchange(
            lambda d: r.w_up_v.at[pl.ds(dp * kept, kept), columns((d + shift) % size, units)],
            ref,
            sems,
            kept,
        )

    up_weights = up_exchange(r.w_up_all, r.exchange2, 0)
    up_weights_far = up_exchange(r.w_up_far, r.exchange6, size // 2)
    d_atts = exchange(lambda d: r.d_att.at[d], r.att_recv, r.exchange3, HEAD_DIM)
    up_grads = exchange(lambda d: r.up_send[0].at[d], r.up_recv[0], r.exchange4, kept)
    up_grads_far = exchange(lambda d: r.up_send[1].at[d], r.up_recv[1], r.exchange7, kept)
    head_grads = exchange(lambda d: r.head_send.at[d], r.head_all, r.exchange5, packed)

    def swapped(source, target, slot):
        return swap(source, target, r.swap_send.at[slot], r.swap_recv.at[slot])

    head_other = swapped(mine(r.head_recv), mine(r.head_recv), 0)
    up_other = swapped(mine(r.w_up_all), mine(r.w_up_all), 1)
    up_other_far = swapped(mine(r.w_up_far), mine(r.w_up_far), 8)
    units_mine = pl.ds(dp * (units // 2), units // 2)
    units_theirs = pl.ds((1 - dp) * (units // 2), units // 2)
    down_far = remote(
        r.w_down_v.at[units_mine],
        r.w_down_far.at[units_mine],
        r.far_sems.at[0],
        r.far_sems.at[1],
        far,
    )
    down_other_far = swapped(r.w_down_far.at[units_mine], r.w_down_far.at[units_mine], 9)
    up_half = [swapped(theirs(r.up_grad[b]), r.up_peer[b], 2 + 8 * b) for b in range(2)]
    down_half = [
        swapped(r.down_grad[b].at[units_theirs], r.down_peer[b], 3 + 8 * b) for b in range(2)
    ]
    down_back_far = remote(r.down_send, r.down_recv, r.far_sems.at[2], r.far_sems.at[3], far)
    down_back = swapped(r.down_sum.at[units_mine], r.down_sum.at[units_mine], 12)
    out_whole = swapped(r.out_mine, r.out_peer, 4)
    up_back = swapped(mine(r.up_all), mine(r.up_all), 5)
    head_half = swapped(theirs(r.head_parts), r.head_peer, 6)
    head_back = swapped(mine(r.head_all), mine(r.head_all), 7)

    loads["w_qkv"].wait()
    rows_mine = pl.ds(dp * kept, kept)
    for h in range(HEADS):
        q, k, v = (
            r.w_qkv_v[rows_mine, i * width + h * HEAD_DIM : i * width + (h + 1) * HEAD_DIM]
            for i in range(3)
        )
        r.head_send[h, 0:kept] = jnp.concatenate([q, k], 1)
        r.head_send[h, kept:packed] = jnp.concatenate([v[: kept // 2], v[kept // 2 :]], 1)
    r.head_recv[me, pl.ds(dp * packed, packed)] = r.head_send[me]
    loads["gains"].wait()
    loads["biases"].wait()
    r.norm_send[...] = jnp.zeros_like(r.norm_send)
    r.norm_send[0:4, 0:w_rows] = r.gains_v[...].astype(full)
    r.norm_send[4:8, 0:w_rows] = r.biases_v[...].astype(full)
    r.norm_recv[me] = r.norm_send[...]
    loads["tokens"].wait()
    r.big[me] = r.tokens_v[...]
    pl.semaphore_wait(barrier, size)
    tokens_in.start()
    for q in (0, 3, 1, 2):
        over(q).start()
    norm_rows.start()
    head_weights.start()

    def gain(i):
        return r.norms[i : i + 1, :]

    def bias(i):
        return r.norms[4 + i : 5 + i, :]

    loads["w_out"].wait()
    r.w_out_all[me] = r.w_out_v[...]
    loads["w_up"].wait()
    r.w_up_all[me, rows_mine] = r.w_up_v[rows_mine, columns(me, units)]
    r.w_up_far[me, rows_mine] = r.w_up_v[rows_mine, columns(far, units)]
    loads["cos"].wait()
    loads["sin"].wait()
    for name in ("w_down", "cotangent", "corpus"):
        loads[name].wait()

    def unpack_heads():
        head_other.wait_recv()
        for j in range(size // 2):
            span = pl.ds(j * 2 * w_rows, 2 * w_rows)
            qk, v = [], []
            for d in (2 * j, 2 * j + 1):
                for h in range(2):
                    p = r.head_recv[d, h * packed : (h + 1) * packed]
                    qk.append(p[:kept])
                    v += [p[kept:, :HEAD_DIM], p[kept:, HEAD_DIM:]]
            r.w_t[0 : 2 * HEAD_DIM, span] = jnp.concatenate(qk, 0).astype(full).T.astype(low)
            r.w_t[2 * HEAD_DIM :, span] = jnp.concatenate(v, 0).astype(full).T.astype(low)

    def project(ahead, shift=0):
        base = near.device(ahead, 0) + shift
        x = r.big[pl.ds(base, 2)].reshape(pair, width).astype(full)
        hat, _ = normalized(x)
        normed = (hat * gain(0) + bias(0)).astype(low)
        r.normed_all[pl.ds(base, 2)] = normed.reshape(2, rows, width)
        qkv = dot(r.w_t[...], normed, NT)
        span = pl.ds(pl.multiple_of(base * rows, pair), pair)
        c, s = r.cos_v[:, span], r.sin_v[:, span]
        for i, (ref, nat, scale) in enumerate(
            ((r.q_t, r.q_nat, HEAD_DIM**-0.5), (r.k_t, r.k_nat, 1.0))
        ):
            first = qkv[i * HEAD_DIM : i * HEAD_DIM + half]
            second = qkv[i * HEAD_DIM + half : (i + 1) * HEAD_DIM]
            turned = jnp.concatenate([first * c - second * s, first * s + second * c], 0) * scale
            ref[:, span] = turned.astype(low)
            nat[span, :] = turned.T.astype(low)
        v = qkv[2 * HEAD_DIM :]
        r.v_t[:, span] = v.astype(low)
        r.v_nat[span, :] = v.T.astype(low)

    def out_swap(ref, way, j):
        return swap(ref, ref, r.out_swap_send.at[0], r.out_swap_recv.at[way, j])

    def out_other(way, j):
        k, q = j // 2 + 1, j % 2
        q = q if way == 0 else 1 - q
        device = ring.device(-k if way == 0 else k, core)
        return r.w_out_all.at[device, pl.ds((1 - dp) * kept + q * (kept // 2), kept // 2)]

    def out_side(ref, slot):
        send, recv = r.out_side_send.at[slot], r.out_side_recv.at[slot]
        return remote(ref, ref, send, recv, ring.sibling)

    def out_own():
        return out_side(r.w_out_all.at[me, pl.ds((1 - dp) * kept, kept)], 0)

    def out_others():
        return out_side(w_outs.blocks(chips - 1), 1)

    def pass_out(j):
        w_outs.pass_on(j)
        for way in range(2):
            out_swap(w_outs.landed(way, j), way, j).start()

    def pass_other(j):
        for way in range(2):
            ref = out_other(way, j)
            out_swap(ref, way, j).wait_recv()
            out_side(ref, 1).start()

    tokens_in.pass_on(0)
    tokens_in.pass_on(1)
    over_again(0)
    tokens_in.pass_on(2)
    tokens_in.pass_on(3)
    norm_rows.wait()
    for j in range(size // 2):
        r.norms[:, j * 128 : (j + 1) * 128] = jnp.concatenate(
            [r.norm_recv[2 * j][:, :w_rows], r.norm_recv[2 * j + 1][:, :w_rows]], 1
        )
    head_weights.wait()
    head_other.start()
    over_again(3)
    for j in range(4, 6):
        tokens_in.pass_on(j)
    over_again(1)
    over_again(2)
    tokens_far.side(tokens_far.block(me), 0).start()
    w_outs.start()
    out_own().start()
    up_weights.start()
    up_weights_far.start()
    down_far.start()
    tokens_far.pass_on(0)
    tokens_far.pass_on(1)
    unpack_heads()
    for ahead in (0, 1, -1):
        tokens_in.wait_chip(ahead)
        project(ahead)
    tokens_far.pass_on(2)
    tokens_far.pass_on(3)
    pass_out(0)
    pass_out(1)
    tokens_in.wait_chip(2)
    project(2)
    for ahead in (0, 1, -1):
        tokens_far.wait_chip(ahead)
        project(ahead, other - near.base)
    for j in range(4, 6):
        tokens_far.pass_on(j)
    tokens_far.wait_chip(2)
    project(2, other - near.base)
    tokens_in.finish()
    tokens_far.finish()
    for q in range(4):
        over(q).wait_send()
    pass_out(2)
    pass_out(3)
    pass_other(0)
    pass_other(1)

    for t in range(tiles):
        span = pl.ds(t * TILE, TILE)
        query = r.q_t[:, span]
        top = None
        for j in range(t + 1):
            keys = pl.ds(j * TILE, TILE)
            s = dot(r.k_nat[keys, :], query)
            if j == t:
                s = jnp.where(causal(s.shape), s, -1e30)
            r.scores[keys, :] = s
            here = jnp.max(s, 0, keepdims=True)
            top = here if top is None else jnp.maximum(top, here)
        acc, norm = None, None
        for j in range(t + 1):
            keys = pl.ds(j * TILE, TILE)
            p = jnp.exp(r.scores[keys, :] - top)
            here = jnp.sum(p, 0, keepdims=True)
            add = dot(r.v_t[:, keys], p.astype(low))
            acc = add if acc is None else acc + add
            norm = here if norm is None else norm + here
        acc = acc / norm
        r.total[:, span] = acc
        r.lse[:, span] = top + jnp.log(norm)
        for b in range(TILE // rows):
            to = t * (TILE // rows) + b
            block = acc[:, b * rows : (b + 1) * rows].astype(low)
            r.att_send[to] = block

            @pl.when(me != to)
            def _(to=to):
                remote(
                    r.att_send.at[to], r.att_t.at[me], r.att_ssem.at[0], r.att_rsem.at[0], to
                ).start()

            @pl.when(me == to)
            def _(block=block):
                r.att_t[me] = block

        if t == 4:
            pass_out(4)
            pass_out(5)
            up_weights.wait()
            up_other.start()
            pass_other(2)
            pass_other(3)
        if t == 6:
            pass_out(6)
            up_weights_far.wait()
            up_other_far.start()
            pass_other(4)
            pass_other(5)
    pass_other(6)
    for ahead in range(chips):
        w_outs.wait_chip(ahead)
    out_own().wait_recv()
    out_others().wait_recv()
    attended = r.att_t.at[pl.ds(0, size - 1)]
    attended = remote(attended, attended, r.att_ssem.at[0], r.att_rsem.at[0], ring.right)
    down_far.wait_recv()
    down_other_far.start()
    attended.wait()

    att_t = r.att_t[...].reshape(width, rows)
    w_out_all = r.w_out_all
    proj = dot(att_t, w_out_all[...].reshape(width, width), TN)
    r.proj[...] = proj
    hat1, _ = normalized(proj)
    hidden = r.tokens_v[...].astype(full) + hat1 * gain(1) + bias(1)
    r.hidden[...] = hidden
    hat2, _ = normalized(hidden)
    r.big[mid_place] = (hat2 * gain(2) + bias(2)).astype(low)
    mids.start()
    w_outs.finish()

    def weights(b):
        up, down = ((r.w_up_all, r.w_down_v), (r.w_up_far, r.w_down_far))[b]
        return up[...].reshape(width, units), down[...]

    def forward(ahead):
        place = pl.ds(near.device(ahead, 0) - near.base, 2)
        x = r.big[place].reshape(pair, width)
        part = None
        for b in range(2):
            w_up, w_down = weights(b)
            act, slope = gelu_and_slope(dot(x, w_up))
            act = act.astype(low)
            r.act_all[b, place] = act.reshape(2, rows, units)
            r.slope_all[b, place] = slope.reshape(2, rows, units)
            add = dot(act, w_down)
            part = add if part is None else part + add
        r.parts[place] = part.astype(low).reshape(2, rows, width)
        sum_down.across(ahead).start()

    def backward(ahead):
        place = pl.ds(near.device(ahead, 0) - near.base, 2)
        x = r.big[pl.ds(near.device(ahead, 0) - near.base + close, 2)].reshape(pair, width)
        part = None
        for b in range(2):
            w_up, w_down = weights(b)
            d_act = dot(x, w_down, NT)
            d_up = (d_act * r.slope_all[b, place].reshape(pair, units)).astype(low)
            r.d_up_all[b, place] = d_up.reshape(2, rows, units)
            add = dot(d_up, w_up, NT)
            part = add if part is None else part + add
        r.parts[place] = part.astype(low).reshape(2, rows, width)
        sum_mid.across(ahead).start()

    def there_and_back(gather, scatter, ready, work, fill):
        last = near.steps
        for k in range(1, last + 1):
            if k == last:
                ready()
                gather.wait_chip(0)
                work(0)
                for ahead in range(1, last):
                    for chip in (ahead, -ahead):
                        gather.wait_chip(chip)
                        work(chip)
                scatter.step(2)
                scatter.step(3)
            for j in range(4 * (k - 1), min(4 * k, gather.messages)):
                gather.pass_on(j)
        gather.wait_chip(last)
        work(last)
        scatter.step(0)
        scatter.step(1)
        for j in range(4, scatter.messages):
            fill(j)
            scatter.step(j)
        fill(scatter.messages)

    def weights_here():
        up_other.wait_recv()
        up_other_far.wait_recv()
        down_other_far.wait_recv()

    there_and_back(mids, sum_down, weights_here, forward, lambda j: None)

    weight_row = jnp.zeros((1, rows), full)
    for c in range(r.weight.shape[0]):
        weight_row += jnp.where(r.corpus_v[...] == c, r.weight[c], 0.0)
    row_weight = jnp.broadcast_to(weight_row, (rows, rows)).T[:, 0:1]
    for q in range(4):
        span = pl.ds(q * quarter, quarter)
        down = sum_down.result(q)
        hat3, scale3 = normalized(down)
        r.output_v[span, :] = (r.hidden[span, :] + hat3 * gain(3) + bias(3)).astype(low)
        grad_y = r.cotangent_v[span, :].astype(full) * row_weight[q * quarter : (q + 1) * quarter]
        r.d_hidden[span, :] = grad_y
        r.big[dd_place, span] = norm_back(grad_y, hat3, scale3, gain(3)).astype(low)
        g3 = jnp.sum(grad_y * hat3, 0, keepdims=True)
        b3 = jnp.sum(grad_y, 0, keepdims=True)
        r.norm_grads[3:4, :] = g3 if q == 0 else r.norm_grads[3:4, :] + g3
        r.norm_grads[7:8, :] = b3 if q == 0 else r.norm_grads[7:8, :] + b3
    mids.finish()
    sum_down.finish()
    d_downs.start()
    saves = {}

    def save(name):
        i = OUTPUTS.index(name)
        saves[name] = pltpu.make_async_copy(
            getattr(r, name + "_v"), getattr(r, name), r.save_sem.at[i]
        )
        saves[name].start()

    save("output")

    def up_gradient(b):
        d_up = r.d_up_all[b].reshape(near_length, units)
        blocks = size // 4
        for i in range(4):
            span = pl.ds(i * (width // 4), width // 4)
            x = r.big[:close, :, span].reshape(near_length, width // 4)
            grad = dot(d_up, x, TN).T.astype(low)
            r.up_grad[b][i * blocks : (i + 1) * blocks] = grad.reshape(blocks, w_rows, units)
        up_half[b].start()

    def down_gradient(b):
        act = r.act_all[b].reshape(near_length, units)
        for i in range(4):
            span = pl.ds(i * (width // 4), width // 4)
            dd = r.big[close:, :, span].reshape(near_length, width // 4)
            r.down_grad[b][:, span] = dot(act, dd, TN).astype(low)
        down_half[b].start()

    def fill(j):
        if j < 6:
            up_gradient(j - 4)

    there_and_back(d_downs, sum_mid, lambda: None, backward, fill)

    hat1, scale1 = normalized(r.proj[...])
    hat2, scale2 = normalized(r.hidden[...])
    hat0, scale0 = normalized(r.tokens_v[...].astype(full))
    r.hat0[...] = hat0
    d_mid = sum_mid.whole()
    r.norm_grads[2:3, :] = jnp.sum(d_mid * hat2, 0, keepdims=True)
    r.norm_grads[6:7, :] = jnp.sum(d_mid, 0, keepdims=True)
    d_hidden = r.d_hidden[...] + norm_back(d_mid, hat2, scale2, gain(2))
    r.d_hidden[...] = d_hidden
    r.norm_grads[1:2, :] = jnp.sum(d_hidden * hat1, 0, keepdims=True)
    r.norm_grads[5:6, :] = jnp.sum(d_hidden, 0, keepdims=True)
    d_proj = norm_back(d_hidden, hat1, scale1, gain(1)).astype(low)
    d_att = dot(w_out_all[...].reshape(width, width), d_proj, NT).astype(low)
    r.d_att[...] = d_att.reshape(HEADS, HEAD_DIM, rows)
    d_atts.start()

    out = dot(att_t, d_proj).astype(low).reshape(size, w_rows, width)
    r.out_parts[:, :w_rows] = out[:close]
    r.out_parts[:, w_rows:] = out[close:]
    for ahead in range(near.chips):
        sum_out.across(ahead).start()
    r.att_recv[me] = r.d_att[me]
    d_downs.finish()
    sum_mid.finish()
    r.dq[...] = jnp.zeros_like(r.dq)
    for b in (1, 0):
        down_gradient(b)
    for b in range(2):
        up_half[b].wait_recv()
        up_mine = r.up_grad[b][:, rows_mine].astype(full)
        r.up_send[b][...] = (up_mine + r.up_peer[b][...].astype(full)).astype(low)
        r.up_recv[b][me] = r.up_send[b][me]
        (up_grads, up_grads_far)[b].start()
    for j in range(4):
        sum_out.step(j)
    d_atts.wait()
    for b in range(size):
        r.do_t[:, b * rows : (b + 1) * rows] = r.att_recv[b]
    for t in range(tiles):
        span = pl.ds(t * TILE, TILE)
        do = r.do_t[:, span].astype(full)
        r.do_nat[span, :] = do.T.astype(low)
        r.delta[:, span] = jnp.sum(do * r.total[:, span], 0, keepdims=True)

    def turned_back(u, span, base):
        c, s = r.cos_v[:, span], r.sin_v[:, span]
        first, second = u[:half], u[half:]
        r.d_t[base : base + half, span] = (first * c + second * s).astype(low)
        r.d_t[base + half : base + 2 * half, span] = (second * c - first * s).astype(low)

    high = near.base // close
    out_own_rows, out_far_rows = pl.ds(high * w_rows, w_rows), pl.ds((1 - high) * w_rows, w_rows)

    def beside_attention(j):
        if j in (0, 1):
            sum_out.step(4 + j)
        if j == 1:
            down_half[1].wait_recv()
            down_mine = r.down_grad[1][units_mine].astype(full)
            r.down_send[...] = (down_mine + r.down_peer[1][...].astype(full)).astype(low)
            down_back_far.start()
        if j == 3:
            r.out_sum[...] = sum_out.whole()
            r.out_send[...] = r.out_sum[out_far_rows].astype(low)
            out_over.start()

    def collect_up():
        up_grads.wait()
        up_grads_far.wait()
        for h in range(size):
            both = r.up_recv[0][h].astype(full) + r.up_recv[1][(h + close) % size].astype(full)
            r.up_all[h, rows_mine] = both.astype(low)
        up_back.start()

    def collect_out():
        out_over.wait_recv()
        r.out_mine[...] = (r.out_sum[out_own_rows] + r.out_recv[...].astype(full)).astype(low)
        out_whole.start()

    def collect_down():
        down_half[0].wait_recv()
        down_back_far.wait_recv()
        both = r.down_grad[0][units_mine].astype(full) + r.down_peer[0][...].astype(full)
        r.down_sum[units_mine] = (both + r.down_recv[...].astype(full)).astype(low)
        down_back.start()

    for j in range(tiles):
        keys = pl.ds(j * TILE, TILE)
        dk, dv = None, None
        for t in range(j, tiles):
            span = pl.ds(t * TILE, TILE)
            s = dot(r.k_nat[keys, :], r.q_t[:, span])
            p = jnp.exp(s - r.lse[:, span])
            if j == t:
                p = jnp.where(causal(p.shape), p, 0.0)
            d_p = dot(r.v_nat[keys, :], r.do_t[:, span])
            d_s = (p * (d_p - r.delta[:, span])).astype(low)
            dv_add = dot(p.astype(low), r.do_nat[span, :])
            dk_add = dot(d_s, r.q_nat[span, :])
            dv = dv_add if dv is None else dv + dv_add
            dk = dk_add if dk is None else dk + dk_add
            r.dq[:, span] += dot(r.k_t[:, keys], d_s)
        turned_back(dk.T, keys, HEAD_DIM)
        r.d_t[2 * HEAD_DIM :, keys] = dv.T.astype(low)
        turned_back(r.dq[:, keys] * HEAD_DIM**-0.5, keys, 0)
        beside_attention(j)

    def part(ahead):
        base = ring.device(ahead, 0)
        span = pl.ds(pl.multiple_of(base * rows, pair), pair)
        d_x = dot(r.d_t[:, span], r.w_t[...], TN).astype(low)
        r.parts[pl.ds(base, 2)] = d_x.reshape(2, rows, width)
        sum_in.across(ahead).start()

    def head_gradient(j):
        x = r.normed_all[:, :, j * 128 : (j + 1) * 128].reshape(length, 128)
        d_w = dot(r.d_t[...], x).T
        for i in range(2):
            for h in range(2):
                base = i * w_rows + h * kept
                block = d_w[base : base + kept]
                v = block[:, 2 * HEAD_DIM :]
                v = jnp.concatenate([v[: kept // 2], v[kept // 2 :]], 1)
                at = h * packed
                r.head_parts[2 * j + i, at : at + kept] = block[:, : 2 * HEAD_DIM].astype(low)
                r.head_parts[2 * j + i, at + kept : at + packed] = v.astype(low)

    part(steps)
    part(steps - 1)
    part(1 - steps)
    for j in range(4):
        sum_in.step(j)
    for j in range(size // 2):
        head_gradient(j)
    head_weights.finish()
    head_half.start()
    for k in range(steps - 2, 0, -1):
        part(k)
        part(-k)
    part(0)
    sum_in.step(4)
    sum_in.step(5)
    for j in range(6, 8):
        sum_in.step(j)
    head_half.wait_recv()
    own_half = r.head_parts[:, pl.ds(dp * packed, packed)].astype(full)
    r.head_send[...] = (own_half + r.head_peer[...].astype(full)).astype(low)
    r.head_all[me, pl.ds(dp * packed, packed)] = r.head_send[me]
    head_grads.start()
    collect_up()
    collect_out()
    for j in range(8, 10):
        sum_in.step(j)
    for j in range(10, 12):
        sum_in.step(j)
    collect_down()
    for j in range(12, 14):
        sum_in.step(j)
    out_whole.wait_recv()
    r.grad_out_v[...] = r.out_mine[...].astype(full) + r.out_peer[...].astype(full)
    save("grad_out")
    d_normed = sum_in.whole()
    up_back.wait_recv()
    for h in range(size):
        r.grad_up_v[:, h * units : (h + 1) * units] = r.up_all[h].astype(full)
    save("grad_up")
    down_back.wait_recv()
    r.grad_down_v[...] = r.down_sum[...].astype(full)
    save("grad_down")
    head_grads.wait()
    head_back.start()

    hat0 = r.hat0[...]
    r.norm_grads[0:1, :] = jnp.sum(d_normed * hat0, 0, keepdims=True)
    r.norm_grads[4:5, :] = jnp.sum(d_normed, 0, keepdims=True)

    def norm_copy(i, other):
        to = (me + i) % size
        return pltpu.make_async_remote_copy(
            src_ref=r.norm_grads.at[:, columns(to // 2, 128)],
            dst_ref=r.norm_sums.at[2 * i + other],
            send_sem=r.norm_ssem.at[0],
            recv_sem=r.norm_rsem.at[0],
            device_id={"seq": to, "dp": (dp + other) % 2},
            device_id_type=MESH,
        )

    partners = [(i, other) for i in range(size) for other in range(2) if i or other]
    for i, other in partners:
        norm_copy(i, other).start()
    r.norm_sums[0] = r.norm_grads[:, columns(me // 2, 128)]
    _, scale0 = normalized(r.tokens_v[...].astype(full))
    r.grad_tokens_v[...] = r.d_hidden[...] + norm_back(d_normed, hat0, scale0, gain(0))
    save("grad_tokens")
    head_back.wait_recv()
    for h in range(2):
        for j in range(size // 2):
            blocks = [
                r.head_all[2 * j + i, h * packed : (h + 1) * packed].astype(full) for i in range(2)
            ]
            span = slice(h * kept, (h + 1) * kept)
            for b in range(2):
                place = slice(b * width + j * 128, b * width + (j + 1) * 128)
                r.grad_qkv_v[span, place] = jnp.concatenate(
                    [p[:kept, b * HEAD_DIM : (b + 1) * HEAD_DIM] for p in blocks], 1
                )
            v = [jnp.concatenate([p[kept:, :HEAD_DIM], p[kept:, HEAD_DIM:]], 0) for p in blocks]
            place = slice(2 * width + j * 128, 2 * width + (j + 1) * 128)
            r.grad_qkv_v[span, place] = jnp.concatenate(v, 1)
    save("grad_qkv")
    norm_all = r.norm_sums.at[pl.ds(1, 2 * size - 1)]
    norm_all = swap(norm_all, norm_all, r.norm_ssem.at[0], r.norm_rsem.at[0])
    norm_all.wait_recv()
    sums = jnp.sum(r.norm_sums[...], 0)
    sums = jnp.where(core == 0, sums[:, :w_rows], sums[:, w_rows:])
    r.grad_gains_v[...] = sums[0:4]
    r.grad_biases_v[...] = sums[4:8]
    save("grad_gains")
    save("grad_biases")

    norm_all.wait_send()
    sum_in.finish()
    sum_out.finish()
    for moved in (
        norm_rows, up_weights, up_weights_far, d_atts, up_grads, up_grads_far, head_grads
    ):
        moved.finish()
    for copy in (
        head_other,
        up_other,
        up_other_far,
        down_far,
        down_other_far,
        *up_half,
        *down_half,
        down_back_far,
        down_back,
        out_over,
        out_whole,
        up_back,
        head_half,
        head_back,
    ):
        copy.wait_send()
    out_own().wait_send()
    out_others().wait_send()
    out_swap(w_outs.blocks(chips - 1), 0, 0).wait_send()
    for copy in saves.values():
        copy.wait()


def hand_over_kernel(count, *refs):
    ins, outs, held = (refs[i * count : (i + 1) * count] for i in range(3))
    sems = refs[-1]
    loads = [pltpu.make_async_copy(ins[i], held[i], sems.at[0, i]) for i in range(count)]
    saves = [pltpu.make_async_copy(held[i], outs[i], sems.at[1, i]) for i in range(count)]
    for copy in loads:
        copy.start()
    for load, copy in zip(loads, saves):
        load.wait()
        copy.start()
    for copy in saves:
        copy.wait()


def hand_over(arrays):
    count = len(arrays)
    return pl.pallas_call(
        functools.partial(hand_over_kernel, count),
        out_shape=[jax.ShapeDtypeStruct(a.shape, a.dtype) for a in arrays],
        in_specs=[ANY] * count,
        out_specs=[ANY] * count,
        scratch_shapes=[pltpu.VMEM(a.shape, a.dtype) for a in arrays] + [DMA((2, count))],
    )(*arrays)


def split_heads(
    tokens, w_qkv, w_out, w_up, w_down, norm_gains, norm_biases, corpus_id, corpus_weight, cotangent
):
    size = lax.axis_size("seq")
    chips = size // 2
    _, rows, width = tokens.shape
    w_rows = w_out.shape[0]
    units = w_down.shape[0]
    length = rows * size
    shape = jax.ShapeDtypeStruct
    cos, sin = turn_tables(length)
    inputs = dict(
        tokens=tokens[0],
        w_qkv=w_qkv,
        w_out=w_out,
        w_up=w_up,
        w_down=w_down,
        gains=norm_gains,
        biases=norm_biases,
        corpus=corpus_id,
        cotangent=cotangent[0],
        cos=cos,
        sin=sin,
    )
    outputs = dict(
        output=shape((rows, width), low),
        grad_tokens=shape((rows, width), full),
        grad_qkv=shape((w_rows, 3 * width), full),
        grad_out=shape((w_rows, width), full),
        grad_up=shape((w_rows, size * units), full),
        grad_down=shape((units, width), full),
        grad_gains=shape((4, w_rows), full),
        grad_biases=shape((4, w_rows), full),
    )

    def vmem(*dims, kind=low):
        return pltpu.VMEM(dims, kind)

    head_rows = 3 * w_rows // 2
    blocks = vmem(size, rows, width)
    nat, turned = vmem(length, HEAD_DIM), vmem(HEAD_DIM, length)
    side, inbox, outbox = Scatter.buffers(chips, rows, width, 4)
    side, inbox, outbox = Scatter.buffers(chips // 2, rows, width, 4)
    in_side, in_inbox, in_outbox = Scatter.buffers(chips, rows, width, 4)
    scratch = {name + "_v": vmem(*a.shape, kind=a.dtype) for name, a in inputs.items()}
    scratch |= {name + "_v": vmem(*a.shape, kind=a.dtype) for name, a in outputs.items()}
    scratch |= dict(
        big=blocks,
        normed_all=blocks,
        parts=blocks,
        side=[side] * 2,
        inbox=[inbox] * 2,
        outbox=[outbox] * 2,
        in_side=in_side,
        in_inbox=in_inbox,
        in_outbox=in_outbox,
        out_parts=vmem(size // 2, 2 * w_rows, width),
        out_sum=vmem(2 * w_rows, width, kind=full),
        out_send=vmem(w_rows, width),
        out_recv=vmem(w_rows, width),
        out_mine=vmem(w_rows, width),
        out_peer=vmem(w_rows, width),
        w_out_all=vmem(size, w_rows, width),
        w_up_all=vmem(size, w_rows, units),
        w_up_far=vmem(size, w_rows, units),
        w_down_far=vmem(units, width),
        w_t=vmem(3 * HEAD_DIM, width),
        head_send=vmem(size, head_rows // 2, 128),
        head_recv=vmem(size, head_rows, 128),
        head_parts=vmem(size, head_rows, 128),
        head_peer=vmem(size, head_rows // 2, 128),
        head_all=vmem(size, head_rows, 128),
        norm_send=vmem(8, 128, kind=full),
        norm_recv=vmem(size, 8, 128, kind=full),
        norms=vmem(8, width, kind=full),
        norm_grads=vmem(8, width, kind=full),
        norm_sums=vmem(2 * size, 8, 128, kind=full),
        q_t=turned,
        k_t=turned,
        v_t=turned,
        do_t=turned,
        q_nat=nat,
        k_nat=nat,
        v_nat=nat,
        do_nat=nat,
        total=vmem(HEAD_DIM, length, kind=full),
        dq=vmem(HEAD_DIM, length, kind=full),
        d_t=vmem(3 * HEAD_DIM, length),
        lse=vmem(1, length, kind=full),
        delta=vmem(1, length, kind=full),
        scores=vmem(length, TILE, kind=full),
        att_send=vmem(size, HEAD_DIM, rows),
        att_t=vmem(size, HEAD_DIM, rows),
        d_att=vmem(size, HEAD_DIM, rows),
        att_recv=vmem(size, HEAD_DIM, rows),
        proj=vmem(rows, width, kind=full),
        hidden=vmem(rows, width, kind=full),
        d_hidden=vmem(rows, width, kind=full),
        hat0=vmem(rows, width, kind=full),
        act_all=vmem(2, size // 2, rows, units),
        slope_all=vmem(2, size // 2, rows, units, kind=full),
        d_up_all=vmem(2, size // 2, rows, units),
        up_grad=[vmem(size, w_rows, units)] * 2,
        up_peer=[vmem(size, w_rows // 2, units)] * 2,
        up_send=[vmem(size, w_rows // 2, units)] * 2,
        up_recv=[vmem(size, w_rows // 2, units)] * 2,
        up_all=vmem(size, w_rows, units),
        down_grad=[vmem(units, width)] * 2,
        down_peer=[vmem(units // 2, width)] * 2,
        down_send=vmem(units // 2, width),
        down_recv=vmem(units // 2, width),
        down_sum=vmem(units, width),
        far_sems=DMA((10,)),
        over_send=DMA((4,)),
        over_recv=DMA((4,)),
        load_sem=DMA((len(inputs),)),
        save_sem=DMA((len(outputs),)),
        swap_send=DMA((13,)),
        swap_recv=DMA((13,)),
        out_side_send=DMA((2,)),
        out_side_recv=DMA((2,)),
        out_swap_send=DMA((1,)),
        out_swap_recv=DMA((2, Gather.count(chips, 2))),
        att_ssem=DMA((1,)),
        att_rsem=DMA((1,)),
        norm_ssem=DMA((1,)),
        norm_rsem=DMA((1,)),
    )
    for i, (count, pieces) in enumerate(((chips // 2, 4), (chips, 2), (chips // 2, 4))):
        scratch[f"gather{i}"] = Gather.sems(count, pieces)
    for i in range(3):
        scratch[f"scatter{i}"] = Scatter.sems(chips if i == 2 else chips // 2, 4)
    for i in range(8):
        scratch[f"exchange{i}"] = [DMA((1,)), DMA((1,))]
    flat, groups = [], []
    for name, entry in scratch.items():
        entries = entry if isinstance(entry, list) else [entry]
        groups.append((name, len(entries) if isinstance(entry, list) else 0))
        flat += entries

    def kernel(*refs):
        count = len(inputs) + 1 + len(outputs)
        names = [*inputs, "weight", *outputs]
        values = list(refs[:count])
        rest = list(refs[count:])
        for name, many in groups:
            names.append(name)
            if many:
                values.append(tuple(rest[:many]))
                rest = rest[many:]
            else:
                values.append(rest.pop(0))
        layer_kernel(names, *values)

    results = pl.pallas_call(
        kernel,
        out_shape=list(outputs.values()),
        in_specs=[ANY] * len(inputs) + [pl.BlockSpec(memory_space=pltpu.SMEM)],
        out_specs=[ANY] * len(outputs),
        scratch_shapes=flat,
        compiler_params=pltpu.CompilerParams(
            collective_id=1, has_side_effects=True, vmem_limit_bytes=61 * 2**20
        ),
    )(*inputs.values(), corpus_weight)
    results = hand_over(results)
    return (results[0][None], results[1][None], *results[2:])


def shifted(x, axis, by):
    size = lax.axis_size(axis)
    return lax.ppermute(x, axis, [(i, (i + by) % size) for i in range(size)])


def passed_along(value, axis, steps):
    count = lax.axis_size(axis)
    first, last = (max(0, -steps), min(count, count - steps))
    return lax.ppermute(value, axis, [(source, source + steps) for source in range(first, last)])


def layer_norm(values, gain, bias):
    center = values - jnp.mean(values, -1, keepdims=True)
    variance = jnp.mean(center * center, -1, keepdims=True)
    return center * lax.rsqrt(variance + 1e-05) * gain + bias


def rotate(values, position, direction):
    half_size = values.shape[-1] // 2
    freq = jnp.exp(
        jnp.arange(half_size).astype(jnp.float32) * (-2.0 * math.log(10000.0) / values.shape[-1])
    )
    angle = position[:, None] * freq[None, :]
    cosine = jnp.cos(angle)[:, None, :]
    sine = direction * jnp.sin(angle)[:, None, :]
    first = values[..., :half_size]
    second = values[..., half_size:]
    return jnp.concatenate([first * cosine - second * sine, first * sine + second * cosine], -1)


def gelu_tanh(values):
    return jax.nn.gelu(values, approximate=True)


def per_device(
    tokens, w_qkv, w_out, w_up, w_down, norm_gains, norm_biases, corpus_id, corpus_weight, cotangent
):
    full_qkv, full_out, full_up, full_down, gains_low, biases_low = (
        lax.all_gather(w_qkv, "seq", axis=0, tiled=True),
        lax.all_gather(w_out, "seq", axis=0, tiled=True),
        lax.all_gather(w_up, "seq", axis=0, tiled=True),
        lax.all_gather(w_down, "seq", axis=0, tiled=True),
        lax.all_gather(norm_gains, "seq", axis=1, tiled=True),
        lax.all_gather(norm_biases, "seq", axis=1, tiled=True),
    )
    gains = gains_low.astype(jnp.float32)
    biases = biases_low.astype(jnp.float32)
    seq_count, row_count, model_width = tokens.shape
    shape_heads = (seq_count, row_count, HEADS, HEAD_DIM)
    scale = HEAD_DIM ** (-0.5)
    cycle_size = lax.axis_size("seq")
    cycle_index = lax.axis_index("seq")
    query_pos = cycle_index * row_count + jnp.arange(row_count)
    position = query_pos.astype(jnp.float32)
    x_float = tokens.astype(jnp.float32)
    normed_low = layer_norm(x_float, gains[0], biases[0]).astype(jnp.bfloat16)
    qkv = jnp.einsum("std,de->ste", normed_low, full_qkv, preferred_element_type=jnp.float32)
    query_low = rotate(qkv[..., :model_width].reshape(shape_heads), position, 1.0).astype(
        jnp.bfloat16
    )
    key_low = rotate(
        qkv[..., model_width : 2 * model_width].reshape(shape_heads), position, 1.0
    ).astype(jnp.bfloat16)
    value_low = qkv[..., 2 * model_width :].reshape(shape_heads).astype(jnp.bfloat16)

    def block_scores(key_piece, key_pos):
        scores = (
            jnp.einsum("sqhd,skhd->shqk", query_low, key_piece, preferred_element_type=jnp.float32)
            * scale
        )
        allowed = query_pos[:, None] >= key_pos[None, :]
        return (scores, allowed)

    stat_shape = (seq_count, HEADS, row_count)
    key_piece = lax.all_gather(key_low, "seq", axis=1, tiled=True)
    value_piece = lax.all_gather(value_low, "seq", axis=1, tiled=True)
    key_pos = jnp.arange(key_piece.shape[1])
    run_max = jnp.full(stat_shape, -1e30, jnp.float32)
    scores, allowed = block_scores(key_piece, key_pos)
    new_max = jnp.maximum(run_max, jnp.max(jnp.where(allowed, scores, -1e30), -1))
    weights = jnp.where(allowed, jnp.exp(scores - new_max[..., None]), 0.0)
    run_sum = jnp.sum(weights, -1)
    total = jnp.einsum(
        "shqk,skhd->sqhd",
        weights.astype(jnp.bfloat16),
        value_piece,
        preferred_element_type=jnp.float32,
    )
    run_max, run_sum, total = (new_max, run_sum, total)
    log_sum = run_max + jnp.log(run_sum)
    attended = total / jnp.transpose(run_sum, (0, 2, 1))[..., None]
    attended_low = attended.reshape(seq_count, row_count, model_width).astype(jnp.bfloat16)
    proj = jnp.einsum("std,de->ste", attended_low, full_out, preferred_element_type=jnp.float32)
    hidden = x_float + layer_norm(proj, gains[1], biases[1])
    mid_low = layer_norm(hidden, gains[2], biases[2]).astype(jnp.bfloat16)
    up_proj = jnp.einsum("std,df->stf", mid_low, full_up, preferred_element_type=jnp.float32)
    act_low = gelu_tanh(up_proj).astype(jnp.bfloat16)
    down = jnp.einsum("stf,fd->std", act_low, full_down, preferred_element_type=jnp.float32)
    output = (hidden + layer_norm(down, gains[3], biases[3])).astype(jnp.bfloat16)
    matches = (corpus_id[..., None] == jnp.arange(corpus_weight.shape[0])).astype(jnp.float32)
    row_weight = jnp.sum(matches * corpus_weight, -1)
    grad_y = cotangent.astype(jnp.float32) * row_weight[..., None]
    _, down_back = jax.vjp(layer_norm, down, gains[3], biases[3])
    d_down, gain_three, bias_three = down_back(grad_y)
    d_down_low = d_down.astype(jnp.bfloat16)
    grad_down = jnp.einsum("stf,std->fd", act_low, d_down_low, preferred_element_type=jnp.float32)
    d_act = jnp.einsum("std,fd->stf", d_down_low, full_down, preferred_element_type=jnp.float32)
    _, gelu_back = jax.vjp(gelu_tanh, up_proj)
    d_up_low = gelu_back(d_act)[0].astype(jnp.bfloat16)
    grad_up = jnp.einsum("std,stf->df", mid_low, d_up_low, preferred_element_type=jnp.float32)
    d_mid = jnp.einsum("stf,df->std", d_up_low, full_up, preferred_element_type=jnp.float32)
    _, mid_back = jax.vjp(layer_norm, hidden, gains[2], biases[2])
    d_hidden_mid, gain_two, bias_two = mid_back(d_mid)
    d_hidden = grad_y + d_hidden_mid
    _, proj_back = jax.vjp(layer_norm, proj, gains[1], biases[1])
    d_proj, gain_one, bias_one = proj_back(d_hidden)
    d_proj_low = d_proj.astype(jnp.bfloat16)
    grad_out = jnp.einsum(
        "std,ste->de", attended_low, d_proj_low, preferred_element_type=jnp.float32
    )
    d_att_low = (
        jnp.einsum("ste,de->std", d_proj_low, full_out, preferred_element_type=jnp.float32)
        .astype(jnp.bfloat16)
        .reshape(shape_heads)
    )
    delta = jnp.transpose(jnp.sum(d_att_low.astype(jnp.float32) * attended, -1), (0, 2, 1))

    def contribute(d_query, key_piece, value_piece, d_key, d_value, owner):
        key_pos = owner * row_count + jnp.arange(row_count)
        query_sum = d_query
        key_sum = d_key
        value_sum = d_value
        scores, allowed = block_scores(key_piece, key_pos)
        probs = jnp.where(allowed, jnp.exp(scores - log_sum[..., None]), 0.0)
        value_sum = value_sum + jnp.einsum(
            "shqk,sqhd->skhd",
            probs.astype(jnp.bfloat16),
            d_att_low,
            preferred_element_type=jnp.float32,
        )
        d_probs = jnp.einsum(
            "sqhd,skhd->shqk", d_att_low, value_piece, preferred_element_type=jnp.float32
        )
        d_scores = (probs * (d_probs - delta[..., None]) * scale).astype(jnp.bfloat16)
        query_sum = query_sum + jnp.einsum(
            "shqk,skhd->sqhd", d_scores, key_piece, preferred_element_type=jnp.float32
        )
        key_sum = key_sum + jnp.einsum(
            "shqk,sqhd->skhd", d_scores, query_low, preferred_element_type=jnp.float32
        )
        return (query_sum, key_sum, value_sum)

    zeros_heads = jnp.zeros(shape_heads, jnp.float32)

    def pass_grads(d_key, d_value):
        return (
            shifted(d_key.astype(jnp.bfloat16), "seq", 1).astype(d_key.dtype),
            shifted(d_value.astype(jnp.bfloat16), "seq", 1).astype(d_value.dtype),
        )

    def cycle_turn(turn_index, state):
        d_query, key_piece, value_piece, d_key, d_value = state
        owner = (cycle_index - turn_index) % cycle_size
        d_query, d_key, d_value = contribute(d_query, key_piece, value_piece, d_key, d_value, owner)
        d_key, d_value = pass_grads(d_key, d_value)
        key_piece, value_piece = passed_along((key_piece, value_piece), "seq", 1)
        return (d_query, key_piece, value_piece, d_key, d_value)

    d_query, key_piece, value_piece, d_key, d_value = lax.fori_loop(
        0, cycle_size - 1, cycle_turn, (zeros_heads, key_low, value_low, zeros_heads, zeros_heads)
    )
    last_owner = (cycle_index + 1) % cycle_size
    d_query, d_key, d_value = contribute(
        d_query, key_piece, value_piece, d_key, d_value, last_owner
    )
    d_key, d_value = pass_grads(d_key, d_value)
    flat_shape = (seq_count, row_count, model_width)
    d_qkv_low = jnp.concatenate(
        [
            rotate(d_query, position, -1.0).reshape(flat_shape),
            rotate(d_key, position, -1.0).reshape(flat_shape),
            d_value.reshape(flat_shape),
        ],
        -1,
    ).astype(jnp.bfloat16)
    grad_qkv = jnp.einsum("std,ste->de", normed_low, d_qkv_low, preferred_element_type=jnp.float32)
    d_normed = jnp.einsum("ste,de->std", d_qkv_low, full_qkv, preferred_element_type=jnp.float32)
    _, input_back = jax.vjp(layer_norm, x_float, gains[0], biases[0])
    d_input, gain_zero, bias_zero = input_back(d_normed)
    grad_tokens = d_hidden + d_input
    grad_gains = jnp.stack([gain_zero, gain_one, gain_two, gain_three])
    grad_biases = jnp.stack([bias_zero, bias_one, bias_two, bias_three])
    all_grads = (grad_qkv, grad_out, grad_up, grad_down, grad_gains, grad_biases)
    pieces = (
        lax.psum_scatter(
            all_grads[0].astype(jnp.bfloat16), "seq", scatter_dimension=0, tiled=True
        ).astype(jnp.float32),
        lax.psum_scatter(
            all_grads[1].astype(jnp.bfloat16), "seq", scatter_dimension=0, tiled=True
        ).astype(jnp.float32),
        lax.psum_scatter(
            all_grads[2].astype(jnp.bfloat16), "seq", scatter_dimension=0, tiled=True
        ).astype(jnp.float32),
        lax.psum_scatter(
            all_grads[3].astype(jnp.bfloat16), "seq", scatter_dimension=0, tiled=True
        ).astype(jnp.float32),
        lax.psum_scatter(
            all_grads[4].astype(jnp.bfloat16), "seq", scatter_dimension=1, tiled=True
        ).astype(jnp.float32),
        lax.psum_scatter(
            all_grads[5].astype(jnp.bfloat16), "seq", scatter_dimension=1, tiled=True
        ).astype(jnp.float32),
    )
    shards = (
        lax.psum(pieces[0].astype(jnp.bfloat16), "dp").astype(jnp.float32),
        lax.psum(pieces[1].astype(jnp.bfloat16), "dp").astype(jnp.float32),
        lax.psum(pieces[2].astype(jnp.bfloat16), "dp").astype(jnp.float32),
        lax.psum(pieces[3].astype(jnp.bfloat16), "dp").astype(jnp.float32),
        lax.psum(pieces[4].astype(jnp.bfloat16), "dp").astype(jnp.float32),
        lax.psum(pieces[5].astype(jnp.bfloat16), "dp").astype(jnp.float32),
    )
    return (output, grad_tokens, shards[0], shards[1], shards[2], shards[3], shards[4], shards[5])


def solution(mesh):
    placed = (
        P("dp", "seq", None),
        P("seq", None),
        P("seq", None),
        P("seq", None),
        P("seq", None),
        P(None, "seq"),
        P(None, "seq"),
        P("dp", "seq"),
        P(),
        P("dp", "seq", None),
    )
    fits = mesh.shape["seq"] == HEADS and mesh.shape["dp"] == 2
    return jax.shard_map(
        split_heads if fits else per_device,
        mesh=mesh,
        in_specs=placed,
        out_specs=(
            P("dp", "seq", None),
            P("dp", "seq", None),
            P("seq", None),
            P("seq", None),
            P("seq", None),
            P("seq", None),
            P(None, "seq"),
            P(None, "seq"),
        ),
        check_vma=False,
    )
```
